32 devices in a mesh: section: 2 (over core), ctx: 4 (over y, x), tp: 4 (over z).
Axes of the slice: x: 2, y: 2, z: 4, core: 2. Of those that a mesh axis runs over, the one named last changes fastest.
Arguments:
- layer_inputs: bfloat16 [2, 6, 2, 1024, 1024], P('section', None, None, ('ctx', 'tp')), may hold values from -6 to 6
- out_grad: bfloat16 [6, 2, 1024, 1024], P(None, None, ('ctx', 'tp')), may hold values from -6 to 6
- src_seg: int32 [6, 2, 1024], P(None, None, 'ctx'), may hold values from 0 to 3, as said below
- tgt_seg: int32 [6, 2, 1024], P(None, None, 'ctx'), may hold values from 0 to 3, as said below
- qkv_weights: bfloat16 [2, 3, 1024, 1024], P('section', None, None, 'tp'), may hold values from -0.1875 to 0.1875
- out_weights: bfloat16 [2, 1024, 1024], P('section', None, 'tp'), may hold values from -0.75 to 0.75
- cross_weights: bfloat16 [2, 2, 1024, 1024], P('section', None, None, 'tp'), may hold values from -0.5 to 0.5, as said below
- ffn_in: bfloat16 [2, 1024, 4096], P('section', None, 'tp'), may hold values from -0.1875 to 0.1875
- ffn_out: bfloat16 [2, 4096, 1024], P('section', 'tp'), may hold values from -0.09375 to 0.09375
- adapter_in: bfloat16 [2, 1024, 512], P('section', None, 'tp'), may hold values from -0.1875 to 0.1875
- adapter_in_bias: bfloat16 [2, 512], P('section', 'tp'), may hold values from -4 to 4
- adapter_out: bfloat16 [2, 512, 1024], P('section', 'tp'), may hold values from -0.0625 to 0.0625
- adapter_out_bias: bfloat16 [2, 1024], P('section'), may hold values from -0.875 to 0.875
Outputs:
- layer_outputs: bfloat16 [2, 6, 2, 1024, 1024], P('section', None, None, ('ctx', 'tp'))
- input_grads: float32 [2, 6, 2, 1024, 1024], P('section', None, None, ('ctx', 'tp'))
- adapter_in_grad: float32 [2, 1024, 512], P('section', None, 'tp')
- adapter_in_bias_grad: float32 [2, 512], P('section', 'tp')
- adapter_out_grad: float32 [2, 512, 1024], P('section', 'tp')
- adapter_out_bias_grad: float32 [2, 1024], P('section')
The draws below stay inside these ranges and needn't reach their ends.
Inputs may be any that keep to these rules, and one draw needn't show every extreme that they name: Along each row the ids never fall. In every micro-batch one row, drawn, holds the single id 0 in both src_seg and tgt_seg; every other row holds each of the ids 0 to 3 in both arrays. Every id of a row of tgt_seg also appears in the same row of src_seg, and the reverse. `cross_weights`: independent entries of mean zero.
All inputs are finite; a program needn't handle non-finite values.
Results may differ from the reference program's by a relative error of at most 0.022.
Values may be sent and summed in bfloat16 or wider, within the bound.
A program may use at most 576 MiB of HBM per device.

```python
from functools import partial
import jax
import jax.numpy as jnp
from jax import lax

D = 1024
FF = 4096
HEAD = 64
HA = 512
L = 1024
ROWS = 2
MICRO = 6


def segment_pair(key):
    full_key = jax.random.fold_in(key, 101)
    full_row = jax.random.randint(full_key, (MICRO, 1, 1), 0, ROWS)
    row_index = jnp.arange(ROWS, dtype=jnp.int32)[None, :, None]
    position = jnp.arange(L, dtype=jnp.int32)[None, None, :]
    one_third = L // 3

    def cut_ids(salt_value):
        cut_key = jax.random.fold_in(key, salt_value)
        first_key, second_key, third_key = jax.random.split(cut_key, 3)
        first_cut = jax.random.randint(first_key, (MICRO, ROWS, 1), 1, one_third + 1)
        second_cut = jax.random.randint(second_key, (MICRO, ROWS, 1), one_third + 1, 2 * one_third + 1)
        last_cut = jax.random.randint(third_key, (MICRO, ROWS, 1), 2 * one_third + 1, L)
        segment = (position >= first_cut).astype(jnp.int32) + (position >= second_cut).astype(jnp.int32) + (position >= last_cut).astype(jnp.int32)
        return jnp.where(row_index == full_row, 0, segment).astype(jnp.int32)
    return (cut_ids(202), cut_ids(303))


def draw_src_seg(key, part):
    return segment_pair(key)[0]


def draw_tgt_seg(key, part):
    return segment_pair(key)[1]


def draw_cross_weights(key, part):
    standard = jax.random.truncated_normal(jax.random.fold_in(key, 404), -4.0, 4.0, (2, 2, D, D), jnp.float32)
    section_index = jnp.arange(2)[:, None, None, None]
    slot_index = jnp.arange(2)[None, :, None, None]
    factor = jnp.where((section_index == 1) & (slot_index == 1), 4.0, 1.0)
    scaled = jnp.clip(standard * factor * D ** (-0.5), -0.5, 0.5)
    return scaled.astype(jnp.bfloat16)


def block_scale(own_key, shape, pieces, smallest, top_value):
    gain = 1.0
    for dim, blocks in pieces:
        draws = jax.random.uniform(jax.random.fold_in(jax.random.fold_in(own_key, 6), dim), (blocks,), jnp.float32, smallest / len(pieces), top_value / len(pieces))
        gain = gain * jnp.repeat(jnp.exp(draws), shape[dim] // blocks).reshape((-1,) + (1,) * (len(shape) - 1 - dim))
    return gain


def bell_draw(own_key, extent, scale, bound, cuts=(), kind=jnp.bfloat16):
    entries = scale * jax.random.normal(own_key, extent, jnp.float32)
    if cuts:
        entries = entries * block_scale(own_key, extent, cuts, -0.22, 0.18)
    return jnp.clip(entries, -bound, bound).astype(kind)


def setup_inputs(seed: int = 0) -> dict:
    keys = jax.random.split(jax.random.key(seed), 14)
    layer_inputs = bell_draw(keys[0], (2, MICRO, ROWS, L, D), 1.0, 6.0, ((0, 2), (3, 16)))
    out_grad = bell_draw(keys[1], (MICRO, ROWS, L, D), 1.0, 6.0, ((2, 16),))
    src_seg = draw_src_seg(jax.random.fold_in(keys[13], 71), 0)
    tgt_seg = draw_tgt_seg(jax.random.fold_in(keys[13], 71), 0)
    qkv_weights = bell_draw(keys[4], (2, 3, D, D), D ** -0.5, 0.1875, ((0, 2), (3, 4)))
    out_weights = bell_draw(keys[5], (2, D, D), (D // 16) ** -0.5, 0.75, ((0, 2), (2, 4)))
    cross_weights = draw_cross_weights(jax.random.fold_in(keys[13], 71), 0)
    ffn_in = bell_draw(keys[7], (2, D, FF), D ** -0.5, 0.1875, ((0, 2), (2, 4)))
    ffn_out = bell_draw(keys[8], (2, FF, D), FF ** -0.5, 0.09375, ((0, 2), (1, 4)))
    adapter_in = bell_draw(keys[9], (2, D, HA), D ** -0.5, 0.1875, ((0, 2), (2, 4)))
    adapter_in_bias = bell_draw(keys[10], (2, HA), 1.0, 4.0, ((0, 2), (1, 4)))
    adapter_out = bell_draw(keys[11], (2, HA, D), (HA * 16) ** -0.5, 0.0625, ((0, 2), (1, 4)))
    adapter_out_bias = bell_draw(keys[12], (2, D), 0.15, 0.875, ((0, 2),))
    return dict(layer_inputs=layer_inputs, out_grad=out_grad, src_seg=src_seg, tgt_seg=tgt_seg, qkv_weights=qkv_weights, out_weights=out_weights, cross_weights=cross_weights, ffn_in=ffn_in, ffn_out=ffn_out, adapter_in=adapter_in, adapter_in_bias=adapter_in_bias, adapter_out=adapter_out, adapter_out_bias=adapter_out_bias)


@jax.custom_vjp
def low(v):
    return lax.optimization_barrier(v.astype(jnp.bfloat16)).astype(jnp.float32)

@jax.custom_vjp
def low_back(v):
    return v

def low_keep(v):
    return (low(v), None)

def low_pass(kept, grad):
    return (grad,)

def back_keep(v):
    return (v, None)

def back_low(kept, grad):
    return (low(grad),)
low.defvjp(low_keep, low_pass)
low_back.defvjp(back_keep, back_low)
eps = 1e-05
masked = -1e+30

def exact_dot(operand, matrix):
    return jnp.dot(operand, matrix, precision=lax.Precision.HIGHEST, preferred_element_type=jnp.float32)

def layer_norm(tensor):
    row_mean = lax.optimization_barrier(jnp.mean(tensor, axis=-1, keepdims=True))
    centered = tensor - row_mean
    return centered * lax.rsqrt(lax.optimization_barrier(jnp.mean(centered * centered, axis=-1, keepdims=True)) + eps)

def round_both(tensor):
    return low_back(low(tensor))

def attend_row(packed, causal):
    queries, keys_all, values, seg_query, seg_key = packed
    length_q = queries.shape[0]
    length_k = keys_all.shape[0]
    heads_q = queries.reshape(length_q, -1, HEAD)
    heads_k = keys_all.reshape(length_k, -1, HEAD)
    heads_v = values.reshape(length_k, -1, HEAD)
    scores = jnp.einsum('qhd,khd->hqk', heads_q, heads_k, precision=lax.Precision.HIGHEST) * HEAD ** (-0.5)
    scores = low_back(scores)
    allowed = seg_query[:, None] == seg_key[None, :]
    if causal:
        allowed = allowed & (jnp.arange(length_q)[:, None] >= jnp.arange(length_k)[None, :])
    scores = jnp.where(allowed[None], scores, masked)
    row_max = lax.optimization_barrier(jnp.max(scores, axis=-1, keepdims=True))
    weights = jnp.exp(scores - row_max)
    soft_weights = weights / lax.optimization_barrier(jnp.sum(weights, axis=-1, keepdims=True))
    attn_out = jnp.einsum('hqk,khd->qhd', low(soft_weights), heads_v, precision=lax.Precision.HIGHEST)
    return attn_out.reshape(length_q, -1)

def attend(queries, keys_all, values, seg_query, seg_key, causal):
    row_fn = jax.checkpoint(partial(attend_row, causal=causal))
    return lax.map(row_fn, (queries, keys_all, values, seg_query, seg_key))

def self_block(inputs, w_qkv, w_out, segments, causal):
    row_shape = inputs.shape
    flat_rows = low(inputs).reshape(-1, row_shape[-1])
    queries = round_both(exact_dot(flat_rows, w_qkv[0])).reshape(row_shape)
    keys_all = round_both(exact_dot(flat_rows, w_qkv[1])).reshape(row_shape)
    values = round_both(exact_dot(flat_rows, w_qkv[2])).reshape(row_shape)
    attn_out = round_both(attend(queries, keys_all, values, segments, segments, causal)).reshape(-1, row_shape[-1])
    branch = low_back(exact_dot(attn_out, w_out.T))
    return layer_norm(inputs + branch.reshape(row_shape))

def cross_block(hidden, mem_keys, mem_values, w_query, w_back, seg_query, seg_key):
    row_shape = hidden.shape
    flat_rows = low(hidden).reshape(-1, row_shape[-1])
    queries = round_both(exact_dot(flat_rows, w_query)).reshape(row_shape)
    attn_out = round_both(attend(queries, mem_keys, mem_values, seg_query, seg_key, False)).reshape(-1, row_shape[-1])
    branch = low_back(exact_dot(attn_out, w_back.T))
    return layer_norm(hidden + branch.reshape(row_shape))

def tail(hidden, w_in, w_out, a_in, b_in, a_out, b_out):
    row_shape = hidden.shape
    flat_rows = low(hidden).reshape(-1, row_shape[-1])
    inner = low_back(exact_dot(flat_rows, w_in))
    gelu_out = low(jax.nn.gelu(inner, approximate=False))
    adapter_pre = low_back(exact_dot(flat_rows, a_in) + b_in)
    gated = low(jax.nn.silu(adapter_pre))
    branch = low_back(exact_dot(gelu_out, w_out) + 4.0 * (exact_dot(gated, a_out) + b_out))
    return layer_norm(hidden + branch.reshape(row_shape))

def reference(layer_inputs, out_grad, src_seg, tgt_seg, qkv_weights, out_weights, cross_weights, ffn_in, ffn_out, adapter_in, adapter_in_bias, adapter_out, adapter_out_bias):
    row_count = MICRO * ROWS
    src_ids = src_seg.reshape(row_count, L)
    tgt_ids = tgt_seg.reshape(row_count, L)
    qkv_all = qkv_weights.astype(jnp.float32)
    out_all = out_weights.astype(jnp.float32)
    cross_all = cross_weights.astype(jnp.float32)
    ffn_first = ffn_in.astype(jnp.float32)
    ffn_second = ffn_out.astype(jnp.float32)

    def forward(inputs, a_in, b_in, a_out, b_out):
        source = inputs[0].reshape(row_count, L, D)
        target = inputs[1].reshape(row_count, L, D)
        encoder_mid = self_block(source, qkv_all[0], out_all[0], src_ids, False)
        encoded = tail(encoder_mid, ffn_first[0], ffn_second[0], a_in[0], b_in[0], a_out[0], b_out[0])
        flat_rows = low(encoded).reshape(-1, D)
        mem_keys = round_both(exact_dot(flat_rows, cross_all[0, 0])).reshape(encoded.shape)
        mem_values = round_both(exact_dot(flat_rows, cross_all[0, 1])).reshape(encoded.shape)
        decoder_mid = self_block(target, qkv_all[1], out_all[1], tgt_ids, True)
        decoder_cross = cross_block(decoder_mid, mem_keys, mem_values, cross_all[1, 0], cross_all[1, 1], tgt_ids, src_ids)
        decoded = tail(decoder_cross, ffn_first[1], ffn_second[1], a_in[1], b_in[1], a_out[1], b_out[1])
        return jnp.stack([encoded, decoded]).reshape(inputs.shape)
    primal = (layer_inputs.astype(jnp.float32), adapter_in.astype(jnp.float32), adapter_in_bias.astype(jnp.float32), adapter_out.astype(jnp.float32), adapter_out_bias.astype(jnp.float32))
    outputs, pull_back = jax.vjp(forward, *primal)
    cotangent = jnp.stack([jnp.zeros(out_grad.shape, jnp.float32), out_grad.astype(jnp.float32)])
    gradients = pull_back(cotangent)
    return (outputs.astype(jnp.bfloat16), gradients[0], gradients[1], gradients[2], gradients[3], gradients[4])
```

```python
import functools

import jax
import jax.numpy as jnp
from jax import lax
from jax.experimental import pallas as pl
from jax.experimental.pallas import tpu as pltpu
from jax.sharding import PartitionSpec as P

HEAD = 64
SCALE = HEAD**-0.5
EPS = 1e-05
MASKED = -1e30
F32 = jnp.float32
BF16 = jnp.bfloat16


def swap(value):
    return lax.ppermute(value, "section", [(0, 1), (1, 0)])


def dot_nt(left, right, **kw):
    return lax.dot_general(
        left, right, (((1,), (1,)), ((), ())), preferred_element_type=F32, **kw
    )


def dot_nn(left, right):
    return lax.dot_general(
        left, right, (((1,), (0,)), ((), ())), preferred_element_type=F32
    )


def dot_tn(left, right):
    return lax.dot_general(
        left, right, (((0,), (0,)), ((), ())), preferred_element_type=F32
    )


def attn_fwd_kernel(
    causal, q_ref, ko_ref, kx_ref, vo_ref, vx_ref, qi_ref, ki_ref, o_ref, lse_ref
):
    length = q_ref.shape[1]
    heads = q_ref.shape[2] // HEAD
    block = length // 2
    segq = qi_ref[:, 0:1]
    posq = qi_ref[:, 1:2]
    for h in range(heads):
        cols = slice(h * HEAD, (h + 1) * HEAD)
        for b in range(2):
            rows = slice(b * block, (b + 1) * block)
            span = (b + 1) * block if causal else length
            q = q_ref[0, rows, cols] * jnp.asarray(SCALE, BF16)
            parts = []
            for kk, (k_ref, i) in enumerate(((ko_ref, 0), (kx_ref, 2))):
                s = dot_nt(q, k_ref[0, :span, cols])
                ok = segq[rows] == ki_ref[i : i + 1, :span]
                if causal:
                    ok = ok & (posq[rows] >= ki_ref[i + 1 : i + 2, :span])
                parts.append(jnp.where(ok, s, MASKED))
            top = jnp.maximum(
                jnp.max(parts[0], axis=1, keepdims=True),
                jnp.max(parts[1], axis=1, keepdims=True),
            )
            ex = [jnp.exp(p - top) for p in parts]
            total = jnp.sum(ex[0], axis=1, keepdims=True) + jnp.sum(
                ex[1], axis=1, keepdims=True
            )
            out = dot_nn(ex[0].astype(BF16), vo_ref[0, :span, cols]) + dot_nn(
                ex[1].astype(BF16), vx_ref[0, :span, cols]
            )
            o_ref[0, rows, cols] = (out / total).astype(BF16)
            lse = top + jnp.log(total)
            lse_ref[0, h : h + 1, rows] = jnp.broadcast_to(lse, (block, 128)).T[0:1]


def attention_forward(q, k_own, k_oth, v_own, v_oth, qi, ki, causal):
    groups, length, width = q.shape
    heads = width // HEAD
    spec = pl.BlockSpec((1, length, width), lambda t: (t, 0, 0))
    return pl.pallas_call(
        functools.partial(attn_fwd_kernel, causal),
        grid=(groups,),
        in_specs=[spec] * 5
        + [
            pl.BlockSpec(qi.shape, lambda t: (0, 0)),
            pl.BlockSpec(ki.shape, lambda t: (0, 0)),
        ],
        out_specs=[spec, pl.BlockSpec((1, heads, length), lambda t: (t, 0, 0))],
        out_shape=[
            jax.ShapeDtypeStruct(q.shape, BF16),
            jax.ShapeDtypeStruct((groups, heads, length), F32),
        ],
        compiler_params=pltpu.CompilerParams(vmem_limit_bytes=48 * 2**20),
        name="attn_fwd",
    )(q, k_own, k_oth, v_own, v_oth, qi, ki)


def attn_bwd_kernel(
    causal,
    q_ref,
    ko_ref,
    kx_ref,
    vo_ref,
    vx_ref,
    o_ref,
    do_ref,
    lse_ref,
    qi_ref,
    ki_ref,
    dq_ref,
    dko_ref,
    dkx_ref,
    dvo_ref,
    dvx_ref,
):
    length = q_ref.shape[1]
    heads = q_ref.shape[2] // HEAD
    block = length // 2
    segq = qi_ref[0:1, :]
    posq = qi_ref[1:2, :]
    ones = jnp.ones((8, HEAD), F32)
    for h in range(heads):
        cols = slice(h * HEAD, (h + 1) * HEAD)
        q_all = q_ref[0, :, cols] * jnp.asarray(SCALE, BF16)
        do_all = do_ref[0, :, cols]
        prod = do_all.astype(F32) * o_ref[0, :, cols].astype(F32)
        delta = dot_nt(ones, prod, precision=lax.Precision.HIGHEST)[0:1]
        lse = lse_ref[0, h : h + 1, :]
        dq = [jnp.zeros((block, HEAD), F32), jnp.zeros((block, HEAD), F32)]
        for k_ref, v_ref, dk_ref, dv_ref, i in (
            (ko_ref, vo_ref, dko_ref, dvo_ref, 0),
            (kx_ref, vx_ref, dkx_ref, dvx_ref, 2),
        ):
            for b in range(2):
                rows = slice(b * block, (b + 1) * block)
                first = b * block if causal else 0
                q = q_all[first:]
                do = do_all[first:]
                k = k_ref[0, rows, cols]
                s = dot_nt(k, q)
                ok = ki_ref[rows, i : i + 1] == segq[:, first:]
                if causal:
                    ok = ok & (posq[:, first:] >= ki_ref[rows, i + 1 : i + 2])
                p = jnp.where(ok, jnp.exp(s - lse[:, first:]), 0.0)
                dp = dot_nt(v_ref[0, rows, cols], do)
                ds = (p * (dp - delta[:, first:])).astype(BF16)
                dv_ref[0, rows, cols] = dot_nn(p.astype(BF16), do).astype(BF16)
                dk_ref[0, rows, cols] = dot_nn(ds, q).astype(BF16)
                part = dot_tn(ds, k)
                if first:
                    dq[1] = dq[1] + part
                else:
                    dq[0] = dq[0] + part[:block]
                    dq[1] = dq[1] + part[block:]
        dq_ref[0, :block, cols] = (dq[0] * SCALE).astype(BF16)
        dq_ref[0, block:, cols] = (dq[1] * SCALE).astype(BF16)


def attention_backward(q, k_own, k_oth, v_own, v_oth, o, do, lse, qi, ki, causal):
    groups, length, width = q.shape
    heads = width // HEAD
    spec = pl.BlockSpec((1, length, width), lambda t: (t, 0, 0))
    return pl.pallas_call(
        functools.partial(attn_bwd_kernel, causal),
        grid=(groups,),
        in_specs=[spec] * 7
        + [
            pl.BlockSpec((1, heads, length), lambda t: (t, 0, 0)),
            pl.BlockSpec(qi.shape, lambda t: (0, 0)),
            pl.BlockSpec(ki.shape, lambda t: (0, 0)),
        ],
        out_specs=[spec] * 5,
        out_shape=[jax.ShapeDtypeStruct(q.shape, BF16)] * 5,
        compiler_params=pltpu.CompilerParams(vmem_limit_bytes=48 * 2**20),
        name="attn_bwd",
    )(q, k_own, k_oth, v_own, v_oth, o, do, lse, qi, ki)


def norm(value):
    mean = jnp.mean(value, axis=-1, keepdims=True)
    centered = value - mean
    rstd = lax.rsqrt(jnp.mean(centered * centered, axis=-1, keepdims=True) + EPS)
    return centered * rstd, rstd


def norm_back(normed, rstd, grad):
    return rstd * (
        grad
        - jnp.mean(grad, axis=-1, keepdims=True)
        - normed * jnp.mean(grad * normed, axis=-1, keepdims=True)
    )


def project(rows, weight):
    return jnp.einsum("pk,tkm->tpm", rows, weight, preferred_element_type=F32)


def unproject(blocks, weight):
    return jnp.einsum("tpm,tkm->pk", blocks, weight, preferred_element_type=F32)


def self_forward(rows_bf, rows, w_attn, ids, causal):
    kv = [project(rows_bf, w_attn[:, j]).astype(BF16) for j in (1, 2)]
    other = swap(jnp.stack(kv))
    q = project(rows_bf, w_attn[:, 0]).astype(BF16)
    keys = (kv[0], other[0], kv[1], other[1])
    o, lse = attention_forward(q, *keys, *ids[0], causal)
    h, rstd = norm(rows + unproject(o, w_attn[:, 3]))
    return h, (q, keys, o, lse, h, rstd)


def attend_back(q, keys, o, do, lse, ids, causal):
    dq, dko, dkx, dvo, dvx = attention_backward(q, *keys, o, do, lse, *ids[1], causal)
    other = swap(jnp.stack([dkx, dvx])).astype(F32)
    dk = (dko.astype(F32) + other[0]).astype(BF16)
    dv = (dvo.astype(F32) + other[1]).astype(BF16)
    return dq, dk, dv


def self_backward(grad, kept, w_attn, ids, causal):
    q, keys, o, lse, h, rstd = kept
    dpre = norm_back(h, rstd, grad)
    do = project(dpre.astype(BF16), w_attn[:, 3]).astype(BF16)
    dq, dk, dv = attend_back(q, keys, o, do, lse, ids, causal)
    return (
        unproject(dq, w_attn[:, 0])
        + unproject(dk, w_attn[:, 1])
        + unproject(dv, w_attn[:, 2])
        + dpre
    )


def tail_forward(h, tail_w):
    w_in, w_out, a_in, b_in, a_out, b_out = tail_w
    rows = h.astype(BF16)
    inner = project(rows, w_in)
    phi = 0.5 * (1.0 + lax.erf(inner * 0.7071067811865476))
    g = (inner * phi).astype(BF16)
    slope = phi + inner * jnp.exp(inner * inner * -0.5) * 0.3989422804014327
    pre = project(rows, a_in) + b_in.astype(F32)[:, None, :]
    sig = jax.nn.sigmoid(pre)
    s = (pre * sig).astype(BF16)
    a_slope = sig * (1.0 + pre * (1.0 - sig))
    total = jnp.einsum("tpm,tmk->pk", g, w_out, preferred_element_type=F32)
    total += 4.0 * (
        jnp.einsum("tpm,tmk->pk", s, a_out, preferred_element_type=F32)
        + b_out.astype(F32)
    )
    y, rstd = norm(h + total)
    return y, (rows, slope.astype(BF16), s, a_slope.astype(BF16), y, rstd)


def tail_backward(grad, kept, tail_w):
    w_in, w_out, a_in, b_in, a_out, b_out = tail_w
    rows, slope, s, a_slope, y, rstd = kept
    dpre = norm_back(y, rstd, grad)
    db = dpre.astype(BF16)
    dg = jnp.einsum("pk,tmk->tpm", db, w_out, preferred_element_type=F32)
    df = (dg * slope.astype(F32)).astype(BF16)
    ds = 4.0 * jnp.einsum("pk,tmk->tpm", db, a_out, preferred_element_type=F32)
    du = (ds * a_slope.astype(F32)).astype(BF16)
    terms = (
        jnp.einsum("pk,tpm->tkm", rows, du, preferred_element_type=F32),
        jnp.sum(du.astype(F32), axis=1),
        4.0 * jnp.einsum("tpm,pk->tmk", s, db, preferred_element_type=F32),
        4.0 * jnp.sum(db.astype(F32), axis=0),
    )
    return unproject(df, w_in) + unproject(du, a_in) + dpre, terms


def gather_weights(shards):
    def one(shard):
        return lax.all_gather(lax.all_gather(shard, "tp"), "section")

    return [one(shard) for shard in shards]


def spread(blocks):
    chips = lax.axis_size("ctx") * lax.axis_size("tp")
    kinds, rows, part, width = blocks.shape
    blocks = jnp.pad(blocks, ((0, 0), (0, chips - rows), (0, 0), (0, 0)))
    moved = lax.all_to_all(
        jnp.moveaxis(blocks, 1, 0), ("ctx", "tp"), 0, 0, tiled=True
    )
    return jnp.moveaxis(moved, 0, 1).reshape(kinds, chips * part, width)


def collect(tokens, rows):
    chips = lax.axis_size("ctx") * lax.axis_size("tp")
    kinds, length, width = tokens.shape
    part = length // chips
    blocks = jnp.moveaxis(tokens.reshape(kinds, chips, part, width), 1, 0)
    moved = lax.all_to_all(blocks, ("ctx", "tp"), 0, 0, tiled=True)
    return jnp.moveaxis(moved, 0, 1)[:, :rows]


def per_device(
    layer_inputs,
    out_grad,
    src_seg,
    tgt_seg,
    qkv_weights,
    out_weights,
    cross_weights,
    ffn_in,
    ffn_out,
    adapter_in,
    adapter_in_bias,
    adapter_out,
    adapter_out_bias,
):
    core = lax.axis_index("section")
    is_first = core == 0
    tp = lax.axis_size("tp")
    chips = lax.axis_size("ctx") * tp
    chip = lax.axis_index("ctx") * tp + lax.axis_index("tp")
    _, micro, per_micro, part, width = layer_inputs.shape
    row_count = micro * per_micro
    half = part // 2
    length = half * chips

    def pick(first, second):
        return jnp.where(is_first, first, second)

    x = layer_inputs.reshape(row_count, part, width)
    low, high = x[:, :half], x[:, half:]
    other = swap(pick(high, low))
    grads = out_grad.reshape(row_count, part, width)
    stacked = jnp.stack(
        [pick(low, other), pick(other, high), pick(grads[:, :half], grads[:, half:])]
    )
    source, target, cotangent = spread(stacked)

    def ids_of(segments):
        flat = lax.all_gather(
            segments.reshape(row_count, -1), "ctx", axis=1, tiled=True
        )
        row = lax.dynamic_index_in_dim(
            flat, jnp.minimum(chip, row_count - 1), 0, keepdims=False
        )
        return row.reshape(chips, 2, half)

    index = jnp.arange(length, dtype=jnp.int32)
    place = (index // half) * part + index % half

    def cut(seg, which):
        own = lax.dynamic_index_in_dim(seg, which, 1, keepdims=False).reshape(length)
        return own, place + which * half

    src_ids, tgt_ids = ids_of(src_seg), ids_of(tgt_seg)

    def id_arrays(seg_q, seg_k):
        qi = jnp.stack(cut(seg_q, core))
        ki = jnp.stack(cut(seg_k, core) + cut(seg_k, 1 - core))
        return (qi.T, ki), (qi, ki.T)

    enc_ids = id_arrays(src_ids, src_ids)
    dec_ids = id_arrays(tgt_ids, tgt_ids)
    cross_ids = id_arrays(tgt_ids, src_ids)

    w_attn, w_cross, w_in, w_out, a_in, b_in, a_out = gather_weights(
        [
            jnp.concatenate([qkv_weights[0], out_weights], axis=0),
            cross_weights[0],
            ffn_in[0],
            ffn_out[0],
            adapter_in[0],
            adapter_in_bias[0],
            adapter_out[0],
        ]
    )
    b_out = lax.all_gather(adapter_out_bias[0], "section")
    tails = [
        (w_in[e], w_out[e], a_in[e], b_in[e], a_out[e], b_out[e]) for e in range(2)
    ]

    enc_mid, enc_self = self_forward(
        source, source.astype(F32), w_attn[0], enc_ids, False
    )
    encoded, enc_tail = tail_forward(enc_mid, tails[0])
    encoded_bf = encoded.astype(BF16)
    memory = [project(encoded_bf, w_cross[0, :, j]).astype(BF16) for j in range(2)]
    memory_other = swap(jnp.stack(memory))
    mem_keys = (memory[0], memory_other[0], memory[1], memory_other[1])

    dec_mid, dec_self = self_forward(
        target, target.astype(F32), w_attn[1], dec_ids, True
    )
    queries = project(dec_mid.astype(BF16), w_cross[1, :, 0]).astype(BF16)
    cross_o, cross_lse = attention_forward(
        queries, *mem_keys, *cross_ids[0], False
    )
    second, second_rstd = norm(dec_mid + unproject(cross_o, w_cross[1, :, 1]))
    decoded, dec_tail = tail_forward(second, tails[1])

    grad_second, dec_terms = tail_backward(cotangent.astype(F32), dec_tail, tails[1])
    grad_cross = norm_back(second, second_rstd, grad_second)
    do = project(grad_cross.astype(BF16), w_cross[1, :, 1]).astype(BF16)
    dqc, dmk, dmv = attend_back(
        queries, mem_keys, cross_o, do, cross_lse, cross_ids, False
    )
    grad_first = unproject(dqc, w_cross[1, :, 0]) + grad_cross
    grad_target = self_backward(grad_first, dec_self, w_attn[1], dec_ids, True)

    grad_encoded = unproject(dmk, w_cross[0, :, 0]) + unproject(dmv, w_cross[0, :, 1])
    grad_mid, enc_terms = tail_backward(grad_encoded, enc_tail, tails[0])
    grad_source = self_backward(grad_mid, enc_self, w_attn[0], enc_ids, False)

    has_row = chip < row_count

    def total(enc_term, dec_term):
        enc_term = jnp.where(has_row, enc_term, 0.0).astype(BF16)
        dec_term = jnp.where(has_row, dec_term, 0.0).astype(BF16)
        got = swap(pick(dec_term, enc_term))
        return (pick(enc_term, dec_term).astype(F32) + got.astype(F32)).astype(BF16)

    sums = [total(e, d) for e, d in zip(enc_terms, dec_terms)]
    scattered = [
        lax.psum_scatter(v, "tp", scatter_dimension=0, tiled=False) for v in sums[:3]
    ]
    scattered = [lax.psum(v, "ctx").astype(F32) for v in scattered]
    bias_sum = lax.psum(sums[3], ("ctx", "tp")).astype(F32)

    results = jnp.stack(
        [
            encoded_bf,
            decoded.astype(BF16),
            grad_source.astype(BF16),
            grad_target.astype(BF16),
        ]
    )
    placed = collect(results, row_count)

    def join(enc_part, dec_part):
        mine = pick(enc_part, dec_part)
        got = swap(pick(dec_part, enc_part))
        return jnp.concatenate([pick(mine, got), pick(got, mine)], axis=1)

    outs = join(placed[0], placed[1]).reshape(layer_inputs.shape)
    grads = join(placed[2], placed[3]).astype(F32).reshape(layer_inputs.shape)
    return (
        outs,
        grads,
        scattered[0][None],
        scattered[1][None],
        scattered[2][None],
        bias_sum[None],
    )


def solution(mesh):
    return jax.shard_map(
        per_device,
        mesh=mesh,
        in_specs=(
            P("section", None, None, ("ctx", "tp"), None),
            P(None, None, ("ctx", "tp"), None),
            P(None, None, "ctx"),
            P(None, None, "ctx"),
            P("section", None, None, "tp"),
            P("section", None, "tp"),
            P("section", None, None, "tp"),
            P("section", None, "tp"),
            P("section", "tp", None),
            P("section", None, "tp"),
            P("section", "tp"),
            P("section", "tp", None),
            P("section", None),
        ),
        out_specs=(
            P("section", None, None, ("ctx", "tp"), None),
            P("section", None, None, ("ctx", "tp"), None),
            P("section", None, "tp"),
            P("section", "tp"),
            P("section", "tp", None),
            P("section", None),
        ),
        check_vma=False,
    )
```

```python
import functools

import jax
import jax.numpy as jnp
from jax import lax
from jax.experimental import pallas as pl
from jax.experimental.pallas import tpu as pltpu
from jax.sharding import PartitionSpec as P

HEAD = 64
SCALE = HEAD**-0.5
EPS = 1e-05
MASKED = -1e30
F32 = jnp.float32
BF16 = jnp.bfloat16


def swap(value):
    return lax.ppermute(value, "section", [(0, 1), (1, 0)])


def dot_nt(left, right, **kw):
    return lax.dot_general(
        left, right, (((1,), (1,)), ((), ())), preferred_element_type=F32, **kw
    )


def dot_nn(left, right):
    return lax.dot_general(
        left, right, (((1,), (0,)), ((), ())), preferred_element_type=F32
    )


def dot_tn(left, right):
    return lax.dot_general(
        left, right, (((0,), (0,)), ((), ())), preferred_element_type=F32
    )


def attn_fwd_kernel(
    causal, q_ref, ko_ref, kx_ref, vo_ref, vx_ref, qi_ref, ki_ref, o_ref, lse_ref
):
    length = q_ref.shape[1]
    heads = q_ref.shape[2] // HEAD
    block = length // 2
    segq = qi_ref[:, 0:1]
    posq = qi_ref[:, 1:2]
    for h in range(heads):
        cols = slice(h * HEAD, (h + 1) * HEAD)
        for b in range(2):
            rows = slice(b * block, (b + 1) * block)
            span = (b + 1) * block if causal else length
            q = q_ref[0, rows, cols] * jnp.asarray(SCALE, BF16)
            parts = []
            for kk, (k_ref, i) in enumerate(((ko_ref, 0), (kx_ref, 2))):
                s = dot_nt(q, k_ref[0, :span, cols])
                ok = segq[rows] == ki_ref[i : i + 1, :span]
                if causal:
                    ok = ok & (posq[rows] >= ki_ref[i + 1 : i + 2, :span])
                parts.append(jnp.where(ok, s, MASKED))
            top = jnp.maximum(
                jnp.max(parts[0], axis=1, keepdims=True),
                jnp.max(parts[1], axis=1, keepdims=True),
            )
            ex = [jnp.exp(p - top) for p in parts]
            total = jnp.sum(ex[0], axis=1, keepdims=True) + jnp.sum(
                ex[1], axis=1, keepdims=True
            )
            out = dot_nn(ex[0].astype(BF16), vo_ref[0, :span, cols]) + dot_nn(
                ex[1].astype(BF16), vx_ref[0, :span, cols]
            )
            o_ref[0, rows, cols] = (out / total).astype(BF16)
            lse = top + jnp.log(total)
            lse_ref[0, h : h + 1, rows] = jnp.broadcast_to(lse, (block, 128)).T[0:1]


def attention_forward(q, k_own, k_oth, v_own, v_oth, qi, ki, causal):
    groups, length, width = q.shape
    heads = width // HEAD
    spec = pl.BlockSpec((1, length, width), lambda t: (t, 0, 0))
    return pl.pallas_call(
        functools.partial(attn_fwd_kernel, causal),
        grid=(groups,),
        in_specs=[spec] * 5
        + [
            pl.BlockSpec(qi.shape, lambda t: (0, 0)),
            pl.BlockSpec(ki.shape, lambda t: (0, 0)),
        ],
        out_specs=[spec, pl.BlockSpec((1, heads, length), lambda t: (t, 0, 0))],
        out_shape=[
            jax.ShapeDtypeStruct(q.shape, BF16),
            jax.ShapeDtypeStruct((groups, heads, length), F32),
        ],
        compiler_params=pltpu.CompilerParams(vmem_limit_bytes=48 * 2**20),
        name="attn_fwd",
    )(q, k_own, k_oth, v_own, v_oth, qi, ki)


def attn_bwd_kernel(
    causal,
    q_ref,
    ko_ref,
    kx_ref,
    vo_ref,
    vx_ref,
    o_ref,
    do_ref,
    lse_ref,
    qi_ref,
    ki_ref,
    dq_ref,
    dko_ref,
    dkx_ref,
    dvo_ref,
    dvx_ref,
):
    length = q_ref.shape[1]
    heads = q_ref.shape[2] // HEAD
    block = length // 2
    segq = qi_ref[0:1, :]
    posq = qi_ref[1:2, :]
    ones = jnp.ones((8, HEAD), F32)
    for h in range(heads):
        cols = slice(h * HEAD, (h + 1) * HEAD)
        q_all = q_ref[0, :, cols] * jnp.asarray(SCALE, BF16)
        do_all = do_ref[0, :, cols]
        prod = do_all.astype(F32) * o_ref[0, :, cols].astype(F32)
        delta = dot_nt(ones, prod, precision=lax.Precision.HIGHEST)[0:1]
        lse = lse_ref[0, h : h + 1, :]
        dq = [jnp.zeros((block, HEAD), F32), jnp.zeros((block, HEAD), F32)]
        for k_ref, v_ref, dk_ref, dv_ref, i in (
            (ko_ref, vo_ref, dko_ref, dvo_ref, 0),
            (kx_ref, vx_ref, dkx_ref, dvx_ref, 2),
        ):
            for b in range(2):
                rows = slice(b * block, (b + 1) * block)
                first = b * block if causal else 0
                q = q_all[first:]
                do = do_all[first:]
                k = k_ref[0, rows, cols]
                s = dot_nt(k, q)
                ok = ki_ref[rows, i : i + 1] == segq[:, first:]
                if causal:
                    ok = ok & (posq[:, first:] >= ki_ref[rows, i + 1 : i + 2])
                p = jnp.where(ok, jnp.exp(s - lse[:, first:]), 0.0)
                dp = dot_nt(v_ref[0, rows, cols], do)
                ds = (p * (dp - delta[:, first:])).astype(BF16)
                dv_ref[0, rows, cols] = dot_nn(p.astype(BF16), do).astype(BF16)
                dk_ref[0, rows, cols] = dot_nn(ds, q).astype(BF16)
                part = dot_tn(ds, k)
                if first:
                    dq[1] = dq[1] + part
                else:
                    dq[0] = dq[0] + part[:block]
                    dq[1] = dq[1] + part[block:]
        dq_ref[0, :block, cols] = (dq[0] * SCALE).astype(BF16)
        dq_ref[0, block:, cols] = (dq[1] * SCALE).astype(BF16)


def attention_backward(q, k_own, k_oth, v_own, v_oth, o, do, lse, qi, ki, causal):
    groups, length, width = q.shape
    heads = width // HEAD
    spec = pl.BlockSpec((1, length, width), lambda t: (t, 0, 0))
    return pl.pallas_call(
        functools.partial(attn_bwd_kernel, causal),
        grid=(groups,),
        in_specs=[spec] * 7
        + [
            pl.BlockSpec((1, heads, length), lambda t: (t, 0, 0)),
            pl.BlockSpec(qi.shape, lambda t: (0, 0)),
            pl.BlockSpec(ki.shape, lambda t: (0, 0)),
        ],
        out_specs=[spec] * 5,
        out_shape=[jax.ShapeDtypeStruct(q.shape, BF16)] * 5,
        compiler_params=pltpu.CompilerParams(vmem_limit_bytes=48 * 2**20),
        name="attn_bwd",
    )(q, k_own, k_oth, v_own, v_oth, o, do, lse, qi, ki)


def norm(value):
    mean = jnp.mean(value, axis=-1, keepdims=True)
    centered = value - mean
    rstd = lax.rsqrt(jnp.mean(centered * centered, axis=-1, keepdims=True) + EPS)
    return centered * rstd, rstd


def norm_back(normed, rstd, grad):
    return rstd * (
        grad
        - jnp.mean(grad, axis=-1, keepdims=True)
        - normed * jnp.mean(grad * normed, axis=-1, keepdims=True)
    )


def project(rows, weight):
    return jnp.einsum("pk,tkm->tpm", rows, weight, preferred_element_type=F32)


def unproject(blocks, weight):
    return jnp.einsum("tpm,tkm->pk", blocks, weight, preferred_element_type=F32)


def self_forward(rows_bf, rows, w_attn, ids, causal):
    kv = [project(rows_bf, w_attn[:, j]).astype(BF16) for j in (1, 2)]
    other = swap(jnp.stack(kv))
    q = project(rows_bf, w_attn[:, 0]).astype(BF16)
    keys = (kv[0], other[0], kv[1], other[1])
    o, lse = attention_forward(q, *keys, *ids[0], causal)
    h, rstd = norm(rows + unproject(o, w_attn[:, 3]))
    return h, (q, keys, o, lse, h, rstd)


def attend_back(q, keys, o, do, lse, ids, causal):
    dq, dko, dkx, dvo, dvx = attention_backward(q, *keys, o, do, lse, *ids[1], causal)
    other = swap(jnp.stack([dkx, dvx])).astype(F32)
    dk = (dko.astype(F32) + other[0]).astype(BF16)
    dv = (dvo.astype(F32) + other[1]).astype(BF16)
    return dq, dk, dv


def self_backward(grad, kept, w_attn, ids, causal):
    q, keys, o, lse, h, rstd = kept
    dpre = norm_back(h, rstd, grad)
    do = project(dpre.astype(BF16), w_attn[:, 3]).astype(BF16)
    dq, dk, dv = attend_back(q, keys, o, do, lse, ids, causal)
    return (
        unproject(dq, w_attn[:, 0])
        + unproject(dk, w_attn[:, 1])
        + unproject(dv, w_attn[:, 2])
        + dpre
    )


def tail_forward(h, tail_w):
    w_in, w_out, a_in, b_in, a_out, b_out = tail_w
    rows = h.astype(BF16)
    inner = project(rows, w_in)
    phi = 0.5 * (1.0 + lax.erf(inner * 0.7071067811865476))
    g = (inner * phi).astype(BF16)
    slope = phi + inner * jnp.exp(inner * inner * -0.5) * 0.3989422804014327
    pre = project(rows, a_in) + b_in.astype(F32)[:, None, :]
    sig = jax.nn.sigmoid(pre)
    s = (pre * sig).astype(BF16)
    a_slope = sig * (1.0 + pre * (1.0 - sig))
    total = jnp.einsum("tpm,tmk->pk", g, w_out, preferred_element_type=F32)
    total += 4.0 * (
        jnp.einsum("tpm,tkm->pk", s, a_out, preferred_element_type=F32)
        + b_out.astype(F32)
    )
    y, rstd = norm(h + total)
    return y, (rows, slope.astype(BF16), s, a_slope.astype(BF16), y, rstd)


def tail_backward(grad, kept, tail_w):
    w_in, w_out, a_in, b_in, a_out, b_out = tail_w
    rows, slope, s, a_slope, y, rstd = kept
    dpre = norm_back(y, rstd, grad)
    db = dpre.astype(BF16)
    dg = jnp.einsum("pk,tmk->tpm", db, w_out, preferred_element_type=F32)
    df = (dg * slope.astype(F32)).astype(BF16)
    ds = 4.0 * jnp.einsum("pk,tkm->tpm", db, a_out, preferred_element_type=F32)
    du = (ds * a_slope.astype(F32)).astype(BF16)
    terms = (
        jnp.einsum("pk,tpm->tkm", rows, du, preferred_element_type=F32),
        jnp.sum(du.astype(F32), axis=1),
        4.0 * jnp.einsum("tpm,pk->tmk", s, db, preferred_element_type=F32),
        4.0 * jnp.sum(db.astype(F32), axis=0),
    )
    return unproject(df, w_in) + unproject(du, a_in) + dpre, terms


def remote(src, dst, send, recv, where):
    return pltpu.make_async_remote_copy(
        src_ref=src,
        dst_ref=dst,
        send_sem=send,
        recv_sem=recv,
        device_id=where,
        device_id_type=pl.DeviceIdType.MESH,
    )


def gather_kernel(entry, groups, window, *refs):
    shards = refs[:groups]
    tokens, = refs[groups : groups + 1]
    outs = refs[groups + 1 : 2 * groups + 1]
    placed = refs[2 * groups + 1]
    (
        z_send,
        z_recv,
        n_send,
        n_recv,
        f_send,
        f_recv,
        s_send,
        s_recv,
        own_sem,
        t_send,
        t_recv,
    ) = refs[2 * groups + 2 : 2 * groups + 13]
    stores = refs[2 * groups + 13 : 3 * groups + 13]
    token_store = refs[3 * groups + 13]
    s = lax.axis_index("section")
    c = lax.axis_index("ctx")
    t = lax.axis_index("tp")
    chips = 16
    rows = tokens.shape[1]
    chip = c * 4 + t
    cx = c + 1 - 2 * lax.rem(c, 2)
    cy = lax.rem(c + 2, 4)
    cd = 3 - c
    sib = (1 - s, c, t)

    def xor(k):
        low = t + 1 - 2 * lax.rem(t, 2)
        return {1: low, 2: lax.rem(t + 2, 4), 3: 3 - t}[k]

    barrier = pltpu.get_barrier_semaphore()
    for i in range(1, chips):
        p = lax.rem(chip + i, chips)
        pl.semaphore_signal(
            barrier, 1, device_id=(s, p // 4, lax.rem(p, 4)), device_id_type=pl.DeviceIdType.MESH
        )
    for k in range(4):
        where = (1 - s, c, t if k == 0 else xor(k))
        pl.semaphore_signal(barrier, 1, device_id=where, device_id_type=pl.DeviceIdType.MESH)
    pl.semaphore_wait(barrier, chips - 1 + 4)

    def token_copy(i):
        p = lax.rem(chip + i, chips)
        return p, remote(
            tokens.at[:, jnp.minimum(p, rows - 1)],
            placed.at[:, chip],
            t_send.at[i],
            t_recv.at[i],
            (s, p // 4, lax.rem(p, 4)),
        )

    for i in range(1, chips):
        p, copy = token_copy(i)
        pl.when(p < rows)(copy.start)
    bring = pltpu.make_async_copy(
        tokens.at[:, jnp.minimum(chip, rows - 1)], token_store, t_recv.at[0]
    )
    keep = pltpu.make_async_copy(token_store, placed.at[:, chip], t_send.at[0])
    bring.start()

    def block(g, who, h, q, u=None):
        size = shards[g].shape[0]
        start = h * (size // 2) + q * (size // 8)
        length = size // 8
        if u is not None:
            length = size // 16
            start = start + u * length
        return outs[g].at[who, pl.ds(pl.multiple_of(start, 16), length)]

    def z_copy(g, k, h):
        size = shards[g].shape[0]
        start = h * (size // 2) + c * (size // 8)
        return remote(
            shards[g].at[pl.ds(pl.multiple_of(start, 16), size // 8)],
            block(g, t, h, c),
            z_send.at[g, k - 1, h],
            z_recv.at[g, k - 1],
            (h, c, xor(k)),
        )

    def own_copies(g):
        return (
            pltpu.make_async_copy(shards[g], stores[g], own_sem.at[g, 3]),
            pltpu.make_async_copy(stores[g], outs[g].at[t], own_sem.at[g, 0]),
            remote(
                shards[g], outs[g].at[t], own_sem.at[g, 1], own_sem.at[g, 2], sib
            ),
        )

    items = [(g, k) for g in range(groups) for k in (1, 2, 3)]
    mine = s == entry

    def start_z(i):
        g, k = items[i]

        @pl.when(mine)
        def _():
            if k == 1:
                fetch, _, far = own_copies(g)
                fetch.start()
                far.start()
            for h in range(2):
                z_copy(g, k, h).start()

    def spread_copies(g, k):
        who = xor(k)
        src = block(g, who, s, c)
        return (
            remote(src, src, n_send.at[g, k - 1, 0], n_recv.at[g, k - 1, 0], (s, cx, t)),
            remote(src, src, n_send.at[g, k - 1, 1], n_recv.at[g, k - 1, 1], (s, cy, t)),
            sibling_copy(g, k, 0),
        )

    def sibling_copy(g, k, j):
        q = (c, cx, cy, cd)[j]
        src = block(g, xor(k), s, q)
        return remote(src, src, s_send.at[g, k - 1, j], s_recv.at[g, k - 1, j], sib)

    def forward_copies(g, k):
        x_got = block(g, xor(k), s, cx, 0)
        y_got = block(g, xor(k), s, cy, 1)
        return (
            remote(x_got, x_got, f_send.at[g, k - 1, 0], f_recv.at[g, k - 1, 0], (s, cy, t)),
            remote(y_got, y_got, f_send.at[g, k - 1, 1], f_recv.at[g, k - 1, 1], (s, cx, t)),
        )

    def got(region, sem):
        remote(region, region, own_sem.at[0, 1], sem, sib).wait_recv()

    def stage2(i):
        g, k = items[i]
        got(block(g, xor(k), s, c), z_recv.at[g, k - 1])
        for copy in spread_copies(g, k):
            copy.start()

    def stage3(i):
        g, k = items[i]
        ways = forward_copies(g, k)
        for j, q in ((0, cx), (1, cy)):
            got(block(g, xor(k), s, q), n_recv.at[g, k - 1, j])
            ways[j].start()
            sibling_copy(g, k, j + 1).start()

    def stage4(i):
        g, k = items[i]
        for u in range(2):
            got(block(g, xor(k), s, cd, u), f_recv.at[g, k - 1, u])
        sibling_copy(g, k, 3).start()

    count = len(items)
    for i in range(min(window, count)):
        start_z(i)
    bring.wait()
    keep.start()
    lag = LAG
    for step in range(count + 2 * lag):
        if step < count:
            stage2(step)
            if step + window < count:
                start_z(step + window)
            if step % 3 == 2:

                @pl.when(mine)
                def _():
                    fetch, local, _ = own_copies(step // 3)
                    fetch.wait()
                    local.start()

        if 0 <= step - lag < count:
            stage3(step - lag)
        if 0 <= step - 2 * lag < count:
            stage4(step - 2 * lag)

    for g, k in items:
        for j, q in enumerate((c, cx, cy, cd)):
            got(block(g, xor(k), 1 - s, q), s_recv.at[g, k - 1, j])
        for copy in spread_copies(g, k) + forward_copies(g, k):
            copy.wait_send()
        for j in (1, 2, 3):
            sibling_copy(g, k, j).wait_send()

    @pl.when(mine)
    def _():
        for g in range(groups):
            _, local, far = own_copies(g)
            local.wait()
            far.wait_send()
        for g, k in items:
            for h in range(2):
                z_copy(g, k, h).wait_send()

    @pl.when(jnp.logical_not(mine))
    def _():
        for g in range(groups):
            got(outs[g].at[t], own_sem.at[g, 2])

    keep.wait()
    for i in range(1, chips):
        p, copy = token_copy(i)
        pl.when(p < rows)(copy.wait_send)

        @pl.when(chip < rows)
        def _():
            region = placed.at[:, lax.rem(chip + chips - i, chips)]
            got(region, t_recv.at[i])


LAG = 2


def gather_call(entry, shards, tokens, window=4):
    groups = len(shards)
    kinds, _, part, width = tokens.shape
    dma = pltpu.SemaphoreType.DMA
    anywhere = pl.BlockSpec(memory_space=pl.ANY)
    sizes = [
        (groups, 3, 2),
        (groups, 3),
        (groups, 3, 2),
        (groups, 3, 2),
        (groups, 3, 2),
        (groups, 3, 2),
        (groups, 3, 4),
        (groups, 3, 4),
        (groups, 4),
        (16,),
        (16,),
    ]
    result = pl.pallas_call(
        functools.partial(gather_kernel, entry, groups, window),
        in_specs=[anywhere] * (groups + 1),
        out_specs=[anywhere] * (groups + 1),
        out_shape=[jax.ShapeDtypeStruct((4,) + v.shape, v.dtype) for v in shards]
        + [jax.ShapeDtypeStruct((kinds, 16, part, width), tokens.dtype)],
        scratch_shapes=[dma(size) for size in sizes]
        + [pltpu.VMEM(v.shape, v.dtype) for v in shards]
        + [pltpu.VMEM((kinds, part, width), tokens.dtype)],
        compiler_params=pltpu.CompilerParams(
            collective_id=entry, has_side_effects=True, vmem_limit_bytes=24 * 2**20
        ),
        name="gather_%d" % entry,
    )(*shards, tokens)
    return result[:groups], result[groups]


def gather_plain(entry, shards):
    full = [lax.all_gather(lax.all_gather(v, "tp"), "section") for v in shards]
    return [v[entry] for v in full]


def spread(blocks):
    chips = lax.axis_size("ctx") * lax.axis_size("tp")
    kinds, rows, part, width = blocks.shape
    blocks = jnp.pad(blocks, ((0, 0), (0, chips - rows), (0, 0), (0, 0)))
    moved = lax.all_to_all(
        jnp.moveaxis(blocks, 1, 0), ("ctx", "tp"), 0, 0, tiled=True
    )
    return jnp.moveaxis(moved, 0, 1).reshape(kinds, chips * part, width)


def collect(tokens, rows):
    chips = lax.axis_size("ctx") * lax.axis_size("tp")
    kinds, length, width = tokens.shape
    part = length // chips
    blocks = jnp.moveaxis(tokens.reshape(kinds, chips, part, width), 1, 0)
    moved = lax.all_to_all(blocks, ("ctx", "tp"), 0, 0, tiled=True)
    return jnp.moveaxis(moved, 0, 1)[:, :rows]


def per_device(
    layer_inputs,
    out_grad,
    src_seg,
    tgt_seg,
    qkv_weights,
    out_weights,
    cross_weights,
    ffn_in,
    ffn_out,
    adapter_in,
    adapter_in_bias,
    adapter_out,
    adapter_out_bias,
):
    core = lax.axis_index("section")
    is_first = core == 0
    tp = lax.axis_size("tp")
    chips = lax.axis_size("ctx") * tp
    chip = lax.axis_index("ctx") * tp + lax.axis_index("tp")
    _, micro, per_micro, part, width = layer_inputs.shape
    row_count = micro * per_micro
    half = part // 2
    length = half * chips

    def pick(first, second):
        return jnp.where(is_first, first, second)

    x = layer_inputs.reshape(row_count, part, width)
    low, high = x[:, :half], x[:, half:]
    other = swap(pick(high, low))
    grads = out_grad.reshape(row_count, part, width)
    stacked = jnp.stack(
        [pick(low, other), pick(other, high), pick(grads[:, :half], grads[:, half:])]
    )
    tail_rows = adapter_out[0].T
    biases = jnp.concatenate([adapter_in_bias[0], adapter_out_bias[0]])
    lanes = adapter_in_bias.shape[1]
    biases = jnp.pad(biases.reshape(-1, lanes), ((0, 256 - biases.size // lanes), (0, 0)))
    shards = [
        jnp.concatenate([qkv_weights[0], out_weights], axis=0).reshape(-1, out_weights.shape[2]),
        ffn_in[0],
        jnp.concatenate([adapter_in[0], tail_rows], axis=1),
        ffn_out[0],
        cross_weights[0].reshape(-1, cross_weights.shape[3]),
        biases,
    ]
    if lax.axis_size("ctx") == 4 and tp == 4:
        enc_w, placed = gather_call(0, shards, stacked[:1])
        source = placed.reshape(length, width)
        dec_w, placed = gather_call(1, shards, stacked[1:])
        target, cotangent = placed.reshape(2, length, width)
    else:
        source, target, cotangent = spread(stacked)
        enc_w, dec_w = gather_plain(0, shards), gather_plain(1, shards)

    def unpack(full):
        attn, w_in, adapter, w_out, cross, bias = full
        cols = lanes
        attn = attn.reshape(tp, 4, -1, attn.shape[2])
        cross = cross.reshape(tp, 2, -1, cross.shape[2])
        b_out = bias[0, 1 : 1 + width // cols].reshape(width)
        tail = (
            w_in,
            w_out,
            adapter[:, :, :cols],
            bias[:, 0],
            adapter[:, :, cols:],
            b_out,
        )
        return attn, cross, tail

    enc_attn, enc_cross, enc_tail_w = unpack(enc_w)
    dec_attn, dec_cross, dec_tail_w = unpack(dec_w)

    def ids_of(segments):
        flat = lax.all_gather(
            segments.reshape(row_count, -1), "ctx", axis=1, tiled=True
        )
        row = lax.dynamic_index_in_dim(
            flat, jnp.minimum(chip, row_count - 1), 0, keepdims=False
        )
        return row.reshape(chips, 2, half)

    index = jnp.arange(length, dtype=jnp.int32)
    place = (index // half) * part + index % half

    def cut(seg, which):
        own = lax.dynamic_index_in_dim(seg, which, 1, keepdims=False).reshape(length)
        return own, place + which * half

    src_ids, tgt_ids = ids_of(src_seg), ids_of(tgt_seg)

    def id_arrays(seg_q, seg_k):
        qi = jnp.stack(cut(seg_q, core))
        ki = jnp.stack(cut(seg_k, core) + cut(seg_k, 1 - core))
        return (qi.T, ki), (qi, ki.T)

    enc_ids = id_arrays(src_ids, src_ids)
    dec_ids = id_arrays(tgt_ids, tgt_ids)
    cross_ids = id_arrays(tgt_ids, src_ids)

    enc_mid, enc_self = self_forward(
        source, source.astype(F32), enc_attn, enc_ids, False
    )
    encoded, enc_tail = tail_forward(enc_mid, enc_tail_w)
    encoded_bf = encoded.astype(BF16)
    memory = [project(encoded_bf, enc_cross[:, j]).astype(BF16) for j in range(2)]
    memory_other = swap(jnp.stack(memory))
    mem_keys = (memory[0], memory_other[0], memory[1], memory_other[1])

    dec_mid, dec_self = self_forward(
        target, target.astype(F32), dec_attn, dec_ids, True
    )
    queries = project(dec_mid.astype(BF16), dec_cross[:, 0]).astype(BF16)
    cross_o, cross_lse = attention_forward(
        queries, *mem_keys, *cross_ids[0], False
    )
    second, second_rstd = norm(dec_mid + unproject(cross_o, dec_cross[:, 1]))
    decoded, dec_tail = tail_forward(second, dec_tail_w)

    grad_second, dec_terms = tail_backward(cotangent.astype(F32), dec_tail, dec_tail_w)
    grad_cross = norm_back(second, second_rstd, grad_second)
    do = project(grad_cross.astype(BF16), dec_cross[:, 1]).astype(BF16)
    dqc, dmk, dmv = attend_back(
        queries, mem_keys, cross_o, do, cross_lse, cross_ids, False
    )
    grad_first = unproject(dqc, dec_cross[:, 0]) + grad_cross
    grad_target = self_backward(grad_first, dec_self, dec_attn, dec_ids, True)

    grad_encoded = unproject(dmk, enc_cross[:, 0]) + unproject(dmv, enc_cross[:, 1])
    grad_mid, enc_terms = tail_backward(grad_encoded, enc_tail, enc_tail_w)
    grad_source = self_backward(grad_mid, enc_self, enc_attn, enc_ids, False)

    has_row = chip < row_count

    def total(enc_term, dec_term):
        enc_term = jnp.where(has_row, enc_term, 0.0).astype(BF16)
        dec_term = jnp.where(has_row, dec_term, 0.0).astype(BF16)
        got = swap(pick(dec_term, enc_term))
        return (pick(enc_term, dec_term).astype(F32) + got.astype(F32)).astype(BF16)

    sums = [total(e, d) for e, d in zip(enc_terms, dec_terms)]
    scattered = [
        lax.psum_scatter(v, "tp", scatter_dimension=0, tiled=False) for v in sums[:3]
    ]
    scattered = [lax.psum(v, "ctx").astype(F32) for v in scattered]
    bias_sum = lax.psum(sums[3], ("ctx", "tp")).astype(F32)

    results = jnp.stack(
        [
            encoded_bf,
            decoded.astype(BF16),
            grad_source.astype(BF16),
            grad_target.astype(BF16),
        ]
    )
    placed = collect(results, row_count)

    def join(enc_part, dec_part):
        mine = pick(enc_part, dec_part)
        got = swap(pick(dec_part, enc_part))
        return jnp.concatenate([pick(mine, got), pick(got, mine)], axis=1)

    outs = join(placed[0], placed[1]).reshape(layer_inputs.shape)
    grads = join(placed[2], placed[3]).astype(F32).reshape(layer_inputs.shape)
    return (
        outs,
        grads,
        scattered[0][None],
        scattered[1][None],
        scattered[2][None],
        bias_sum[None],
    )


def solution(mesh):
    return jax.shard_map(
        per_device,
        mesh=mesh,
        in_specs=(
            P("section", None, None, ("ctx", "tp"), None),
            P(None, None, ("ctx", "tp"), None),
            P(None, None, "ctx"),
            P(None, None, "ctx"),
            P("section", None, None, "tp"),
            P("section", None, "tp"),
            P("section", None, None, "tp"),
            P("section", None, "tp"),
            P("section", "tp", None),
            P("section", None, "tp"),
            P("section", "tp"),
            P("section", "tp", None),
            P("section", None),
        ),
        out_specs=(
            P("section", None, None, ("ctx", "tp"), None),
            P("section", None, None, ("ctx", "tp"), None),
            P("section", None, "tp"),
            P("section", "tp"),
            P("section", "tp", None),
            P("section", None),
        ),
        check_vma=False,
    )
```

```python
import functools

import jax
import jax.numpy as jnp
from jax import lax
from jax.experimental import pallas as pl
from jax.experimental.pallas import tpu as pltpu
from jax.sharding import PartitionSpec as P

HEAD = 64
SCALE = HEAD**-0.5
EPS = 1e-05
MASKED = -1e30
F32 = jnp.float32
BF16 = jnp.bfloat16


def swap(value):
    return lax.ppermute(value, "section", [(0, 1), (1, 0)])


def remote(src, dst, send, recv, where):
    return pltpu.make_async_remote_copy(
        src_ref=src,
        dst_ref=dst,
        send_sem=send,
        recv_sem=recv,
        device_id=where,
        device_id_type=pl.DeviceIdType.MESH,
    )


def device_of(section, chip):
    return (section, chip // 4, lax.rem(chip, 4))


def greet_all():
    s = lax.axis_index("section")
    chip = lax.axis_index("ctx") * 4 + lax.axis_index("tp")
    barrier = pltpu.get_barrier_semaphore()
    for core in (0, 1):
        for i in range(core, 16):
            pl.semaphore_signal(
                barrier,
                1,
                device_id=device_of(lax.rem(s + 1 - core, 2), lax.rem(chip + i, 16)),
                device_id_type=pl.DeviceIdType.MESH,
            )
    pl.semaphore_wait(barrier, 31)


class Scatter:
    BRING = 2

    def __init__(self, arrays, rows, call_id):
        self.inputs = [a for a, _ in arrays]
        self.kinds = [k for _, k in arrays]
        self.rows = rows
        self.call_id = call_id
        self.shapes = [
            jax.ShapeDtypeStruct(
                ((16,) if k == self.BRING else (rows, 2)) + a.shape[1:], a.dtype
            )
            for a, k in arrays
        ]
        count = len(arrays)
        self.scratch = [
            pltpu.SemaphoreType.DMA((count, 16)),
            pltpu.SemaphoreType.DMA((count, 16, 2)),
        ]

    def sends(self, ins, outs, sems):
        send, recv = sems
        s = lax.axis_index("section")
        chip = lax.axis_index("ctx") * 4 + lax.axis_index("tp")
        for a, kind in enumerate(self.kinds):
            for i in range(16):
                p = lax.rem(chip + i, 16)
                if kind == self.BRING:
                    ready = p < self.rows
                    src = ins[a].at[jnp.minimum(p, self.rows - 1)]
                    dst = outs[a].at[chip]
                    core, mark = s, 0
                    stays = True
                else:
                    ready = chip < self.rows
                    src = ins[a].at[p]
                    dst = outs[a].at[jnp.minimum(chip, self.rows - 1), s]
                    core, mark = kind, s
                    stays = s == kind
                near = pltpu.make_async_copy(src, dst, send.at[a, i])
                far = remote(
                    src, dst, send.at[a, i], recv.at[a, i, mark], device_of(core, p)
                )
                yield i, ready, stays, near, far

    def start(self, ins, outs, sems):
        greet_all()
        for i, ready, stays, near, far in self.sends(ins, outs, sems):

            @pl.when(ready)
            def _():
                if i:
                    far.start()
                elif stays is True:
                    near.start()
                else:
                    pl.when(stays)(near.start)
                    pl.when(jnp.logical_not(stays))(far.start)

    def finish(self, ins, outs, sems):
        send, recv = sems
        s = lax.axis_index("section")
        chip = lax.axis_index("ctx") * 4 + lax.axis_index("tp")
        for i, ready, stays, near, far in self.sends(ins, outs, sems):

            @pl.when(ready)
            def _():
                if i:
                    far.wait_send()
                elif stays is True:
                    near.wait()
                else:
                    pl.when(stays)(near.wait)
                    pl.when(jnp.logical_not(stays))(far.wait_send)

        def got(region, sem):
            remote(region, region, send.at[0, 0], sem, (1 - s, 0, 0)).wait_recv()

        for a, kind in enumerate(self.kinds):
            for i in range(16):
                sender = lax.rem(chip + 16 - i, 16)
                if kind == self.BRING:
                    if i:

                        @pl.when(chip < self.rows)
                        def _():
                            got(outs[a].at[sender], recv.at[a, i, 0])

                    continue

                @pl.when((s == kind) & (sender < self.rows))
                def _():
                    for core in (0, 1) if i else (1 - kind,):
                        region = outs[a].at[jnp.minimum(sender, self.rows - 1), core]
                        got(region, recv.at[a, i, core])


def split_refs(rider, refs, own_outs):
    count = len(rider.inputs) if rider else 0
    mine = refs[count : count + own_outs]
    outs = refs[count + own_outs : 2 * count + own_outs]
    sems = refs[2 * count + own_outs :]
    return mine, (refs[:count], outs, sems)


def ride_start(rider, parts):
    if rider:
        pl.when(pl.program_id(0) == 0)(lambda: rider.start(*parts))


def ride_finish(rider, parts):
    if rider:
        last = pl.num_programs(0) - 1
        pl.when(pl.program_id(0) == last)(lambda: rider.finish(*parts))


def send_kernel(rider, *refs):
    n = len(rider.inputs)
    block_in, (own, spread_out) = refs[n], (refs[n], refs[2 * n + 1])
    ins, outs = refs[:n], refs[n + 1 : 2 * n + 1]
    sems = refs[2 * n + 2 : 2 * n + 4]
    b_send, b_recv = refs[2 * n + 4 :]
    rider.start(ins, outs, sems)
    s = lax.axis_index("section")
    c = lax.axis_index("ctx")
    t = lax.axis_index("tp")
    dst = spread_out.at[c]
    keep = pltpu.make_async_copy(own, dst, b_send.at[0])
    keep.start()
    ways = [
        remote(own, dst, b_send.at[j], b_recv.at[j], (s, lax.rem(c + j, 4), t))
        for j in (1, 2, 3)
    ]
    for way in ways:
        way.start()
    keep.wait()
    for j, way in enumerate(ways):
        way.wait_send()
        region = spread_out.at[lax.rem(c + 3 - j, 4)]
        remote(region, region, b_send.at[0], b_recv.at[j + 1], (s, c, t)).wait_recv()
    rider.finish(ins, outs, sems)


def send_call(rider, block):
    anywhere = pl.BlockSpec(memory_space=pl.ANY)
    count = len(rider.inputs)
    result = pl.pallas_call(
        functools.partial(send_kernel, rider),
        in_specs=[anywhere] * (count + 1),
        out_specs=[anywhere] * (count + 1),
        out_shape=rider.shapes + [jax.ShapeDtypeStruct((4,) + block.shape, block.dtype)],
        scratch_shapes=rider.scratch
        + [pltpu.SemaphoreType.DMA((4,)), pltpu.SemaphoreType.DMA((4,))],
        compiler_params=pltpu.CompilerParams(
            collective_id=rider.call_id, has_side_effects=True
        ),
        name="send_last",
    )(*rider.inputs, block)
    return result[:count], result[count]


def dot_nt(left, right, **kw):
    return lax.dot_general(
        left, right, (((1,), (1,)), ((), ())), preferred_element_type=F32, **kw
    )


def dot_nn(left, right):
    return lax.dot_general(
        left, right, (((1,), (0,)), ((), ())), preferred_element_type=F32
    )


def dot_tn(left, right):
    return lax.dot_general(
        left, right, (((0,), (0,)), ((), ())), preferred_element_type=F32
    )


def attn_fwd_kernel(
    causal, rider, q_ref, ko_ref, kx_ref, vo_ref, vx_ref, qi_ref, ki_ref, *rest
):
    (o_ref, lse_ref), parts_ride = split_refs(rider, rest, 2)
    ride_start(rider, parts_ride)
    length = q_ref.shape[1]
    heads = q_ref.shape[2] // HEAD
    block = length // 2
    segq = qi_ref[:, 0:1]
    posq = qi_ref[:, 1:2]
    for h in range(heads):
        cols = slice(h * HEAD, (h + 1) * HEAD)
        for b in range(2):
            rows = slice(b * block, (b + 1) * block)
            span = (b + 1) * block if causal else length
            q = q_ref[0, rows, cols] * jnp.asarray(SCALE, BF16)
            parts = []
            for kk, (k_ref, i) in enumerate(((ko_ref, 0), (kx_ref, 2))):
                s = dot_nt(q, k_ref[0, :span, cols])
                ok = segq[rows] == ki_ref[i : i + 1, :span]
                if causal:
                    ok = ok & (posq[rows] >= ki_ref[i + 1 : i + 2, :span])
                parts.append(jnp.where(ok, s, MASKED))
            top = jnp.maximum(
                jnp.max(parts[0], axis=1, keepdims=True),
                jnp.max(parts[1], axis=1, keepdims=True),
            )
            ex = [jnp.exp(p - top) for p in parts]
            total = jnp.sum(ex[0], axis=1, keepdims=True) + jnp.sum(
                ex[1], axis=1, keepdims=True
            )
            out = dot_nn(ex[0].astype(BF16), vo_ref[0, :span, cols]) + dot_nn(
                ex[1].astype(BF16), vx_ref[0, :span, cols]
            )
            o_ref[0, rows, cols] = (out / total).astype(BF16)
            lse = top + jnp.log(total)
            lse_ref[0, h : h + 1, rows] = jnp.broadcast_to(lse, (block, 128)).T[0:1]
    ride_finish(rider, parts_ride)


def attention_call(kernel, name, causal, rider, blocks, small, outs):
    groups = blocks[0].shape[0]
    anywhere = pl.BlockSpec(memory_space=pl.ANY)
    extra = rider.inputs if rider else []
    params = {"vmem_limit_bytes": 48 * 2**20}
    if rider:
        params.update(collective_id=rider.call_id, has_side_effects=True)

    def group_spec(shape):
        return pl.BlockSpec((1,) + shape[1:], lambda t: (t, 0, 0))

    result = pl.pallas_call(
        functools.partial(kernel, causal, rider),
        grid=(groups,),
        in_specs=[group_spec(v.shape) for v in blocks]
        + [pl.BlockSpec(v.shape, lambda t: (0, 0)) for v in small]
        + [anywhere] * len(extra),
        out_specs=[group_spec(v.shape) for v in outs] + [anywhere] * len(extra),
        out_shape=outs + (rider.shapes if rider else []),
        scratch_shapes=rider.scratch if rider else [],
        compiler_params=pltpu.CompilerParams(**params),
        name=name,
    )(*blocks, *small, *extra)
    return result[: len(outs)], result[len(outs) :]


def attention_forward(q, keys, ids, causal, rider=None):
    groups, length, width = q.shape
    outs = [
        jax.ShapeDtypeStruct(q.shape, BF16),
        jax.ShapeDtypeStruct((groups, width // HEAD, length), F32),
    ]
    return attention_call(
        attn_fwd_kernel, "attn_fwd", causal, rider, [q, *keys], ids, outs
    )


def attn_bwd_kernel(
    causal,
    rider,
    q_ref,
    ko_ref,
    kx_ref,
    vo_ref,
    vx_ref,
    o_ref,
    do_ref,
    lse_ref,
    qi_ref,
    ki_ref,
    *rest,
):
    (dq_ref, dko_ref, dkx_ref, dvo_ref, dvx_ref), parts_ride = split_refs(rider, rest, 5)
    ride_start(rider, parts_ride)
    length = q_ref.shape[1]
    heads = q_ref.shape[2] // HEAD
    block = length // 2
    segq = qi_ref[0:1, :]
    posq = qi_ref[1:2, :]
    ones = jnp.ones((8, HEAD), F32)
    for h in range(heads):
        cols = slice(h * HEAD, (h + 1) * HEAD)
        q_all = q_ref[0, :, cols] * jnp.asarray(SCALE, BF16)
        do_all = do_ref[0, :, cols]
        prod = do_all.astype(F32) * o_ref[0, :, cols].astype(F32)
        delta = dot_nt(ones, prod, precision=lax.Precision.HIGHEST)[0:1]
        lse = lse_ref[0, h : h + 1, :]
        dq = [jnp.zeros((block, HEAD), F32), jnp.zeros((block, HEAD), F32)]
        for k_ref, v_ref, dk_ref, dv_ref, i in (
            (ko_ref, vo_ref, dko_ref, dvo_ref, 0),
            (kx_ref, vx_ref, dkx_ref, dvx_ref, 2),
        ):
            for b in range(2):
                rows = slice(b * block, (b + 1) * block)
                first = b * block if causal else 0
                q = q_all[first:]
                do = do_all[first:]
                k = k_ref[0, rows, cols]
                s = dot_nt(k, q)
                ok = ki_ref[rows, i : i + 1] == segq[:, first:]
                if causal:
                    ok = ok & (posq[:, first:] >= ki_ref[rows, i + 1 : i + 2])
                p = jnp.where(ok, jnp.exp(s - lse[:, first:]), 0.0)
                dp = dot_nt(v_ref[0, rows, cols], do)
                ds = (p * (dp - delta[:, first:])).astype(BF16)
                dv_ref[0, rows, cols] = dot_nn(p.astype(BF16), do).astype(BF16)
                dk_ref[0, rows, cols] = dot_nn(ds, q).astype(BF16)
                part = dot_tn(ds, k)
                if first:
                    dq[1] = dq[1] + part
                else:
                    dq[0] = dq[0] + part[:block]
                    dq[1] = dq[1] + part[block:]
        dq_ref[0, :block, cols] = (dq[0] * SCALE).astype(BF16)
        dq_ref[0, block:, cols] = (dq[1] * SCALE).astype(BF16)
    ride_finish(rider, parts_ride)


def attention_backward(q, keys, o, do, lse, ids, causal, rider=None):
    outs = [jax.ShapeDtypeStruct(q.shape, BF16)] * 5
    return attention_call(
        attn_bwd_kernel, "attn_bwd", causal, rider, [q, *keys, o, do, lse], ids, outs
    )


def norm(value):
    mean = jnp.mean(value, axis=-1, keepdims=True)
    centered = value - mean
    rstd = lax.rsqrt(jnp.mean(centered * centered, axis=-1, keepdims=True) + EPS)
    return centered * rstd, rstd


def norm_back(normed, rstd, grad):
    return rstd * (
        grad
        - jnp.mean(grad, axis=-1, keepdims=True)
        - normed * jnp.mean(grad * normed, axis=-1, keepdims=True)
    )


def project(rows, weight):
    return jnp.einsum("pk,tkm->tpm", rows, weight, preferred_element_type=F32)


def unproject(blocks, weight):
    return jnp.einsum("tpm,tkm->pk", blocks, weight, preferred_element_type=F32)


def self_forward(rows_bf, rows, w_attn, ids, causal, rider=None):
    kv = [project(rows_bf, w_attn[:, j]).astype(BF16) for j in (1, 2)]
    other = swap(jnp.stack(kv))
    q = project(rows_bf, w_attn[:, 0]).astype(BF16)
    keys = (kv[0], other[0], kv[1], other[1])
    (o, lse), moved = attention_forward(q, keys, ids[0], causal, rider)
    h, rstd = norm(rows + unproject(o, w_attn[:, 3]))
    return h, (q, keys, o, lse, h, rstd), moved


def attend_back(q, keys, o, do, lse, ids, causal, rider=None):
    (dq, dko, dkx, dvo, dvx), moved = attention_backward(
        q, keys, o, do, lse, ids[1], causal, rider
    )
    other = swap(jnp.stack([dkx, dvx])).astype(F32)
    dk = (dko.astype(F32) + other[0]).astype(BF16)
    dv = (dvo.astype(F32) + other[1]).astype(BF16)
    return (dq, dk, dv), moved


def self_backward(grad, kept, w_attn, ids, causal, rider=None):
    q, keys, o, lse, h, rstd = kept
    dpre = norm_back(h, rstd, grad)
    do = project(dpre.astype(BF16), w_attn[:, 3]).astype(BF16)
    (dq, dk, dv), moved = attend_back(q, keys, o, do, lse, ids, causal, rider)
    total = (
        unproject(dq, w_attn[:, 0])
        + unproject(dk, w_attn[:, 1])
        + unproject(dv, w_attn[:, 2])
        + dpre
    )
    return total, moved


def tail_forward(h, tail_w):
    w_in, w_out, a_in, b_in, a_out, b_out = tail_w
    rows = h.astype(BF16)
    inner = project(rows, w_in)
    phi = 0.5 * (1.0 + lax.erf(inner * 0.7071067811865476))
    g = (inner * phi).astype(BF16)
    slope = phi + inner * jnp.exp(inner * inner * -0.5) * 0.3989422804014327
    pre = project(rows, a_in) + b_in.astype(F32)[:, None, :]
    sig = jax.nn.sigmoid(pre)
    s = (pre * sig).astype(BF16)
    a_slope = sig * (1.0 + pre * (1.0 - sig))
    total = jnp.einsum("tpm,tmk->pk", g, w_out, preferred_element_type=F32)
    total += 4.0 * (
        jnp.einsum("tpm,tkm->pk", s, a_out, preferred_element_type=F32)
        + b_out.astype(F32)
    )
    y, rstd = norm(h + total)
    return y, (rows, slope.astype(BF16), s, a_slope.astype(BF16), y, rstd)


def tail_backward(grad, kept, tail_w):
    w_in, w_out, a_in, b_in, a_out, b_out = tail_w
    rows, slope, s, a_slope, y, rstd = kept
    dpre = norm_back(y, rstd, grad)
    db = dpre.astype(BF16)
    dg = jnp.einsum("pk,tmk->tpm", db, w_out, preferred_element_type=F32)
    df = (dg * slope.astype(F32)).astype(BF16)
    ds = 4.0 * jnp.einsum("pk,tkm->tpm", db, a_out, preferred_element_type=F32)
    du = (ds * a_slope.astype(F32)).astype(BF16)
    terms = (
        jnp.einsum("pk,tpm->tkm", rows, du, preferred_element_type=F32),
        jnp.sum(du.astype(F32), axis=1),
        4.0 * jnp.einsum("pk,tpm->tkm", db, s, preferred_element_type=F32),
        4.0 * jnp.sum(db.astype(F32), axis=0),
    )
    return unproject(df, w_in) + unproject(du, a_in) + dpre, terms


def gather_kernel(entry, groups, window, *refs):
    shards = refs[:groups]
    tokens, ids = refs[groups : groups + 2]
    outs = refs[groups + 2 : 2 * groups + 2]
    placed, all_ids = refs[2 * groups + 2 : 2 * groups + 4]
    (
        z_send,
        z_recv,
        n_send,
        n_recv,
        f_send,
        f_recv,
        s_send,
        s_recv,
        own_sem,
        t_send,
        t_recv,
        i_send,
        i_recv,
    ) = refs[2 * groups + 4 : 2 * groups + 17]
    stores = refs[2 * groups + 17 : 3 * groups + 17]
    token_store = refs[3 * groups + 17]
    s = lax.axis_index("section")
    c = lax.axis_index("ctx")
    t = lax.axis_index("tp")
    chips = 16
    rows = tokens.shape[1]
    chip = c * 4 + t
    cx = c + 1 - 2 * lax.rem(c, 2)
    cy = lax.rem(c + 2, 4)
    cd = 3 - c
    sib = (1 - s, c, t)

    def xor(k):
        low = t + 1 - 2 * lax.rem(t, 2)
        return {1: low, 2: lax.rem(t + 2, 4), 3: 3 - t}[k]

    barrier = pltpu.get_barrier_semaphore()
    for i in range(1, chips):
        p = lax.rem(chip + i, chips)
        pl.semaphore_signal(
            barrier, 1, device_id=(s, p // 4, lax.rem(p, 4)), device_id_type=pl.DeviceIdType.MESH
        )
    for k in range(4):
        where = (1 - s, c, t if k == 0 else xor(k))
        pl.semaphore_signal(barrier, 1, device_id=where, device_id_type=pl.DeviceIdType.MESH)
    pl.semaphore_wait(barrier, chips - 1 + 4)

    keep_ids = pltpu.make_async_copy(ids, all_ids.at[c], i_send.at[0])
    keep_ids.start()
    id_copies = [
        remote(ids, all_ids.at[c], i_send.at[j], i_recv.at[j], (s, lax.rem(c + j, 4), t))
        for j in (1, 2, 3)
    ]
    for copy in id_copies:
        copy.start()

    def token_copy(i):
        p = lax.rem(chip + i, chips)
        return p, remote(
            tokens.at[:, jnp.minimum(p, rows - 1)],
            placed.at[:, chip],
            t_send.at[i],
            t_recv.at[i],
            (s, p // 4, lax.rem(p, 4)),
        )

    for i in range(1, chips):
        p, copy = token_copy(i)
        pl.when(p < rows)(copy.start)
    bring = pltpu.make_async_copy(
        tokens.at[:, jnp.minimum(chip, rows - 1)], token_store, t_recv.at[0]
    )
    keep = pltpu.make_async_copy(token_store, placed.at[:, chip], t_send.at[0])
    bring.start()

    def block(g, who, h, q, u=None):
        size = shards[g].shape[0]
        start = h * (size // 2) + q * (size // 8)
        length = size // 8
        if u is not None:
            length = size // 16
            start = start + u * length
        return outs[g].at[who, pl.ds(pl.multiple_of(start, 16), length)]

    def z_copy(g, k, h):
        size = shards[g].shape[0]
        start = h * (size // 2) + c * (size // 8)
        return remote(
            shards[g].at[pl.ds(pl.multiple_of(start, 16), size // 8)],
            block(g, t, h, c),
            z_send.at[g, k - 1, h],
            z_recv.at[g, k - 1],
            (h, c, xor(k)),
        )

    def own_copies(g):
        return (
            pltpu.make_async_copy(shards[g], stores[g], own_sem.at[g, 3]),
            pltpu.make_async_copy(stores[g], outs[g].at[t], own_sem.at[g, 0]),
            remote(
                shards[g], outs[g].at[t], own_sem.at[g, 1], own_sem.at[g, 2], sib
            ),
        )

    items = [(g, k) for g in range(groups) for k in (1, 2, 3)]
    mine = s == entry

    def start_z(i):
        g, k = items[i]

        @pl.when(mine)
        def _():
            if k == 1:
                fetch, _, far = own_copies(g)
                fetch.start()
                far.start()
            for h in range(2):
                z_copy(g, k, h).start()

    def spread_copies(g, k):
        who = xor(k)
        src = block(g, who, s, c)
        return (
            remote(src, src, n_send.at[g, k - 1, 0], n_recv.at[g, k - 1, 0], (s, cx, t)),
            remote(src, src, n_send.at[g, k - 1, 1], n_recv.at[g, k - 1, 1], (s, cy, t)),
            sibling_copy(g, k, 0),
        )

    def sibling_copy(g, k, j):
        q = (c, cx, cy, cd)[j]
        src = block(g, xor(k), s, q)
        return remote(src, src, s_send.at[g, k - 1, j], s_recv.at[g, k - 1, j], sib)

    def forward_copies(g, k):
        x_got = block(g, xor(k), s, cx, 0)
        y_got = block(g, xor(k), s, cy, 1)
        return (
            remote(x_got, x_got, f_send.at[g, k - 1, 0], f_recv.at[g, k - 1, 0], (s, cy, t)),
            remote(y_got, y_got, f_send.at[g, k - 1, 1], f_recv.at[g, k - 1, 1], (s, cx, t)),
        )

    def got(region, sem):
        remote(region, region, own_sem.at[0, 1], sem, sib).wait_recv()

    def stage2(i):
        g, k = items[i]
        got(block(g, xor(k), s, c), z_recv.at[g, k - 1])
        for copy in spread_copies(g, k):
            copy.start()

    def stage3(i):
        g, k = items[i]
        ways = forward_copies(g, k)
        for j, q in ((0, cx), (1, cy)):
            got(block(g, xor(k), s, q), n_recv.at[g, k - 1, j])
            ways[j].start()
            sibling_copy(g, k, j + 1).start()

    def stage4(i):
        g, k = items[i]
        for u in range(2):
            got(block(g, xor(k), s, cd, u), f_recv.at[g, k - 1, u])
        sibling_copy(g, k, 3).start()

    count = len(items)
    for i in range(min(window, count)):
        start_z(i)
    bring.wait()
    keep.start()
    lag = 2
    for step in range(count + 2 * lag):
        if step < count:
            stage2(step)
            if step + window < count:
                start_z(step + window)
            if step % 3 == 2:

                @pl.when(mine)
                def _():
                    fetch, local, _ = own_copies(step // 3)
                    fetch.wait()
                    local.start()

        if 0 <= step - lag < count:
            stage3(step - lag)
        if 0 <= step - 2 * lag < count:
            stage4(step - 2 * lag)

    for g, k in items:
        for j, q in enumerate((c, cx, cy, cd)):
            got(block(g, xor(k), 1 - s, q), s_recv.at[g, k - 1, j])
        for copy in spread_copies(g, k) + forward_copies(g, k):
            copy.wait_send()
        for j in (1, 2, 3):
            sibling_copy(g, k, j).wait_send()

    @pl.when(mine)
    def _():
        for g in range(groups):
            _, local, far = own_copies(g)
            local.wait()
            far.wait_send()
        for g, k in items:
            for h in range(2):
                z_copy(g, k, h).wait_send()

    @pl.when(jnp.logical_not(mine))
    def _():
        for g in range(groups):
            got(outs[g].at[t], own_sem.at[g, 2])

    keep.wait()
    keep_ids.wait()
    for j, copy in enumerate(id_copies):
        copy.wait_send()
        got(all_ids.at[lax.rem(c + 3 - j, 4)], i_recv.at[j + 1])
    for i in range(1, chips):
        p, copy = token_copy(i)
        pl.when(p < rows)(copy.wait_send)

        @pl.when(chip < rows)
        def _():
            region = placed.at[:, lax.rem(chip + chips - i, chips)]
            got(region, t_recv.at[i])


def gather_call(entry, shards, tokens, ids, window=4):
    groups = len(shards)
    kinds, _, part, width = tokens.shape
    dma = pltpu.SemaphoreType.DMA
    anywhere = pl.BlockSpec(memory_space=pl.ANY)
    sizes = [
        (groups, 3, 2),
        (groups, 3),
        (groups, 3, 2),
        (groups, 3, 2),
        (groups, 3, 2),
        (groups, 3, 2),
        (groups, 3, 4),
        (groups, 3, 4),
        (groups, 4),
        (16,),
        (16,),
        (4,),
        (4,),
    ]
    result = pl.pallas_call(
        functools.partial(gather_kernel, entry, groups, window),
        in_specs=[anywhere] * (groups + 2),
        out_specs=[anywhere] * (groups + 2),
        out_shape=[jax.ShapeDtypeStruct((4,) + v.shape, v.dtype) for v in shards]
        + [
            jax.ShapeDtypeStruct((kinds, 16, part, width), tokens.dtype),
            jax.ShapeDtypeStruct((4,) + ids.shape, ids.dtype),
        ],
        scratch_shapes=[dma(size) for size in sizes]
        + [pltpu.VMEM(v.shape, v.dtype) for v in shards]
        + [pltpu.VMEM((kinds, part, width), tokens.dtype)],
        compiler_params=pltpu.CompilerParams(
            collective_id=entry, has_side_effects=True, vmem_limit_bytes=24 * 2**20
        ),
        name="gather_%d" % entry,
    )(*shards, tokens, ids)
    return result[:groups], result[groups], result[groups + 1]


def gather_plain(entry, shards):
    full = [lax.all_gather(lax.all_gather(v, "tp"), "section") for v in shards]
    return [v[entry] for v in full]


def spread(blocks):
    chips = lax.axis_size("ctx") * lax.axis_size("tp")
    kinds, rows, part, width = blocks.shape
    blocks = jnp.pad(blocks, ((0, 0), (0, chips - rows), (0, 0), (0, 0)))
    moved = lax.all_to_all(
        jnp.moveaxis(blocks, 1, 0), ("ctx", "tp"), 0, 0, tiled=True
    )
    return jnp.moveaxis(moved, 0, 1).reshape(kinds, chips * part, width)


def collect(tokens, rows):
    chips = lax.axis_size("ctx") * lax.axis_size("tp")
    kinds, length, width = tokens.shape
    part = length // chips
    blocks = jnp.moveaxis(tokens.reshape(kinds, chips, part, width), 1, 0)
    moved = lax.all_to_all(blocks, ("ctx", "tp"), 0, 0, tiled=True)
    return jnp.moveaxis(moved, 0, 1)[:, :rows]


def per_device(
    layer_inputs,
    out_grad,
    src_seg,
    tgt_seg,
    qkv_weights,
    out_weights,
    cross_weights,
    ffn_in,
    ffn_out,
    adapter_in,
    adapter_in_bias,
    adapter_out,
    adapter_out_bias,
):
    core = lax.axis_index("section")
    is_first = core == 0
    tp = lax.axis_size("tp")
    chips = lax.axis_size("ctx") * tp
    chip = lax.axis_index("ctx") * tp + lax.axis_index("tp")
    _, micro, per_micro, part, width = layer_inputs.shape
    row_count = micro * per_micro
    half = part // 2
    length = half * chips

    def pick(first, second):
        return jnp.where(is_first, first, second)

    x = layer_inputs.reshape(row_count, part, width)
    low, high = x[:, :half], x[:, half:]
    other = swap(pick(high, low))
    grads = out_grad.reshape(row_count, part, width)
    stacked = jnp.stack(
        [pick(low, other), pick(other, high), pick(grads[:, :half], grads[:, half:])]
    )
    tail_rows = adapter_out[0].T
    biases = jnp.concatenate([adapter_in_bias[0], adapter_out_bias[0]])
    lanes = adapter_in_bias.shape[1]
    biases = jnp.pad(biases.reshape(-1, lanes), ((0, 256 - biases.size // lanes), (0, 0)))
    shards = [
        jnp.concatenate([qkv_weights[0], out_weights], axis=0).reshape(-1, out_weights.shape[2]),
        ffn_in[0],
        jnp.concatenate([adapter_in[0], tail_rows], axis=1),
        ffn_out[0],
        cross_weights[0].reshape(-1, cross_weights.shape[3]),
        biases,
    ]
    near = lax.axis_size("ctx") == 4 and tp == 4
    if near:
        ids = jnp.stack([src_seg, tgt_seg]).reshape(2 * row_count, -1)
        enc_w, placed, ids = gather_call(0, shards, stacked[:1], ids)
        source = placed.reshape(length, width)
        dec_w, placed, _ = gather_call(1, shards, stacked[1:2], ids[0])
        target = placed.reshape(length, width)
        flat_ids = ids.swapaxes(0, 1).reshape(2, row_count, -1)
    else:
        source, target, cotangent = spread(stacked)
        enc_w, dec_w = gather_plain(0, shards), gather_plain(1, shards)
        flat_ids = [
            lax.all_gather(v.reshape(row_count, -1), "ctx", axis=1, tiled=True)
            for v in (src_seg, tgt_seg)
        ]

    def unpack(full):
        attn, w_in, adapter, w_out, cross, bias = full
        cols = lanes
        attn = attn.reshape(tp, 4, -1, attn.shape[2])
        cross = cross.reshape(tp, 2, -1, cross.shape[2])
        b_out = bias[0, 1 : 1 + width // cols].reshape(width)
        tail = (
            w_in,
            w_out,
            adapter[:, :, :cols],
            bias[:, 0],
            adapter[:, :, cols:],
            b_out,
        )
        return attn, cross, tail

    enc_attn, enc_cross, enc_tail_w = unpack(enc_w)
    dec_attn, dec_cross, dec_tail_w = unpack(dec_w)

    def ids_of(flat):
        row = lax.dynamic_index_in_dim(
            flat, jnp.minimum(chip, row_count - 1), 0, keepdims=False
        )
        return row.reshape(chips, 2, half)

    index = jnp.arange(length, dtype=jnp.int32)
    place = (index // half) * part + index % half

    def cut(seg, which):
        own = lax.dynamic_index_in_dim(seg, which, 1, keepdims=False).reshape(length)
        return own, place + which * half

    src_ids, tgt_ids = ids_of(flat_ids[0]), ids_of(flat_ids[1])

    def id_arrays(seg_q, seg_k):
        qi = jnp.stack(cut(seg_q, core))
        ki = jnp.stack(cut(seg_k, core) + cut(seg_k, 1 - core))
        return (qi.T, ki), (qi, ki.T)

    enc_ids = id_arrays(src_ids, src_ids)
    dec_ids = id_arrays(tgt_ids, tgt_ids)
    cross_ids = id_arrays(tgt_ids, src_ids)

    def scatter(arrays, call_id):
        return Scatter(arrays, row_count, call_id) if near else None

    def tokens(value):
        return value.astype(BF16).reshape(chips, half, width)

    ride = scatter([(stacked[2], Scatter.BRING)], 6)
    enc_mid, enc_self, moved = self_forward(
        source, source.astype(F32), enc_attn, enc_ids, False, ride
    )
    if near:
        cotangent = moved[0].reshape(length, width)
    encoded, enc_tail = tail_forward(enc_mid, enc_tail_w)
    encoded_bf = encoded.astype(BF16)
    memory = [project(encoded_bf, enc_cross[:, j]).astype(BF16) for j in range(2)]
    memory_other = swap(jnp.stack(memory))
    mem_keys = (memory[0], memory_other[0], memory[1], memory_other[1])

    dec_mid, dec_self, _ = self_forward(
        target, target.astype(F32), dec_attn, dec_ids, True
    )
    queries = project(dec_mid.astype(BF16), dec_cross[:, 0]).astype(BF16)
    ride = scatter([(tokens(encoded_bf), 0)], 7)
    (cross_o, cross_lse), out_enc = attention_forward(
        queries, mem_keys, cross_ids[0], False, ride
    )
    second, second_rstd = norm(dec_mid + unproject(cross_o, dec_cross[:, 1]))
    decoded, dec_tail = tail_forward(second, dec_tail_w)

    def pieces(terms):
        d_in, d_bias, d_out, d_last = terms
        cuts = [v.reshape(tp, 4, width // 4, lanes).swapaxes(0, 1) for v in (d_in, d_out)]
        tail = jnp.concatenate(
            [
                d_bias[:, None, :],
                jnp.broadcast_to(d_last.reshape(1, -1, lanes), (tp, width // lanes, lanes)),
            ],
            axis=1,
        )
        tail = jnp.pad(tail, ((0, 0), (0, 16 - tail.shape[1]), (0, 0)))
        tail = jnp.broadcast_to(tail, (4,) + tail.shape)
        first, other = [
            jnp.concatenate([v, tail], axis=2).reshape(4 * tp, -1, lanes) for v in cuts
        ]
        got = swap(pick(other, first).astype(BF16)).astype(F32)
        return (pick(first, other) + got).astype(BF16)

    grad_second, dec_terms = tail_backward(cotangent.astype(F32), dec_tail, dec_tail_w)
    grad_cross = norm_back(second, second_rstd, grad_second)
    do = project(grad_cross.astype(BF16), dec_cross[:, 1]).astype(BF16)
    ride = scatter([(tokens(decoded), 1)], 2)
    (dqc, dmk, dmv), out_dec = attend_back(
        queries, mem_keys, cross_o, do, cross_lse, cross_ids, False, ride
    )
    grad_first = unproject(dqc, dec_cross[:, 0]) + grad_cross
    ride = scatter([(pieces(dec_terms), 1)], 3) if near else None
    grad_target, dec_sum = self_backward(
        grad_first, dec_self, dec_attn, dec_ids, True, ride
    )

    grad_encoded = unproject(dmk, enc_cross[:, 0]) + unproject(dmv, enc_cross[:, 1])
    grad_mid, enc_terms = tail_backward(grad_encoded, enc_tail, enc_tail_w)
    ride = (
        scatter([(pieces(enc_terms), 0), (tokens(grad_target), 1)], 4) if near else None
    )
    grad_source, moved = self_backward(
        grad_mid, enc_self, enc_attn, enc_ids, False, ride
    )

    if near:
        outs = pick(out_enc[0], out_dec[0])
        sums = jnp.sum(pick(moved[0], dec_sum[0]).astype(F32), axis=0)
        last, whole = send_call(
            scatter([(tokens(grad_source), 0)], 5), sums[:, : width // 4].reshape(-1, lanes).astype(BF16)
        )
        grads = pick(last[0], moved[1]).astype(F32)
        whole = whole.astype(F32).reshape(4, 2, width // 4, lanes).swapaxes(0, 1)
        whole = whole.reshape(2, width, lanes)
        return (
            outs.reshape(layer_inputs.shape),
            grads.reshape(layer_inputs.shape),
            whole[0][None],
            sums[0, width // 4][None],
            whole[1].T[None],
            sums[0, width // 4 + 1 : width // 4 + 1 + width // lanes].reshape(1, width),
        )

    has_row = chip < row_count

    def total(enc_term, dec_term):
        enc_term = jnp.where(has_row, enc_term, 0.0).astype(BF16)
        dec_term = jnp.where(has_row, dec_term, 0.0).astype(BF16)
        got = swap(pick(dec_term, enc_term))
        return (pick(enc_term, dec_term).astype(F32) + got.astype(F32)).astype(BF16)

    sums = [total(e, d) for e, d in zip(enc_terms, dec_terms)]
    scattered = [
        lax.psum_scatter(v, "tp", scatter_dimension=0, tiled=False) for v in sums[:3]
    ]
    scattered = [lax.psum(v, "ctx").astype(F32) for v in scattered]
    bias_sum = lax.psum(sums[3], ("ctx", "tp")).astype(F32)

    results = jnp.stack(
        [
            encoded_bf,
            decoded.astype(BF16),
            grad_source.astype(BF16),
            grad_target.astype(BF16),
        ]
    )
    placed = collect(results, row_count)

    def join(enc_part, dec_part):
        mine = pick(enc_part, dec_part)
        got = swap(pick(dec_part, enc_part))
        return jnp.concatenate([pick(mine, got), pick(got, mine)], axis=1)

    outs = join(placed[0], placed[1]).reshape(layer_inputs.shape)
    grads = join(placed[2], placed[3]).astype(F32).reshape(layer_inputs.shape)
    return (
        outs,
        grads,
        scattered[0][None],
        scattered[1][None],
        scattered[2].T[None],
        bias_sum[None],
    )


def solution(mesh):
    return jax.shard_map(
        per_device,
        mesh=mesh,
        in_specs=(
            P("section", None, None, ("ctx", "tp"), None),
            P(None, None, ("ctx", "tp"), None),
            P(None, None, "ctx"),
            P(None, None, "ctx"),
            P("section", None, None, "tp"),
            P("section", None, "tp"),
            P("section", None, None, "tp"),
            P("section", None, "tp"),
            P("section", "tp", None),
            P("section", None, "tp"),
            P("section", "tp"),
            P("section", "tp", None),
            P("section", None),
        ),
        out_specs=(
            P("section", None, None, ("ctx", "tp"), None),
            P("section", None, None, ("ctx", "tp"), None),
            P("section", None, "tp"),
            P("section", "tp"),
            P("section", "tp", None),
            P("section", None),
        ),
        check_vma=False,
    )
```

```python
import functools

import jax
import jax.numpy as jnp
from jax import lax
from jax.experimental import pallas as pl
from jax.experimental.pallas import tpu as pltpu
from jax.sharding import PartitionSpec as P

HEAD = 64
SCALE = HEAD**-0.5
EPS = 1e-05
MASKED = -1e30
F32 = jnp.float32
BF16 = jnp.bfloat16


def swap(value):
    return lax.ppermute(value, "section", [(0, 1), (1, 0)])


def remote(src, dst, send, recv, where):
    return pltpu.make_async_remote_copy(
        src_ref=src,
        dst_ref=dst,
        send_sem=send,
        recv_sem=recv,
        device_id=where,
        device_id_type=pl.DeviceIdType.MESH,
    )


def device_of(section, chip):
    return (section, chip // 4, lax.rem(chip, 4))


def greet_all():
    s = lax.axis_index("section")
    chip = lax.axis_index("ctx") * 4 + lax.axis_index("tp")
    barrier = pltpu.get_barrier_semaphore()
    for core in (0, 1):
        for i in range(core, 16):
            pl.semaphore_signal(
                barrier,
                1,
                device_id=device_of(lax.rem(s + 1 - core, 2), lax.rem(chip + i, 16)),
                device_id_type=pl.DeviceIdType.MESH,
            )
    pl.semaphore_wait(barrier, 31)


class Scatter:
    BRING = 2

    def __init__(self, arrays, rows, call_id):
        self.inputs = [a for a, _ in arrays]
        self.kinds = [k for _, k in arrays]
        self.rows = rows
        self.call_id = call_id
        self.shapes = [
            jax.ShapeDtypeStruct(
                ((16,) if k == self.BRING else (rows, 2)) + a.shape[1:], a.dtype
            )
            for a, k in arrays
        ]
        count = len(arrays)
        self.scratch = [
            pltpu.SemaphoreType.DMA((count, 16)),
            pltpu.SemaphoreType.DMA((count, 16, 2)),
        ]

    def sends(self, ins, outs, sems):
        send, recv = sems
        s = lax.axis_index("section")
        chip = lax.axis_index("ctx") * 4 + lax.axis_index("tp")
        for a, kind in enumerate(self.kinds):
            for i in range(16):
                p = lax.rem(chip + i, 16)
                if kind == self.BRING:
                    ready = p < self.rows
                    src = ins[a].at[jnp.minimum(p, self.rows - 1)]
                    dst = outs[a].at[chip]
                    core, mark = s, 0
                    stays = True
                else:
                    ready = chip < self.rows
                    src = ins[a].at[p]
                    dst = outs[a].at[jnp.minimum(chip, self.rows - 1), s]
                    core, mark = kind, s
                    stays = s == kind
                near = pltpu.make_async_copy(src, dst, send.at[a, i])
                far = remote(
                    src, dst, send.at[a, i], recv.at[a, i, mark], device_of(core, p)
                )
                yield i, ready, stays, near, far

    def start(self, ins, outs, sems):
        greet_all()
        for i, ready, stays, near, far in self.sends(ins, outs, sems):

            @pl.when(ready)
            def _():
                if i:
                    far.start()
                elif stays is True:
                    near.start()
                else:
                    pl.when(stays)(near.start)
                    pl.when(jnp.logical_not(stays))(far.start)

    def finish(self, ins, outs, sems):
        send, recv = sems
        s = lax.axis_index("section")
        chip = lax.axis_index("ctx") * 4 + lax.axis_index("tp")
        for i, ready, stays, near, far in self.sends(ins, outs, sems):

            @pl.when(ready)
            def _():
                if i:
                    far.wait_send()
                elif stays is True:
                    near.wait()
                else:
                    pl.when(stays)(near.wait)
                    pl.when(jnp.logical_not(stays))(far.wait_send)

        def got(region, sem):
            remote(region, region, send.at[0, 0], sem, (1 - s, 0, 0)).wait_recv()

        for a, kind in enumerate(self.kinds):
            for i in range(16):
                sender = lax.rem(chip + 16 - i, 16)
                if kind == self.BRING:
                    if i:

                        @pl.when(chip < self.rows)
                        def _():
                            got(outs[a].at[sender], recv.at[a, i, 0])

                    continue

                @pl.when((s == kind) & (sender < self.rows))
                def _():
                    for core in (0, 1) if i else (1 - kind,):
                        region = outs[a].at[jnp.minimum(sender, self.rows - 1), core]
                        got(region, recv.at[a, i, core])


def split_refs(rider, refs, own_outs):
    count = len(rider.inputs) if rider else 0
    mine = refs[count : count + own_outs]
    outs = refs[count + own_outs : 2 * count + own_outs]
    sems = refs[2 * count + own_outs :]
    return mine, (refs[:count], outs, sems)


def ride_start(rider, parts):
    if rider:
        pl.when(pl.program_id(0) == 0)(lambda: rider.start(*parts))


def ride_finish(rider, parts):
    if rider:
        last = pl.num_programs(0) - 1
        pl.when(pl.program_id(0) == last)(lambda: rider.finish(*parts))


def send_kernel(rider, *refs):
    n = len(rider.inputs)
    block_in, (own, spread_out) = refs[n], (refs[n], refs[2 * n + 1])
    ins, outs = refs[:n], refs[n + 1 : 2 * n + 1]
    sems = refs[2 * n + 2 : 2 * n + 4]
    b_send, b_recv = refs[2 * n + 4 :]
    rider.start(ins, outs, sems)
    s = lax.axis_index("section")
    c = lax.axis_index("ctx")
    t = lax.axis_index("tp")
    dst = spread_out.at[c]
    keep = pltpu.make_async_copy(own, dst, b_send.at[0])
    keep.start()
    ways = [
        remote(own, dst, b_send.at[j], b_recv.at[j], (s, lax.rem(c + j, 4), t))
        for j in (1, 2, 3)
    ]
    for way in ways:
        way.start()
    keep.wait()
    for j, way in enumerate(ways):
        way.wait_send()
        region = spread_out.at[lax.rem(c + 3 - j, 4)]
        remote(region, region, b_send.at[0], b_recv.at[j + 1], (s, c, t)).wait_recv()
    rider.finish(ins, outs, sems)


def send_call(rider, block):
    anywhere = pl.BlockSpec(memory_space=pl.ANY)
    count = len(rider.inputs)
    result = pl.pallas_call(
        functools.partial(send_kernel, rider),
        in_specs=[anywhere] * (count + 1),
        out_specs=[anywhere] * (count + 1),
        out_shape=rider.shapes + [jax.ShapeDtypeStruct((4,) + block.shape, block.dtype)],
        scratch_shapes=rider.scratch
        + [pltpu.SemaphoreType.DMA((4,)), pltpu.SemaphoreType.DMA((4,))],
        compiler_params=pltpu.CompilerParams(
            collective_id=rider.call_id, has_side_effects=True
        ),
        name="send_last",
    )(*rider.inputs, block)
    return result[:count], result[count]


def dot_nt(left, right, **kw):
    return lax.dot_general(
        left, right, (((1,), (1,)), ((), ())), preferred_element_type=F32, **kw
    )


def dot_nn(left, right):
    return lax.dot_general(
        left, right, (((1,), (0,)), ((), ())), preferred_element_type=F32
    )


def dot_tn(left, right):
    return lax.dot_general(
        left, right, (((0,), (0,)), ((), ())), preferred_element_type=F32
    )


def attn_fwd_kernel(
    causal, rider, q_ref, ko_ref, kx_ref, vo_ref, vx_ref, qi_ref, ki_ref, o_ref, lse_ref
):
    attend_group(
        0,
        q_ref,
        (ko_ref, kx_ref),
        (vo_ref, vx_ref),
        o_ref,
        lse_ref,
        (qi_ref[:, 0:1], qi_ref[:, 1:2]),
        [(ki_ref[i : i + 1, :], ki_ref[i + 1 : i + 2, :]) for i in (0, 2)],
        causal,
    )


def attention_call(kernel, name, causal, rider, blocks, small, outs):
    groups = blocks[0].shape[0]
    anywhere = pl.BlockSpec(memory_space=pl.ANY)
    extra = rider.inputs if rider else []
    params = {"vmem_limit_bytes": 48 * 2**20}
    if rider:
        params.update(collective_id=rider.call_id, has_side_effects=True)

    def group_spec(shape):
        return pl.BlockSpec((1,) + shape[1:], lambda t: (t, 0, 0))

    result = pl.pallas_call(
        functools.partial(kernel, causal, rider),
        grid=(groups,),
        in_specs=[group_spec(v.shape) for v in blocks]
        + [pl.BlockSpec(v.shape, lambda t: (0, 0)) for v in small]
        + [anywhere] * len(extra),
        out_specs=[group_spec(v.shape) for v in outs] + [anywhere] * len(extra),
        out_shape=outs + (rider.shapes if rider else []),
        scratch_shapes=rider.scratch if rider else [],
        compiler_params=pltpu.CompilerParams(**params),
        name=name,
    )(*blocks, *small, *extra)
    return result[: len(outs)], result[len(outs) :]


def attention_forward(q, keys, ids, causal, rider=None):
    groups, length, width = q.shape
    outs = [
        jax.ShapeDtypeStruct(q.shape, BF16),
        jax.ShapeDtypeStruct((groups, width // HEAD, length), F32),
    ]
    return attention_call(
        attn_fwd_kernel, "attn_fwd", causal, rider, [q, *keys], ids, outs
    )


def attn_bwd_kernel(
    causal,
    rider,
    q_ref,
    ko_ref,
    kx_ref,
    vo_ref,
    vx_ref,
    o_ref,
    do_ref,
    lse_ref,
    qi_ref,
    ki_ref,
    *rest,
):
    (dq_ref, dko_ref, dkx_ref, dvo_ref, dvx_ref), parts_ride = split_refs(rider, rest, 5)
    ride_start(rider, parts_ride)
    length = q_ref.shape[1]
    heads = q_ref.shape[2] // HEAD
    block = length // 2
    segq = qi_ref[0:1, :]
    posq = qi_ref[1:2, :]
    ones = jnp.ones((8, HEAD), F32)
    for h in range(heads):
        cols = slice(h * HEAD, (h + 1) * HEAD)
        q_all = q_ref[0, :, cols] * jnp.asarray(SCALE, BF16)
        do_all = do_ref[0, :, cols]
        prod = do_all.astype(F32) * o_ref[0, :, cols].astype(F32)
        delta = dot_nt(ones, prod, precision=lax.Precision.HIGHEST)[0:1]
        lse = lse_ref[0, h : h + 1, :]
        dq = [jnp.zeros((block, HEAD), F32), jnp.zeros((block, HEAD), F32)]
        for k_ref, v_ref, dk_ref, dv_ref, i in (
            (ko_ref, vo_ref, dko_ref, dvo_ref, 0),
            (kx_ref, vx_ref, dkx_ref, dvx_ref, 2),
        ):
            for b in range(2):
                rows = slice(b * block, (b + 1) * block)
                first = b * block if causal else 0
                q = q_all[first:]
                do = do_all[first:]
                k = k_ref[0, rows, cols]
                s = dot_nt(k, q)
                ok = ki_ref[rows, i : i + 1] == segq[:, first:]
                if causal:
                    ok = ok & (posq[:, first:] >= ki_ref[rows, i + 1 : i + 2])
                p = jnp.where(ok, jnp.exp(s - lse[:, first:]), 0.0)
                dp = dot_nt(v_ref[0, rows, cols], do)
                ds = (p * (dp - delta[:, first:])).astype(BF16)
                dv_ref[0, rows, cols] = dot_nn(p.astype(BF16), do).astype(BF16)
                dk_ref[0, rows, cols] = dot_nn(ds, q).astype(BF16)
                part = dot_tn(ds, k)
                if first:
                    dq[1] = dq[1] + part
                else:
                    dq[0] = dq[0] + part[:block]
                    dq[1] = dq[1] + part[block:]
        dq_ref[0, :block, cols] = (dq[0] * SCALE).astype(BF16)
        dq_ref[0, block:, cols] = (dq[1] * SCALE).astype(BF16)
    ride_finish(rider, parts_ride)


def attention_backward(q, keys, o, do, lse, ids, causal, rider=None):
    outs = [jax.ShapeDtypeStruct(q.shape, BF16)] * 5
    return attention_call(
        attn_bwd_kernel, "attn_bwd", causal, rider, [q, *keys, o, do, lse], ids, outs
    )


def norm(value):
    mean = jnp.mean(value, axis=-1, keepdims=True)
    centered = value - mean
    rstd = lax.rsqrt(jnp.mean(centered * centered, axis=-1, keepdims=True) + EPS)
    return centered * rstd, rstd


def norm_back(normed, rstd, grad):
    return rstd * (
        grad
        - jnp.mean(grad, axis=-1, keepdims=True)
        - normed * jnp.mean(grad * normed, axis=-1, keepdims=True)
    )


def project(rows, weight):
    return jnp.einsum("pk,tkm->tpm", rows, weight, preferred_element_type=F32)


def unproject(blocks, weight):
    return jnp.einsum("tpm,tkm->pk", blocks, weight, preferred_element_type=F32)


def self_forward(rows_bf, rows, w_attn, ids, causal, rider=None):
    kv = [project(rows_bf, w_attn[:, j]).astype(BF16) for j in (1, 2)]
    other = swap(jnp.stack(kv))
    q = project(rows_bf, w_attn[:, 0]).astype(BF16)
    keys = (kv[0], other[0], kv[1], other[1])
    (o, lse), moved = attention_forward(q, keys, ids[0], causal, rider)
    h, rstd = norm(rows + unproject(o, w_attn[:, 3]))
    return h, (q, keys, o, lse, h, rstd), moved


def attend_back(q, keys, o, do, lse, ids, causal, rider=None):
    (dq, dko, dkx, dvo, dvx), moved = attention_backward(
        q, keys, o, do, lse, ids[1], causal, rider
    )
    other = swap(jnp.stack([dkx, dvx])).astype(F32)
    dk = (dko.astype(F32) + other[0]).astype(BF16)
    dv = (dvo.astype(F32) + other[1]).astype(BF16)
    return (dq, dk, dv), moved


def self_backward(grad, kept, w_attn, ids, causal, rider=None):
    q, keys, o, lse, h, rstd = kept
    dpre = norm_back(h, rstd, grad)
    do = project(dpre.astype(BF16), w_attn[:, 3]).astype(BF16)
    (dq, dk, dv), moved = attend_back(q, keys, o, do, lse, ids, causal, rider)
    total = (
        unproject(dq, w_attn[:, 0])
        + unproject(dk, w_attn[:, 1])
        + unproject(dv, w_attn[:, 2])
        + dpre
    )
    return total, moved


def tail_forward(h, tail_w):
    w_in, w_out, a_in, b_in, a_out, b_out = tail_w
    rows = h.astype(BF16)
    inner = project(rows, w_in)
    phi = 0.5 * (1.0 + lax.erf(inner * 0.7071067811865476))
    g = (inner * phi).astype(BF16)
    slope = phi + inner * jnp.exp(inner * inner * -0.5) * 0.3989422804014327
    pre = project(rows, a_in) + b_in.astype(F32)[:, None, :]
    sig = jax.nn.sigmoid(pre)
    s = (pre * sig).astype(BF16)
    a_slope = sig * (1.0 + pre * (1.0 - sig))
    total = jnp.einsum("tpm,tmk->pk", g, w_out, preferred_element_type=F32)
    total += 4.0 * (
        jnp.einsum("tpm,tkm->pk", s, a_out, preferred_element_type=F32)
        + b_out.astype(F32)
    )
    y, rstd = norm(h + total)
    return y, (rows, slope.astype(BF16), s, a_slope.astype(BF16), y, rstd)


def tail_backward(grad, kept, tail_w):
    w_in, w_out, a_in, b_in, a_out, b_out = tail_w
    rows, slope, s, a_slope, y, rstd = kept
    dpre = norm_back(y, rstd, grad)
    db = dpre.astype(BF16)
    dg = jnp.einsum("pk,tmk->tpm", db, w_out, preferred_element_type=F32)
    df = (dg * slope.astype(F32)).astype(BF16)
    ds = 4.0 * jnp.einsum("pk,tkm->tpm", db, a_out, preferred_element_type=F32)
    du = (ds * a_slope.astype(F32)).astype(BF16)
    terms = (
        jnp.einsum("pk,tpm->tkm", rows, du, preferred_element_type=F32),
        jnp.sum(du.astype(F32), axis=1),
        4.0 * jnp.einsum("pk,tpm->tkm", db, s, preferred_element_type=F32),
        4.0 * jnp.sum(db.astype(F32), axis=0),
    )
    return unproject(df, w_in) + unproject(du, a_in) + dpre, terms


def attend_group(t, q_ref, k_refs, v_refs, o_ref, lse_ref, col, row, causal):
    length = q_ref.shape[1]
    heads = q_ref.shape[2] // HEAD
    block = length // 2
    segq, posq = col
    for h in range(heads):
        cols = slice(h * HEAD, (h + 1) * HEAD)
        for b in range(2):
            rows = slice(b * block, (b + 1) * block)
            span = (b + 1) * block if causal else length
            q = q_ref[t, rows, cols] * jnp.asarray(SCALE, BF16)
            parts = []
            for k_ref, (segk, posk) in zip(k_refs, row):
                s = dot_nt(q, k_ref[t, :span, cols])
                ok = segq[rows] == segk[:, :span]
                if causal:
                    ok = ok & (posq[rows] >= posk[:, :span])
                parts.append(jnp.where(ok, s, MASKED))
            top = jnp.maximum(
                jnp.max(parts[0], axis=1, keepdims=True),
                jnp.max(parts[1], axis=1, keepdims=True),
            )
            ex = [jnp.exp(p - top) for p in parts]
            total = jnp.sum(ex[0], axis=1, keepdims=True) + jnp.sum(
                ex[1], axis=1, keepdims=True
            )
            out = dot_nn(ex[0].astype(BF16), v_refs[0][t, :span, cols]) + dot_nn(
                ex[1].astype(BF16), v_refs[1][t, :span, cols]
            )
            o_ref[t, rows, cols] = (out / total).astype(BF16)
            lse = top + jnp.log(total)
            lse_ref[t, h : h + 1, rows] = jnp.broadcast_to(lse, (block, 128)).T[0:1]


ATTN, FFN_IN, FFN_OUT, ADAPTER, CROSS = range(5)
ORDER = (
    (0, ATTN),
    (1, ATTN),
    (0, FFN_IN),
    (0, FFN_OUT),
    (0, ADAPTER),
    (0, CROSS),
    (1, CROSS),
    (1, FFN_IN),
    (1, FFN_OUT),
    (1, ADAPTER),
)
WORK = (
    ("enc_qkv", 4, (0, ATTN), 2.0),
    ("enc_attn", 4, None, 5.5),
    ("enc_out", 1, None, 4.0),
    ("dec_qkv", 4, (1, ATTN), 2.0),
    ("dec_attn", 4, None, 5.5),
    ("dec_out", 1, None, 4.0),
    ("ffn", 8, (0, FFN_OUT), 2.5),
    ("adapter", 1, (0, ADAPTER), 4.0),
    ("memory", 4, (0, CROSS), 1.5),
    ("cross_q", 1, (1, CROSS), 4.0),
    ("cross_attn", 4, None, 5.5),
    ("cross_out", 1, None, 4.0),
    ("end", 1, (1, ADAPTER), 0.0),
)


def plan_steps(sizes):
    ready, clock = [], 20.0
    for e, g in ORDER:
        for _ in range(3):
            clock += sizes[g] / 3 * 14e-6
            ready.append(clock)
    ticks = len(ready) + 2
    ready += [clock + 4, clock + 8]
    starts, at, step, now, done = {}, {}, 0, 0.0, 0
    for name, count, need, cost in WORK:
        starts[name] = step
        for n in range(count):
            while done < ticks and (
                ready[done] <= now
                or (need and done <= 3 * ORDER.index(need) + 4)
            ):
                at[done] = step
                now = max(now, ready[done])
                done += 1
            now += cost
            step += 1
    for n in range(done, ticks):
        at[n] = step - 1
    return starts, at, step


KEPT = (
    ("eq", "heads"),
    ("ek", "heads"),
    ("ekx", "heads"),
    ("ev", "heads"),
    ("evx", "heads"),
    ("eo", "heads"),
    ("el", "lse"),
    ("eh", "wide"),
    ("er", "rstd"),
    ("es", "adapter"),
    ("ea", "adapter"),
    ("ey", "wide"),
    ("eyr", "rstd"),
    ("dq", "heads"),
    ("dk", "heads"),
    ("dkx", "heads"),
    ("dv", "heads"),
    ("dvx", "heads"),
    ("do", "heads"),
    ("dl", "lse"),
    ("dh", "wide"),
    ("dr", "rstd"),
    ("mk", "heads"),
    ("mkx", "heads"),
    ("mv", "heads"),
    ("mvx", "heads"),
    ("cq", "heads"),
    ("co", "heads"),
    ("cl", "lse"),
    ("c2", "wide"),
    ("c2r", "rstd"),
)


def forward_kernel(plan, rows, *refs):
    starts, tick_step, steps = plan
    refs = list(refs)

    def take(count):
        got = refs[:count]
        del refs[:count]
        return got

    shards = take(5)
    tokens = take(3)
    col_ref, row_ref = take(2)
    full = (take(5), take(5))
    (grads_out,) = take(1)
    (slope_out,) = take(1)
    kept_out = dict(zip([n for n, _ in KEPT], take(len(KEPT))))
    kept = dict(zip([n for n, _ in KEPT], take(len(KEPT))))
    xs = take(2)
    wb, wi, wo, wad, slope = take(5)
    store_a, store_f = take(2)
    (
        z_send,
        z_recv,
        n_send,
        n_recv,
        f_send,
        f_recv,
        s_send,
        s_recv,
        own_sem,
        t_send,
        t_recv,
        kv_send,
        kv_recv,
        load_sem,
        out_sem,
        slope_sem,
    ) = refs
    step = pl.program_id(0)
    s = lax.axis_index("section")
    c = lax.axis_index("ctx")
    t = lax.axis_index("tp")
    chips = 16
    chip = c * 4 + t
    cx = c + 1 - 2 * lax.rem(c, 2)
    cy = lax.rem(c + 2, 4)
    cd = 3 - c
    sib = (1 - s, c, t)

    def xor(k):
        return {1: t + 1 - 2 * lax.rem(t, 2), 2: lax.rem(t + 2, 4), 3: 3 - t}[k]

    landing = (xs[0], xs[1], grads_out)

    def token_copy(kind, i):
        p = lax.rem(chip + i, chips)
        src = tokens[kind].at[jnp.minimum(p, rows - 1)]
        dst = landing[kind].at[chip]
        if i == 0:
            return p, pltpu.make_async_copy(src, dst, t_send.at[kind, 0])
        return p, remote(
            src, dst, t_send.at[kind, i], t_recv.at[kind, i], device_of(s, p)
        )

    def send_tokens(kind):
        for i in range(chips):
            p, copy = token_copy(kind, i)
            pl.when(p < rows)(copy.start)

    def got(region, sem):
        remote(region, region, load_sem.at[0], sem, sib).wait_recv()

    def wait_tokens(kind):
        for i in range(chips):
            p, copy = token_copy(kind, i)
            pl.when(p < rows)(copy.wait if i == 0 else copy.wait_send)
            if i:

                @pl.when(chip < rows)
                def _():
                    got(
                        landing[kind].at[lax.rem(chip + chips - i, chips)],
                        t_recv.at[kind, i],
                    )

    items = [(n, k) for n in range(len(ORDER)) for k in (1, 2, 3)]
    window = 4

    def block(n, who, h, q, u=None):
        e, g = ORDER[n]
        size = shards[g].shape[0]
        start = h * (size // 2) + q * (size // 8)
        length = size // 8
        if u is not None:
            length = size // 16
            start = start + u * length
        return full[e][g].at[who, pl.ds(pl.multiple_of(start, 16), length)]

    def z_copy(n, k, h):
        g = ORDER[n][1]
        size = shards[g].shape[0]
        start = h * (size // 2) + c * (size // 8)
        return remote(
            shards[g].at[pl.ds(pl.multiple_of(start, 16), size // 8)],
            block(n, t, h, c),
            z_send.at[n, k - 1, h],
            z_recv.at[n, k - 1],
            (h, c, xor(k)),
        )

    def store(g):
        if g in (FFN_IN, FFN_OUT):
            return store_f
        return store_a.at[pl.ds(0, shards[g].shape[0])]

    def fetch(n):
        g = ORDER[n][1]
        return pltpu.make_async_copy(shards[g], store(g), own_sem.at[n, 3])

    def put(n):
        e, g = ORDER[n]
        return pltpu.make_async_copy(store(g), full[e][g].at[t], own_sem.at[n, 0])

    def far(n):
        e, g = ORDER[n]
        return remote(
            shards[g], full[e][g].at[t], own_sem.at[n, 1], own_sem.at[n, 2], sib
        )

    def before(n):
        e, g = ORDER[n]
        pool = (FFN_IN, FFN_OUT) if g in (FFN_IN, FFN_OUT) else (ATTN, ADAPTER, CROSS)
        olds = [m for m in range(n) if ORDER[m][0] == e and ORDER[m][1] in pool]
        return olds[-1] if olds else None

    def start_z(i):
        n, k = items[i]

        @pl.when(s == ORDER[n][0])
        def _():
            if k == 1:
                far(n).start()
            for h in range(2):
                z_copy(n, k, h).start()

    def near_copy(n, k, j):
        src = block(n, xor(k), s, c)
        return remote(
            src,
            src,
            n_send.at[n, k - 1, j],
            n_recv.at[n, k - 1, j],
            (s, (cx, cy)[j], t),
        )

    def sibling_copy(n, k, j):
        src = block(n, xor(k), s, (c, cx, cy, cd)[j])
        return remote(src, src, s_send.at[n, k - 1, j], s_recv.at[n, k - 1, j], sib)

    def forward_copy(n, k, j):
        src = block(n, xor(k), s, (cx, cy)[j], j)
        return remote(
            src,
            src,
            f_send.at[n, k - 1, j],
            f_recv.at[n, k - 1, j],
            (s, (cy, cx)[j], t),
        )

    def stage2(i):
        n, k = items[i]
        got(block(n, xor(k), s, c), z_recv.at[n, k - 1])
        near_copy(n, k, 0).start()
        near_copy(n, k, 1).start()
        sibling_copy(n, k, 0).start()
        if k == 2:
            return

        @pl.when(s == ORDER[n][0])
        def _():
            if k == 1:
                old = before(n)
                if old is not None and not put_read_first(old, i):
                    put(old).wait()
                fetch(n).start()
            else:
                fetch(n).wait()
                put(n).start()

    def stage3(i):
        n, k = items[i]
        for j, q in ((0, cx), (1, cy)):
            got(block(n, xor(k), s, q), n_recv.at[n, k - 1, j])
            forward_copy(n, k, j).start()
            sibling_copy(n, k, j + 1).start()

    def stage4(i):
        n, k = items[i]
        for u in range(2):
            got(block(n, xor(k), s, cd, u), f_recv.at[n, k - 1, u])
        sibling_copy(n, k, 3).start()

    count = len(items)

    def tick(i):
        if i < count:
            stage2(i)
            if i + window < count:
                start_z(i + window)
        if 0 <= i - 1 < count:
            stage3(i - 1)
        if 0 <= i - 2 < count:
            stage4(i - 2)
        if i == 3:
            send_tokens(1)
        if i == 18:
            send_tokens(2)

    def arrive_step(n):
        for name, _, need, _ in WORK[:-1]:
            if need == ORDER[n]:
                return starts[name]
        return starts["ffn"] if ORDER[n] == (0, FFN_IN) else steps - 1

    def put_read_first(n, i):
        return arrive_step(n) < tick_step[i]

    def put_left(n):
        after = [m for m in range(len(ORDER)) if before(m) == n]
        return not after or put_read_first(n, 3 * after[0])

    def arrive(n):
        e, g = ORDER[n]
        for k in (1, 2, 3):
            for j, q in enumerate((c, cx, cy, cd)):
                got(block(n, xor(k), 1 - s, q), s_recv.at[n, k - 1, j])

        @pl.when(s == e)
        def _():
            if put_left(n):
                put(n).wait()

        @pl.when(s != e)
        def _():
            got(full[e][g].at[t], own_sem.at[n, 2])

    @pl.when(step == 0)
    def _():
        greet_all()
        send_tokens(0)
        for i in range(window):
            start_z(i)

    for i in range(count + 2):
        pl.when(step == tick_step[i])(functools.partial(tick, i))

    def on(name):
        first = starts[name]
        last = first + [w[1] for w in WORK if w[0] == name][0]
        need = [w[2] for w in WORK if w[0] == name][0]
        if need and name != "end":
            pl.when(step == first)(functools.partial(arrive, ORDER.index(need)))
        return step - first, pl.when((step >= first) & (step < last))

    def load(src, dst, slot=0):
        return pltpu.make_async_copy(src, dst, load_sem.at[slot])

    def keep(*names):
        for n in names:
            pltpu.make_async_copy(kept[n], kept_out[n], out_sem.at[KEYS.index(n)]).start()

    KEYS = [n for n, _ in KEPT]
    attn_rows = full[0][ATTN].shape[1] // 4

    def kv_copies(which, g, names):
        k, kx, v, vx = names
        return [
            remote(
                kept[a].at[g], kept[b].at[g], kv_send.at[which, g, j], kv_recv.at[which, g, j], sib
            )
            for j, (a, b) in enumerate(((k, kx), (v, vx)))
        ]

    def projections(name, which, e, g_id, x, names, first_row, last_step):
        i, when = on(name)
        tiles = len(names)
        height = tiles * attn_rows

        def source(j):
            return full[e][g_id].at[j, pl.ds(first_row, height)]

        @when
        def _():
            slot = lax.rem(i, 2)

            @pl.when(i == 0)
            def _():
                load(source(0), wb.at[0, pl.ds(0, height)]).start()

            load(source(0), wb.at[slot, pl.ds(0, height)]).wait()

            @pl.when(i < 3)
            def _():
                load(source(jnp.minimum(i + 1, 3)), wb.at[1 - slot, pl.ds(0, height)]).start()

            rows_in = x()
            for n, name_out in enumerate(names):
                w = wb[slot, n * attn_rows : (n + 1) * attn_rows, :]
                kept[name_out][i] = dot_nn(rows_in, w).astype(BF16)
            keys = {0: ("ek", "ekx", "ev", "evx"), 1: ("dk", "dkx", "dv", "dvx"), 2: ("mk", "mkx", "mv", "mvx")}[which]
            for copy in kv_copies(which, i, keys):
                copy.start()

        return keys_of[which]

    keys_of = (
        ("ek", "ekx", "ev", "evx"),
        ("dk", "dkx", "dv", "dvx"),
        ("mk", "mkx", "mv", "mvx"),
    )

    def attend(name, which, prefix, col_id, row_ids, causal):
        i, when = on(name)
        k, kx, v, vx = keys_of[which]

        @when
        def _():
            for j, copy in enumerate(kv_copies(which, i, keys_of[which])):
                copy.wait_send()
                copy.wait_recv()
            attend_group(
                i,
                kept[prefix + "q"],
                (kept[k], kept[kx]),
                (kept[v], kept[vx]),
                kept[prefix + "o"],
                kept[prefix + "l"],
                (col_ref[:, col_id : col_id + 1], col_ref[:, 2:3]),
                [
                    (row_ref[r : r + 1, :], row_ref[p : p + 1, :])
                    for r, p in zip(row_ids, (4, 5))
                ],
                causal,
            )

            @pl.when(i == 3)
            def _():
                keep(prefix + "q", k, kx, v, vx, prefix + "o", prefix + "l")

    def tiles4(e, g_id, first_row):
        copies = [
            load(
                full[e][g_id].at[j, pl.ds(first_row, attn_rows)],
                wb.at[0, pl.ds(j * attn_rows, attn_rows)],
                j,
            )
            for j in range(4)
        ]
        for copy in copies:
            copy.start()
        for copy in copies:
            copy.wait()

    def out_norm(name, e, g_id, first_row, residual, source, wide, rstd_name):
        _, when = on(name)

        @when
        def _():
            tiles4(e, g_id, first_row)
            total = residual()
            for j in range(4):
                total = total + dot_nt(
                    kept[source][j], wb[0, j * attn_rows : (j + 1) * attn_rows, :]
                )
            normed, rstd = norm(total)
            kept[wide][...] = normed
            kept[rstd_name][...] = jnp.broadcast_to(rstd, kept[rstd_name].shape)
            keep(wide, rstd_name)

    def flat_x(n):
        shape = xs[n].shape
        return xs[n][...].reshape(shape[0] * shape[1], shape[2])

    for e, (name, p) in enumerate((("enc", "e"), ("dec", "d"))):

        @pl.when(step == starts[name + "_qkv"])
        def _():
            wait_tokens(e)

        projections(
            name + "_qkv",
            e,
            e,
            ATTN,
            functools.partial(flat_x, e),
            (p + "q", p + "k", p + "v"),
            0,
            None,
        )
        attend(name + "_attn", e, p, e, ((0, 1), (2, 3))[e], e == 1)
        out_norm(
            name + "_out",
            e,
            ATTN,
            3 * attn_rows,
            lambda: flat_x(e).astype(F32),
            p + "o",
            p + "h",
            p + "r",
        )

    i, when = on("ffn")
    hidden = wi.shape[2]

    @pl.when(step == starts["ffn"])
    def _():
        arrive(ORDER.index((0, FFN_IN)))

    def ffn_loads(j, slot):
        g, u = j // 2, lax.rem(j, 2)
        span = pl.ds(pl.multiple_of(u * hidden, 128), hidden)
        return (
            load(full[0][FFN_IN].at[g, :, span], wi.at[slot], 2 * slot),
            load(full[0][FFN_OUT].at[g, span], wo.at[slot], 2 * slot + 1),
        )

    def slope_copy(j, slot):
        g, u = j // 2, lax.rem(j, 2)
        span = pl.ds(pl.multiple_of(u * hidden, 128), hidden)
        return pltpu.make_async_copy(
            slope.at[slot], slope_out.at[g, :, span], slope_sem.at[slot]
        )

    @when
    def _():
        slot = lax.rem(i, 2)

        @pl.when(i == 0)
        def _():
            for copy in ffn_loads(0, 0):
                copy.start()
            kept["ey"][...] = jnp.zeros_like(kept["ey"])

        for copy in ffn_loads(i, slot):
            copy.wait()

        @pl.when(i < 7)
        def _():
            for copy in ffn_loads(i + 1, 1 - slot):
                copy.start()

        @pl.when(i >= 2)
        def _():
            slope_copy(i - 2, slot).wait()

        inner = dot_nn(kept["eh"][...].astype(BF16), wi[slot])
        phi = 0.5 * (1.0 + lax.erf(inner * 0.7071067811865476))
        slope[slot] = (
            phi + inner * jnp.exp(inner * inner * -0.5) * 0.3989422804014327
        ).astype(BF16)
        slope_copy(i, slot).start()
        kept["ey"][...] += dot_nn((inner * phi).astype(BF16), wo[slot])

    i, when = on("adapter")

    @when
    def _():
        for j in range(2):
            slope_copy(6 + j, j).wait()
        copy = load(full[0][ADAPTER], wad)
        copy.start()
        copy.wait()
        h = kept["eh"][...]
        rows_in = h.astype(BF16)
        lanes = wad.shape[2] // 2
        extra = wad[0, attn_rows : attn_rows + 16, :].astype(F32)
        last = jnp.concatenate([extra[1 + r : 2 + r] for r in range(4)], axis=1)
        total = 4.0 * last
        for j in range(4):
            bias = wad[j, attn_rows : attn_rows + 16, :lanes].astype(F32)[0:1]
            pre = dot_nn(rows_in, wad[j, :attn_rows, :lanes]) + bias
            sig = 1.0 / (1.0 + jnp.exp(-pre))
            gated = (pre * sig).astype(BF16)
            kept["es"][j] = gated
            kept["ea"][j] = (sig * (1.0 + pre * (1.0 - sig))).astype(BF16)
            total = total + 4.0 * dot_nt(gated, wad[j, :attn_rows, lanes:])
        normed, rstd = norm(h + (kept["ey"][...] + total))
        kept["ey"][...] = normed
        kept["eyr"][...] = jnp.broadcast_to(rstd, kept["eyr"].shape)
        keep("es", "ea", "ey", "eyr")

    projections(
        "memory", 2, 0, CROSS, lambda: kept["ey"][...].astype(BF16), ("mk", "mv"), 0, None
    )
    _, when = on("cross_q")

    @when
    def _():
        tiles4(1, CROSS, 0)
        rows_in = kept["dh"][...].astype(BF16)
        for j in range(4):
            kept["cq"][j] = dot_nn(
                rows_in, wb[0, j * attn_rows : (j + 1) * attn_rows, :]
            ).astype(BF16)

    attend("cross_attn", 2, "c", 1, (0, 1), False)
    out_norm(
        "cross_out", 1, CROSS, attn_rows, lambda: kept["dh"][...], "co", "c2", "c2r"
    )

    @pl.when(step == steps - 1)
    def _():
        for g in (FFN_IN, FFN_OUT, ADAPTER):
            arrive(ORDER.index((1, g)))
        wait_tokens(2)
        for n, k in items:
            for j in range(2):
                near_copy(n, k, j).wait_send()
                forward_copy(n, k, j).wait_send()
            for j in range(4):
                sibling_copy(n, k, j).wait_send()
        for n in range(len(ORDER)):

            @pl.when(s == ORDER[n][0])
            def _():
                far(n).wait_send()
                for k in (1, 2, 3):
                    for h in range(2):
                        z_copy(n, k, h).wait_send()

        for n, (name, _) in enumerate(KEPT):
            pltpu.make_async_copy(kept[name], kept_out[name], out_sem.at[n]).wait()


def forward_call(shards, tokens, col, row):
    part, width = tokens[0].shape[1:]
    length = 16 * part
    groups = len(ORDER)
    dma = pltpu.SemaphoreType.DMA
    anywhere = pl.BlockSpec(memory_space=pl.ANY)
    shapes = {
        "heads": ((4, length, shards[ATTN].shape[1]), BF16),
        "lse": ((4, shards[ATTN].shape[1] // HEAD, length), F32),
        "wide": ((length, width), F32),
        "rstd": ((length, 128), F32),
        "adapter": ((4, length, shards[ADAPTER].shape[1] // 2), BF16),
    }
    kept = [shapes[kind] for _, kind in KEPT]
    hidden = shards[FFN_IN].shape[1]
    sizes = [
        (groups, 3, 2),
        (groups, 3),
        (groups, 3, 2),
        (groups, 3, 2),
        (groups, 3, 2),
        (groups, 3, 2),
        (groups, 3, 4),
        (groups, 3, 4),
        (groups, 4),
        (3, 16),
        (3, 16),
        (3, 4, 2),
        (3, 4, 2),
        (4,),
        (len(KEPT),),
        (2,),
    ]
    plan = plan_steps([v.size * 2 for v in shards])
    result = pl.pallas_call(
        functools.partial(forward_kernel, plan, tokens[0].shape[0]),
        grid=(plan[2],),
        in_specs=[anywhere] * 8
        + [
            pl.BlockSpec(col.shape, lambda i: (0, 0)),
            pl.BlockSpec(row.shape, lambda i: (0, 0)),
        ],
        out_specs=[anywhere] * (12 + len(KEPT)),
        out_shape=[jax.ShapeDtypeStruct((4,) + v.shape, v.dtype) for v in shards] * 2
        + [
            jax.ShapeDtypeStruct((16, part, width), BF16),
            jax.ShapeDtypeStruct((4, length, hidden), BF16),
        ]
        + [jax.ShapeDtypeStruct(*v) for v in kept],
        scratch_shapes=[pltpu.VMEM(*v) for v in kept]
        + [pltpu.VMEM((16, part, width), BF16)] * 2
        + [
            pltpu.VMEM((2,) + shards[ATTN].shape, BF16),
            pltpu.VMEM((2, width, hidden // 2), BF16),
            pltpu.VMEM((2, hidden // 2, width), BF16),
            pltpu.VMEM((4,) + shards[ADAPTER].shape, BF16),
            pltpu.VMEM((2, length, hidden // 2), BF16),
            pltpu.VMEM(shards[ATTN].shape, BF16),
            pltpu.VMEM(shards[FFN_IN].shape, BF16),
        ]
        + [dma(size) for size in sizes],
        compiler_params=pltpu.CompilerParams(
            collective_id=0, has_side_effects=True, vmem_limit_bytes=60 * 2**20
        ),
        name="forward",
    )(*shards, *tokens, col, row)
    kept = dict(zip([n for n, _ in KEPT], result[12:]))
    return result[:5], result[5:10], result[10], result[11], kept


def ids_kernel(ids, out, send, recv):
    s = lax.axis_index("section")
    c = lax.axis_index("ctx")
    t = lax.axis_index("tp")
    barrier = pltpu.get_barrier_semaphore()
    for j in (1, 2, 3):
        pl.semaphore_signal(
            barrier,
            1,
            device_id=(s, lax.rem(c + j, 4), t),
            device_id_type=pl.DeviceIdType.MESH,
        )
    pl.semaphore_wait(barrier, 3)
    out[c] = ids[...]
    ways = [
        remote(ids, out.at[c], send.at[j - 1], recv.at[j - 1], (s, lax.rem(c + j, 4), t))
        for j in (1, 2, 3)
    ]
    for way in ways:
        way.start()
    for j, way in enumerate(ways):
        way.wait_send()
        region = out.at[lax.rem(c + 3 - j, 4)]
        remote(region, region, send.at[j], recv.at[j], (s, c, t)).wait_recv()


def ids_call(ids):
    spec = pl.BlockSpec(memory_space=pltpu.VMEM)
    return pl.pallas_call(
        ids_kernel,
        in_specs=[spec],
        out_specs=spec,
        out_shape=jax.ShapeDtypeStruct((4,) + ids.shape, ids.dtype),
        scratch_shapes=[pltpu.SemaphoreType.DMA((3,)), pltpu.SemaphoreType.DMA((3,))],
        compiler_params=pltpu.CompilerParams(collective_id=1, has_side_effects=True),
        name="ids",
    )(ids)


def gather_plain(entry, shards):
    full = [lax.all_gather(lax.all_gather(v, "tp"), "section") for v in shards]
    return [v[entry] for v in full]


def spread(blocks):
    chips = lax.axis_size("ctx") * lax.axis_size("tp")
    kinds, rows, part, width = blocks.shape
    blocks = jnp.pad(blocks, ((0, 0), (0, chips - rows), (0, 0), (0, 0)))
    moved = lax.all_to_all(
        jnp.moveaxis(blocks, 1, 0), ("ctx", "tp"), 0, 0, tiled=True
    )
    return jnp.moveaxis(moved, 0, 1).reshape(kinds, chips * part, width)


def collect(tokens, rows):
    chips = lax.axis_size("ctx") * lax.axis_size("tp")
    kinds, length, width = tokens.shape
    part = length // chips
    blocks = jnp.moveaxis(tokens.reshape(kinds, chips, part, width), 1, 0)
    moved = lax.all_to_all(blocks, ("ctx", "tp"), 0, 0, tiled=True)
    return jnp.moveaxis(moved, 0, 1)[:, :rows]


def per_device(
    layer_inputs,
    out_grad,
    src_seg,
    tgt_seg,
    qkv_weights,
    out_weights,
    cross_weights,
    ffn_in,
    ffn_out,
    adapter_in,
    adapter_in_bias,
    adapter_out,
    adapter_out_bias,
):
    core = lax.axis_index("section")
    is_first = core == 0
    tp = lax.axis_size("tp")
    chips = lax.axis_size("ctx") * tp
    chip = lax.axis_index("ctx") * tp + lax.axis_index("tp")
    _, micro, per_micro, part, width = layer_inputs.shape
    row_count = micro * per_micro
    half = part // 2
    length = half * chips

    def pick(first, second):
        return jnp.where(is_first, first, second)

    x = layer_inputs.reshape(row_count, part, width)
    low, high = x[:, :half], x[:, half:]
    other = swap(pick(high, low))
    grads = out_grad.reshape(row_count, part, width)
    stacked = jnp.stack(
        [pick(low, other), pick(other, high), pick(grads[:, :half], grads[:, half:])]
    )
    near = lax.axis_size("ctx") == 4 and tp == 4
    lanes = adapter_in_bias.shape[1]
    cols = out_weights.shape[2]
    pad = lambda v, n: jnp.pad(v, [(0, n - v.shape[0])] + [(0, 0)] * (v.ndim - 1))
    biases = jnp.concatenate(
        [pad(adapter_in_bias[0], cols)[None], adapter_out_bias[0].reshape(-1, cols)]
    )
    shards = [
        jnp.concatenate([qkv_weights[0], out_weights], axis=0).reshape(-1, cols),
        ffn_in[0],
        ffn_out[0],
        jnp.concatenate(
            [
                jnp.concatenate([adapter_in[0], adapter_out[0].T], axis=1),
                pad(biases, 256),
            ],
            axis=0,
        ),
        cross_weights[0].reshape(-1, cols),
    ]
    if near:
        ids = ids_call(jnp.stack([src_seg, tgt_seg]).reshape(2 * row_count, -1))
        flat_ids = ids.swapaxes(0, 1).reshape(2, row_count, -1)
    else:
        flat_ids = [
            lax.all_gather(v.reshape(row_count, -1), "ctx", axis=1, tiled=True)
            for v in (src_seg, tgt_seg)
        ]

    def unpack(full):
        attn, w_in, w_out, adapter, cross = full
        attn = attn.reshape(tp, 4, -1, cols)
        cross = cross.reshape(tp, 2, -1, cols)
        b_out = adapter[0, width + 1 : width + 1 + width // cols].reshape(width)
        tail = (
            w_in,
            w_out,
            adapter[:, :width, :lanes],
            adapter[:, width, :lanes],
            adapter[:, :width, lanes:],
            b_out,
        )
        return attn, cross, tail

    def ids_of(flat):
        row = lax.dynamic_index_in_dim(
            flat, jnp.minimum(chip, row_count - 1), 0, keepdims=False
        )
        return row.reshape(chips, 2, half)

    index = jnp.arange(length, dtype=jnp.int32)
    place = (index // half) * part + index % half

    def cut(seg, which):
        own = lax.dynamic_index_in_dim(seg, which, 1, keepdims=False).reshape(length)
        return own, place + which * half

    src_ids, tgt_ids = ids_of(flat_ids[0]), ids_of(flat_ids[1])

    def id_arrays(seg_q, seg_k):
        qi = jnp.stack(cut(seg_q, core))
        ki = jnp.stack(cut(seg_k, core) + cut(seg_k, 1 - core))
        return (qi.T, ki), (qi, ki.T)

    enc_ids = id_arrays(src_ids, src_ids)
    dec_ids = id_arrays(tgt_ids, tgt_ids)
    cross_ids = id_arrays(tgt_ids, src_ids)

    def scatter(arrays, call_id):
        return Scatter(arrays, row_count, call_id) if near else None

    def tokens(value):
        return value.astype(BF16).reshape(chips, half, width)

    def scatter(arrays, call_id):
        return Scatter(arrays, row_count, call_id) if near else None

    def tokens(value):
        return value.astype(BF16).reshape(chips, half, width)

    if near:
        src_own, place_own = cut(src_ids, core)
        src_oth, place_oth = cut(src_ids, 1 - core)
        tgt_own, tgt_oth = cut(tgt_ids, core)[0], cut(tgt_ids, 1 - core)[0]
        col = jnp.stack([src_own, tgt_own, place_own], axis=1)
        row = jnp.stack([src_own, src_oth, tgt_own, tgt_oth, place_own, place_oth] * 2)[:8]
        enc_w, dec_w, placed, slope, kept = forward_call(
            shards, [stacked[0], stacked[1], stacked[2]], col, row
        )
        enc_attn, enc_cross, enc_tail_w = unpack(enc_w)
        dec_attn, dec_cross, dec_tail_w = unpack(dec_w)
        cotangent = placed.reshape(length, width)

        def kept_self(p):
            keys = tuple(kept[p + n] for n in ("k", "kx", "v", "vx"))
            return kept[p + "q"], keys, kept[p + "o"], kept[p + "l"], kept[p + "h"], kept[p + "r"][:, :1]

        enc_self, dec_self = kept_self("e"), kept_self("d")
        encoded = kept["ey"]
        encoded_bf = encoded.astype(BF16)
        enc_tail = (
            kept["eh"].astype(BF16), slope, kept["es"], kept["ea"], encoded, kept["eyr"][:, :1],
        )
        mem_keys = tuple(kept[n] for n in ("mk", "mkx", "mv", "mvx"))
        queries, cross_o, cross_lse = kept["cq"], kept["co"], kept["cl"]
        second, second_rstd = kept["c2"], kept["c2r"][:, :1]
    else:
        source, target, cotangent = spread(stacked)
        enc_attn, enc_cross, enc_tail_w = unpack(gather_plain(0, shards))
        dec_attn, dec_cross, dec_tail_w = unpack(gather_plain(1, shards))
        enc_mid, enc_self, _ = self_forward(
            source, source.astype(F32), enc_attn, enc_ids, False
        )
        encoded, enc_tail = tail_forward(enc_mid, enc_tail_w)
        encoded_bf = encoded.astype(BF16)
        memory = [project(encoded_bf, enc_cross[:, j]).astype(BF16) for j in range(2)]
        memory_other = swap(jnp.stack(memory))
        mem_keys = (memory[0], memory_other[0], memory[1], memory_other[1])
        dec_mid, dec_self, _ = self_forward(
            target, target.astype(F32), dec_attn, dec_ids, True
        )
        queries = project(dec_mid.astype(BF16), dec_cross[:, 0]).astype(BF16)
        (cross_o, cross_lse), _ = attention_forward(
            queries, mem_keys, cross_ids[0], False
        )
        second, second_rstd = norm(dec_mid + unproject(cross_o, dec_cross[:, 1]))
    decoded, dec_tail = tail_forward(second, dec_tail_w)

    def pieces(terms):
        d_in, d_bias, d_out, d_last = terms
        cuts = [v.reshape(tp, 4, width // 4, lanes).swapaxes(0, 1) for v in (d_in, d_out)]
        tail = jnp.concatenate(
            [
                d_bias[:, None, :],
                jnp.broadcast_to(d_last.reshape(1, -1, lanes), (tp, width // lanes, lanes)),
            ],
            axis=1,
        )
        tail = jnp.pad(tail, ((0, 0), (0, 16 - tail.shape[1]), (0, 0)))
        tail = jnp.broadcast_to(tail, (4,) + tail.shape)
        first, other = [
            jnp.concatenate([v, tail], axis=2).reshape(4 * tp, -1, lanes) for v in cuts
        ]
        got = swap(pick(other, first).astype(BF16)).astype(F32)
        return (pick(first, other) + got).astype(BF16)

    grad_second, dec_terms = tail_backward(cotangent.astype(F32), dec_tail, dec_tail_w)
    grad_cross = norm_back(second, second_rstd, grad_second)
    do = project(grad_cross.astype(BF16), dec_cross[:, 1]).astype(BF16)
    ride = scatter([(tokens(encoded_bf), 0), (tokens(decoded), 1)], 2)
    (dqc, dmk, dmv), placed = attend_back(
        queries, mem_keys, cross_o, do, cross_lse, cross_ids, False, ride
    )
    grad_first = unproject(dqc, dec_cross[:, 0]) + grad_cross
    ride = scatter([(pieces(dec_terms), 1)], 3) if near else None
    grad_target, dec_sum = self_backward(
        grad_first, dec_self, dec_attn, dec_ids, True, ride
    )

    grad_encoded = unproject(dmk, enc_cross[:, 0]) + unproject(dmv, enc_cross[:, 1])
    grad_mid, enc_terms = tail_backward(grad_encoded, enc_tail, enc_tail_w)
    ride = (
        scatter([(pieces(enc_terms), 0), (tokens(grad_target), 1)], 4) if near else None
    )
    grad_source, moved = self_backward(
        grad_mid, enc_self, enc_attn, enc_ids, False, ride
    )

    if near:
        outs = pick(placed[0], placed[1])
        sums = jnp.sum(pick(moved[0], dec_sum[0]).astype(F32), axis=0)
        last, whole = send_call(
            scatter([(tokens(grad_source), 0)], 5), sums[:, : width // 4].reshape(-1, lanes).astype(BF16)
        )
        grads = pick(last[0], moved[1]).astype(F32)
        whole = whole.astype(F32).reshape(4, 2, width // 4, lanes).swapaxes(0, 1)
        whole = whole.reshape(2, width, lanes)
        return (
            outs.reshape(layer_inputs.shape),
            grads.reshape(layer_inputs.shape),
            whole[0][None],
            sums[0, width // 4][None],
            whole[1].T[None],
            sums[0, width // 4 + 1 : width // 4 + 1 + width // lanes].reshape(1, width),
        )

    has_row = chip < row_count

    def total(enc_term, dec_term):
        enc_term = jnp.where(has_row, enc_term, 0.0).astype(BF16)
        dec_term = jnp.where(has_row, dec_term, 0.0).astype(BF16)
        got = swap(pick(dec_term, enc_term))
        return (pick(enc_term, dec_term).astype(F32) + got.astype(F32)).astype(BF16)

    sums = [total(e, d) for e, d in zip(enc_terms, dec_terms)]
    scattered = [
        lax.psum_scatter(v, "tp", scatter_dimension=0, tiled=False) for v in sums[:3]
    ]
    scattered = [lax.psum(v, "ctx").astype(F32) for v in scattered]
    bias_sum = lax.psum(sums[3], ("ctx", "tp")).astype(F32)

    results = jnp.stack(
        [
            encoded_bf,
            decoded.astype(BF16),
            grad_source.astype(BF16),
            grad_target.astype(BF16),
        ]
    )
    placed = collect(results, row_count)

    def join(enc_part, dec_part):
        mine = pick(enc_part, dec_part)
        got = swap(pick(dec_part, enc_part))
        return jnp.concatenate([pick(mine, got), pick(got, mine)], axis=1)

    outs = join(placed[0], placed[1]).reshape(layer_inputs.shape)
    grads = join(placed[2], placed[3]).astype(F32).reshape(layer_inputs.shape)
    return (
        outs,
        grads,
        scattered[0][None],
        scattered[1][None],
        scattered[2].T[None],
        bias_sum[None],
    )


def solution(mesh):
    return jax.shard_map(
        per_device,
        mesh=mesh,
        in_specs=(
            P("section", None, None, ("ctx", "tp"), None),
            P(None, None, ("ctx", "tp"), None),
            P(None, None, "ctx"),
            P(None, None, "ctx"),
            P("section", None, None, "tp"),
            P("section", None, "tp"),
            P("section", None, None, "tp"),
            P("section", None, "tp"),
            P("section", "tp", None),
            P("section", None, "tp"),
            P("section", "tp"),
            P("section", "tp", None),
            P("section", None),
        ),
        out_specs=(
            P("section", None, None, ("ctx", "tp"), None),
            P("section", None, None, ("ctx", "tp"), None),
            P("section", None, "tp"),
            P("section", "tp"),
            P("section", "tp", None),
            P("section", None),
        ),
        check_vma=False,
    )
```

```python
import functools

import jax
import jax.numpy as jnp
from jax import lax
from jax.experimental import pallas as pl
from jax.experimental.pallas import tpu as pltpu
from jax.sharding import PartitionSpec as P

HEAD = 64
SCALE = HEAD**-0.5
EPS = 1e-05
MASKED = -1e30
F32 = jnp.float32
BF16 = jnp.bfloat16
SECTION, CTX, TP = "section", "ctx", "tp"


def swap(value):
    return lax.ppermute(value, SECTION, [(0, 1), (1, 0)])


def remote(src, dst, send, recv, where):
    return pltpu.make_async_remote_copy(
        src_ref=src,
        dst_ref=dst,
        send_sem=send,
        recv_sem=recv,
        device_id=where,
        device_id_type=pl.DeviceIdType.MESH,
    )


def device_of(section, chip):
    return (section, chip // 4, lax.rem(chip, 4))


def greet_all():
    s = lax.axis_index(SECTION)
    chip = lax.axis_index(CTX) * 4 + lax.axis_index(TP)
    barrier = pltpu.get_barrier_semaphore()
    for core in (0, 1):
        for i in range(core, 16):
            pl.semaphore_signal(
                barrier,
                1,
                device_id=device_of(lax.rem(s + 1 - core, 2), lax.rem(chip + i, 16)),
                device_id_type=pl.DeviceIdType.MESH,
            )
    pl.semaphore_wait(barrier, 31)


class Scatter:
    BRING = 2

    def __init__(self, arrays, rows, call_id):
        self.inputs = [a for a, _ in arrays]
        self.kinds = [k for _, k in arrays]
        self.rows = rows
        self.call_id = call_id
        self.shapes = [
            jax.ShapeDtypeStruct(
                ((16,) if k == self.BRING else (rows, 2)) + a.shape[1:], a.dtype
            )
            for a, k in arrays
        ]
        count = len(arrays)
        self.scratch = [
            pltpu.SemaphoreType.DMA((count, 16)),
            pltpu.SemaphoreType.DMA((count, 16, 2)),
        ]

    def sends(self, ins, outs, sems):
        send, recv = sems
        s = lax.axis_index(SECTION)
        chip = lax.axis_index(CTX) * 4 + lax.axis_index(TP)
        for a, kind in enumerate(self.kinds):
            for i in range(16):
                p = lax.rem(chip + i, 16)
                if kind == self.BRING:
                    ready = p < self.rows
                    src = ins[a].at[jnp.minimum(p, self.rows - 1)]
                    dst = outs[a].at[chip]
                    core, mark = s, 0
                    stays = True
                else:
                    ready = chip < self.rows
                    src = ins[a].at[p]
                    dst = outs[a].at[jnp.minimum(chip, self.rows - 1), s]
                    core, mark = kind, s
                    stays = s == kind
                near = pltpu.make_async_copy(src, dst, send.at[a, i])
                far = remote(
                    src, dst, send.at[a, i], recv.at[a, i, mark], device_of(core, p)
                )
                yield i, ready, stays, near, far

    def start(self, ins, outs, sems):
        greet_all()
        for i, ready, stays, near, far in self.sends(ins, outs, sems):

            @pl.when(ready)
            def _():
                if i:
                    far.start()
                elif stays is True:
                    near.start()
                else:
                    pl.when(stays)(near.start)
                    pl.when(jnp.logical_not(stays))(far.start)

    def finish(self, ins, outs, sems):
        send, recv = sems
        s = lax.axis_index(SECTION)
        chip = lax.axis_index(CTX) * 4 + lax.axis_index(TP)
        for i, ready, stays, near, far in self.sends(ins, outs, sems):

            @pl.when(ready)
            def _():
                if i:
                    far.wait_send()
                elif stays is True:
                    near.wait()
                else:
                    pl.when(stays)(near.wait)
                    pl.when(jnp.logical_not(stays))(far.wait_send)

        def got(region, sem):
            remote(region, region, send.at[0, 0], sem, (1 - s, 0, 0)).wait_recv()

        for a, kind in enumerate(self.kinds):
            for i in range(16):
                sender = lax.rem(chip + 16 - i, 16)
                if kind == self.BRING:
                    if i:

                        @pl.when(chip < self.rows)
                        def _():
                            got(outs[a].at[sender], recv.at[a, i, 0])

                    continue

                @pl.when((s == kind) & (sender < self.rows))
                def _():
                    for core in (0, 1) if i else (1 - kind,):
                        region = outs[a].at[jnp.minimum(sender, self.rows - 1), core]
                        got(region, recv.at[a, i, core])


def send_kernel(rider, *refs):
    n = len(rider.inputs)
    block_in, (own, spread_out) = refs[n], (refs[n], refs[2 * n + 1])
    ins, outs = refs[:n], refs[n + 1 : 2 * n + 1]
    sems = refs[2 * n + 2 : 2 * n + 4]
    b_send, b_recv = refs[2 * n + 4 :]
    rider.start(ins, outs, sems)
    s = lax.axis_index(SECTION)
    c = lax.axis_index(CTX)
    t = lax.axis_index(TP)
    dst = spread_out.at[c]
    keep = pltpu.make_async_copy(own, dst, b_send.at[0])
    keep.start()
    ways = [
        remote(own, dst, b_send.at[j], b_recv.at[j], (s, lax.rem(c + j, 4), t))
        for j in (1, 2, 3)
    ]
    for way in ways:
        way.start()
    keep.wait()
    for j, way in enumerate(ways):
        way.wait_send()
        region = spread_out.at[lax.rem(c + 3 - j, 4)]
        remote(region, region, b_send.at[0], b_recv.at[j + 1], (s, c, t)).wait_recv()
    rider.finish(ins, outs, sems)


def send_call(rider, block):
    anywhere = pl.BlockSpec(memory_space=pl.ANY)
    count = len(rider.inputs)
    result = pl.pallas_call(
        functools.partial(send_kernel, rider),
        in_specs=[anywhere] * (count + 1),
        out_specs=[anywhere] * (count + 1),
        out_shape=rider.shapes + [jax.ShapeDtypeStruct((4,) + block.shape, block.dtype)],
        scratch_shapes=rider.scratch
        + [pltpu.SemaphoreType.DMA((4,)), pltpu.SemaphoreType.DMA((4,))],
        compiler_params=pltpu.CompilerParams(
            collective_id=rider.call_id, has_side_effects=True
        ),
        name="send_last",
    )(*rider.inputs, block)
    return result[:count], result[count]


def dot_nt(left, right, **kw):
    return lax.dot_general(
        left, right, (((1,), (1,)), ((), ())), preferred_element_type=F32, **kw
    )


def dot_nn(left, right):
    return lax.dot_general(
        left, right, (((1,), (0,)), ((), ())), preferred_element_type=F32
    )


def dot_tn(left, right):
    return lax.dot_general(
        left, right, (((0,), (0,)), ((), ())), preferred_element_type=F32
    )


def attn_fwd_kernel(
    causal, q_ref, ko_ref, kx_ref, vo_ref, vx_ref, fq, fo, fx, qi_ref, ki_ref, o_ref, lse_ref
):
    for pair in range(lse_ref.shape[1]):
        attend_pair(
            0,
            pair,
            q_ref,
            (ko_ref, kx_ref),
            (vo_ref, vx_ref),
            o_ref,
            lse_ref,
            (fq, fo, fx),
            (qi_ref[:, 1:2], (ki_ref[1:2, :], ki_ref[3:4, :])),
            causal,
        )


def attention_call(kernel, name, causal, blocks, small, outs):
    def group_spec(v):
        return pl.BlockSpec((1,) + v.shape[1:], lambda t: (t,) + (0,) * (len(v.shape) - 1))

    return pl.pallas_call(
        functools.partial(kernel, causal),
        grid=(blocks[0].shape[0],),
        in_specs=[group_spec(v) for v in blocks]
        + [pl.BlockSpec(v.shape, lambda t: (0, 0)) for v in small],
        out_specs=[group_spec(v) for v in outs],
        out_shape=outs,
        compiler_params=pltpu.CompilerParams(vmem_limit_bytes=48 * 2**20),
        name=name,
    )(*blocks, *small)


def id_columns(ids, keys):
    lane = jnp.arange(2 * HEAD, dtype=jnp.int32)[None] % HEAD
    same = ids[:, None] == lane
    value = jnp.where(same, 1.0, 0.0) if keys else jnp.where(same, 0.0, MASKED)
    return jnp.where(lane < 4, value, 0.0).astype(BF16)


def attention_forward(q, keys, ids, causal):
    groups, length, width = q.shape
    pairs = width // HEAD // 2
    outs = [
        jax.ShapeDtypeStruct(q.shape, BF16),
        jax.ShapeDtypeStruct((groups, pairs, 2, length), F32),
    ]
    feats = [
        id_columns(ids[0][:, 0], False),
        id_columns(ids[1][0], True),
        id_columns(ids[1][2], True),
    ]
    o, lse = attention_call(
        attn_fwd_kernel, "attn_fwd", causal, [q, *keys], [*feats, *ids], outs
    )
    return o, lse.reshape(groups, 2 * pairs, length)


def attend_back_group(ins, dq_out, dk_outs, dv_outs, qi_ref, ki_ref, causal):
    q_ref, k_refs, v_refs, o_ref, do_ref, lse_ref = ins
    length = q_ref.shape[1]
    heads = q_ref.shape[2] // HEAD
    block = length // 2
    segq = qi_ref[0:1, :]
    posq = qi_ref[1:2, :]
    ones = jnp.ones((8, HEAD), F32)

    def put(out, rows, cols, value):
        out[0][out[1], rows, cols] = value.astype(out[0].dtype)

    for h in range(heads):
        cols = slice(h * HEAD, (h + 1) * HEAD)
        q_all = q_ref[0, :, cols] * jnp.asarray(SCALE, BF16)
        do_all = do_ref[0, :, cols]
        prod = do_all.astype(F32) * o_ref[0, :, cols].astype(F32)
        delta = dot_nt(ones, prod, precision=lax.Precision.HIGHEST)[0:1]
        lse = lse_ref[0, h : h + 1, :]
        dq = [jnp.zeros((block, HEAD), F32), jnp.zeros((block, HEAD), F32)]
        for n in range(2):
            i = 2 * n
            for b in range(2):
                rows = slice(b * block, (b + 1) * block)
                first = b * block if causal else 0
                q = q_all[first:]
                do = do_all[first:]
                k = k_refs[n][0, rows, cols]
                s = dot_nt(k, q)
                ok = ki_ref[rows, i : i + 1] == segq[:, first:]
                if causal:
                    ok = ok & (posq[:, first:] >= ki_ref[rows, i + 1 : i + 2])
                p = jnp.where(ok, jnp.exp(s - lse[:, first:]), 0.0)
                dp = dot_nt(v_refs[n][0, rows, cols], do)
                ds = (p * (dp - delta[:, first:])).astype(BF16)
                put(dv_outs[n], rows, cols, dot_nn(p.astype(BF16), do))
                put(dk_outs[n], rows, cols, dot_nn(ds, q))
                part = dot_tn(ds, k)
                if first:
                    dq[1] = dq[1] + part
                else:
                    dq[0] = dq[0] + part[:block]
                    dq[1] = dq[1] + part[block:]
        put(dq_out, slice(0, block), cols, dq[0] * SCALE)
        put(dq_out, slice(block, length), cols, dq[1] * SCALE)


def attn_bwd_kernel(
    causal,
    q_ref,
    ko_ref,
    kx_ref,
    vo_ref,
    vx_ref,
    o_ref,
    do_ref,
    lse_ref,
    qi_ref,
    ki_ref,
    dq_ref,
    dko_ref,
    dkx_ref,
    dvo_ref,
    dvx_ref,
):
    attend_back_group(
        (q_ref, (ko_ref, kx_ref), (vo_ref, vx_ref), o_ref, do_ref, lse_ref),
        (dq_ref, 0),
        ((dko_ref, 0), (dkx_ref, 0)),
        ((dvo_ref, 0), (dvx_ref, 0)),
        qi_ref,
        ki_ref,
        causal,
    )


def attention_backward(q, keys, o, do, lse, ids, causal):
    outs = [jax.ShapeDtypeStruct(q.shape, BF16)] * 5
    return attention_call(
        attn_bwd_kernel, "attn_bwd", causal, [q, *keys, o, do, lse], ids, outs
    )


def norm(value):
    mean = jnp.mean(value, axis=-1, keepdims=True)
    centered = value - mean
    rstd = lax.rsqrt(jnp.mean(centered * centered, axis=-1, keepdims=True) + EPS)
    return centered * rstd, rstd


def norm_back(normed, rstd, grad):
    return rstd * (
        grad
        - jnp.mean(grad, axis=-1, keepdims=True)
        - normed * jnp.mean(grad * normed, axis=-1, keepdims=True)
    )


def project(rows, weight):
    return jnp.einsum("pk,tkm->tpm", rows, weight, preferred_element_type=F32)


def unproject(blocks, weight):
    return jnp.einsum("tpm,tkm->pk", blocks, weight, preferred_element_type=F32)


def self_forward(rows_bf, rows, w_attn, ids, causal):
    kv = [project(rows_bf, w_attn[:, j]).astype(BF16) for j in (1, 2)]
    other = swap(jnp.stack(kv))
    q = project(rows_bf, w_attn[:, 0]).astype(BF16)
    keys = (kv[0], other[0], kv[1], other[1])
    o, lse = attention_forward(q, keys, ids[0], causal)
    h, rstd = norm(rows + unproject(o, w_attn[:, 3]))
    return h, (q, keys, o, lse, h, rstd)


def attend_back(q, keys, o, do, lse, ids, causal):
    dq, dko, dkx, dvo, dvx = attention_backward(q, keys, o, do, lse, ids[1], causal)
    other = swap(jnp.stack([dkx, dvx])).astype(F32)
    dk = (dko.astype(F32) + other[0]).astype(BF16)
    dv = (dvo.astype(F32) + other[1]).astype(BF16)
    return dq, dk, dv


def self_backward(grad, kept, w_attn, ids, causal):
    q, keys, o, lse, h, rstd = kept
    dpre = norm_back(h, rstd, grad)
    do = project(dpre.astype(BF16), w_attn[:, 3]).astype(BF16)
    dq, dk, dv = attend_back(q, keys, o, do, lse, ids, causal)
    return (
        unproject(dq, w_attn[:, 0])
        + unproject(dk, w_attn[:, 1])
        + unproject(dv, w_attn[:, 2])
        + dpre
    )


def tail_forward(h, tail_w):
    w_in, w_out, a_in, b_in, a_out, b_out = tail_w
    rows = h.astype(BF16)
    inner = project(rows, w_in)
    phi = 0.5 * (1.0 + lax.erf(inner * 0.7071067811865476))
    g = (inner * phi).astype(BF16)
    slope = phi + inner * jnp.exp(inner * inner * -0.5) * 0.3989422804014327
    pre = project(rows, a_in) + b_in.astype(F32)[:, None, :]
    sig = jax.nn.sigmoid(pre)
    s = (pre * sig).astype(BF16)
    a_slope = sig * (1.0 + pre * (1.0 - sig))
    total = jnp.einsum("tpm,tmk->pk", g, w_out, preferred_element_type=F32)
    total += 4.0 * (
        jnp.einsum("tpm,tkm->pk", s, a_out, preferred_element_type=F32)
        + b_out.astype(F32)
    )
    y, rstd = norm(h + total)
    return y, (rows, slope.astype(BF16), s, a_slope.astype(BF16), y, rstd)


def tail_backward(grad, kept, tail_w):
    w_in, w_out, a_in, b_in, a_out, b_out = tail_w
    rows, slope, s, a_slope, y, rstd = kept
    dpre = norm_back(y, rstd, grad)
    db = dpre.astype(BF16)
    dg = jnp.einsum("pk,tmk->tpm", db, w_out, preferred_element_type=F32)
    df = (dg * slope.astype(F32)).astype(BF16)
    ds = 4.0 * jnp.einsum("pk,tkm->tpm", db, a_out, preferred_element_type=F32)
    du = (ds * a_slope.astype(F32)).astype(BF16)
    terms = (
        jnp.einsum("pk,tpm->tkm", rows, du, preferred_element_type=F32),
        jnp.sum(du.astype(F32), axis=1),
        4.0 * jnp.einsum("pk,tpm->tkm", db, s, preferred_element_type=F32),
        4.0 * jnp.sum(db.astype(F32), axis=0),
    )
    return unproject(df, w_in) + unproject(du, a_in) + dpre, terms


def head_mask(rows, j):
    lane = lax.broadcasted_iota(jnp.int32, (rows, 2 * HEAD), 1)
    return (lane < HEAD) if j == 0 else (lane >= HEAD)


def attend_pair(t, pair, q_ref, k_refs, v_refs, o_ref, lse_ref, feats, places, causal):
    length = q_ref.shape[1]
    block = length // 2
    lanes = pl.ds(pl.multiple_of(pair * 2 * HEAD, 2 * HEAD), 2 * HEAD)
    posq, posk = places
    for b in range(2):
        rows = slice(b * block, (b + 1) * block)
        q2 = q_ref[t, rows, lanes] * jnp.asarray(SCALE, BF16)
        cuts = [(n, a) for n in range(2) for a in range(b + 1 if causal else 2)]
        outs = []
        for j in range(2):
            q = jnp.where(head_mask(block, j), q2, feats[0][rows])
            parts = []
            for n, a in cuts:
                span = slice(a * block, (a + 1) * block)
                k = jnp.where(
                    head_mask(block, j), k_refs[n][t, span, lanes], feats[1 + n][span]
                )
                s = dot_nt(q, k)
                if causal and a == b:
                    s = jnp.where(posq[rows] >= posk[n][:, span], s, MASKED)
                parts.append(s)
            top = functools.reduce(
                jnp.maximum, [jnp.max(s, axis=1, keepdims=True) for s in parts]
            )
            ex = [jnp.exp(s - top) for s in parts]
            total = sum(jnp.sum(e, axis=1, keepdims=True) for e in ex)
            out = sum(
                dot_nn(
                    e.astype(BF16), v_refs[n][t, a * block : (a + 1) * block, lanes]
                )
                for e, (n, a) in zip(ex, cuts)
            )
            outs.append(out / total)
            lse = top + jnp.log(total)
            lse_ref[t, pair, j : j + 1, rows] = jnp.broadcast_to(lse, (block, 128)).T[
                0:1
            ]
        o_ref[t, rows, lanes] = jnp.where(head_mask(block, 0), *outs).astype(BF16)


ATTN, FFN_IN, FFN_OUT, ADAPTER, CROSS = range(5)
ORDER = (
    (0, ATTN),
    (1, ATTN),
    (0, FFN_IN),
    (0, FFN_OUT),
    (0, ADAPTER),
    (0, CROSS),
    (1, CROSS),
    (1, FFN_IN),
    (1, FFN_OUT),
    (1, ADAPTER),
)
(
    ENC_QKV,
    ENC_ATTN,
    ENC_OUT,
    DEC_QKV,
    DEC_ATTN,
    DEC_OUT,
    HIDDEN,
    GATED,
    MEMORY,
    CROSS_Q,
    CROSS_ATTN,
    CROSS_OUT,
    END,
) = range(13)
WORK = (
    (ENC_QKV, 4, (0, ATTN), 2.0),
    (ENC_ATTN, 8, None, 2.3),
    (ENC_OUT, 1, None, 4.0),
    (DEC_QKV, 4, (1, ATTN), 2.0),
    (DEC_ATTN, 8, None, 2.1),
    (DEC_OUT, 1, None, 4.0),
    (HIDDEN, 8, (0, FFN_OUT), 2.5),
    (GATED, 1, (0, ADAPTER), 4.0),
    (MEMORY, 4, (0, CROSS), 1.5),
    (CROSS_Q, 1, (1, CROSS), 4.0),
    (CROSS_ATTN, 8, None, 2.3),
    (CROSS_OUT, 1, None, 4.0),
    (END, 1, (1, ADAPTER), 0.0),
)


def plan_steps(sizes):
    ready, clock = [], 20.0
    for e, g in ORDER:
        for _ in range(3):
            clock += sizes[g] / 3 * 14e-6
            ready.append(clock)
    ticks = len(ready) + 2
    ready += [clock + 4, clock + 8]
    starts, at, step, now, done = {}, {}, 0, 0.0, 0
    for name, count, need, cost in WORK:
        starts[name] = step
        for n in range(count):
            while done < ticks and (
                ready[done] <= now
                or (need and done <= 3 * ORDER.index(need) + 4)
            ):
                at[done] = step
                now = max(now, ready[done])
                done += 1
            now += cost
            step += 1
    for n in range(done, ticks):
        at[n] = step - 1
    return starts, at, step


HEADS, LSE, WIDE, RSTD, LANES = range(5)
(
    EQ,
    EK,
    EKX,
    EV,
    EVX,
    EO,
    EL,
    EH,
    ER,
    ES,
    EA,
    EY,
    EYR,
    DQ,
    DK,
    DKX,
    DV,
    DVX,
    DO,
    DL,
    DH,
    DR,
    MK,
    MKX,
    MV,
    MVX,
    CQ,
    CO,
    CL,
    C2,
    C2R,
) = range(31)
KEPT = {
    EQ: HEADS,
    EK: HEADS,
    EKX: HEADS,
    EV: HEADS,
    EVX: HEADS,
    EO: HEADS,
    EL: LSE,
    EH: WIDE,
    ER: RSTD,
    ES: LANES,
    EA: LANES,
    EY: WIDE,
    EYR: RSTD,
    DQ: HEADS,
    DK: HEADS,
    DKX: HEADS,
    DV: HEADS,
    DVX: HEADS,
    DO: HEADS,
    DL: LSE,
    DH: WIDE,
    DR: RSTD,
    MK: HEADS,
    MKX: HEADS,
    MV: HEADS,
    MVX: HEADS,
    CQ: HEADS,
    CO: HEADS,
    CL: LSE,
    C2: WIDE,
    C2R: RSTD,
}


def forward_kernel(plan, rows, *refs):
    starts, tick_step, steps = plan
    refs = list(refs)

    def take(count):
        got = refs[:count]
        del refs[:count]
        return got

    shards = take(5)
    tokens = take(2)
    col_ref, row_ref, feat_ref = take(3)
    full = (take(5), take(5))
    (slope_out,) = take(1)
    kept_out = take(len(KEPT))
    kept = take(len(KEPT))
    xs = take(2)
    wb, wi, wo, wad, slope = take(5)
    store_a, store_f = take(2)
    (
        z_send,
        z_recv,
        n_send,
        n_recv,
        f_send,
        f_recv,
        s_send,
        s_recv,
        own_sem,
        t_send,
        t_recv,
        kv_send,
        kv_recv,
        load_sem,
        out_sem,
        slope_sem,
    ) = refs
    step = pl.program_id(0)
    s = lax.axis_index(SECTION)
    c = lax.axis_index(CTX)
    t = lax.axis_index(TP)
    chips = 16
    chip = c * 4 + t
    cx = c + 1 - 2 * lax.rem(c, 2)
    cy = lax.rem(c + 2, 4)
    cd = 3 - c
    sib = (1 - s, c, t)

    def xor(k):
        return {1: t + 1 - 2 * lax.rem(t, 2), 2: lax.rem(t + 2, 4), 3: 3 - t}[k]

    def token_copy(kind, i):
        p = lax.rem(chip + i, chips)
        src = tokens[kind].at[jnp.minimum(p, rows - 1)]
        dst = xs[kind].at[chip]
        if i == 0:
            return p, pltpu.make_async_copy(src, dst, t_send.at[kind, 0])
        return p, remote(
            src, dst, t_send.at[kind, i], t_recv.at[kind, i], device_of(s, p)
        )

    def send_tokens(kind):
        for i in range(chips):
            p, copy = token_copy(kind, i)
            pl.when(p < rows)(copy.start)

    def got(region, sem):
        remote(region, region, load_sem.at[0], sem, sib).wait_recv()

    def wait_tokens(kind):
        for i in range(chips):
            p, copy = token_copy(kind, i)
            pl.when(p < rows)(copy.wait if i == 0 else copy.wait_send)
            if i:

                @pl.when(chip < rows)
                def _():
                    got(
                        xs[kind].at[lax.rem(chip + chips - i, chips)],
                        t_recv.at[kind, i],
                    )

    items = [(n, k) for n in range(len(ORDER)) for k in (1, 2, 3)]
    window = 4

    def block(n, who, h, q, u=None):
        e, g = ORDER[n]
        size = shards[g].shape[0]
        start = h * (size // 2) + q * (size // 8)
        length = size // 8
        if u is not None:
            length = size // 16
            start = start + u * length
        return full[e][g].at[who, pl.ds(pl.multiple_of(start, 16), length)]

    def z_copy(n, k, h):
        g = ORDER[n][1]
        size = shards[g].shape[0]
        start = h * (size // 2) + c * (size // 8)
        return remote(
            shards[g].at[pl.ds(pl.multiple_of(start, 16), size // 8)],
            block(n, t, h, c),
            z_send.at[n, k - 1, h],
            z_recv.at[n, k - 1],
            (h, c, xor(k)),
        )

    def store(g):
        if g in (FFN_IN, FFN_OUT):
            return store_f
        return store_a.at[pl.ds(0, shards[g].shape[0])]

    def fetch(n):
        g = ORDER[n][1]
        return pltpu.make_async_copy(shards[g], store(g), own_sem.at[n, 3])

    def put(n):
        e, g = ORDER[n]
        return pltpu.make_async_copy(store(g), full[e][g].at[t], own_sem.at[n, 0])

    def far(n):
        e, g = ORDER[n]
        return remote(
            shards[g], full[e][g].at[t], own_sem.at[n, 1], own_sem.at[n, 2], sib
        )

    def before(n):
        e, g = ORDER[n]
        pool = (FFN_IN, FFN_OUT) if g in (FFN_IN, FFN_OUT) else (ATTN, ADAPTER, CROSS)
        olds = [m for m in range(n) if ORDER[m][0] == e and ORDER[m][1] in pool]
        return olds[-1] if olds else None

    def start_z(i):
        n, k = items[i]

        @pl.when(s == ORDER[n][0])
        def _():
            if k == 1:
                far(n).start()
            for h in range(2):
                z_copy(n, k, h).start()

    def near_copy(n, k, j):
        src = block(n, xor(k), s, c)
        return remote(
            src,
            src,
            n_send.at[n, k - 1, j],
            n_recv.at[n, k - 1, j],
            (s, (cx, cy)[j], t),
        )

    def sibling_copy(n, k, j):
        src = block(n, xor(k), s, (c, cx, cy, cd)[j])
        return remote(src, src, s_send.at[n, k - 1, j], s_recv.at[n, k - 1, j], sib)

    def forward_copy(n, k, j):
        src = block(n, xor(k), s, (cx, cy)[j], j)
        return remote(
            src,
            src,
            f_send.at[n, k - 1, j],
            f_recv.at[n, k - 1, j],
            (s, (cy, cx)[j], t),
        )

    def stage2(i):
        n, k = items[i]
        got(block(n, xor(k), s, c), z_recv.at[n, k - 1])
        near_copy(n, k, 0).start()
        near_copy(n, k, 1).start()
        sibling_copy(n, k, 0).start()
        if k == 2:
            return

        @pl.when(s == ORDER[n][0])
        def _():
            if k == 1:
                old = before(n)
                if old is not None and not put_read_first(old, i):
                    put(old).wait()
                fetch(n).start()
            else:
                fetch(n).wait()
                put(n).start()

    def stage3(i):
        n, k = items[i]
        for j, q in ((0, cx), (1, cy)):
            got(block(n, xor(k), s, q), n_recv.at[n, k - 1, j])
            forward_copy(n, k, j).start()
            sibling_copy(n, k, j + 1).start()

    def stage4(i):
        n, k = items[i]
        for u in range(2):
            got(block(n, xor(k), s, cd, u), f_recv.at[n, k - 1, u])
        sibling_copy(n, k, 3).start()

    count = len(items)

    def tick(i):
        if i < count:
            stage2(i)
            if i + window < count:
                start_z(i + window)
        if 0 <= i - 1 < count:
            stage3(i - 1)
        if 0 <= i - 2 < count:
            stage4(i - 2)
        if i == 3:
            send_tokens(1)

    def arrive_step(n):
        for name, _, need, _ in WORK[:-1]:
            if need == ORDER[n]:
                return starts[name]
        return starts[HIDDEN] if ORDER[n] == (0, FFN_IN) else steps - 1

    def put_read_first(n, i):
        return arrive_step(n) < tick_step[i]

    def put_left(n):
        after = [m for m in range(len(ORDER)) if before(m) == n]
        return not after or put_read_first(n, 3 * after[0])

    def arrive(n):
        e, g = ORDER[n]
        for k in (1, 2, 3):
            for j, q in enumerate((c, cx, cy, cd)):
                got(block(n, xor(k), 1 - s, q), s_recv.at[n, k - 1, j])

        @pl.when(s == e)
        def _():
            if put_left(n):
                put(n).wait()

        @pl.when(s != e)
        def _():
            got(full[e][g].at[t], own_sem.at[n, 2])

    @pl.when(step == 0)
    def _():
        greet_all()
        send_tokens(0)
        for i in range(window):
            start_z(i)

    for i in range(count + 2):
        pl.when(step == tick_step[i])(functools.partial(tick, i))

    def on(name):
        first = starts[name]
        last = first + [w[1] for w in WORK if w[0] == name][0]
        need = [w[2] for w in WORK if w[0] == name][0]
        if need and name != END:
            pl.when(step == first)(functools.partial(arrive, ORDER.index(need)))
        return step - first, pl.when((step >= first) & (step < last))

    def load(src, dst, slot=0):
        return pltpu.make_async_copy(src, dst, load_sem.at[slot])

    def keep(*names):
        for n in names:
            pltpu.make_async_copy(kept[n], kept_out[n], out_sem.at[n]).start()

    attn_rows = full[0][ATTN].shape[1] // 4

    def kv_copies(which, g, names):
        k, kx, v, vx = names
        return [
            remote(
                kept[a].at[g], kept[b].at[g], kv_send.at[which, g, j], kv_recv.at[which, g, j], sib
            )
            for j, (a, b) in enumerate(((k, kx), (v, vx)))
        ]

    def projections(name, which, e, g_id, x, names):
        i, when = on(name)
        tiles = len(names)
        height = tiles * attn_rows

        def source(j):
            return full[e][g_id].at[j, pl.ds(0, height)]

        @when
        def _():
            slot = lax.rem(i, 2)

            @pl.when(i == 0)
            def _():
                load(source(0), wb.at[0, pl.ds(0, height)]).start()

            load(source(0), wb.at[slot, pl.ds(0, height)]).wait()

            @pl.when(i < 3)
            def _():
                load(source(jnp.minimum(i + 1, 3)), wb.at[1 - slot, pl.ds(0, height)]).start()

            rows_in = x()
            for n, name_out in enumerate(names):
                w = wb[slot, n * attn_rows : (n + 1) * attn_rows, :]
                kept[name_out][i] = dot_nn(rows_in, w).astype(BF16)
            for copy in kv_copies(which, i, keys_of[which]):
                copy.start()

    keys_of = (
        (EK, EKX, EV, EVX),
        (DK, DKX, DV, DVX),
        (MK, MKX, MV, MVX),
    )

    def attend(name, which, q, o, lse, feats, causal):
        i, when = on(name)
        k, kx, v, vx = keys_of[which]

        @when
        def _():
            g, pair = i // 2, lax.rem(i, 2)

            @pl.when(pair == 0)
            def _():
                for copy in kv_copies(which, g, keys_of[which]):
                    copy.wait_send()
                    copy.wait_recv()

            attend_pair(
                g,
                pair,
                kept[q],
                (kept[k], kept[kx]),
                (kept[v], kept[vx]),
                kept[o],
                kept[lse],
                [feat_ref.at[f] for f in feats],
                (col_ref[...], (row_ref[0:1, :], row_ref[1:2, :])),
                causal,
            )

            @pl.when(i == 7)
            def _():
                keep(q, k, kx, v, vx, o, lse)

    def tiles4(e, g_id, first_row):
        copies = [
            load(
                full[e][g_id].at[j, pl.ds(first_row, attn_rows)],
                wb.at[0, pl.ds(j * attn_rows, attn_rows)],
                j,
            )
            for j in range(4)
        ]
        for copy in copies:
            copy.start()
        for copy in copies:
            copy.wait()

    def out_norm(name, e, g_id, first_row, residual, source, wide, rstd_name):
        _, when = on(name)

        @when
        def _():
            tiles4(e, g_id, first_row)
            total = residual()
            for j in range(4):
                total = total + dot_nt(
                    kept[source][j], wb[0, j * attn_rows : (j + 1) * attn_rows, :]
                )
            normed, rstd = norm(total)
            kept[wide][...] = normed
            kept[rstd_name][...] = jnp.broadcast_to(rstd, kept[rstd_name].shape)
            keep(wide, rstd_name)

    def flat_x(n):
        shape = xs[n].shape
        return xs[n][...].reshape(shape[0] * shape[1], shape[2])

    blocks = (
        (ENC_QKV, ENC_ATTN, ENC_OUT, EQ, EK, EV, EO, EL, EH, ER, (0, 1, 2)),
        (DEC_QKV, DEC_ATTN, DEC_OUT, DQ, DK, DV, DO, DL, DH, DR, (3, 4, 5)),
    )
    for e, (qkv, attn, out, q, k, v, o, lse, h, r, feats) in enumerate(blocks):
        pl.when(step == starts[qkv])(functools.partial(wait_tokens, e))
        projections(qkv, e, e, ATTN, functools.partial(flat_x, e), (q, k, v))
        attend(attn, e, q, o, lse, feats, e == 1)
        residual = lambda e=e: flat_x(e).astype(F32)
        out_norm(out, e, ATTN, 3 * attn_rows, residual, o, h, r)

    i, when = on(HIDDEN)
    hidden = wi.shape[2]

    @pl.when(step == starts[HIDDEN])
    def _():
        arrive(ORDER.index((0, FFN_IN)))

    def ffn_loads(j, slot):
        g, u = j // 2, lax.rem(j, 2)
        span = pl.ds(pl.multiple_of(u * hidden, 128), hidden)
        return (
            load(full[0][FFN_IN].at[g, :, span], wi.at[slot], 2 * slot),
            load(full[0][FFN_OUT].at[g, span], wo.at[slot], 2 * slot + 1),
        )

    def slope_copy(j, slot):
        g, u = j // 2, lax.rem(j, 2)
        span = pl.ds(pl.multiple_of(u * hidden, 128), hidden)
        return pltpu.make_async_copy(
            slope.at[slot], slope_out.at[g, :, span], slope_sem.at[slot]
        )

    @when
    def _():
        slot = lax.rem(i, 2)

        @pl.when(i == 0)
        def _():
            for copy in ffn_loads(0, 0):
                copy.start()
            kept[EY][...] = jnp.zeros_like(kept[EY])

        for copy in ffn_loads(i, slot):
            copy.wait()

        @pl.when(i < 7)
        def _():
            for copy in ffn_loads(i + 1, 1 - slot):
                copy.start()

        @pl.when(i >= 2)
        def _():
            slope_copy(i - 2, slot).wait()

        inner = dot_nn(kept[EH][...].astype(BF16), wi[slot])
        phi = 0.5 * (1.0 + lax.erf(inner * 0.7071067811865476))
        slope[slot] = (
            phi + inner * jnp.exp(inner * inner * -0.5) * 0.3989422804014327
        ).astype(BF16)
        slope_copy(i, slot).start()
        kept[EY][...] += dot_nn((inner * phi).astype(BF16), wo[slot])

    i, when = on(GATED)

    @when
    def _():
        for j in range(2):
            slope_copy(6 + j, j).wait()
        copy = load(full[0][ADAPTER], wad)
        copy.start()
        copy.wait()
        h = kept[EH][...]
        rows_in = h.astype(BF16)
        lanes = wad.shape[2] // 2
        extra = wad[0, attn_rows : attn_rows + 16, :].astype(F32)
        last = jnp.concatenate([extra[1 + r : 2 + r] for r in range(4)], axis=1)
        total = 4.0 * last
        for j in range(4):
            bias = wad[j, attn_rows : attn_rows + 16, :lanes].astype(F32)[0:1]
            pre = dot_nn(rows_in, wad[j, :attn_rows, :lanes]) + bias
            sig = 1.0 / (1.0 + jnp.exp(-pre))
            gated = (pre * sig).astype(BF16)
            kept[ES][j] = gated
            kept[EA][j] = (sig * (1.0 + pre * (1.0 - sig))).astype(BF16)
            total = total + 4.0 * dot_nt(gated, wad[j, :attn_rows, lanes:])
        normed, rstd = norm(h + (kept[EY][...] + total))
        kept[EY][...] = normed
        kept[EYR][...] = jnp.broadcast_to(rstd, kept[EYR].shape)
        keep(ES, EA, EY, EYR)

    projections(MEMORY, 2, 0, CROSS, lambda: kept[EY][...].astype(BF16), (MK, MV))
    _, when = on(CROSS_Q)

    @when
    def _():
        tiles4(1, CROSS, 0)
        rows_in = kept[DH][...].astype(BF16)
        for j in range(4):
            kept[CQ][j] = dot_nn(
                rows_in, wb[0, j * attn_rows : (j + 1) * attn_rows, :]
            ).astype(BF16)

    attend(CROSS_ATTN, 2, CQ, CO, CL, (3, 1, 2), False)
    out_norm(CROSS_OUT, 1, CROSS, attn_rows, lambda: kept[DH][...], CO, C2, C2R)

    @pl.when(step == steps - 1)
    def _():
        for g in (FFN_IN, FFN_OUT, ADAPTER):
            arrive(ORDER.index((1, g)))
        for n, k in items:
            for j in range(2):
                near_copy(n, k, j).wait_send()
                forward_copy(n, k, j).wait_send()
            for j in range(4):
                sibling_copy(n, k, j).wait_send()
        for n in range(len(ORDER)):

            @pl.when(s == ORDER[n][0])
            def _():
                far(n).wait_send()
                for k in (1, 2, 3):
                    for h in range(2):
                        z_copy(n, k, h).wait_send()

        for n in KEPT:
            pltpu.make_async_copy(kept[n], kept_out[n], out_sem.at[n]).wait()


def forward_call(shards, tokens, col, row, feats):
    part, width = tokens[0].shape[1:]
    length = 16 * part
    groups = len(ORDER)
    dma = pltpu.SemaphoreType.DMA
    anywhere = pl.BlockSpec(memory_space=pl.ANY)
    cols = shards[ATTN].shape[1]
    shapes = (
        ((4, length, cols), BF16),
        ((4, cols // HEAD // 2, 2, length), F32),
        ((length, width), F32),
        ((length, 128), F32),
        ((4, length, shards[ADAPTER].shape[1] // 2), BF16),
    )
    kept = [shapes[kind] for kind in KEPT.values()]
    hidden = shards[FFN_IN].shape[1]
    sizes = [
        (groups, 3, 2),
        (groups, 3),
        (groups, 3, 2),
        (groups, 3, 2),
        (groups, 3, 2),
        (groups, 3, 2),
        (groups, 3, 4),
        (groups, 3, 4),
        (groups, 4),
        (2, 16),
        (2, 16),
        (3, 4, 2),
        (3, 4, 2),
        (4,),
        (len(KEPT),),
        (2,),
    ]
    plan = plan_steps([v.size * 2 for v in shards])
    result = pl.pallas_call(
        functools.partial(forward_kernel, plan, tokens[0].shape[0]),
        grid=(plan[2],),
        in_specs=[anywhere] * 7
        + [
            pl.BlockSpec(col.shape, lambda i: (0, 0)),
            pl.BlockSpec(row.shape, lambda i: (0, 0)),
            pl.BlockSpec(feats.shape, lambda i: (0, 0, 0)),
        ],
        out_specs=[anywhere] * (11 + len(KEPT)),
        out_shape=[jax.ShapeDtypeStruct((4,) + v.shape, v.dtype) for v in shards] * 2
        + [jax.ShapeDtypeStruct((4, length, hidden), BF16)]
        + [jax.ShapeDtypeStruct(*v) for v in kept],
        scratch_shapes=[pltpu.VMEM(*v) for v in kept]
        + [pltpu.VMEM((16, part, width), BF16)] * 2
        + [
            pltpu.VMEM((2,) + shards[ATTN].shape, BF16),
            pltpu.VMEM((2, width, hidden // 2), BF16),
            pltpu.VMEM((2, hidden // 2, width), BF16),
            pltpu.VMEM((4,) + shards[ADAPTER].shape, BF16),
            pltpu.VMEM((2, length, hidden // 2), BF16),
            pltpu.VMEM(shards[ATTN].shape, BF16),
            pltpu.VMEM(shards[FFN_IN].shape, BF16),
        ]
        + [dma(size) for size in sizes],
        compiler_params=pltpu.CompilerParams(
            collective_id=0, has_side_effects=True, vmem_limit_bytes=60 * 2**20
        ),
        name="forward",
    )(*shards, *tokens, col, row, feats)
    return result[:5], result[5:10], result[10], result[11:]


def ids_kernel(ids, out, send, recv):
    s = lax.axis_index(SECTION)
    c = lax.axis_index(CTX)
    t = lax.axis_index(TP)
    barrier = pltpu.get_barrier_semaphore()
    for j in (1, 2, 3):
        pl.semaphore_signal(
            barrier,
            1,
            device_id=(s, lax.rem(c + j, 4), t),
            device_id_type=pl.DeviceIdType.MESH,
        )
    pl.semaphore_wait(barrier, 3)
    out[c] = ids[...]
    ways = [
        remote(ids, out.at[c], send.at[j - 1], recv.at[j - 1], (s, lax.rem(c + j, 4), t))
        for j in (1, 2, 3)
    ]
    for way in ways:
        way.start()
    for j, way in enumerate(ways):
        way.wait_send()
        region = out.at[lax.rem(c + 3 - j, 4)]
        remote(region, region, send.at[j], recv.at[j], (s, c, t)).wait_recv()


def ids_call(ids):
    spec = pl.BlockSpec(memory_space=pltpu.VMEM)
    return pl.pallas_call(
        ids_kernel,
        in_specs=[spec],
        out_specs=spec,
        out_shape=jax.ShapeDtypeStruct((4,) + ids.shape, ids.dtype),
        scratch_shapes=[pltpu.SemaphoreType.DMA((3,)), pltpu.SemaphoreType.DMA((3,))],
        compiler_params=pltpu.CompilerParams(collective_id=1, has_side_effects=True),
        name="ids",
    )(ids)


def tail_kernel(rider, *refs):
    refs = list(refs)

    def take(count):
        got = refs[:count]
        del refs[:count]
        return got

    h_ref, w_in_ref, w_out_ref, adapter_ref = take(4)
    ride_ins = take(len(rider.inputs))
    slope_ref, s_ref, a_ref, y_ref, yr_ref, out_ref = take(6)
    ride = (ride_ins, take(len(rider.inputs)), take(len(rider.scratch)))
    rows_in, acc = refs
    step = pl.program_id(0)
    width = acc.shape[1]
    lanes = adapter_ref.shape[2] // 2

    @pl.when(step == 0)
    def _():
        rider.start(*ride)
        extra = adapter_ref[0, width : width + 16, :].astype(F32)
        cuts = width // adapter_ref.shape[2]
        last = jnp.concatenate([extra[1 + r : 2 + r] for r in range(cuts)], axis=1)
        acc[...] = h_ref[...] + 4.0 * last
        rows_in[...] = h_ref[...].astype(BF16)

    @pl.when(step < 4)
    def _():
        bias = adapter_ref[0, width : width + 16, :lanes].astype(F32)[0:1]
        pre = dot_nn(rows_in[...], adapter_ref[0, :width, :lanes]) + bias
        sig = 1.0 / (1.0 + jnp.exp(-pre))
        gated = (pre * sig).astype(BF16)
        s_ref[0] = gated
        a_ref[0] = (sig * (1.0 + pre * (1.0 - sig))).astype(BF16)
        acc[...] += 4.0 * dot_nt(gated, adapter_ref[0, :width, lanes:])

    @pl.when((step >= 4) & (step < 12))
    def _():
        inner = dot_nn(rows_in[...], w_in_ref[0])
        phi = 0.5 * (1.0 + lax.erf(inner * 0.7071067811865476))
        slope_ref[0] = (
            phi + inner * jnp.exp(inner * inner * -0.5) * 0.3989422804014327
        ).astype(BF16)
        acc[...] += dot_nn((inner * phi).astype(BF16), w_out_ref[0])

    @pl.when(step == 12)
    def _():
        normed, rstd = norm(acc[...])
        y_ref[...] = normed
        yr_ref[...] = jnp.broadcast_to(rstd, yr_ref.shape)
        out_ref[...] = normed.astype(BF16)
        rider.finish(*ride)


def tail_call(h, tail_w, rider):
    w_in, w_out, adapter = tail_w
    length, width = h.shape
    groups, _, hidden = w_in.shape
    lanes = adapter.shape[2] // 2
    anywhere = pl.BlockSpec(memory_space=pl.ANY)

    def tile(j):
        j = jnp.clip(j - groups, 0, 7)
        return j // 2, lax.rem(j, 2)

    def group(j):
        return jnp.minimum(j, groups - 1)

    wide = pl.BlockSpec((length, width), lambda j: (0, 0))
    gated = pl.BlockSpec((1, length, lanes), lambda j: (group(j), 0, 0))
    cut = lambda rows: pl.BlockSpec(
        (1, rows, hidden // 2), lambda j: (tile(j)[0], 0, tile(j)[1])
    )
    result = pl.pallas_call(
        functools.partial(tail_kernel, rider),
        grid=(groups + 9,),
        in_specs=[
            wide,
            cut(width),
            pl.BlockSpec((1, hidden // 2, width), lambda j: (tile(j)[0], tile(j)[1], 0)),
            pl.BlockSpec((1,) + adapter.shape[1:], lambda j: (group(j), 0, 0)),
        ]
        + [anywhere] * len(rider.inputs),
        out_specs=[
            cut(length),
            gated,
            gated,
            wide,
            pl.BlockSpec((length, 128), lambda j: (0, 0)),
            wide,
        ]
        + [anywhere] * len(rider.inputs),
        out_shape=[
            jax.ShapeDtypeStruct((groups, length, hidden), BF16),
            jax.ShapeDtypeStruct((groups, length, lanes), BF16),
            jax.ShapeDtypeStruct((groups, length, lanes), BF16),
            jax.ShapeDtypeStruct((length, width), F32),
            jax.ShapeDtypeStruct((length, 128), F32),
            jax.ShapeDtypeStruct((length, width), BF16),
        ]
        + rider.shapes,
        scratch_shapes=rider.scratch
        + [pltpu.VMEM((length, width), BF16), pltpu.VMEM((length, width), F32)],
        compiler_params=pltpu.CompilerParams(
            collective_id=rider.call_id, has_side_effects=True, vmem_limit_bytes=60 * 2**20
        ),
        name="tail",
    )(h, w_in, w_out, adapter, *rider.inputs)
    return result[:6], result[6:]


def norm_back_rows(normed, rstd, grad):
    return rstd * (
        grad
        - jnp.mean(grad, axis=-1, keepdims=True)
        - normed * jnp.mean(grad * normed, axis=-1, keepdims=True)
    )


def head_grads(da, w_ref, do_ref):
    for g in range(w_ref.shape[0]):
        do_ref[g] = dot_nn(da, w_ref[g]).astype(BF16)


def sibling_of():
    return (1 - lax.axis_index(SECTION), lax.axis_index(CTX), lax.axis_index(TP))


def tail_back_kernel(rider, *refs):
    refs = list(refs)

    def take(count):
        got = refs[:count]
        del refs[:count]
        return got

    grad_ref, y_ref, yr_ref, h_ref, hr_ref, slope_ref = take(6)
    w_out_ref, w_in_ref, adapter_ref, s_ref, a_ref, w_do_ref = take(6)
    ride_ins = take(len(rider.inputs))
    dpre_ref, do_ref, pieces_ref, tails_ref = take(4)
    ride = (ride_ins, take(len(rider.inputs)), take(len(rider.scratch)))
    db, acc, mine, away, got, send, recv = refs
    step = pl.program_id(0)
    groups = away.shape[0]
    width = acc.shape[1]
    lanes = adapter_ref.shape[2] // 2
    first = lax.axis_index(SECTION) == 0

    def to_sibling(g):
        return remote(
            away.at[g], got.at[g], send.at[g], recv.at[g], sibling_of()
        )

    @pl.when(step == 0)
    def _():
        rider.start(*ride)
        dpre = norm_back_rows(y_ref[...], yr_ref[:, 0:1], grad_ref[...].astype(F32))
        acc[...] = dpre
        db[...] = dpre.astype(BF16)

    @pl.when(step < groups)
    def _():
        branch = db[...]
        ds = 4.0 * dot_nn(branch, adapter_ref[0, :width, lanes:])
        du = (ds * a_ref[0].astype(F32)).astype(BF16)
        acc[...] += dot_nt(du, adapter_ref[0, :width, :lanes])
        d_in = dot_tn(du, h_ref[...].astype(BF16))
        d_out = 4.0 * dot_tn(s_ref[0], branch)
        last = 4.0 * jnp.sum(branch.astype(F32), axis=0, keepdims=True)
        bias = jnp.sum(du.astype(F32), axis=0, keepdims=True)
        cut = width // 4
        bias = jnp.concatenate([bias, jnp.zeros((1, cut - lanes), F32)], axis=1)
        row = lax.broadcasted_iota(jnp.int32, (16, cut), 0)
        part = lanes // 4
        for c in range(4):
            one = d_in[c * part : (c + 1) * part]
            two = d_out[c * part : (c + 1) * part]
            mine[step, c] = jnp.where(first, one, two)
            away[step, c] = jnp.where(first, two, one).astype(BF16)
            tails_ref[c, step] = jnp.where(
                row == 0,
                last[:, c * cut : (c + 1) * cut],
                jnp.where(row == 1, bias, 0.0),
            ).astype(BF16)
        to_sibling(step).start()

    @pl.when((step >= groups) & (step < groups + 8))
    def _():
        dg = dot_nt(db[...], w_out_ref[0])
        df = (dg * slope_ref[0].astype(F32)).astype(BF16)
        acc[...] += dot_nt(df, w_in_ref[0])

    @pl.when(step == groups + 8)
    def _():
        dpre = norm_back_rows(h_ref[...], hr_ref[:, 0:1], acc[...])
        dpre_ref[...] = dpre
        head_grads(dpre.astype(BF16), w_do_ref, do_ref)
        for g in range(groups):
            copy = to_sibling(g)
            copy.wait_send()
            copy.wait_recv()
            for c in range(4):
                pieces_ref[c, g] = (mine[g, c] + got[g, c].astype(F32)).astype(BF16)
        rider.finish(*ride)


def tail_back(grad, y, yr, h, hr, slope, tail_w, s_act, a_slope, w_do, do_block, rider):
    w_in, w_out, adapter = tail_w
    length, width = y.shape
    groups, _, hidden = slope.shape
    lanes = s_act.shape[2]
    cols = w_do.shape[2]
    part = lanes // 4
    anywhere = pl.BlockSpec(memory_space=pl.ANY)

    def whole(v):
        return pl.BlockSpec(v.shape, lambda j: (0, 0))

    def tile(j):
        j = jnp.clip(j - groups, 0, 7)
        return j // 2, lax.rem(j, 2)

    def group(j):
        return jnp.minimum(j, groups - 1)

    result = pl.pallas_call(
        functools.partial(tail_back_kernel, rider),
        grid=(groups + 9,),
        in_specs=[whole(v) for v in (grad, y, yr, h, hr)]
        + [
            pl.BlockSpec((1, length, hidden // 2), lambda j: (tile(j)[0], 0, tile(j)[1])),
            pl.BlockSpec((1, hidden // 2, width), lambda j: (tile(j)[0], tile(j)[1], 0)),
            pl.BlockSpec((1, width, hidden // 2), lambda j: (tile(j)[0], 0, tile(j)[1])),
            pl.BlockSpec((1,) + adapter.shape[1:], lambda j: (group(j), 0, 0)),
            pl.BlockSpec((1, length, lanes), lambda j: (group(j), 0, 0)),
            pl.BlockSpec((1, length, lanes), lambda j: (group(j), 0, 0)),
            pl.BlockSpec((groups, width, cols), lambda j: (0, do_block, 0)),
        ]
        + [anywhere] * len(rider.inputs),
        out_specs=[
            pl.BlockSpec((length, width), lambda j: (0, 0)),
            pl.BlockSpec((groups, length, cols), lambda j: (0, 0, 0)),
            pl.BlockSpec((4, groups, part, width), lambda j: (0, 0, 0, 0)),
            pl.BlockSpec((4, groups, 16, width // 4), lambda j: (0, 0, 0, 0)),
        ]
        + [anywhere] * len(rider.inputs),
        out_shape=[
            jax.ShapeDtypeStruct((length, width), F32),
            jax.ShapeDtypeStruct((groups, length, cols), BF16),
            jax.ShapeDtypeStruct((4, groups, part, width), BF16),
            jax.ShapeDtypeStruct((4, groups, 16, width // 4), BF16),
        ]
        + rider.shapes,
        scratch_shapes=rider.scratch
        + [
            pltpu.VMEM((length, width), BF16),
            pltpu.VMEM((length, width), F32),
            pltpu.VMEM((groups, 4, part, width), F32),
            pltpu.VMEM((groups, 4, part, width), BF16),
            pltpu.VMEM((groups, 4, part, width), BF16),
            pltpu.SemaphoreType.DMA((groups,)),
            pltpu.SemaphoreType.DMA((groups,)),
        ],
        compiler_params=pltpu.CompilerParams(
            collective_id=rider.call_id, has_side_effects=True, vmem_limit_bytes=60 * 2**20
        ),
        name="tail_back",
    )(grad, y, yr, h, hr, slope, w_out, w_in, adapter, s_act, a_slope, w_do, *rider.inputs)
    return result[:2], result[2:4], result[4:]


def attn_back_kernel(causal, cross, rider, *refs):
    refs = list(refs)

    def take(count):
        got = refs[:count]
        del refs[:count]
        return got

    q_ref, k_ref, kx_ref, v_ref, vx_ref, o_ref, do_ref, lse_ref = take(8)
    if cross:
        wq_ref, wkv_ref, rest_ref, h_ref, hr_ref, w_do_ref = take(6)
    else:
        w_ref, rest_ref = take(2)
    qi_ref, ki_ref = take(2)
    ride_ins = take(len(rider.inputs))
    if cross:
        dpre_ref, do_next_ref, memory_ref = take(3)
    else:
        (dx_ref,) = take(1)
    ride_outs = take(len(rider.inputs))
    ride_sems = take(len(rider.scratch))
    ride = (ride_ins, ride_outs, ride_sems)
    dq_s, own_k, own_v, away_k, away_v, got_k, got_v, acc, send, recv = take(10)
    if cross:
        (acc2,) = take(1)
    step = pl.program_id(0)
    groups = away_k.shape[0]
    width = acc.shape[1]

    def to_sibling(g):
        return [
            remote(a.at[g], b.at[g], send.at[g, j], recv.at[g, j], sibling_of())
            for j, (a, b) in enumerate(((away_k, got_k), (away_v, got_v)))
        ]

    @pl.when(step == 0)
    def _():
        rider.start(*ride)
        acc[...] = rest_ref[...]
        if cross:
            acc2[...] = jnp.zeros_like(acc2)

    @pl.when(step > 0)
    def _():
        g = step - 1
        slot = lax.rem(g, 2)
        for copy in to_sibling(g):
            copy.wait_send()
            copy.wait_recv()
        dk = (own_k[slot] + got_k[g].astype(F32)).astype(BF16)
        dv = (own_v[slot] + got_v[g].astype(F32)).astype(BF16)
        dq = dq_s[slot]
        if cross:
            acc[...] += dot_nt(dq, wq_ref[0])
            acc2[...] += dot_nt(dk, wkv_ref[0, :width]) + dot_nt(dv, wkv_ref[0, width:])
        else:
            acc[...] += (
                dot_nt(dq, w_ref[0, :width])
                + dot_nt(dk, w_ref[0, width : 2 * width])
                + dot_nt(dv, w_ref[0, 2 * width :])
            )

    @pl.when(step < groups)
    def _():
        slot = lax.rem(step, 2)
        attend_back_group(
            (q_ref, (k_ref, kx_ref), (v_ref, vx_ref), o_ref, do_ref, lse_ref),
            (dq_s, slot),
            ((own_k, slot), (away_k, step)),
            ((own_v, slot), (away_v, step)),
            qi_ref,
            ki_ref,
            causal,
        )
        for copy in to_sibling(step):
            copy.start()

    @pl.when(step == groups)
    def _():
        if cross:
            dpre = norm_back_rows(h_ref[...], hr_ref[:, 0:1], acc[...])
            dpre_ref[...] = dpre
            head_grads(dpre.astype(BF16), w_do_ref, do_next_ref)
            memory_ref[...] = acc2[...]
        else:
            dx_ref[...] = acc[...].astype(dx_ref.dtype)
        rider.finish(*ride)


def attn_back(heads, ids, causal, rider, rest, weights, cross=None):
    groups, length, cols = heads[0].shape
    width = rest.shape[1]
    anywhere = pl.BlockSpec(memory_space=pl.ANY)

    def now(shape):
        return pl.BlockSpec((1,) + shape[1:], lambda t: (jnp.minimum(t, groups - 1), 0, 0))

    def past(rows):
        return pl.BlockSpec((1, rows, cols), lambda t: (jnp.maximum(t - 1, 0), 0, 0))

    def whole(v):
        return pl.BlockSpec(v.shape, lambda t: (0,) * len(v.shape))

    wide = jax.ShapeDtypeStruct((length, width), F32)
    if cross:
        h, hr, w_do = cross
        wq, wkv = weights
        extra = [wq, wkv, rest, h, hr, w_do]
        specs = [
            past(width),
            past(2 * width),
            whole(rest),
            whole(h),
            whole(hr),
            pl.BlockSpec((groups, width, cols), lambda t: (0, 3, 0)),
        ]
        outs = [wide, jax.ShapeDtypeStruct(heads[0].shape, BF16), wide]
    else:
        extra = [weights, rest]
        specs = [past(3 * width), whole(rest)]
        outs = [jax.ShapeDtypeStruct((length, width), BF16)]
    moving = pltpu.VMEM((groups, length, cols), BF16)
    result = pl.pallas_call(
        functools.partial(attn_back_kernel, causal, bool(cross), rider),
        grid=(groups + 1,),
        in_specs=[now(v.shape) for v in heads]
        + specs
        + [whole(v) for v in ids]
        + [anywhere] * len(rider.inputs),
        out_specs=[whole(v) for v in outs] + [anywhere] * len(rider.inputs),
        out_shape=outs + rider.shapes,
        scratch_shapes=rider.scratch
        + [
            pltpu.VMEM((2, length, cols), BF16),
            pltpu.VMEM((2, length, cols), F32),
            pltpu.VMEM((2, length, cols), F32),
            moving,
            moving,
            moving,
            moving,
            pltpu.VMEM((length, width), F32),
            pltpu.SemaphoreType.DMA((groups, 2)),
            pltpu.SemaphoreType.DMA((groups, 2)),
        ]
        + ([pltpu.VMEM((length, width), F32)] if cross else []),
        compiler_params=pltpu.CompilerParams(
            collective_id=rider.call_id,
            has_side_effects=True,
            vmem_limit_bytes=60 * 2**20,
        ),
        name="attn_back",
    )(*heads, *extra, *ids, *rider.inputs)
    return result[: len(outs)], result[len(outs) :]


def gather_plain(entry, shards):
    full = [lax.all_gather(lax.all_gather(v, TP), SECTION) for v in shards]
    return [v[entry] for v in full]


def spread(blocks):
    chips = lax.axis_size(CTX) * lax.axis_size(TP)
    kinds, rows, part, width = blocks.shape
    blocks = jnp.pad(blocks, ((0, 0), (0, chips - rows), (0, 0), (0, 0)))
    moved = lax.all_to_all(
        jnp.moveaxis(blocks, 1, 0), (CTX, TP), 0, 0, tiled=True
    )
    return jnp.moveaxis(moved, 0, 1).reshape(kinds, chips * part, width)


def collect(tokens, rows):
    chips = lax.axis_size(CTX) * lax.axis_size(TP)
    kinds, length, width = tokens.shape
    part = length // chips
    blocks = jnp.moveaxis(tokens.reshape(kinds, chips, part, width), 1, 0)
    moved = lax.all_to_all(blocks, (CTX, TP), 0, 0, tiled=True)
    return jnp.moveaxis(moved, 0, 1)[:, :rows]


def per_device(
    layer_inputs,
    out_grad,
    src_seg,
    tgt_seg,
    qkv_weights,
    out_weights,
    cross_weights,
    ffn_in,
    ffn_out,
    adapter_in,
    adapter_in_bias,
    adapter_out,
    adapter_out_bias,
):
    core = lax.axis_index(SECTION)
    is_first = core == 0
    tp = lax.axis_size(TP)
    chips = lax.axis_size(CTX) * tp
    chip = lax.axis_index(CTX) * tp + lax.axis_index(TP)
    _, micro, per_micro, part, width = layer_inputs.shape
    row_count = micro * per_micro
    half = part // 2
    length = half * chips

    def pick(first, second):
        return jnp.where(is_first, first, second)

    x = layer_inputs.reshape(row_count, part, width)
    low, high = x[:, :half], x[:, half:]
    other = swap(pick(high, low))
    grads = out_grad.reshape(row_count, part, width)
    stacked = jnp.stack(
        [pick(low, other), pick(other, high), pick(grads[:, :half], grads[:, half:])]
    )
    near = lax.axis_size(CTX) == 4 and tp == 4
    lanes = adapter_in_bias.shape[1]
    cols = out_weights.shape[2]
    pad = lambda v, n: jnp.pad(v, [(0, n - v.shape[0])] + [(0, 0)] * (v.ndim - 1))
    biases = jnp.concatenate(
        [pad(adapter_in_bias[0], cols)[None], adapter_out_bias[0].reshape(-1, cols)]
    )
    shards = [
        jnp.concatenate([qkv_weights[0], out_weights], axis=0).reshape(-1, cols),
        ffn_in[0],
        ffn_out[0],
        jnp.concatenate(
            [
                jnp.concatenate([adapter_in[0], adapter_out[0].T], axis=1),
                pad(biases, 256),
            ],
            axis=0,
        ),
        cross_weights[0].reshape(-1, cols),
    ]
    if near:
        ids = ids_call(jnp.stack([src_seg, tgt_seg]).reshape(2 * row_count, -1))
        flat_ids = ids.swapaxes(0, 1).reshape(2, row_count, -1)
    else:
        flat_ids = [
            lax.all_gather(v.reshape(row_count, -1), CTX, axis=1, tiled=True)
            for v in (src_seg, tgt_seg)
        ]

    def unpack(full):
        attn, w_in, w_out, adapter, cross = full
        attn = attn.reshape(tp, 4, -1, cols)
        cross = cross.reshape(tp, 2, -1, cols)
        b_out = adapter[0, width + 1 : width + 1 + width // cols].reshape(width)
        tail = (
            w_in,
            w_out,
            adapter[:, :width, :lanes],
            adapter[:, width, :lanes],
            adapter[:, :width, lanes:],
            b_out,
        )
        return attn, cross, tail

    def ids_of(flat):
        row = lax.dynamic_index_in_dim(
            flat, jnp.minimum(chip, row_count - 1), 0, keepdims=False
        )
        return row.reshape(chips, 2, half)

    index = jnp.arange(length, dtype=jnp.int32)
    place = (index // half) * part + index % half

    def cut(seg, which):
        own = lax.dynamic_index_in_dim(seg, which, 1, keepdims=False).reshape(length)
        return own, place + which * half

    src_ids, tgt_ids = ids_of(flat_ids[0]), ids_of(flat_ids[1])

    def id_arrays(seg_q, seg_k):
        qi = jnp.stack(cut(seg_q, core))
        ki = jnp.stack(cut(seg_k, core) + cut(seg_k, 1 - core))
        return (qi.T, ki), (qi, ki.T)

    enc_ids = id_arrays(src_ids, src_ids)
    dec_ids = id_arrays(tgt_ids, tgt_ids)
    cross_ids = id_arrays(tgt_ids, src_ids)

    def scatter(arrays, call_id):
        return Scatter(arrays, row_count, call_id) if near else None

    def tokens(value):
        return value.astype(BF16).reshape(chips, half, width)

    def scatter(arrays, call_id):
        return Scatter(arrays, row_count, call_id) if near else None

    def tokens(value):
        return value.astype(BF16).reshape(chips, half, width)

    if near:
        src_own, place_own = cut(src_ids, core)
        src_oth, place_oth = cut(src_ids, 1 - core)
        tgt_own, tgt_oth = cut(tgt_ids, core)[0], cut(tgt_ids, 1 - core)[0]
        feats = jnp.stack(
            [
                id_columns(src_own, False),
                id_columns(src_own, True),
                id_columns(src_oth, True),
                id_columns(tgt_own, False),
                id_columns(tgt_own, True),
                id_columns(tgt_oth, True),
            ]
        )
        enc_w, dec_w, slope, kept = forward_call(
            shards,
            [stacked[0], stacked[1]],
            place_own[:, None],
            jnp.stack([place_own, place_oth] * 4),
            feats,
        )
        (dec_slope, dec_s, dec_a, dec_y, dec_yr, decoded), (placed,) = tail_call(
            kept[C2],
            (dec_w[1], dec_w[2], dec_w[3]),
            scatter([(stacked[2], Scatter.BRING)], 8),
        )
        cotangent = placed.reshape(length, width)
        encoded_bf = kept[EY].astype(BF16)
    else:
        source, target, cotangent = spread(stacked)
        enc_attn, enc_cross, enc_tail_w = unpack(gather_plain(0, shards))
        dec_attn, dec_cross, dec_tail_w = unpack(gather_plain(1, shards))
        enc_mid, enc_self = self_forward(
            source, source.astype(F32), enc_attn, enc_ids, False
        )
        encoded, enc_tail = tail_forward(enc_mid, enc_tail_w)
        encoded_bf = encoded.astype(BF16)
        memory = [project(encoded_bf, enc_cross[:, j]).astype(BF16) for j in range(2)]
        memory_other = swap(jnp.stack(memory))
        mem_keys = (memory[0], memory_other[0], memory[1], memory_other[1])
        dec_mid, dec_self = self_forward(
            target, target.astype(F32), dec_attn, dec_ids, True
        )
        queries = project(dec_mid.astype(BF16), dec_cross[:, 0]).astype(BF16)
        cross_o, cross_lse = attention_forward(
            queries, mem_keys, cross_ids[0], False
        )
        second, second_rstd = norm(dec_mid + unproject(cross_o, dec_cross[:, 1]))
        decoded, dec_tail = tail_forward(second, dec_tail_w)

    if near:

        def heads(q, k, kx, v, vx, o, lse, do):
            flat = kept[lse].reshape(kept[lse].shape[0], -1, length)
            return [kept[n] for n in (q, k, kx, v, vx, o)] + [do, flat]

        def pieces(parts):
            return [v.reshape((chips,) + v.shape[2:]) for v in parts]

        (grad_cross, do), dec_parts, (out_enc,) = tail_back(
            cotangent,
            dec_y,
            dec_yr,
            kept[C2],
            kept[C2R],
            dec_slope,
            (dec_w[1], dec_w[2], dec_w[3]),
            dec_s,
            dec_a,
            dec_w[4],
            1,
            scatter([(tokens(encoded_bf), 0)], 2),
        )
        (dpre, do, grad_encoded), (out_dec,) = attn_back(
            heads(CQ, MK, MKX, MV, MVX, CO, CL, do),
            cross_ids[1],
            False,
            scatter([(tokens(decoded), 1)], 3),
            grad_cross,
            (dec_w[4], enc_w[4]),
            (kept[DH], kept[DR], dec_w[0]),
        )
        (grad_target,), dec_sum = attn_back(
            heads(DQ, DK, DKX, DV, DVX, DO, DL, do),
            dec_ids[1],
            True,
            scatter([(v, 1) for v in pieces(dec_parts)], 4),
            dpre,
            dec_w[0],
        )
        (dpre, do), enc_parts, (moved,) = tail_back(
            grad_encoded,
            kept[EY],
            kept[EYR],
            kept[EH],
            kept[ER],
            slope,
            (enc_w[1], enc_w[2], enc_w[3]),
            kept[ES],
            kept[EA],
            enc_w[0],
            3,
            scatter([(tokens(grad_target), 1)], 5),
        )
        (grad_source,), enc_sum = attn_back(
            heads(EQ, EK, EKX, EV, EVX, EO, EL, do),
            enc_ids[1],
            False,
            scatter([(v, 0) for v in pieces(enc_parts)], 6),
            dpre,
            enc_w[0],
        )
        outs = pick(out_enc, out_dec)
        sums, ends = [
            jnp.sum(pick(a, b).astype(F32), axis=0) for a, b in zip(enc_sum, dec_sum)
        ]
        part_rows = lanes // 4
        ends = jnp.pad(jnp.sum(ends, axis=0), ((0, 0), (0, width - width // 4)))
        mine = jnp.concatenate([sums.reshape(2 * part_rows, width), ends]).astype(BF16)
        (last,), whole = send_call(scatter([(tokens(grad_source), 0)], 7), mine)
        grads = pick(last, moved).astype(F32)
        whole = whole.astype(F32)
        weights = whole[:, : 2 * part_rows].reshape(4, 2, part_rows, width)
        ends = whole[:, 2 * part_rows :, : width // 4]
        return (
            outs.reshape(layer_inputs.shape),
            grads.reshape(layer_inputs.shape),
            weights[:, 0].reshape(lanes, width).T[None],
            ends[0, 1, :lanes][None],
            weights[:, 1].reshape(1, lanes, width),
            ends[:, 0].reshape(1, width),
        )

    grad_second, dec_terms = tail_backward(cotangent.astype(F32), dec_tail, dec_tail_w)
    grad_cross = norm_back(second, second_rstd, grad_second)
    do = project(grad_cross.astype(BF16), dec_cross[:, 1]).astype(BF16)
    dqc, dmk, dmv = attend_back(
        queries, mem_keys, cross_o, do, cross_lse, cross_ids, False
    )
    grad_first = unproject(dqc, dec_cross[:, 0]) + grad_cross
    grad_target = self_backward(grad_first, dec_self, dec_attn, dec_ids, True)

    grad_encoded = unproject(dmk, enc_cross[:, 0]) + unproject(dmv, enc_cross[:, 1])
    grad_mid, enc_terms = tail_backward(grad_encoded, enc_tail, enc_tail_w)
    grad_source = self_backward(grad_mid, enc_self, enc_attn, enc_ids, False)

    has_row = chip < row_count

    def total(enc_term, dec_term):
        enc_term = jnp.where(has_row, enc_term, 0.0).astype(BF16)
        dec_term = jnp.where(has_row, dec_term, 0.0).astype(BF16)
        got = swap(pick(dec_term, enc_term))
        return (pick(enc_term, dec_term).astype(F32) + got.astype(F32)).astype(BF16)

    sums = [total(e, d) for e, d in zip(enc_terms, dec_terms)]
    scattered = [
        lax.psum_scatter(v, TP, scatter_dimension=0, tiled=False) for v in sums[:3]
    ]
    scattered = [lax.psum(v, CTX).astype(F32) for v in scattered]
    bias_sum = lax.psum(sums[3], (CTX, TP)).astype(F32)

    results = jnp.stack(
        [
            encoded_bf,
            decoded.astype(BF16),
            grad_source.astype(BF16),
            grad_target.astype(BF16),
        ]
    )
    placed = collect(results, row_count)

    def join(enc_part, dec_part):
        mine = pick(enc_part, dec_part)
        got = swap(pick(dec_part, enc_part))
        return jnp.concatenate([pick(mine, got), pick(got, mine)], axis=1)

    outs = join(placed[0], placed[1]).reshape(layer_inputs.shape)
    grads = join(placed[2], placed[3]).astype(F32).reshape(layer_inputs.shape)
    return (
        outs,
        grads,
        scattered[0][None],
        scattered[1][None],
        scattered[2].T[None],
        bias_sum[None],
    )


def solution(mesh):
    return jax.shard_map(
        per_device,
        mesh=mesh,
        in_specs=(
            P(SECTION, None, None, (CTX, TP), None),
            P(None, None, (CTX, TP), None),
            P(None, None, CTX),
            P(None, None, CTX),
            P(SECTION, None, None, TP),
            P(SECTION, None, TP),
            P(SECTION, None, None, TP),
            P(SECTION, None, TP),
            P(SECTION, TP, None),
            P(SECTION, None, TP),
            P(SECTION, TP),
            P(SECTION, TP, None),
            P(SECTION, None),
        ),
        out_specs=(
            P(SECTION, None, None, (CTX, TP), None),
            P(SECTION, None, None, (CTX, TP), None),
            P(SECTION, None, TP),
            P(SECTION, TP),
            P(SECTION, TP, None),
            P(SECTION, None),
        ),
        check_vma=False,
    )
```

```python
import functools

import jax
import jax.numpy as jnp
from jax import lax
from jax.experimental import pallas as pl
from jax.experimental.pallas import tpu as pltpu
from jax.sharding import PartitionSpec as P

HEAD = 64
SCALE = HEAD**-0.5
EPS = 1e-05
MASKED = -1e30
F32 = jnp.float32
BF16 = jnp.bfloat16
SECTION, CTX, TP = "section", "ctx", "tp"


def swap(value):
    return lax.ppermute(value, SECTION, [(0, 1), (1, 0)])


def remote(src, dst, send, recv, where):
    return pltpu.make_async_remote_copy(
        src_ref=src,
        dst_ref=dst,
        send_sem=send,
        recv_sem=recv,
        device_id=where,
        device_id_type=pl.DeviceIdType.MESH,
    )


def device_of(section, chip):
    return (section, chip // 4, lax.rem(chip, 4))


def greet_all():
    s = lax.axis_index(SECTION)
    chip = lax.axis_index(CTX) * 4 + lax.axis_index(TP)
    barrier = pltpu.get_barrier_semaphore()
    for core in (0, 1):
        for i in range(core, 16):
            pl.semaphore_signal(
                barrier,
                1,
                device_id=device_of(lax.rem(s + 1 - core, 2), lax.rem(chip + i, 16)),
                device_id_type=pl.DeviceIdType.MESH,
            )
    pl.semaphore_wait(barrier, 31)


class Scatter:
    BRING = 2

    def __init__(self, arrays, rows, call_id):
        self.inputs = [a for a, _ in arrays]
        self.kinds = [k for _, k in arrays]
        self.rows = rows
        self.call_id = call_id
        self.shapes = [
            jax.ShapeDtypeStruct(
                ((16,) if k == self.BRING else (rows, 2)) + a.shape[1:], a.dtype
            )
            for a, k in arrays
        ]
        count = len(arrays)
        self.scratch = [
            pltpu.SemaphoreType.DMA((count, 16)),
            pltpu.SemaphoreType.DMA((count, 16, 2)),
        ]

    def sends(self, ins, outs, sems):
        send, recv = sems
        s = lax.axis_index(SECTION)
        chip = lax.axis_index(CTX) * 4 + lax.axis_index(TP)
        for a, kind in enumerate(self.kinds):
            for i in range(16):
                p = lax.rem(chip + i, 16)
                if kind == self.BRING:
                    ready = p < self.rows
                    src = ins[a].at[jnp.minimum(p, self.rows - 1)]
                    dst = outs[a].at[chip]
                    core, mark = s, 0
                    stays = True
                else:
                    ready = chip < self.rows
                    src = ins[a].at[p]
                    dst = outs[a].at[jnp.minimum(chip, self.rows - 1), s]
                    core, mark = kind, s
                    stays = s == kind
                near = pltpu.make_async_copy(src, dst, send.at[a, i])
                far = remote(
                    src, dst, send.at[a, i], recv.at[a, i, mark], device_of(core, p)
                )
                yield i, ready, stays, near, far

    def start(self, ins, outs, sems):
        greet_all()
        for i, ready, stays, near, far in self.sends(ins, outs, sems):

            @pl.when(ready)
            def _():
                if i:
                    far.start()
                elif stays is True:
                    near.start()
                else:
                    pl.when(stays)(near.start)
                    pl.when(jnp.logical_not(stays))(far.start)

    def finish(self, ins, outs, sems):
        send, recv = sems
        s = lax.axis_index(SECTION)
        chip = lax.axis_index(CTX) * 4 + lax.axis_index(TP)
        for i, ready, stays, near, far in self.sends(ins, outs, sems):

            @pl.when(ready)
            def _():
                if i:
                    far.wait_send()
                elif stays is True:
                    near.wait()
                else:
                    pl.when(stays)(near.wait)
                    pl.when(jnp.logical_not(stays))(far.wait_send)

        def got(region, sem):
            remote(region, region, send.at[0, 0], sem, (1 - s, 0, 0)).wait_recv()

        for a, kind in enumerate(self.kinds):
            for i in range(16):
                sender = lax.rem(chip + 16 - i, 16)
                if kind == self.BRING:
                    if i:

                        @pl.when(chip < self.rows)
                        def _():
                            got(outs[a].at[sender], recv.at[a, i, 0])

                    continue

                @pl.when((s == kind) & (sender < self.rows))
                def _():
                    for core in (0, 1) if i else (1 - kind,):
                        region = outs[a].at[jnp.minimum(sender, self.rows - 1), core]
                        got(region, recv.at[a, i, core])


def send_kernel(rider, *refs):
    n = len(rider.inputs)
    block_in, (own, spread_out) = refs[n], (refs[n], refs[2 * n + 1])
    ins, outs = refs[:n], refs[n + 1 : 2 * n + 1]
    sems = refs[2 * n + 2 : 2 * n + 4]
    b_send, b_recv = refs[2 * n + 4 :]
    rider.start(ins, outs, sems)
    s = lax.axis_index(SECTION)
    c = lax.axis_index(CTX)
    t = lax.axis_index(TP)
    dst = spread_out.at[c]
    keep = pltpu.make_async_copy(own, dst, b_send.at[0])
    keep.start()
    ways = [
        remote(own, dst, b_send.at[j], b_recv.at[j], (s, lax.rem(c + j, 4), t))
        for j in (1, 2, 3)
    ]
    for way in ways:
        way.start()
    keep.wait()
    for j, way in enumerate(ways):
        way.wait_send()
        region = spread_out.at[lax.rem(c + 3 - j, 4)]
        remote(region, region, b_send.at[0], b_recv.at[j + 1], (s, c, t)).wait_recv()
    rider.finish(ins, outs, sems)


def send_call(rider, block):
    anywhere = pl.BlockSpec(memory_space=pl.ANY)
    count = len(rider.inputs)
    result = pl.pallas_call(
        functools.partial(send_kernel, rider),
        in_specs=[anywhere] * (count + 1),
        out_specs=[anywhere] * (count + 1),
        out_shape=rider.shapes + [jax.ShapeDtypeStruct((4,) + block.shape, block.dtype)],
        scratch_shapes=rider.scratch
        + [pltpu.SemaphoreType.DMA((4,)), pltpu.SemaphoreType.DMA((4,))],
        compiler_params=pltpu.CompilerParams(
            collective_id=rider.call_id, has_side_effects=True
        ),
        name="send_last",
    )(*rider.inputs, block)
    return result[:count], result[count]


def dot_nt(left, right, **kw):
    return lax.dot_general(
        left, right, (((1,), (1,)), ((), ())), preferred_element_type=F32, **kw
    )


def dot_nn(left, right):
    return lax.dot_general(
        left, right, (((1,), (0,)), ((), ())), preferred_element_type=F32
    )


def dot_tn(left, right):
    return lax.dot_general(
        left, right, (((0,), (0,)), ((), ())), preferred_element_type=F32
    )


def attn_fwd_kernel(
    causal, q_ref, ko_ref, kx_ref, vo_ref, vx_ref, fq, fo, fx, qi_ref, ki_ref, o_ref, lse_ref
):
    for pair in range(lse_ref.shape[1]):
        attend_pair(
            0,
            pair,
            q_ref,
            (ko_ref, kx_ref),
            (vo_ref, vx_ref),
            o_ref,
            lse_ref,
            (fq, fo, fx),
            (qi_ref[:, 1:2], (ki_ref[1:2, :], ki_ref[3:4, :])),
            causal,
        )


def attention_call(kernel, name, causal, blocks, small, outs):
    def group_spec(v):
        return pl.BlockSpec((1,) + v.shape[1:], lambda t: (t,) + (0,) * (len(v.shape) - 1))

    return pl.pallas_call(
        functools.partial(kernel, causal),
        grid=(blocks[0].shape[0],),
        in_specs=[group_spec(v) for v in blocks]
        + [pl.BlockSpec(v.shape, lambda t: (0, 0)) for v in small],
        out_specs=[group_spec(v) for v in outs],
        out_shape=outs,
        compiler_params=pltpu.CompilerParams(vmem_limit_bytes=48 * 2**20),
        name=name,
    )(*blocks, *small)


def id_columns(ids, keys):
    lane = jnp.arange(2 * HEAD, dtype=jnp.int32)[None] % HEAD
    same = ids[:, None] == lane
    value = jnp.where(same, 1.0, 0.0) if keys else jnp.where(same, 0.0, MASKED)
    return jnp.where(lane < 4, value, 0.0).astype(BF16)


def attention_forward(q, keys, ids, causal):
    groups, length, width = q.shape
    pairs = width // HEAD // 2
    outs = [
        jax.ShapeDtypeStruct(q.shape, BF16),
        jax.ShapeDtypeStruct((groups, pairs, 2, length), F32),
    ]
    feats = [
        id_columns(ids[0][:, 0], False),
        id_columns(ids[1][0], True),
        id_columns(ids[1][2], True),
    ]
    o, lse = attention_call(
        attn_fwd_kernel, "attn_fwd", causal, [q, *keys], [*feats, *ids], outs
    )
    return o, lse.reshape(groups, 2 * pairs, length)


def attend_back_group(ins, dq_out, dk_outs, dv_outs, feats, qi_ref, ki_ref, causal):
    q_ref, k_refs, v_refs, o_ref, do_ref, lse_ref = ins
    length = q_ref.shape[1]
    block = length // 2
    posq = qi_ref[1:2, :]
    ones = jnp.ones((8, 2 * HEAD), F32)

    def put(out, rows, lanes, value):
        out[0][out[1], rows, lanes] = value.astype(out[0].dtype)

    for pair in range(q_ref.shape[2] // (2 * HEAD)):
        lanes = slice(pair * 2 * HEAD, (pair + 1) * 2 * HEAD)
        q2 = q_ref[0, :, lanes] * jnp.asarray(SCALE, BF16)
        do2 = do_ref[0, :, lanes]
        prod2 = do2.astype(F32) * o_ref[0, :, lanes].astype(F32)
        dq, dk, dv = [None, None], {}, {}
        for j in range(2):
            here = head_mask(length, j)
            q_all = jnp.where(here, q2, feats[0][...])
            q_only = jnp.where(here, q2, jnp.zeros_like(q2))
            do_all = jnp.where(here, do2, jnp.zeros_like(do2))
            delta = dot_nt(
                ones, jnp.where(here, prod2, 0.0), precision=lax.Precision.HIGHEST
            )[0:1]
            lse = lse_ref[0, 2 * pair + j : 2 * pair + j + 1, :]
            for n in range(2):
                for b in range(2):
                    rows = slice(b * block, (b + 1) * block)
                    first = b * block if causal else 0
                    k2 = k_refs[n][0, rows, lanes]
                    there = head_mask(block, j)
                    k = jnp.where(there, k2, feats[1 + n][rows])
                    k_only = jnp.where(there, k2, jnp.zeros_like(k2))
                    s = dot_nt(k, q_all[first:])
                    p = jnp.exp(s - lse[:, first:])
                    if causal:
                        ok = posq[:, first:] >= ki_ref[rows, 2 * n + 1 : 2 * n + 2]
                        p = jnp.where(ok, p, 0.0)
                    dp = dot_nt(v_refs[n][0, rows, lanes], do_all[first:])
                    ds = (p * (dp - delta[:, first:])).astype(BF16)
                    add = lambda old, new: new if old is None else old + new
                    dv[n, b] = add(
                        dv.get((n, b)), dot_nn(p.astype(BF16), do_all[first:])
                    )
                    dk[n, b] = add(dk.get((n, b)), dot_nn(ds, q_only[first:]))
                    part = dot_tn(k_only, ds)
                    if not first:
                        dq[0] = add(dq[0], part[:, :block])
                    dq[1] = add(dq[1], part[:, block - first :])
        for n in range(2):
            for b in range(2):
                rows = slice(b * block, (b + 1) * block)
                put(dv_outs[n], rows, lanes, dv[n, b])
                put(dk_outs[n], rows, lanes, dk[n, b])
        for b in range(2):
            put(dq_out, slice(b * block, (b + 1) * block), lanes, (dq[b] * SCALE).T)


def attn_bwd_kernel(
    causal,
    q_ref,
    ko_ref,
    kx_ref,
    vo_ref,
    vx_ref,
    o_ref,
    do_ref,
    lse_ref,
    fq,
    fo,
    fx,
    qi_ref,
    ki_ref,
    dq_ref,
    dko_ref,
    dkx_ref,
    dvo_ref,
    dvx_ref,
):
    attend_back_group(
        (q_ref, (ko_ref, kx_ref), (vo_ref, vx_ref), o_ref, do_ref, lse_ref),
        (dq_ref, 0),
        ((dko_ref, 0), (dkx_ref, 0)),
        ((dvo_ref, 0), (dvx_ref, 0)),
        (fq, fo, fx),
        qi_ref,
        ki_ref,
        causal,
    )


def back_feats(ids):
    return [
        id_columns(ids[0][0], False),
        id_columns(ids[1][:, 0], True),
        id_columns(ids[1][:, 2], True),
    ]


def attention_backward(q, keys, o, do, lse, ids, causal):
    outs = [jax.ShapeDtypeStruct(q.shape, BF16)] * 5
    small = [*back_feats(ids), *ids]
    return attention_call(
        attn_bwd_kernel, "attn_bwd", causal, [q, *keys, o, do, lse], small, outs
    )


def norm(value):
    mean = jnp.mean(value, axis=-1, keepdims=True)
    centered = value - mean
    rstd = lax.rsqrt(jnp.mean(centered * centered, axis=-1, keepdims=True) + EPS)
    return centered * rstd, rstd


def norm_back(normed, rstd, grad):
    return rstd * (
        grad
        - jnp.mean(grad, axis=-1, keepdims=True)
        - normed * jnp.mean(grad * normed, axis=-1, keepdims=True)
    )


def project(rows, weight):
    return jnp.einsum("pk,tkm->tpm", rows, weight, preferred_element_type=F32)


def unproject(blocks, weight):
    return jnp.einsum("tpm,tkm->pk", blocks, weight, preferred_element_type=F32)


def self_forward(rows_bf, rows, w_attn, ids, causal):
    kv = [project(rows_bf, w_attn[:, j]).astype(BF16) for j in (1, 2)]
    other = swap(jnp.stack(kv))
    q = project(rows_bf, w_attn[:, 0]).astype(BF16)
    keys = (kv[0], other[0], kv[1], other[1])
    o, lse = attention_forward(q, keys, ids[0], causal)
    h, rstd = norm(rows + unproject(o, w_attn[:, 3]))
    return h, (q, keys, o, lse, h, rstd)


def attend_back(q, keys, o, do, lse, ids, causal):
    dq, dko, dkx, dvo, dvx = attention_backward(q, keys, o, do, lse, ids[1], causal)
    other = swap(jnp.stack([dkx, dvx])).astype(F32)
    dk = (dko.astype(F32) + other[0]).astype(BF16)
    dv = (dvo.astype(F32) + other[1]).astype(BF16)
    return dq, dk, dv


def self_backward(grad, kept, w_attn, ids, causal):
    q, keys, o, lse, h, rstd = kept
    dpre = norm_back(h, rstd, grad)
    do = project(dpre.astype(BF16), w_attn[:, 3]).astype(BF16)
    dq, dk, dv = attend_back(q, keys, o, do, lse, ids, causal)
    return (
        unproject(dq, w_attn[:, 0])
        + unproject(dk, w_attn[:, 1])
        + unproject(dv, w_attn[:, 2])
        + dpre
    )


def tail_forward(h, tail_w):
    w_in, w_out, a_in, b_in, a_out, b_out = tail_w
    rows = h.astype(BF16)
    inner = project(rows, w_in)
    phi = 0.5 * (1.0 + lax.erf(inner * 0.7071067811865476))
    g = (inner * phi).astype(BF16)
    slope = phi + inner * jnp.exp(inner * inner * -0.5) * 0.3989422804014327
    pre = project(rows, a_in) + b_in.astype(F32)[:, None, :]
    sig = jax.nn.sigmoid(pre)
    s = (pre * sig).astype(BF16)
    a_slope = sig * (1.0 + pre * (1.0 - sig))
    total = jnp.einsum("tpm,tmk->pk", g, w_out, preferred_element_type=F32)
    total += 4.0 * (
        jnp.einsum("tpm,tkm->pk", s, a_out, preferred_element_type=F32)
        + b_out.astype(F32)
    )
    y, rstd = norm(h + total)
    return y, (rows, slope.astype(BF16), s, a_slope.astype(BF16), y, rstd)


def tail_backward(grad, kept, tail_w):
    w_in, w_out, a_in, b_in, a_out, b_out = tail_w
    rows, slope, s, a_slope, y, rstd = kept
    dpre = norm_back(y, rstd, grad)
    db = dpre.astype(BF16)
    dg = jnp.einsum("pk,tmk->tpm", db, w_out, preferred_element_type=F32)
    df = (dg * slope.astype(F32)).astype(BF16)
    ds = 4.0 * jnp.einsum("pk,tkm->tpm", db, a_out, preferred_element_type=F32)
    du = (ds * a_slope.astype(F32)).astype(BF16)
    terms = (
        jnp.einsum("pk,tpm->tkm", rows, du, preferred_element_type=F32),
        jnp.sum(du.astype(F32), axis=1),
        4.0 * jnp.einsum("pk,tpm->tkm", db, s, preferred_element_type=F32),
        4.0 * jnp.sum(db.astype(F32), axis=0),
    )
    return unproject(df, w_in) + unproject(du, a_in) + dpre, terms


def head_mask(rows, j):
    lane = lax.broadcasted_iota(jnp.int32, (rows, 2 * HEAD), 1)
    return (lane < HEAD) if j == 0 else (lane >= HEAD)


def attend_pair(t, pair, q_ref, k_refs, v_refs, o_ref, lse_ref, feats, places, causal):
    length = q_ref.shape[1]
    block = length // 2
    lanes = pl.ds(pl.multiple_of(pair * 2 * HEAD, 2 * HEAD), 2 * HEAD)
    posq, posk = places
    for b in range(2):
        rows = slice(b * block, (b + 1) * block)
        q2 = q_ref[t, rows, lanes] * jnp.asarray(SCALE, BF16)
        cuts = [(n, a) for n in range(2) for a in range(b + 1 if causal else 2)]
        outs = []
        for j in range(2):
            q = jnp.where(head_mask(block, j), q2, feats[0][rows])
            parts = []
            for n, a in cuts:
                span = slice(a * block, (a + 1) * block)
                k = jnp.where(
                    head_mask(block, j), k_refs[n][t, span, lanes], feats[1 + n][span]
                )
                s = dot_nt(q, k)
                if causal and a == b:
                    s = jnp.where(posq[rows] >= posk[n][:, span], s, MASKED)
                parts.append(s)
            top = functools.reduce(
                jnp.maximum, [jnp.max(s, axis=1, keepdims=True) for s in parts]
            )
            ex = [jnp.exp(s - top) for s in parts]
            total = sum(jnp.sum(e, axis=1, keepdims=True) for e in ex)
            out = sum(
                dot_nn(
                    e.astype(BF16), v_refs[n][t, a * block : (a + 1) * block, lanes]
                )
                for e, (n, a) in zip(ex, cuts)
            )
            outs.append(out / total)
            lse = top + jnp.log(total)
            lse_ref[t, pair, j : j + 1, rows] = jnp.broadcast_to(lse, (block, 128)).T[
                0:1
            ]
        o_ref[t, rows, lanes] = jnp.where(head_mask(block, 0), *outs).astype(BF16)


ATTN, FFN_IN, FFN_OUT, ADAPTER, CROSS = range(5)
ORDER = (
    (0, ATTN),
    (1, ATTN),
    (0, FFN_IN),
    (0, FFN_OUT),
    (0, ADAPTER),
    (0, CROSS),
    (1, CROSS),
    (1, FFN_IN),
    (1, FFN_OUT),
    (1, ADAPTER),
)
(
    ENC_QKV,
    ENC_ATTN,
    ENC_OUT,
    DEC_QKV,
    DEC_ATTN,
    DEC_OUT,
    HIDDEN,
    GATED,
    MEMORY,
    CROSS_Q,
    CROSS_ATTN,
    CROSS_OUT,
    END,
) = range(13)
WORK = (
    (ENC_QKV, 4, (0, ATTN), 2.0),
    (ENC_ATTN, 8, None, 2.3),
    (ENC_OUT, 1, None, 4.0),
    (DEC_QKV, 4, (1, ATTN), 2.0),
    (DEC_ATTN, 8, None, 2.1),
    (DEC_OUT, 1, None, 4.0),
    (HIDDEN, 8, (0, FFN_OUT), 2.5),
    (GATED, 1, (0, ADAPTER), 4.0),
    (MEMORY, 4, (0, CROSS), 1.5),
    (CROSS_Q, 1, (1, CROSS), 4.0),
    (CROSS_ATTN, 8, None, 2.3),
    (CROSS_OUT, 1, None, 4.0),
    (END, 1, (1, ADAPTER), 0.0),
)


LAG = 2


def plan_steps(sizes):
    ready, clock = [], 20.0
    for e, g in ORDER:
        for _ in range(3):
            clock += sizes[g] / 3 * 11e-6
            ready.append(clock)
    ticks = len(ready) + 2 * LAG
    ready += [clock + 4 * n for n in range(1, 2 * LAG + 1)]
    starts, at, step, now, done = {}, {}, 0, 0.0, 0
    for name, count, need, cost in WORK:
        starts[name] = step
        for n in range(count):
            while done < ticks and (
                ready[done] <= now
                or (need and done <= 3 * ORDER.index(need) + 2 + 2 * LAG)
            ):
                at[done] = step
                now = max(now, ready[done])
                done += 1
            now += cost
            step += 1
    for n in range(done, ticks):
        at[n] = step - 1
    return starts, at, step


HEADS, LSE, WIDE, RSTD, LANES = range(5)
(
    EQ,
    EK,
    EKX,
    EV,
    EVX,
    EO,
    EL,
    EH,
    ER,
    ES,
    EA,
    EY,
    EYR,
    DQ,
    DK,
    DKX,
    DV,
    DVX,
    DO,
    DL,
    DH,
    DR,
    MK,
    MKX,
    MV,
    MVX,
    CQ,
    CO,
    CL,
    C2,
    C2R,
) = range(31)
KEPT = {
    EQ: HEADS,
    EK: HEADS,
    EKX: HEADS,
    EV: HEADS,
    EVX: HEADS,
    EO: HEADS,
    EL: LSE,
    EH: WIDE,
    ER: RSTD,
    ES: LANES,
    EA: LANES,
    EY: WIDE,
    EYR: RSTD,
    DQ: HEADS,
    DK: HEADS,
    DKX: HEADS,
    DV: HEADS,
    DVX: HEADS,
    DO: HEADS,
    DL: LSE,
    DH: WIDE,
    DR: RSTD,
    MK: HEADS,
    MKX: HEADS,
    MV: HEADS,
    MVX: HEADS,
    CQ: HEADS,
    CO: HEADS,
    CL: LSE,
    C2: WIDE,
    C2R: RSTD,
}


def forward_kernel(plan, rows, *refs):
    starts, tick_step, steps = plan
    refs = list(refs)

    def take(count):
        got = refs[:count]
        del refs[:count]
        return got

    shards = take(5)
    tokens = take(2)
    col_ref, row_ref, feat_ref = take(3)
    full = (take(5), take(5))
    (slope_out,) = take(1)
    kept_out = take(len(KEPT))
    kept = take(len(KEPT))
    xs = take(2)
    wb, wi, wo, wad, slope = take(5)
    store_a, store_f = take(2)
    (
        z_send,
        z_recv,
        h_send,
        n_send,
        n_recv,
        f_send,
        f_recv,
        s_send,
        s_recv,
        own_sem,
        t_send,
        t_recv,
        kv_send,
        kv_recv,
        load_sem,
        out_sem,
        slope_sem,
    ) = refs
    step = pl.program_id(0)
    s = lax.axis_index(SECTION)
    c = lax.axis_index(CTX)
    t = lax.axis_index(TP)
    chips = 16
    chip = c * 4 + t
    cx = c + 1 - 2 * lax.rem(c, 2)
    cy = lax.rem(c + 2, 4)
    cd = 3 - c
    sib = (1 - s, c, t)

    inner = (t == 1) | (t == 2)

    def xor(k):
        return {1: t + 1 - 2 * lax.rem(t, 2), 2: 2 - t // 2, 3: 3 - 3 * (t // 2)}[k]

    def token_copy(kind, i):
        p = lax.rem(chip + i, chips)
        src = tokens[kind].at[jnp.minimum(p, rows - 1)]
        dst = xs[kind].at[chip]
        if i == 0:
            return p, pltpu.make_async_copy(src, dst, t_send.at[kind, 0])
        return p, remote(
            src, dst, t_send.at[kind, i], t_recv.at[kind, i], device_of(s, p)
        )

    def send_tokens(kind):
        for i in range(chips):
            p, copy = token_copy(kind, i)
            pl.when(p < rows)(copy.start)

    def got(region, sem):
        remote(region, region, load_sem.at[0], sem, sib).wait_recv()

    def wait_tokens(kind):
        for i in range(chips):
            p, copy = token_copy(kind, i)
            pl.when(p < rows)(copy.wait if i == 0 else copy.wait_send)
            if i:

                @pl.when(chip < rows)
                def _():
                    got(
                        xs[kind].at[lax.rem(chip + chips - i, chips)],
                        t_recv.at[kind, i],
                    )

    items = [(n, k) for n in range(len(ORDER)) for k in (1, 2, 3)]
    window = 4

    def block(n, who, h, q, u=None):
        e, g = ORDER[n]
        size = shards[g].shape[0]
        start = h * (size // 2) + q * (size // 8)
        length = size // 8
        if u is not None:
            length = size // 16
            start = start + u * length
        return full[e][g].at[who, pl.ds(pl.multiple_of(start, 16), length)]

    def z_copy(n, k, h):
        g = ORDER[n][1]
        size = shards[g].shape[0]
        start = h * (size // 2) + c * (size // 8)
        return remote(
            shards[g].at[pl.ds(pl.multiple_of(start, 16), size // 8)],
            block(n, t, h, c),
            z_send.at[n, k - 1, h],
            z_recv.at[n, k - 1],
            (h, c, xor(1) if k == 1 else jnp.clip(3 - t, 1, 2)),
        )

    def z_forward(n, k):
        src = block(n, xor(k), s, c)
        to = 3 - t if k == 1 else 3 * t - 3
        return remote(
            src,
            src,
            h_send.at[n, k - 1],
            z_recv.at[n, (2, 1, 2)[k - 1]],
            (s, c, jnp.clip(to, 0, 3)),
        )

    def store(g):
        if g in (FFN_IN, FFN_OUT):
            return store_f
        return store_a.at[pl.ds(0, shards[g].shape[0])]

    def fetch(n):
        g = ORDER[n][1]
        return pltpu.make_async_copy(shards[g], store(g), own_sem.at[n, 3])

    def put(n):
        e, g = ORDER[n]
        return pltpu.make_async_copy(store(g), full[e][g].at[t], own_sem.at[n, 0])

    def far(n):
        e, g = ORDER[n]
        return remote(
            shards[g], full[e][g].at[t], own_sem.at[n, 1], own_sem.at[n, 2], sib
        )

    def before(n):
        e, g = ORDER[n]
        pool = (FFN_IN, FFN_OUT) if g in (FFN_IN, FFN_OUT) else (ATTN, ADAPTER, CROSS)
        olds = [m for m in range(n) if ORDER[m][0] == e and ORDER[m][1] in pool]
        return olds[-1] if olds else None

    def start_z(i):
        n, k = items[i]

        @pl.when(s == ORDER[n][0])
        def _():
            if k == 1:
                far(n).start()
            if k < 3:

                @pl.when(inner | (k == 1))
                def _():
                    for h in range(2):
                        z_copy(n, k, h).start()

    def near_copy(n, k, j):
        src = block(n, xor(k), s, c)
        return remote(
            src,
            src,
            n_send.at[n, k - 1, j],
            n_recv.at[n, k - 1, j],
            (s, (cx, cy)[j], t),
        )

    def sibling_copy(n, k, j):
        src = block(n, xor(k), s, (c, cx, cy, cd)[j])
        return remote(src, src, s_send.at[n, k - 1, j], s_recv.at[n, k - 1, j], sib)

    def forward_copy(n, k, j):
        src = block(n, xor(k), s, (cx, cy)[j], j)
        return remote(
            src,
            src,
            f_send.at[n, k - 1, j],
            f_recv.at[n, k - 1, j],
            (s, (cy, cx)[j], t),
        )

    def stage2(i):
        n, k = items[i]
        got(block(n, xor(k), s, c), z_recv.at[n, k - 1])
        pl.when(inner)(z_forward(n, k).start)
        near_copy(n, k, 0).start()
        near_copy(n, k, 1).start()
        sibling_copy(n, k, 0).start()
        if k == 2:
            return

        @pl.when(s == ORDER[n][0])
        def _():
            if k == 1:
                old = before(n)
                if old is not None and not put_read_first(old, i):
                    put(old).wait()
                fetch(n).start()
            else:
                fetch(n).wait()
                put(n).start()

    def stage3(i):
        n, k = items[i]
        for j, q in ((0, cx), (1, cy)):
            got(block(n, xor(k), s, q), n_recv.at[n, k - 1, j])
            forward_copy(n, k, j).start()
            sibling_copy(n, k, j + 1).start()

    def stage4(i):
        n, k = items[i]
        for u in range(2):
            got(block(n, xor(k), s, cd, u), f_recv.at[n, k - 1, u])
        sibling_copy(n, k, 3).start()

    count = len(items)

    def tick(i):
        if i < count:
            stage2(i)
            if i + window < count:
                start_z(i + window)
        if 0 <= i - LAG < count:
            stage3(i - LAG)
        if 0 <= i - 2 * LAG < count:
            stage4(i - 2 * LAG)
        if i == 3:
            send_tokens(1)

    def arrive_step(n):
        for name, _, need, _ in WORK[:-1]:
            if need == ORDER[n]:
                return starts[name]
        return starts[HIDDEN] if ORDER[n] == (0, FFN_IN) else steps - 1

    def put_read_first(n, i):
        return arrive_step(n) < tick_step[i]

    def put_left(n):
        after = [m for m in range(len(ORDER)) if before(m) == n]
        return not after or put_read_first(n, 3 * after[0])

    def arrive(n):
        e, g = ORDER[n]
        for k in (1, 2, 3):
            for j, q in enumerate((c, cx, cy, cd)):
                got(block(n, xor(k), 1 - s, q), s_recv.at[n, k - 1, j])

        @pl.when(s == e)
        def _():
            if put_left(n):
                put(n).wait()

        @pl.when(s != e)
        def _():
            got(full[e][g].at[t], own_sem.at[n, 2])

    @pl.when(step == 0)
    def _():
        greet_all()
        send_tokens(0)
        for i in range(window):
            start_z(i)

    for i in range(count + 2 * LAG):
        pl.when(step == tick_step[i])(functools.partial(tick, i))

    def on(name):
        first = starts[name]
        last = first + [w[1] for w in WORK if w[0] == name][0]
        need = [w[2] for w in WORK if w[0] == name][0]
        if need and name != END:
            pl.when(step == first)(functools.partial(arrive, ORDER.index(need)))
        return step - first, pl.when((step >= first) & (step < last))

    def load(src, dst, slot=0):
        return pltpu.make_async_copy(src, dst, load_sem.at[slot])

    def keep(*names):
        for n in names:
            pltpu.make_async_copy(kept[n], kept_out[n], out_sem.at[n]).start()

    attn_rows = full[0][ATTN].shape[1] // 4

    def kv_copies(which, g, names):
        k, kx, v, vx = names
        return [
            remote(
                kept[a].at[g], kept[b].at[g], kv_send.at[which, g, j], kv_recv.at[which, g, j], sib
            )
            for j, (a, b) in enumerate(((k, kx), (v, vx)))
        ]

    def projections(name, which, e, g_id, x, names):
        i, when = on(name)
        tiles = len(names)
        height = tiles * attn_rows

        def source(j):
            return full[e][g_id].at[j, pl.ds(0, height)]

        @when
        def _():
            slot = lax.rem(i, 2)

            @pl.when(i == 0)
            def _():
                load(source(0), wb.at[0, pl.ds(0, height)]).start()

            load(source(0), wb.at[slot, pl.ds(0, height)]).wait()

            @pl.when(i < 3)
            def _():
                load(source(jnp.minimum(i + 1, 3)), wb.at[1 - slot, pl.ds(0, height)]).start()

            rows_in = x()
            for n, name_out in enumerate(names):
                w = wb[slot, n * attn_rows : (n + 1) * attn_rows, :]
                kept[name_out][i] = dot_nn(rows_in, w).astype(BF16)
            for copy in kv_copies(which, i, keys_of[which]):
                copy.start()

    keys_of = (
        (EK, EKX, EV, EVX),
        (DK, DKX, DV, DVX),
        (MK, MKX, MV, MVX),
    )

    def attend(name, which, q, o, lse, feats, causal):
        i, when = on(name)
        k, kx, v, vx = keys_of[which]

        @when
        def _():
            g, pair = i // 2, lax.rem(i, 2)

            @pl.when(pair == 0)
            def _():
                for copy in kv_copies(which, g, keys_of[which]):
                    copy.wait_send()
                    copy.wait_recv()

            attend_pair(
                g,
                pair,
                kept[q],
                (kept[k], kept[kx]),
                (kept[v], kept[vx]),
                kept[o],
                kept[lse],
                [feat_ref.at[f] for f in feats],
                (col_ref[...], (row_ref[0:1, :], row_ref[1:2, :])),
                causal,
            )

            @pl.when(i == 7)
            def _():
                keep(q, k, kx, v, vx, o, lse)

    def tiles4(e, g_id, first_row):
        copies = [
            load(
                full[e][g_id].at[j, pl.ds(first_row, attn_rows)],
                wb.at[0, pl.ds(j * attn_rows, attn_rows)],
                j,
            )
            for j in range(4)
        ]
        for copy in copies:
            copy.start()
        for copy in copies:
            copy.wait()

    def out_norm(name, e, g_id, first_row, residual, source, wide, rstd_name):
        _, when = on(name)

        @when
        def _():
            tiles4(e, g_id, first_row)
            total = residual()
            for j in range(4):
                total = total + dot_nt(
                    kept[source][j], wb[0, j * attn_rows : (j + 1) * attn_rows, :]
                )
            normed, rstd = norm(total)
            kept[wide][...] = normed
            kept[rstd_name][...] = jnp.broadcast_to(rstd, kept[rstd_name].shape)
            keep(wide, rstd_name)

    def flat_x(n):
        shape = xs[n].shape
        return xs[n][...].reshape(shape[0] * shape[1], shape[2])

    blocks = (
        (ENC_QKV, ENC_ATTN, ENC_OUT, EQ, EK, EV, EO, EL, EH, ER, (0, 1, 2)),
        (DEC_QKV, DEC_ATTN, DEC_OUT, DQ, DK, DV, DO, DL, DH, DR, (3, 4, 5)),
    )
    for e, (qkv, attn, out, q, k, v, o, lse, h, r, feats) in enumerate(blocks):
        pl.when(step == starts[qkv])(functools.partial(wait_tokens, e))
        projections(qkv, e, e, ATTN, functools.partial(flat_x, e), (q, k, v))
        attend(attn, e, q, o, lse, feats, e == 1)
        residual = lambda e=e: flat_x(e).astype(F32)
        out_norm(out, e, ATTN, 3 * attn_rows, residual, o, h, r)

    i, when = on(HIDDEN)
    hidden = wi.shape[2]

    @pl.when(step == starts[HIDDEN])
    def _():
        arrive(ORDER.index((0, FFN_IN)))

    def ffn_loads(j, slot):
        g, u = j // 2, lax.rem(j, 2)
        span = pl.ds(pl.multiple_of(u * hidden, 128), hidden)
        return (
            load(full[0][FFN_IN].at[g, :, span], wi.at[slot], 2 * slot),
            load(full[0][FFN_OUT].at[g, span], wo.at[slot], 2 * slot + 1),
        )

    def slope_copy(j, slot):
        g, u = j // 2, lax.rem(j, 2)
        span = pl.ds(pl.multiple_of(u * hidden, 128), hidden)
        return pltpu.make_async_copy(
            slope.at[slot], slope_out.at[g, :, span], slope_sem.at[slot]
        )

    @when
    def _():
        slot = lax.rem(i, 2)

        @pl.when(i == 0)
        def _():
            for copy in ffn_loads(0, 0):
                copy.start()
            kept[EY][...] = jnp.zeros_like(kept[EY])

        for copy in ffn_loads(i, slot):
            copy.wait()

        @pl.when(i < 7)
        def _():
            for copy in ffn_loads(i + 1, 1 - slot):
                copy.start()

        @pl.when(i >= 2)
        def _():
            slope_copy(i - 2, slot).wait()

        inner = dot_nn(kept[EH][...].astype(BF16), wi[slot])
        phi = 0.5 * (1.0 + lax.erf(inner * 0.7071067811865476))
        slope[slot] = (
            phi + inner * jnp.exp(inner * inner * -0.5) * 0.3989422804014327
        ).astype(BF16)
        slope_copy(i, slot).start()
        kept[EY][...] += dot_nn((inner * phi).astype(BF16), wo[slot])

    i, when = on(GATED)

    @when
    def _():
        for j in range(2):
            slope_copy(6 + j, j).wait()
        copy = load(full[0][ADAPTER], wad)
        copy.start()
        copy.wait()
        h = kept[EH][...]
        rows_in = h.astype(BF16)
        lanes = wad.shape[2] // 2
        extra = wad[0, attn_rows : attn_rows + 16, :].astype(F32)
        last = jnp.concatenate([extra[1 + r : 2 + r] for r in range(4)], axis=1)
        total = 4.0 * last
        for j in range(4):
            bias = wad[j, attn_rows : attn_rows + 16, :lanes].astype(F32)[0:1]
            pre = dot_nn(rows_in, wad[j, :attn_rows, :lanes]) + bias
            sig = 1.0 / (1.0 + jnp.exp(-pre))
            gated = (pre * sig).astype(BF16)
            kept[ES][j] = gated
            kept[EA][j] = (sig * (1.0 + pre * (1.0 - sig))).astype(BF16)
            total = total + 4.0 * dot_nt(gated, wad[j, :attn_rows, lanes:])
        normed, rstd = norm(h + (kept[EY][...] + total))
        kept[EY][...] = normed
        kept[EYR][...] = jnp.broadcast_to(rstd, kept[EYR].shape)
        keep(ES, EA, EY, EYR)

    projections(MEMORY, 2, 0, CROSS, lambda: kept[EY][...].astype(BF16), (MK, MV))
    _, when = on(CROSS_Q)

    @when
    def _():
        tiles4(1, CROSS, 0)
        rows_in = kept[DH][...].astype(BF16)
        for j in range(4):
            kept[CQ][j] = dot_nn(
                rows_in, wb[0, j * attn_rows : (j + 1) * attn_rows, :]
            ).astype(BF16)

    attend(CROSS_ATTN, 2, CQ, CO, CL, (3, 1, 2), False)
    out_norm(CROSS_OUT, 1, CROSS, attn_rows, lambda: kept[DH][...], CO, C2, C2R)

    @pl.when(step == steps - 1)
    def _():
        for g in (FFN_IN, FFN_OUT, ADAPTER):
            arrive(ORDER.index((1, g)))
        for n, k in items:
            pl.when(inner)(z_forward(n, k).wait_send)
            for j in range(2):
                near_copy(n, k, j).wait_send()
                forward_copy(n, k, j).wait_send()
            for j in range(4):
                sibling_copy(n, k, j).wait_send()
        for n in range(len(ORDER)):

            @pl.when(s == ORDER[n][0])
            def _():
                far(n).wait_send()
                for h in range(2):
                    z_copy(n, 1, h).wait_send()
                    pl.when(inner)(z_copy(n, 2, h).wait_send)

        for n in KEPT:
            pltpu.make_async_copy(kept[n], kept_out[n], out_sem.at[n]).wait()


def forward_call(shards, tokens, col, row, feats):
    part, width = tokens[0].shape[1:]
    length = 16 * part
    groups = len(ORDER)
    dma = pltpu.SemaphoreType.DMA
    anywhere = pl.BlockSpec(memory_space=pl.ANY)
    cols = shards[ATTN].shape[1]
    shapes = (
        ((4, length, cols), BF16),
        ((4, cols // HEAD // 2, 2, length), F32),
        ((length, width), F32),
        ((length, 128), F32),
        ((4, length, shards[ADAPTER].shape[1] // 2), BF16),
    )
    kept = [shapes[kind] for kind in KEPT.values()]
    hidden = shards[FFN_IN].shape[1]
    sizes = [
        (groups, 2, 2),
        (groups, 3),
        (groups, 3),
        (groups, 3, 2),
        (groups, 3, 2),
        (groups, 3, 2),
        (groups, 3, 2),
        (groups, 3, 4),
        (groups, 3, 4),
        (groups, 4),
        (2, 16),
        (2, 16),
        (3, 4, 2),
        (3, 4, 2),
        (4,),
        (len(KEPT),),
        (2,),
    ]
    plan = plan_steps([v.size * 2 for v in shards])
    result = pl.pallas_call(
        functools.partial(forward_kernel, plan, tokens[0].shape[0]),
        grid=(plan[2],),
        in_specs=[anywhere] * 7
        + [
            pl.BlockSpec(col.shape, lambda i: (0, 0)),
            pl.BlockSpec(row.shape, lambda i: (0, 0)),
            pl.BlockSpec(feats.shape, lambda i: (0, 0, 0)),
        ],
        out_specs=[anywhere] * (11 + len(KEPT)),
        out_shape=[jax.ShapeDtypeStruct((4,) + v.shape, v.dtype) for v in shards] * 2
        + [jax.ShapeDtypeStruct((4, length, hidden), BF16)]
        + [jax.ShapeDtypeStruct(*v) for v in kept],
        scratch_shapes=[pltpu.VMEM(*v) for v in kept]
        + [pltpu.VMEM((16, part, width), BF16)] * 2
        + [
            pltpu.VMEM((2,) + shards[ATTN].shape, BF16),
            pltpu.VMEM((2, width, hidden // 2), BF16),
            pltpu.VMEM((2, hidden // 2, width), BF16),
            pltpu.VMEM((4,) + shards[ADAPTER].shape, BF16),
            pltpu.VMEM((2, length, hidden // 2), BF16),
            pltpu.VMEM(shards[ATTN].shape, BF16),
            pltpu.VMEM(shards[FFN_IN].shape, BF16),
        ]
        + [dma(size) for size in sizes],
        compiler_params=pltpu.CompilerParams(
            collective_id=0, has_side_effects=True, vmem_limit_bytes=60 * 2**20
        ),
        name="forward",
    )(*shards, *tokens, col, row, feats)
    return result[:5], result[5:10], result[10], result[11:]


def ids_kernel(ids, out, send, recv):
    s = lax.axis_index(SECTION)
    c = lax.axis_index(CTX)
    t = lax.axis_index(TP)
    barrier = pltpu.get_barrier_semaphore()
    for j in (1, 2, 3):
        pl.semaphore_signal(
            barrier,
            1,
            device_id=(s, lax.rem(c + j, 4), t),
            device_id_type=pl.DeviceIdType.MESH,
        )
    pl.semaphore_wait(barrier, 3)
    out[c] = ids[...]
    ways = [
        remote(ids, out.at[c], send.at[j - 1], recv.at[j - 1], (s, lax.rem(c + j, 4), t))
        for j in (1, 2, 3)
    ]
    for way in ways:
        way.start()
    for j, way in enumerate(ways):
        way.wait_send()
        region = out.at[lax.rem(c + 3 - j, 4)]
        remote(region, region, send.at[j], recv.at[j], (s, c, t)).wait_recv()


def ids_call(ids):
    spec = pl.BlockSpec(memory_space=pltpu.VMEM)
    return pl.pallas_call(
        ids_kernel,
        in_specs=[spec],
        out_specs=spec,
        out_shape=jax.ShapeDtypeStruct((4,) + ids.shape, ids.dtype),
        scratch_shapes=[pltpu.SemaphoreType.DMA((3,)), pltpu.SemaphoreType.DMA((3,))],
        compiler_params=pltpu.CompilerParams(collective_id=1, has_side_effects=True),
        name="ids",
    )(ids)


SPLIT = 1


def tail_kernel(rider, *refs):
    refs = list(refs)

    def take(count):
        got = refs[:count]
        del refs[:count]
        return got

    h_ref, w_in_ref, w_out_ref, adapter_ref = take(4)
    ride_ins = take(len(rider.inputs))
    slope_ref, s_ref, a_ref, y_ref, yr_ref, out_ref = take(6)
    ride = (ride_ins, take(len(rider.inputs)), take(len(rider.scratch)))
    rows_in, acc = refs
    step = pl.program_id(0)
    width = acc.shape[1]
    lanes = adapter_ref.shape[2] // 2

    @pl.when(step == 0)
    def _():
        rider.start(*ride)
        extra = adapter_ref[0, width : width + 16, :].astype(F32)
        cuts = width // adapter_ref.shape[2]
        last = jnp.concatenate([extra[1 + r : 2 + r] for r in range(cuts)], axis=1)
        acc[...] = h_ref[...] + 4.0 * last
        rows_in[...] = h_ref[...].astype(BF16)

    @pl.when(step < 4)
    def _():
        bias = adapter_ref[0, width : width + 16, :lanes].astype(F32)[0:1]
        pre = dot_nn(rows_in[...], adapter_ref[0, :width, :lanes]) + bias
        sig = 1.0 / (1.0 + jnp.exp(-pre))
        gated = (pre * sig).astype(BF16)
        s_ref[0] = gated
        a_ref[0] = (sig * (1.0 + pre * (1.0 - sig))).astype(BF16)
        acc[...] += 4.0 * dot_nt(gated, adapter_ref[0, :width, lanes:])

    @pl.when((step >= 4) & (step < 4 + 4 * SPLIT))
    def _():
        inner = dot_nn(rows_in[...], w_in_ref[0])
        phi = 0.5 * (1.0 + lax.erf(inner * 0.7071067811865476))
        slope_ref[0] = (
            phi + inner * jnp.exp(inner * inner * -0.5) * 0.3989422804014327
        ).astype(BF16)
        acc[...] += dot_nn((inner * phi).astype(BF16), w_out_ref[0])

    @pl.when(step == 4 + 4 * SPLIT)
    def _():
        normed, rstd = norm(acc[...])
        y_ref[...] = normed
        yr_ref[...] = jnp.broadcast_to(rstd, yr_ref.shape)
        out_ref[...] = normed.astype(BF16)
        rider.finish(*ride)


def tail_call(h, tail_w, rider):
    w_in, w_out, adapter = tail_w
    length, width = h.shape
    groups, _, hidden = w_in.shape
    lanes = adapter.shape[2] // 2
    anywhere = pl.BlockSpec(memory_space=pl.ANY)

    def tile(j):
        j = jnp.clip(j - groups, 0, groups * SPLIT - 1)
        return j // SPLIT, lax.rem(j, SPLIT)

    def group(j):
        return jnp.minimum(j, groups - 1)

    wide = pl.BlockSpec((length, width), lambda j: (0, 0))
    gated = pl.BlockSpec((1, length, lanes), lambda j: (group(j), 0, 0))
    cut = lambda rows: pl.BlockSpec(
        (1, rows, hidden // SPLIT), lambda j: (tile(j)[0], 0, tile(j)[1])
    )
    result = pl.pallas_call(
        functools.partial(tail_kernel, rider),
        grid=(groups * (1 + SPLIT) + 1,),
        in_specs=[
            wide,
            cut(width),
            pl.BlockSpec((1, hidden // SPLIT, width), lambda j: (tile(j)[0], tile(j)[1], 0)),
            pl.BlockSpec((1,) + adapter.shape[1:], lambda j: (group(j), 0, 0)),
        ]
        + [anywhere] * len(rider.inputs),
        out_specs=[
            cut(length),
            gated,
            gated,
            wide,
            pl.BlockSpec((length, 128), lambda j: (0, 0)),
            wide,
        ]
        + [anywhere] * len(rider.inputs),
        out_shape=[
            jax.ShapeDtypeStruct((groups, length, hidden), BF16),
            jax.ShapeDtypeStruct((groups, length, lanes), BF16),
            jax.ShapeDtypeStruct((groups, length, lanes), BF16),
            jax.ShapeDtypeStruct((length, width), F32),
            jax.ShapeDtypeStruct((length, 128), F32),
            jax.ShapeDtypeStruct((length, width), BF16),
        ]
        + rider.shapes,
        scratch_shapes=rider.scratch
        + [pltpu.VMEM((length, width), BF16), pltpu.VMEM((length, width), F32)],
        compiler_params=pltpu.CompilerParams(
            collective_id=rider.call_id, has_side_effects=True, vmem_limit_bytes=60 * 2**20
        ),
        name="tail",
    )(h, w_in, w_out, adapter, *rider.inputs)
    return result[:6], result[6:]


def norm_back_rows(normed, rstd, grad):
    return rstd * (
        grad
        - jnp.mean(grad, axis=-1, keepdims=True)
        - normed * jnp.mean(grad * normed, axis=-1, keepdims=True)
    )


def head_grads(da, w_ref, do_ref):
    for g in range(w_ref.shape[0]):
        do_ref[g] = dot_nn(da, w_ref[g]).astype(BF16)


def sibling_of():
    return (1 - lax.axis_index(SECTION), lax.axis_index(CTX), lax.axis_index(TP))


def tail_back_kernel(rider, *refs):
    refs = list(refs)

    def take(count):
        got = refs[:count]
        del refs[:count]
        return got

    grad_ref, y_ref, yr_ref, h_ref, hr_ref, slope_ref = take(6)
    w_out_ref, w_in_ref, adapter_ref, s_ref, a_ref, w_do_ref = take(6)
    ride_ins = take(len(rider.inputs))
    dpre_ref, do_ref, pieces_ref, tails_ref = take(4)
    ride = (ride_ins, take(len(rider.inputs)), take(len(rider.scratch)))
    db, acc, mine, away, got, send, recv = refs
    step = pl.program_id(0)
    groups = away.shape[0]
    width = acc.shape[1]
    lanes = adapter_ref.shape[2] // 2
    first = lax.axis_index(SECTION) == 0

    def to_sibling(g):
        return remote(
            away.at[g], got.at[g], send.at[g], recv.at[g], sibling_of()
        )

    @pl.when(step == 0)
    def _():
        rider.start(*ride)
        dpre = norm_back_rows(y_ref[...], yr_ref[:, 0:1], grad_ref[...].astype(F32))
        acc[...] = dpre
        db[...] = dpre.astype(BF16)

    @pl.when(step < groups)
    def _():
        branch = db[...]
        ds = 4.0 * dot_nn(branch, adapter_ref[0, :width, lanes:])
        du = (ds * a_ref[0].astype(F32)).astype(BF16)
        acc[...] += dot_nt(du, adapter_ref[0, :width, :lanes])
        d_in = dot_tn(du, h_ref[...].astype(BF16))
        d_out = 4.0 * dot_tn(s_ref[0], branch)
        last = 4.0 * jnp.sum(branch.astype(F32), axis=0, keepdims=True)
        bias = jnp.sum(du.astype(F32), axis=0, keepdims=True)
        cut = width // 4
        bias = jnp.concatenate([bias, jnp.zeros((1, cut - lanes), F32)], axis=1)
        row = lax.broadcasted_iota(jnp.int32, (16, cut), 0)
        part = lanes // 4
        for c in range(4):
            one = d_in[c * part : (c + 1) * part]
            two = d_out[c * part : (c + 1) * part]
            mine[step, c] = jnp.where(first, one, two)
            away[step, c] = jnp.where(first, two, one).astype(BF16)
            tails_ref[c, step] = jnp.where(
                row == 0,
                last[:, c * cut : (c + 1) * cut],
                jnp.where(row == 1, bias, 0.0),
            ).astype(BF16)
        to_sibling(step).start()

    @pl.when((step >= groups) & (step < groups * (1 + SPLIT)))
    def _():
        dg = dot_nt(db[...], w_out_ref[0])
        df = (dg * slope_ref[0].astype(F32)).astype(BF16)
        acc[...] += dot_nt(df, w_in_ref[0])

    @pl.when(step == groups * (1 + SPLIT))
    def _():
        dpre = norm_back_rows(h_ref[...], hr_ref[:, 0:1], acc[...])
        dpre_ref[...] = dpre
        head_grads(dpre.astype(BF16), w_do_ref, do_ref)
        for g in range(groups):
            copy = to_sibling(g)
            copy.wait_send()
            copy.wait_recv()
            for c in range(4):
                pieces_ref[c, g] = (mine[g, c] + got[g, c].astype(F32)).astype(BF16)
        rider.finish(*ride)


def tail_back(grad, y, yr, h, hr, slope, tail_w, s_act, a_slope, w_do, do_block, rider):
    w_in, w_out, adapter = tail_w
    length, width = y.shape
    groups, _, hidden = slope.shape
    lanes = s_act.shape[2]
    cols = w_do.shape[2]
    part = lanes // 4
    anywhere = pl.BlockSpec(memory_space=pl.ANY)

    def whole(v):
        return pl.BlockSpec(v.shape, lambda j: (0, 0))

    def tile(j):
        j = jnp.clip(j - groups, 0, groups * SPLIT - 1)
        return j // SPLIT, lax.rem(j, SPLIT)

    def group(j):
        return jnp.minimum(j, groups - 1)

    result = pl.pallas_call(
        functools.partial(tail_back_kernel, rider),
        grid=(groups * (1 + SPLIT) + 1,),
        in_specs=[whole(v) for v in (grad, y, yr, h, hr)]
        + [
            pl.BlockSpec((1, length, hidden // SPLIT), lambda j: (tile(j)[0], 0, tile(j)[1])),
            pl.BlockSpec((1, hidden // SPLIT, width), lambda j: (tile(j)[0], tile(j)[1], 0)),
            pl.BlockSpec((1, width, hidden // SPLIT), lambda j: (tile(j)[0], 0, tile(j)[1])),
            pl.BlockSpec((1,) + adapter.shape[1:], lambda j: (group(j), 0, 0)),
            pl.BlockSpec((1, length, lanes), lambda j: (group(j), 0, 0)),
            pl.BlockSpec((1, length, lanes), lambda j: (group(j), 0, 0)),
            pl.BlockSpec((groups, width, cols), lambda j: (0, do_block, 0)),
        ]
        + [anywhere] * len(rider.inputs),
        out_specs=[
            pl.BlockSpec((length, width), lambda j: (0, 0)),
            pl.BlockSpec((groups, length, cols), lambda j: (0, 0, 0)),
            pl.BlockSpec((4, groups, part, width), lambda j: (0, 0, 0, 0)),
            pl.BlockSpec((4, groups, 16, width // 4), lambda j: (0, 0, 0, 0)),
        ]
        + [anywhere] * len(rider.inputs),
        out_shape=[
            jax.ShapeDtypeStruct((length, width), F32),
            jax.ShapeDtypeStruct((groups, length, cols), BF16),
            jax.ShapeDtypeStruct((4, groups, part, width), BF16),
            jax.ShapeDtypeStruct((4, groups, 16, width // 4), BF16),
        ]
        + rider.shapes,
        scratch_shapes=rider.scratch
        + [
            pltpu.VMEM((length, width), BF16),
            pltpu.VMEM((length, width), F32),
            pltpu.VMEM((groups, 4, part, width), F32),
            pltpu.VMEM((groups, 4, part, width), BF16),
            pltpu.VMEM((groups, 4, part, width), BF16),
            pltpu.SemaphoreType.DMA((groups,)),
            pltpu.SemaphoreType.DMA((groups,)),
        ],
        compiler_params=pltpu.CompilerParams(
            collective_id=rider.call_id, has_side_effects=True, vmem_limit_bytes=60 * 2**20
        ),
        name="tail_back",
    )(grad, y, yr, h, hr, slope, w_out, w_in, adapter, s_act, a_slope, w_do, *rider.inputs)
    return result[:2], result[2:4], result[4:]


def attn_back_kernel(causal, cross, rider, *refs):
    refs = list(refs)

    def take(count):
        got = refs[:count]
        del refs[:count]
        return got

    q_ref, k_ref, kx_ref, v_ref, vx_ref, o_ref, do_ref, lse_ref = take(8)
    if cross:
        wq_ref, wkv_ref, rest_ref, h_ref, hr_ref, w_do_ref = take(6)
    else:
        w_ref, rest_ref = take(2)
    feats, (qi_ref, ki_ref) = take(3), take(2)
    ride_ins = take(len(rider.inputs))
    if cross:
        dpre_ref, do_next_ref, memory_ref = take(3)
    else:
        (dx_ref,) = take(1)
    ride_outs = take(len(rider.inputs))
    ride_sems = take(len(rider.scratch))
    ride = (ride_ins, ride_outs, ride_sems)
    dq_s, own_k, own_v, away_k, away_v, got_k, got_v, acc, send, recv = take(10)
    if cross:
        (acc2,) = take(1)
    step = pl.program_id(0)
    groups = away_k.shape[0]
    width = acc.shape[1]

    def to_sibling(g):
        return [
            remote(a.at[g], b.at[g], send.at[g, j], recv.at[g, j], sibling_of())
            for j, (a, b) in enumerate(((away_k, got_k), (away_v, got_v)))
        ]

    @pl.when(step == 0)
    def _():
        rider.start(*ride)
        acc[...] = rest_ref[...]
        if cross:
            acc2[...] = jnp.zeros_like(acc2)

    @pl.when(step > 0)
    def _():
        g = step - 1
        slot = lax.rem(g, 2)
        for copy in to_sibling(g):
            copy.wait_send()
            copy.wait_recv()
        dk = (own_k[slot] + got_k[g].astype(F32)).astype(BF16)
        dv = (own_v[slot] + got_v[g].astype(F32)).astype(BF16)
        dq = dq_s[slot]
        if cross:
            acc[...] += dot_nt(dq, wq_ref[0])
            acc2[...] += dot_nt(dk, wkv_ref[0, :width]) + dot_nt(dv, wkv_ref[0, width:])
        else:
            acc[...] += (
                dot_nt(dq, w_ref[0, :width])
                + dot_nt(dk, w_ref[0, width : 2 * width])
                + dot_nt(dv, w_ref[0, 2 * width :])
            )

    @pl.when(step < groups)
    def _():
        slot = lax.rem(step, 2)
        attend_back_group(
            (q_ref, (k_ref, kx_ref), (v_ref, vx_ref), o_ref, do_ref, lse_ref),
            (dq_s, slot),
            ((own_k, slot), (away_k, step)),
            ((own_v, slot), (away_v, step)),
            feats,
            qi_ref,
            ki_ref,
            causal,
        )
        for copy in to_sibling(step):
            copy.start()

    @pl.when(step == groups)
    def _():
        if cross:
            dpre = norm_back_rows(h_ref[...], hr_ref[:, 0:1], acc[...])
            dpre_ref[...] = dpre
            head_grads(dpre.astype(BF16), w_do_ref, do_next_ref)
            memory_ref[...] = acc2[...]
        else:
            dx_ref[...] = acc[...].astype(dx_ref.dtype)
        rider.finish(*ride)


def attn_back(heads, ids, causal, rider, rest, weights, cross=None):
    groups, length, cols = heads[0].shape
    width = rest.shape[1]
    anywhere = pl.BlockSpec(memory_space=pl.ANY)

    def now(shape):
        return pl.BlockSpec((1,) + shape[1:], lambda t: (jnp.minimum(t, groups - 1), 0, 0))

    def past(rows):
        return pl.BlockSpec((1, rows, cols), lambda t: (jnp.maximum(t - 1, 0), 0, 0))

    def whole(v):
        return pl.BlockSpec(v.shape, lambda t: (0,) * len(v.shape))

    wide = jax.ShapeDtypeStruct((length, width), F32)
    if cross:
        h, hr, w_do = cross
        wq, wkv = weights
        extra = [wq, wkv, rest, h, hr, w_do]
        specs = [
            past(width),
            past(2 * width),
            whole(rest),
            whole(h),
            whole(hr),
            pl.BlockSpec((groups, width, cols), lambda t: (0, 3, 0)),
        ]
        outs = [wide, jax.ShapeDtypeStruct(heads[0].shape, BF16), wide]
    else:
        extra = [weights, rest]
        specs = [past(3 * width), whole(rest)]
        outs = [jax.ShapeDtypeStruct((length, width), BF16)]
    moving = pltpu.VMEM((groups, length, cols), BF16)
    result = pl.pallas_call(
        functools.partial(attn_back_kernel, causal, bool(cross), rider),
        grid=(groups + 1,),
        in_specs=[now(v.shape) for v in heads]
        + specs
        + [whole(v) for v in ids]
        + [anywhere] * len(rider.inputs),
        out_specs=[whole(v) for v in outs] + [anywhere] * len(rider.inputs),
        out_shape=outs + rider.shapes,
        scratch_shapes=rider.scratch
        + [
            pltpu.VMEM((2, length, cols), BF16),
            pltpu.VMEM((2, length, cols), F32),
            pltpu.VMEM((2, length, cols), F32),
            moving,
            moving,
            moving,
            moving,
            pltpu.VMEM((length, width), F32),
            pltpu.SemaphoreType.DMA((groups, 2)),
            pltpu.SemaphoreType.DMA((groups, 2)),
        ]
        + ([pltpu.VMEM((length, width), F32)] if cross else []),
        compiler_params=pltpu.CompilerParams(
            collective_id=rider.call_id,
            has_side_effects=True,
            vmem_limit_bytes=60 * 2**20,
        ),
        name="attn_back",
    )(*heads, *extra, *ids, *rider.inputs)
    return result[: len(outs)], result[len(outs) :]


def gather_plain(entry, shards):
    full = [lax.all_gather(lax.all_gather(v, TP), SECTION) for v in shards]
    return [v[entry] for v in full]


def spread(blocks):
    chips = lax.axis_size(CTX) * lax.axis_size(TP)
    kinds, rows, part, width = blocks.shape
    blocks = jnp.pad(blocks, ((0, 0), (0, chips - rows), (0, 0), (0, 0)))
    moved = lax.all_to_all(
        jnp.moveaxis(blocks, 1, 0), (CTX, TP), 0, 0, tiled=True
    )
    return jnp.moveaxis(moved, 0, 1).reshape(kinds, chips * part, width)


def collect(tokens, rows):
    chips = lax.axis_size(CTX) * lax.axis_size(TP)
    kinds, length, width = tokens.shape
    part = length // chips
    blocks = jnp.moveaxis(tokens.reshape(kinds, chips, part, width), 1, 0)
    moved = lax.all_to_all(blocks, (CTX, TP), 0, 0, tiled=True)
    return jnp.moveaxis(moved, 0, 1)[:, :rows]


def per_device(
    layer_inputs,
    out_grad,
    src_seg,
    tgt_seg,
    qkv_weights,
    out_weights,
    cross_weights,
    ffn_in,
    ffn_out,
    adapter_in,
    adapter_in_bias,
    adapter_out,
    adapter_out_bias,
):
    core = lax.axis_index(SECTION)
    is_first = core == 0
    tp = lax.axis_size(TP)
    chips = lax.axis_size(CTX) * tp
    chip = lax.axis_index(CTX) * tp + lax.axis_index(TP)
    _, micro, per_micro, part, width = layer_inputs.shape
    row_count = micro * per_micro
    half = part // 2
    length = half * chips

    def pick(first, second):
        return jnp.where(is_first, first, second)

    x = layer_inputs.reshape(row_count, part, width)
    low, high = x[:, :half], x[:, half:]
    other = swap(pick(high, low))
    grads = out_grad.reshape(row_count, part, width)
    stacked = jnp.stack(
        [pick(low, other), pick(other, high), pick(grads[:, :half], grads[:, half:])]
    )
    near = lax.axis_size(CTX) == 4 and tp == 4
    lanes = adapter_in_bias.shape[1]
    cols = out_weights.shape[2]
    pad = lambda v, n: jnp.pad(v, [(0, n - v.shape[0])] + [(0, 0)] * (v.ndim - 1))
    biases = jnp.concatenate(
        [pad(adapter_in_bias[0], cols)[None], adapter_out_bias[0].reshape(-1, cols)]
    )
    shards = [
        jnp.concatenate([qkv_weights[0], out_weights], axis=0).reshape(-1, cols),
        ffn_in[0],
        ffn_out[0],
        jnp.concatenate(
            [
                jnp.concatenate([adapter_in[0], adapter_out[0].T], axis=1),
                pad(biases, 256),
            ],
            axis=0,
        ),
        cross_weights[0].reshape(-1, cols),
    ]
    if near:
        ids = ids_call(jnp.stack([src_seg, tgt_seg]).reshape(2 * row_count, -1))
        flat_ids = ids.swapaxes(0, 1).reshape(2, row_count, -1)
    else:
        flat_ids = [
            lax.all_gather(v.reshape(row_count, -1), CTX, axis=1, tiled=True)
            for v in (src_seg, tgt_seg)
        ]

    def unpack(full):
        attn, w_in, w_out, adapter, cross = full
        attn = attn.reshape(tp, 4, -1, cols)
        cross = cross.reshape(tp, 2, -1, cols)
        b_out = adapter[0, width + 1 : width + 1 + width // cols].reshape(width)
        tail = (
            w_in,
            w_out,
            adapter[:, :width, :lanes],
            adapter[:, width, :lanes],
            adapter[:, :width, lanes:],
            b_out,
        )
        return attn, cross, tail

    def ids_of(flat):
        row = lax.dynamic_index_in_dim(
            flat, jnp.minimum(chip, row_count - 1), 0, keepdims=False
        )
        return row.reshape(chips, 2, half)

    index = jnp.arange(length, dtype=jnp.int32)
    place = (index // half) * part + index % half

    def cut(seg, which):
        own = lax.dynamic_index_in_dim(seg, which, 1, keepdims=False).reshape(length)
        return own, place + which * half

    src_ids, tgt_ids = ids_of(flat_ids[0]), ids_of(flat_ids[1])

    def id_arrays(seg_q, seg_k):
        qi = jnp.stack(cut(seg_q, core))
        ki = jnp.stack(cut(seg_k, core) + cut(seg_k, 1 - core))
        return (qi.T, ki), (qi, ki.T)

    enc_ids = id_arrays(src_ids, src_ids)
    dec_ids = id_arrays(tgt_ids, tgt_ids)
    cross_ids = id_arrays(tgt_ids, src_ids)

    def scatter(arrays, call_id):
        return Scatter(arrays, row_count, call_id) if near else None

    def tokens(value):
        return value.astype(BF16).reshape(chips, half, width)

    def scatter(arrays, call_id):
        return Scatter(arrays, row_count, call_id) if near else None

    def tokens(value):
        return value.astype(BF16).reshape(chips, half, width)

    if near:
        src_own, place_own = cut(src_ids, core)
        src_oth, place_oth = cut(src_ids, 1 - core)
        tgt_own, tgt_oth = cut(tgt_ids, core)[0], cut(tgt_ids, 1 - core)[0]
        feats = jnp.stack(
            [
                id_columns(src_own, False),
                id_columns(src_own, True),
                id_columns(src_oth, True),
                id_columns(tgt_own, False),
                id_columns(tgt_own, True),
                id_columns(tgt_oth, True),
            ]
        )
        enc_w, dec_w, slope, kept = forward_call(
            shards,
            [stacked[0], stacked[1]],
            place_own[:, None],
            jnp.stack([place_own, place_oth] * 4),
            feats,
        )
        (dec_slope, dec_s, dec_a, dec_y, dec_yr, decoded), (placed,) = tail_call(
            kept[C2],
            (dec_w[1], dec_w[2], dec_w[3]),
            scatter([(stacked[2], Scatter.BRING)], 8),
        )
        cotangent = placed.reshape(length, width)
        encoded_bf = kept[EY].astype(BF16)
    else:
        source, target, cotangent = spread(stacked)
        enc_attn, enc_cross, enc_tail_w = unpack(gather_plain(0, shards))
        dec_attn, dec_cross, dec_tail_w = unpack(gather_plain(1, shards))
        enc_mid, enc_self = self_forward(
            source, source.astype(F32), enc_attn, enc_ids, False
        )
        encoded, enc_tail = tail_forward(enc_mid, enc_tail_w)
        encoded_bf = encoded.astype(BF16)
        memory = [project(encoded_bf, enc_cross[:, j]).astype(BF16) for j in range(2)]
        memory_other = swap(jnp.stack(memory))
        mem_keys = (memory[0], memory_other[0], memory[1], memory_other[1])
        dec_mid, dec_self = self_forward(
            target, target.astype(F32), dec_attn, dec_ids, True
        )
        queries = project(dec_mid.astype(BF16), dec_cross[:, 0]).astype(BF16)
        cross_o, cross_lse = attention_forward(
            queries, mem_keys, cross_ids[0], False
        )
        second, second_rstd = norm(dec_mid + unproject(cross_o, dec_cross[:, 1]))
        decoded, dec_tail = tail_forward(second, dec_tail_w)

    if near:

        def heads(q, k, kx, v, vx, o, lse, do):
            flat = kept[lse].reshape(kept[lse].shape[0], -1, length)
            return [kept[n] for n in (q, k, kx, v, vx, o)] + [do, flat]

        def pieces(parts):
            return [v.reshape((chips,) + v.shape[2:]) for v in parts]

        (grad_cross, do), dec_parts, (out_enc,) = tail_back(
            cotangent,
            dec_y,
            dec_yr,
            kept[C2],
            kept[C2R],
            dec_slope,
            (dec_w[1], dec_w[2], dec_w[3]),
            dec_s,
            dec_a,
            dec_w[4],
            1,
            scatter([(tokens(encoded_bf), 0)], 2),
        )
        (dpre, do, grad_encoded), (out_dec,) = attn_back(
            heads(CQ, MK, MKX, MV, MVX, CO, CL, do),
            [feats[3], feats[1], feats[2], *cross_ids[1]],
            False,
            scatter([(tokens(decoded), 1)], 3),
            grad_cross,
            (dec_w[4], enc_w[4]),
            (kept[DH], kept[DR], dec_w[0]),
        )
        (grad_target,), dec_sum = attn_back(
            heads(DQ, DK, DKX, DV, DVX, DO, DL, do),
            [feats[3], feats[4], feats[5], *dec_ids[1]],
            True,
            scatter([(v, 1) for v in pieces(dec_parts)], 4),
            dpre,
            dec_w[0],
        )
        (dpre, do), enc_parts, (moved,) = tail_back(
            grad_encoded,
            kept[EY],
            kept[EYR],
            kept[EH],
            kept[ER],
            slope,
            (enc_w[1], enc_w[2], enc_w[3]),
            kept[ES],
            kept[EA],
            enc_w[0],
            3,
            scatter([(tokens(grad_target), 1)], 5),
        )
        (grad_source,), enc_sum = attn_back(
            heads(EQ, EK, EKX, EV, EVX, EO, EL, do),
            [feats[0], feats[1], feats[2], *enc_ids[1]],
            False,
            scatter([(v, 0) for v in pieces(enc_parts)], 6),
            dpre,
            enc_w[0],
        )
        outs = pick(out_enc, out_dec)
        sums, ends = [
            jnp.sum(pick(a, b).astype(F32), axis=0) for a, b in zip(enc_sum, dec_sum)
        ]
        part_rows = lanes // 4
        ends = jnp.pad(jnp.sum(ends, axis=0), ((0, 0), (0, width - width // 4)))
        mine = jnp.concatenate([sums.reshape(2 * part_rows, width), ends]).astype(BF16)
        (last,), whole = send_call(scatter([(tokens(grad_source), 0)], 7), mine)
        grads = pick(last, moved).astype(F32)
        whole = whole.astype(F32)
        weights = whole[:, : 2 * part_rows].reshape(4, 2, part_rows, width)
        ends = whole[:, 2 * part_rows :, : width // 4]
        return (
            outs.reshape(layer_inputs.shape),
            grads.reshape(layer_inputs.shape),
            weights[:, 0].reshape(lanes, width).T[None],
            ends[0, 1, :lanes][None],
            weights[:, 1].reshape(1, lanes, width),
            ends[:, 0].reshape(1, width),
        )

    grad_second, dec_terms = tail_backward(cotangent.astype(F32), dec_tail, dec_tail_w)
    grad_cross = norm_back(second, second_rstd, grad_second)
    do = project(grad_cross.astype(BF16), dec_cross[:, 1]).astype(BF16)
    dqc, dmk, dmv = attend_back(
        queries, mem_keys, cross_o, do, cross_lse, cross_ids, False
    )
    grad_first = unproject(dqc, dec_cross[:, 0]) + grad_cross
    grad_target = self_backward(grad_first, dec_self, dec_attn, dec_ids, True)

    grad_encoded = unproject(dmk, enc_cross[:, 0]) + unproject(dmv, enc_cross[:, 1])
    grad_mid, enc_terms = tail_backward(grad_encoded, enc_tail, enc_tail_w)
    grad_source = self_backward(grad_mid, enc_self, enc_attn, enc_ids, False)

    has_row = chip < row_count

    def total(enc_term, dec_term):
        enc_term = jnp.where(has_row, enc_term, 0.0).astype(BF16)
        dec_term = jnp.where(has_row, dec_term, 0.0).astype(BF16)
        got = swap(pick(dec_term, enc_term))
        return (pick(enc_term, dec_term).astype(F32) + got.astype(F32)).astype(BF16)

    sums = [total(e, d) for e, d in zip(enc_terms, dec_terms)]
    scattered = [
        lax.psum_scatter(v, TP, scatter_dimension=0, tiled=False) for v in sums[:3]
    ]
    scattered = [lax.psum(v, CTX).astype(F32) for v in scattered]
    bias_sum = lax.psum(sums[3], (CTX, TP)).astype(F32)

    results = jnp.stack(
        [
            encoded_bf,
            decoded.astype(BF16),
            grad_source.astype(BF16),
            grad_target.astype(BF16),
        ]
    )
    placed = collect(results, row_count)

    def join(enc_part, dec_part):
        mine = pick(enc_part, dec_part)
        got = swap(pick(dec_part, enc_part))
        return jnp.concatenate([pick(mine, got), pick(got, mine)], axis=1)

    outs = join(placed[0], placed[1]).reshape(layer_inputs.shape)
    grads = join(placed[2], placed[3]).astype(F32).reshape(layer_inputs.shape)
    return (
        outs,
        grads,
        scattered[0][None],
        scattered[1][None],
        scattered[2].T[None],
        bias_sum[None],
    )


def solution(mesh):
    return jax.shard_map(
        per_device,
        mesh=mesh,
        in_specs=(
            P(SECTION, None, None, (CTX, TP), None),
            P(None, None, (CTX, TP), None),
            P(None, None, CTX),
            P(None, None, CTX),
            P(SECTION, None, None, TP),
            P(SECTION, None, TP),
            P(SECTION, None, None, TP),
            P(SECTION, None, TP),
            P(SECTION, TP, None),
            P(SECTION, None, TP),
            P(SECTION, TP),
            P(SECTION, TP, None),
            P(SECTION, None),
        ),
        out_specs=(
            P(SECTION, None, None, (CTX, TP), None),
            P(SECTION, None, None, (CTX, TP), None),
            P(SECTION, None, TP),
            P(SECTION, TP),
            P(SECTION, TP, None),
            P(SECTION, None),
        ),
        check_vma=False,
    )
```

```python
import functools

import jax
import jax.numpy as jnp
from jax import lax
from jax.experimental import pallas as pl
from jax.experimental.pallas import tpu as pltpu
from jax.sharding import PartitionSpec as P

HEAD = 64
SCALE = HEAD**-0.5
EPS = 1e-05
MASKED = -1e30
F32 = jnp.float32
BF16 = jnp.bfloat16
SECTION, CTX, TP = "section", "ctx", "tp"


def swap(value):
    return lax.ppermute(value, SECTION, [(0, 1), (1, 0)])


def remote(src, dst, send, recv, where):
    return pltpu.make_async_remote_copy(
        src_ref=src,
        dst_ref=dst,
        send_sem=send,
        recv_sem=recv,
        device_id=where,
        device_id_type=pl.DeviceIdType.MESH,
    )


def device_of(section, chip):
    return (section, chip // 4, lax.rem(chip, 4))


def greet_all():
    s = lax.axis_index(SECTION)
    chip = lax.axis_index(CTX) * 4 + lax.axis_index(TP)
    barrier = pltpu.get_barrier_semaphore()
    for core in (0, 1):
        for i in range(core, 16):
            pl.semaphore_signal(
                barrier,
                1,
                device_id=device_of(lax.rem(s + 1 - core, 2), lax.rem(chip + i, 16)),
                device_id_type=pl.DeviceIdType.MESH,
            )
    pl.semaphore_wait(barrier, 31)


class Scatter:
    BRING = 2

    def __init__(self, arrays, rows, call_id):
        self.inputs = [a for a, _ in arrays]
        self.kinds = [k for _, k in arrays]
        self.rows = rows
        self.call_id = call_id
        self.shapes = [
            jax.ShapeDtypeStruct(
                ((16,) if k == self.BRING else (rows, 2)) + a.shape[1:], a.dtype
            )
            for a, k in arrays
        ]
        count = len(arrays)
        self.scratch = [
            pltpu.SemaphoreType.DMA((count, 16)),
            pltpu.SemaphoreType.DMA((count, 16, 2)),
        ]

    def sends(self, ins, outs, sems):
        send, recv = sems
        s = lax.axis_index(SECTION)
        chip = lax.axis_index(CTX) * 4 + lax.axis_index(TP)
        for a, kind in enumerate(self.kinds):
            for i in range(16):
                p = lax.rem(chip + i, 16)
                if kind == self.BRING:
                    ready = p < self.rows
                    src = ins[a].at[jnp.minimum(p, self.rows - 1)]
                    dst = outs[a].at[chip]
                    core, mark = s, 0
                    stays = True
                else:
                    ready = chip < self.rows
                    src = ins[a].at[p]
                    dst = outs[a].at[jnp.minimum(chip, self.rows - 1), s]
                    core, mark = kind, s
                    stays = s == kind
                near = pltpu.make_async_copy(src, dst, send.at[a, i])
                far = remote(
                    src, dst, send.at[a, i], recv.at[a, i, mark], device_of(core, p)
                )
                yield i, ready, stays, near, far

    def start(self, ins, outs, sems):
        greet_all()
        for i, ready, stays, near, far in self.sends(ins, outs, sems):

            @pl.when(ready)
            def _():
                if i:
                    far.start()
                elif stays is True:
                    near.start()
                else:
                    pl.when(stays)(near.start)
                    pl.when(jnp.logical_not(stays))(far.start)

    def finish(self, ins, outs, sems):
        send, recv = sems
        s = lax.axis_index(SECTION)
        chip = lax.axis_index(CTX) * 4 + lax.axis_index(TP)
        for i, ready, stays, near, far in self.sends(ins, outs, sems):

            @pl.when(ready)
            def _():
                if i:
                    far.wait_send()
                elif stays is True:
                    near.wait()
                else:
                    pl.when(stays)(near.wait)
                    pl.when(jnp.logical_not(stays))(far.wait_send)

        def got(region, sem):
            remote(region, region, send.at[0, 0], sem, (1 - s, 0, 0)).wait_recv()

        for a, kind in enumerate(self.kinds):
            for i in range(16):
                sender = lax.rem(chip + 16 - i, 16)
                if kind == self.BRING:
                    if i:

                        @pl.when(chip < self.rows)
                        def _():
                            got(outs[a].at[sender], recv.at[a, i, 0])

                    continue

                @pl.when((s == kind) & (sender < self.rows))
                def _():
                    for core in (0, 1) if i else (1 - kind,):
                        region = outs[a].at[jnp.minimum(sender, self.rows - 1), core]
                        got(region, recv.at[a, i, core])


def send_kernel(rider, *refs):
    n = len(rider.inputs)
    block_in, (own, spread_out) = refs[n], (refs[n], refs[2 * n + 1])
    ins, outs = refs[:n], refs[n + 1 : 2 * n + 1]
    sems = refs[2 * n + 2 : 2 * n + 4]
    b_send, b_recv = refs[2 * n + 4 :]
    rider.start(ins, outs, sems)
    s = lax.axis_index(SECTION)
    c = lax.axis_index(CTX)
    t = lax.axis_index(TP)
    dst = spread_out.at[c]
    keep = pltpu.make_async_copy(own, dst, b_send.at[0])
    keep.start()
    ways = [
        remote(own, dst, b_send.at[j], b_recv.at[j], (s, lax.rem(c + j, 4), t))
        for j in (1, 2, 3)
    ]
    for way in ways:
        way.start()
    keep.wait()
    for j, way in enumerate(ways):
        way.wait_send()
        region = spread_out.at[lax.rem(c + 3 - j, 4)]
        remote(region, region, b_send.at[0], b_recv.at[j + 1], (s, c, t)).wait_recv()
    rider.finish(ins, outs, sems)


def send_call(rider, block):
    anywhere = pl.BlockSpec(memory_space=pl.ANY)
    count = len(rider.inputs)
    result = pl.pallas_call(
        functools.partial(send_kernel, rider),
        in_specs=[anywhere] * (count + 1),
        out_specs=[anywhere] * (count + 1),
        out_shape=rider.shapes + [jax.ShapeDtypeStruct((4,) + block.shape, block.dtype)],
        scratch_shapes=rider.scratch
        + [pltpu.SemaphoreType.DMA((4,)), pltpu.SemaphoreType.DMA((4,))],
        compiler_params=pltpu.CompilerParams(
            collective_id=rider.call_id, has_side_effects=True
        ),
        name="send_last",
    )(*rider.inputs, block)
    return result[:count], result[count]


def dot_nt(left, right, **kw):
    return lax.dot_general(
        left, right, (((1,), (1,)), ((), ())), preferred_element_type=F32, **kw
    )


def dot_nn(left, right):
    return lax.dot_general(
        left, right, (((1,), (0,)), ((), ())), preferred_element_type=F32
    )


def dot_tn(left, right):
    return lax.dot_general(
        left, right, (((0,), (0,)), ((), ())), preferred_element_type=F32
    )


def attn_fwd_kernel(
    causal, q_ref, ko_ref, kx_ref, vo_ref, vx_ref, fq, fo, fx, qi_ref, ki_ref, o_ref, lse_ref
):
    for pair in range(lse_ref.shape[1]):
        attend_pair(
            0,
            pair,
            q_ref,
            (ko_ref, kx_ref),
            (vo_ref, vx_ref),
            o_ref,
            lse_ref,
            (fq, fo, fx),
            (qi_ref[:, 1:2], (ki_ref[1:2, :], ki_ref[3:4, :])),
            causal,
        )


def attention_call(kernel, name, causal, blocks, small, outs):
    def group_spec(v):
        return pl.BlockSpec((1,) + v.shape[1:], lambda t: (t,) + (0,) * (len(v.shape) - 1))

    return pl.pallas_call(
        functools.partial(kernel, causal),
        grid=(blocks[0].shape[0],),
        in_specs=[group_spec(v) for v in blocks]
        + [pl.BlockSpec(v.shape, lambda t: (0, 0)) for v in small],
        out_specs=[group_spec(v) for v in outs],
        out_shape=outs,
        compiler_params=pltpu.CompilerParams(vmem_limit_bytes=48 * 2**20),
        name=name,
    )(*blocks, *small)


def id_columns(ids, keys):
    lane = jnp.arange(2 * HEAD, dtype=jnp.int32)[None] % HEAD
    same = ids[:, None] == lane
    value = jnp.where(same, 1.0, 0.0) if keys else jnp.where(same, 0.0, MASKED)
    return jnp.where(lane < 4, value, 0.0).astype(BF16)


def attention_forward(q, keys, ids, causal):
    groups, length, width = q.shape
    pairs = width // HEAD // 2
    outs = [
        jax.ShapeDtypeStruct(q.shape, BF16),
        jax.ShapeDtypeStruct((groups, pairs, 2, length), F32),
    ]
    feats = [
        id_columns(ids[0][:, 0], False),
        id_columns(ids[1][0], True),
        id_columns(ids[1][2], True),
    ]
    o, lse = attention_call(
        attn_fwd_kernel, "attn_fwd", causal, [q, *keys], [*feats, *ids], outs
    )
    return o, lse.reshape(groups, 2 * pairs, length)


def attend_back_group(ins, dq_out, dk_outs, dv_outs, feats, qi_ref, ki_ref, causal):
    q_ref, k_refs, v_refs, o_ref, do_ref, lse_ref = ins
    length = q_ref.shape[1]
    block = length // 2
    posq = qi_ref[1:2, :]
    ones = jnp.ones((16, 2 * HEAD), BF16)

    def put(out, rows, lanes, value):
        out[0][out[1], rows, lanes] = value.astype(out[0].dtype)

    for pair in range(q_ref.shape[2] // (2 * HEAD)):
        lanes = slice(pair * 2 * HEAD, (pair + 1) * 2 * HEAD)
        q2 = q_ref[0, :, lanes] * jnp.asarray(SCALE, BF16)
        do2 = do_ref[0, :, lanes]
        prod2 = do2.astype(F32) * o_ref[0, :, lanes].astype(F32)
        dq, dk, dv = [None, None], {}, {}
        for j in range(2):
            here = head_mask(length, j)
            q_all = jnp.where(here, q2, feats[0][...])
            q_only = jnp.where(here, q2, jnp.zeros_like(q2))
            do_all = jnp.where(here, do2, jnp.zeros_like(do2))
            prod = jnp.where(here, prod2, 0.0)
            high = prod.astype(BF16)
            rest = (prod - high.astype(F32)).astype(BF16)
            delta = (dot_nt(ones, high) + dot_nt(ones, rest))[0:1]
            lse = lse_ref[0, 2 * pair + j : 2 * pair + j + 1, :]
            for n in range(2):
                for b in range(2):
                    rows = slice(b * block, (b + 1) * block)
                    first = b * block if causal else 0
                    k2 = k_refs[n][0, rows, lanes]
                    there = head_mask(block, j)
                    k = jnp.where(there, k2, feats[1 + n][rows])
                    k_only = jnp.where(there, k2, jnp.zeros_like(k2))
                    s = dot_nt(k, q_all[first:])
                    p = jnp.exp(s - lse[:, first:])
                    if causal:
                        ok = posq[:, first:] >= ki_ref[rows, 2 * n + 1 : 2 * n + 2]
                        p = jnp.where(ok, p, 0.0)
                    dp = dot_nt(v_refs[n][0, rows, lanes], do_all[first:])
                    ds = (p * (dp - delta[:, first:])).astype(BF16)
                    add = lambda old, new: new if old is None else old + new
                    dv[n, b] = add(
                        dv.get((n, b)), dot_nn(p.astype(BF16), do_all[first:])
                    )
                    dk[n, b] = add(dk.get((n, b)), dot_nn(ds, q_only[first:]))
                    part = dot_tn(k_only, ds)
                    if not first:
                        dq[0] = add(dq[0], part[:, :block])
                    dq[1] = add(dq[1], part[:, block - first :])
        for n in range(2):
            for b in range(2):
                rows = slice(b * block, (b + 1) * block)
                put(dv_outs[n], rows, lanes, dv[n, b])
                put(dk_outs[n], rows, lanes, dk[n, b])
        for b in range(2):
            put(dq_out, slice(b * block, (b + 1) * block), lanes, (dq[b] * SCALE).T)


def attn_bwd_kernel(
    causal,
    q_ref,
    ko_ref,
    kx_ref,
    vo_ref,
    vx_ref,
    o_ref,
    do_ref,
    lse_ref,
    fq,
    fo,
    fx,
    qi_ref,
    ki_ref,
    dq_ref,
    dko_ref,
    dkx_ref,
    dvo_ref,
    dvx_ref,
):
    attend_back_group(
        (q_ref, (ko_ref, kx_ref), (vo_ref, vx_ref), o_ref, do_ref, lse_ref),
        (dq_ref, 0),
        ((dko_ref, 0), (dkx_ref, 0)),
        ((dvo_ref, 0), (dvx_ref, 0)),
        (fq, fo, fx),
        qi_ref,
        ki_ref,
        causal,
    )


def back_feats(ids):
    return [
        id_columns(ids[0][0], False),
        id_columns(ids[1][:, 0], True),
        id_columns(ids[1][:, 2], True),
    ]


def attention_backward(q, keys, o, do, lse, ids, causal):
    outs = [jax.ShapeDtypeStruct(q.shape, BF16)] * 5
    small = [*back_feats(ids), *ids]
    return attention_call(
        attn_bwd_kernel, "attn_bwd", causal, [q, *keys, o, do, lse], small, outs
    )


def norm(value):
    mean = jnp.mean(value, axis=-1, keepdims=True)
    centered = value - mean
    rstd = lax.rsqrt(jnp.mean(centered * centered, axis=-1, keepdims=True) + EPS)
    return centered * rstd, rstd


def norm_back(normed, rstd, grad):
    return rstd * (
        grad
        - jnp.mean(grad, axis=-1, keepdims=True)
        - normed * jnp.mean(grad * normed, axis=-1, keepdims=True)
    )


def project(rows, weight):
    return jnp.einsum("pk,tkm->tpm", rows, weight, preferred_element_type=F32)


def unproject(blocks, weight):
    return jnp.einsum("tpm,tkm->pk", blocks, weight, preferred_element_type=F32)


def self_forward(rows_bf, rows, w_attn, ids, causal):
    kv = [project(rows_bf, w_attn[:, j]).astype(BF16) for j in (1, 2)]
    other = swap(jnp.stack(kv))
    q = project(rows_bf, w_attn[:, 0]).astype(BF16)
    keys = (kv[0], other[0], kv[1], other[1])
    o, lse = attention_forward(q, keys, ids[0], causal)
    h, rstd = norm(rows + unproject(o, w_attn[:, 3]))
    return h, (q, keys, o, lse, h, rstd)


def attend_back(q, keys, o, do, lse, ids, causal):
    dq, dko, dkx, dvo, dvx = attention_backward(q, keys, o, do, lse, ids[1], causal)
    other = swap(jnp.stack([dkx, dvx])).astype(F32)
    dk = (dko.astype(F32) + other[0]).astype(BF16)
    dv = (dvo.astype(F32) + other[1]).astype(BF16)
    return dq, dk, dv


def self_backward(grad, kept, w_attn, ids, causal):
    q, keys, o, lse, h, rstd = kept
    dpre = norm_back(h, rstd, grad)
    do = project(dpre.astype(BF16), w_attn[:, 3]).astype(BF16)
    dq, dk, dv = attend_back(q, keys, o, do, lse, ids, causal)
    return (
        unproject(dq, w_attn[:, 0])
        + unproject(dk, w_attn[:, 1])
        + unproject(dv, w_attn[:, 2])
        + dpre
    )


def tail_forward(h, tail_w):
    w_in, w_out, a_in, b_in, a_out, b_out = tail_w
    rows = h.astype(BF16)
    inner = project(rows, w_in)
    phi = 0.5 * (1.0 + lax.erf(inner * 0.7071067811865476))
    g = (inner * phi).astype(BF16)
    slope = phi + inner * jnp.exp(inner * inner * -0.5) * 0.3989422804014327
    pre = project(rows, a_in) + b_in.astype(F32)[:, None, :]
    sig = jax.nn.sigmoid(pre)
    s = (pre * sig).astype(BF16)
    a_slope = sig * (1.0 + pre * (1.0 - sig))
    total = jnp.einsum("tpm,tmk->pk", g, w_out, preferred_element_type=F32)
    total += 4.0 * (
        jnp.einsum("tpm,tkm->pk", s, a_out, preferred_element_type=F32)
        + b_out.astype(F32)
    )
    y, rstd = norm(h + total)
    return y, (rows, slope.astype(BF16), s, a_slope.astype(BF16), y, rstd)


def tail_backward(grad, kept, tail_w):
    w_in, w_out, a_in, b_in, a_out, b_out = tail_w
    rows, slope, s, a_slope, y, rstd = kept
    dpre = norm_back(y, rstd, grad)
    db = dpre.astype(BF16)
    dg = jnp.einsum("pk,tmk->tpm", db, w_out, preferred_element_type=F32)
    df = (dg * slope.astype(F32)).astype(BF16)
    ds = 4.0 * jnp.einsum("pk,tkm->tpm", db, a_out, preferred_element_type=F32)
    du = (ds * a_slope.astype(F32)).astype(BF16)
    terms = (
        jnp.einsum("pk,tpm->tkm", rows, du, preferred_element_type=F32),
        jnp.sum(du.astype(F32), axis=1),
        4.0 * jnp.einsum("pk,tpm->tkm", db, s, preferred_element_type=F32),
        4.0 * jnp.sum(db.astype(F32), axis=0),
    )
    return unproject(df, w_in) + unproject(du, a_in) + dpre, terms


def head_mask(rows, j):
    lane = lax.broadcasted_iota(jnp.int32, (rows, 2 * HEAD), 1)
    return (lane < HEAD) if j == 0 else (lane >= HEAD)


def attend_pair(t, pair, q_ref, k_refs, v_refs, o_ref, lse_ref, feats, places, causal):
    length = q_ref.shape[1]
    block = length // 2
    lanes = pl.ds(pl.multiple_of(pair * 2 * HEAD, 2 * HEAD), 2 * HEAD)
    posq, posk = places
    for b in range(2):
        rows = slice(b * block, (b + 1) * block)
        q2 = q_ref[t, rows, lanes] * jnp.asarray(SCALE, BF16)
        cuts = [(n, a) for n in range(2) for a in range(b + 1 if causal else 2)]
        outs = []
        for j in range(2):
            q = jnp.where(head_mask(block, j), q2, feats[0][rows])
            parts = []
            for n, a in cuts:
                span = slice(a * block, (a + 1) * block)
                k = jnp.where(
                    head_mask(block, j), k_refs[n][t, span, lanes], feats[1 + n][span]
                )
                s = dot_nt(q, k)
                if causal and a == b:
                    s = jnp.where(posq[rows] >= posk[n][:, span], s, MASKED)
                parts.append(s)
            top = functools.reduce(
                jnp.maximum, [jnp.max(s, axis=1, keepdims=True) for s in parts]
            )
            ex = [jnp.exp(s - top) for s in parts]
            total = sum(jnp.sum(e, axis=1, keepdims=True) for e in ex)
            out = sum(
                dot_nn(
                    e.astype(BF16), v_refs[n][t, a * block : (a + 1) * block, lanes]
                )
                for e, (n, a) in zip(ex, cuts)
            )
            outs.append(out / total)
            lse = top + jnp.log(total)
            lse_ref[t, pair, j : j + 1, rows] = jnp.broadcast_to(lse, (block, 128)).T[
                0:1
            ]
        o_ref[t, rows, lanes] = jnp.where(head_mask(block, 0), *outs).astype(BF16)


ATTN, FFN_IN, FFN_OUT, ADAPTER, CROSS = range(5)
ORDER = (
    (0, ATTN),
    (1, ATTN),
    (0, FFN_IN),
    (0, FFN_OUT),
    (0, ADAPTER),
    (0, CROSS),
    (1, CROSS),
    (1, FFN_IN),
    (1, FFN_OUT),
    (1, ADAPTER),
)
(
    ENC_QKV,
    ENC_ATTN,
    ENC_OUT,
    DEC_QKV,
    DEC_ATTN,
    DEC_OUT,
    HIDDEN,
    GATED,
    MEMORY,
    CROSS_Q,
    CROSS_ATTN,
    CROSS_OUT,
    END,
) = range(13)
WORK = (
    (ENC_QKV, 4, (0, ATTN), 2.0),
    (ENC_ATTN, 8, None, 2.3),
    (ENC_OUT, 1, None, 4.0),
    (DEC_QKV, 4, (1, ATTN), 2.0),
    (DEC_ATTN, 8, None, 2.1),
    (DEC_OUT, 1, None, 4.0),
    (HIDDEN, 8, (0, FFN_OUT), 2.5),
    (GATED, 1, (0, ADAPTER), 4.0),
    (MEMORY, 4, (0, CROSS), 1.5),
    (CROSS_Q, 1, (1, CROSS), 4.0),
    (CROSS_ATTN, 8, None, 2.3),
    (CROSS_OUT, 1, None, 4.0),
    (END, 1, (1, ADAPTER), 0.0),
)


LAG = 2


def plan_steps(sizes):
    ready, clock = [], 20.0
    for e, g in ORDER:
        for _ in range(3):
            clock += sizes[g] / 3 * 11e-6
            ready.append(clock)
    ticks = len(ready) + 2 * LAG
    ready += [clock + 4 * n for n in range(1, 2 * LAG + 1)]
    starts, at, step, now, done = {}, {}, 0, 0.0, 0
    for name, count, need, cost in WORK:
        starts[name] = step
        for n in range(count):
            while done < ticks and (
                ready[done] <= now
                or (need and done <= 3 * ORDER.index(need) + 2 + 2 * LAG)
            ):
                at[done] = step
                now = max(now, ready[done])
                done += 1
            now += cost
            step += 1
    for n in range(done, ticks):
        at[n] = step - 1
    return starts, at, step


HEADS, LSE, WIDE, RSTD, LANES = range(5)
(
    EQ,
    EK,
    EKX,
    EV,
    EVX,
    EO,
    EL,
    EH,
    ER,
    ES,
    EA,
    EY,
    EYR,
    DQ,
    DK,
    DKX,
    DV,
    DVX,
    DO,
    DL,
    DH,
    DR,
    MK,
    MKX,
    MV,
    MVX,
    CQ,
    CO,
    CL,
    C2,
    C2R,
) = range(31)
KEPT = {
    EQ: HEADS,
    EK: HEADS,
    EKX: HEADS,
    EV: HEADS,
    EVX: HEADS,
    EO: HEADS,
    EL: LSE,
    EH: WIDE,
    ER: RSTD,
    ES: LANES,
    EA: LANES,
    EY: WIDE,
    EYR: RSTD,
    DQ: HEADS,
    DK: HEADS,
    DKX: HEADS,
    DV: HEADS,
    DVX: HEADS,
    DO: HEADS,
    DL: LSE,
    DH: WIDE,
    DR: RSTD,
    MK: HEADS,
    MKX: HEADS,
    MV: HEADS,
    MVX: HEADS,
    CQ: HEADS,
    CO: HEADS,
    CL: LSE,
    C2: WIDE,
    C2R: RSTD,
}


def forward_kernel(plan, rows, *refs):
    starts, tick_step, steps = plan
    refs = list(refs)

    def take(count):
        got = refs[:count]
        del refs[:count]
        return got

    shards = take(5)
    (tokens,) = take(1)
    col_ref, row_ref, feat_ref = take(3)
    full = (take(5), take(5))
    (slope_out,) = take(1)
    kept_out = take(len(KEPT))
    kept = take(len(KEPT))
    xs = take(2)
    wb, wi, wo, wad, slope = take(5)
    store_a, store_f = take(2)
    (
        z_send,
        z_recv,
        h_send,
        n_send,
        n_recv,
        f_send,
        f_recv,
        s_send,
        s_recv,
        own_sem,
        t_send,
        t_recv,
        kv_send,
        kv_recv,
        load_sem,
        out_sem,
        slope_sem,
    ) = refs
    step = pl.program_id(0)
    s = lax.axis_index(SECTION)
    c = lax.axis_index(CTX)
    t = lax.axis_index(TP)
    chips = 16
    chip = c * 4 + t
    cx = c + 1 - 2 * lax.rem(c, 2)
    cy = lax.rem(c + 2, 4)
    cd = 3 - c
    sib = (1 - s, c, t)

    inner = (t == 1) | (t == 2)

    def xor(k):
        return {1: t + 1 - 2 * lax.rem(t, 2), 2: 2 - t // 2, 3: 3 - 3 * (t // 2)}[k]

    part = xs[0].shape[1]

    def token_copy(kind, i, h):
        p = lax.rem(chip + i, chips)
        src = tokens.at[jnp.minimum(p, rows - 1), pl.ds(h * part, part)]
        dst = xs[kind].at[chip]
        if i == 0 and h == kind:
            return p, pltpu.make_async_copy(src, dst, t_send.at[kind, 0, h])
        return p, remote(
            src, dst, t_send.at[kind, i, h], t_recv.at[kind, i], device_of(h, p)
        )

    def send_tokens(kind):
        @pl.when(s == kind)
        def _():
            for i in range(chips):
                for h in range(2):
                    p, copy = token_copy(kind, i, h)
                    pl.when(p < rows)(copy.start)

    def got(region, sem):
        remote(region, region, load_sem.at[0], sem, sib).wait_recv()

    def wait_tokens(kind):
        @pl.when(s == kind)
        def _():
            for i in range(chips):
                for h in range(2):
                    p, copy = token_copy(kind, i, h)
                    stays = i == 0 and h == kind
                    pl.when(p < rows)(copy.wait if stays else copy.wait_send)

        @pl.when(chip < rows)
        def _():
            for i in range(chips):
                region = xs[kind].at[lax.rem(chip + chips - i, chips)]
                if i:
                    got(region, t_recv.at[kind, i])
                else:

                    @pl.when(s != kind)
                    def _():
                        got(region, t_recv.at[kind, 0])

    items = [(n, k) for n in range(len(ORDER)) for k in (1, 2, 3)]
    window = 4

    def block(n, who, h, q, u=None):
        e, g = ORDER[n]
        size = shards[g].shape[0]
        start = h * (size // 2) + q * (size // 8)
        length = size // 8
        if u is not None:
            length = size // 16
            start = start + u * length
        return full[e][g].at[who, pl.ds(pl.multiple_of(start, 16), length)]

    def z_copy(n, k, h):
        g = ORDER[n][1]
        size = shards[g].shape[0]
        start = h * (size // 2) + c * (size // 8)
        return remote(
            shards[g].at[pl.ds(pl.multiple_of(start, 16), size // 8)],
            block(n, t, h, c),
            z_send.at[n, k - 1, h],
            z_recv.at[n, k - 1],
            (h, c, xor(1) if k == 1 else jnp.clip(3 - t, 1, 2)),
        )

    def z_forward(n, k):
        src = block(n, xor(k), s, c)
        to = 3 - t if k == 1 else 3 * t - 3
        return remote(
            src,
            src,
            h_send.at[n, k - 1],
            z_recv.at[n, (2, 1, 2)[k - 1]],
            (s, c, jnp.clip(to, 0, 3)),
        )

    def store(g):
        if g in (FFN_IN, FFN_OUT):
            return store_f
        return store_a.at[pl.ds(0, shards[g].shape[0])]

    def fetch(n):
        g = ORDER[n][1]
        return pltpu.make_async_copy(shards[g], store(g), own_sem.at[n, 3])

    def put(n):
        e, g = ORDER[n]
        return pltpu.make_async_copy(store(g), full[e][g].at[t], own_sem.at[n, 0])

    def far(n):
        e, g = ORDER[n]
        return remote(
            shards[g], full[e][g].at[t], own_sem.at[n, 1], own_sem.at[n, 2], sib
        )

    def before(n):
        e, g = ORDER[n]
        pool = (FFN_IN, FFN_OUT) if g in (FFN_IN, FFN_OUT) else (ATTN, ADAPTER, CROSS)
        olds = [m for m in range(n) if ORDER[m][0] == e and ORDER[m][1] in pool]
        return olds[-1] if olds else None

    def start_z(i):
        n, k = items[i]

        @pl.when(s == ORDER[n][0])
        def _():
            if k == 1:
                far(n).start()
            if k < 3:

                @pl.when(inner | (k == 1))
                def _():
                    for h in range(2):
                        z_copy(n, k, h).start()

    def near_copy(n, k, j):
        src = block(n, xor(k), s, c)
        return remote(
            src,
            src,
            n_send.at[n, k - 1, j],
            n_recv.at[n, k - 1, j],
            (s, (cx, cy)[j], t),
        )

    def sibling_copy(n, k, j):
        src = block(n, xor(k), s, (c, cx, cy, cd)[j])
        return remote(src, src, s_send.at[n, k - 1, j], s_recv.at[n, k - 1, j], sib)

    def forward_copy(n, k, j):
        src = block(n, xor(k), s, (cx, cy)[j], j)
        return remote(
            src,
            src,
            f_send.at[n, k - 1, j],
            f_recv.at[n, k - 1, j],
            (s, (cy, cx)[j], t),
        )

    def stage2(i):
        n, k = items[i]
        got(block(n, xor(k), s, c), z_recv.at[n, k - 1])
        pl.when(inner)(z_forward(n, k).start)
        near_copy(n, k, 0).start()
        near_copy(n, k, 1).start()
        sibling_copy(n, k, 0).start()
        if k == 2:
            return

        @pl.when(s == ORDER[n][0])
        def _():
            if k == 1:
                old = before(n)
                if old is not None and not put_read_first(old, i):
                    put(old).wait()
                fetch(n).start()
            else:
                fetch(n).wait()
                put(n).start()

    def stage3(i):
        n, k = items[i]
        for j, q in ((0, cx), (1, cy)):
            got(block(n, xor(k), s, q), n_recv.at[n, k - 1, j])
            forward_copy(n, k, j).start()
            sibling_copy(n, k, j + 1).start()

    def stage4(i):
        n, k = items[i]
        for u in range(2):
            got(block(n, xor(k), s, cd, u), f_recv.at[n, k - 1, u])
        sibling_copy(n, k, 3).start()

    count = len(items)

    def tick(i):
        if i < count:
            stage2(i)
            if i + window < count:
                start_z(i + window)
        if 0 <= i - LAG < count:
            stage3(i - LAG)
        if 0 <= i - 2 * LAG < count:
            stage4(i - 2 * LAG)
        if i == 3:
            send_tokens(1)

    def arrive_step(n):
        for name, _, need, _ in WORK[:-1]:
            if need == ORDER[n]:
                return starts[name]
        return starts[HIDDEN] if ORDER[n] == (0, FFN_IN) else steps - 1

    def put_read_first(n, i):
        return arrive_step(n) < tick_step[i]

    def put_left(n):
        after = [m for m in range(len(ORDER)) if before(m) == n]
        return not after or put_read_first(n, 3 * after[0])

    def arrive(n):
        e, g = ORDER[n]
        for k in (1, 2, 3):
            for j, q in enumerate((c, cx, cy, cd)):
                got(block(n, xor(k), 1 - s, q), s_recv.at[n, k - 1, j])

        @pl.when(s == e)
        def _():
            if put_left(n):
                put(n).wait()

        @pl.when(s != e)
        def _():
            got(full[e][g].at[t], own_sem.at[n, 2])

    @pl.when(step == 0)
    def _():
        greet_all()
        send_tokens(0)
        for i in range(window):
            start_z(i)

    for i in range(count + 2 * LAG):
        pl.when(step == tick_step[i])(functools.partial(tick, i))

    def on(name):
        first = starts[name]
        last = first + [w[1] for w in WORK if w[0] == name][0]
        need = [w[2] for w in WORK if w[0] == name][0]
        if need and name != END:
            pl.when(step == first)(functools.partial(arrive, ORDER.index(need)))
        return step - first, pl.when((step >= first) & (step < last))

    def load(src, dst, slot=0):
        return pltpu.make_async_copy(src, dst, load_sem.at[slot])

    def keep(*names):
        for n in names:
            pltpu.make_async_copy(kept[n], kept_out[n], out_sem.at[n]).start()

    attn_rows = full[0][ATTN].shape[1] // 4

    def kv_copies(which, g, names):
        k, kx, v, vx = names
        return [
            remote(
                kept[a].at[g], kept[b].at[g], kv_send.at[which, g, j], kv_recv.at[which, g, j], sib
            )
            for j, (a, b) in enumerate(((k, kx), (v, vx)))
        ]

    def projections(name, which, e, g_id, x, names):
        i, when = on(name)
        tiles = len(names)
        height = tiles * attn_rows

        def source(j):
            return full[e][g_id].at[j, pl.ds(0, height)]

        @when
        def _():
            slot = lax.rem(i, 2)

            @pl.when(i == 0)
            def _():
                load(source(0), wb.at[0, pl.ds(0, height)]).start()

            load(source(0), wb.at[slot, pl.ds(0, height)]).wait()

            @pl.when(i < 3)
            def _():
                load(source(jnp.minimum(i + 1, 3)), wb.at[1 - slot, pl.ds(0, height)]).start()

            rows_in = x()
            for n, name_out in enumerate(names):
                w = wb[slot, n * attn_rows : (n + 1) * attn_rows, :]
                kept[name_out][i] = dot_nn(rows_in, w).astype(BF16)
            for copy in kv_copies(which, i, keys_of[which]):
                copy.start()

    keys_of = (
        (EK, EKX, EV, EVX),
        (DK, DKX, DV, DVX),
        (MK, MKX, MV, MVX),
    )

    def attend(name, which, q, o, lse, feats, causal):
        i, when = on(name)
        k, kx, v, vx = keys_of[which]

        @when
        def _():
            g, pair = i // 2, lax.rem(i, 2)

            @pl.when(pair == 0)
            def _():
                for copy in kv_copies(which, g, keys_of[which]):
                    copy.wait_send()
                    copy.wait_recv()

            attend_pair(
                g,
                pair,
                kept[q],
                (kept[k], kept[kx]),
                (kept[v], kept[vx]),
                kept[o],
                kept[lse],
                [feat_ref.at[f] for f in feats],
                (col_ref[...], (row_ref[0:1, :], row_ref[1:2, :])),
                causal,
            )

            @pl.when(i == 7)
            def _():
                keep(q, k, kx, v, vx, o, lse)

    def tiles4(e, g_id, first_row):
        copies = [
            load(
                full[e][g_id].at[j, pl.ds(first_row, attn_rows)],
                wb.at[0, pl.ds(j * attn_rows, attn_rows)],
                j,
            )
            for j in range(4)
        ]
        for copy in copies:
            copy.start()
        for copy in copies:
            copy.wait()

    def out_norm(name, e, g_id, first_row, residual, source, wide, rstd_name):
        _, when = on(name)

        @when
        def _():
            tiles4(e, g_id, first_row)
            total = residual()
            for j in range(4):
                total = total + dot_nt(
                    kept[source][j], wb[0, j * attn_rows : (j + 1) * attn_rows, :]
                )
            normed, rstd = norm(total)
            kept[wide][...] = normed
            kept[rstd_name][...] = jnp.broadcast_to(rstd, kept[rstd_name].shape)
            keep(wide, rstd_name)

    def flat_x(n):
        shape = xs[n].shape
        return xs[n][...].reshape(shape[0] * shape[1], shape[2])

    blocks = (
        (ENC_QKV, ENC_ATTN, ENC_OUT, EQ, EK, EV, EO, EL, EH, ER, (0, 1, 2)),
        (DEC_QKV, DEC_ATTN, DEC_OUT, DQ, DK, DV, DO, DL, DH, DR, (3, 4, 5)),
    )
    for e, (qkv, attn, out, q, k, v, o, lse, h, r, feats) in enumerate(blocks):
        pl.when(step == starts[qkv])(functools.partial(wait_tokens, e))
        projections(qkv, e, e, ATTN, functools.partial(flat_x, e), (q, k, v))
        attend(attn, e, q, o, lse, feats, e == 1)
        residual = lambda e=e: flat_x(e).astype(F32)
        out_norm(out, e, ATTN, 3 * attn_rows, residual, o, h, r)

    i, when = on(HIDDEN)
    hidden = wi.shape[2]

    @pl.when(step == starts[HIDDEN])
    def _():
        arrive(ORDER.index((0, FFN_IN)))

    def ffn_loads(j, slot):
        g, u = j // 2, lax.rem(j, 2)
        span = pl.ds(pl.multiple_of(u * hidden, 128), hidden)
        return (
            load(full[0][FFN_IN].at[g, :, span], wi.at[slot], 2 * slot),
            load(full[0][FFN_OUT].at[g, span], wo.at[slot], 2 * slot + 1),
        )

    def slope_copy(j, slot):
        g, u = j // 2, lax.rem(j, 2)
        span = pl.ds(pl.multiple_of(u * hidden, 128), hidden)
        return pltpu.make_async_copy(
            slope.at[slot], slope_out.at[g, :, span], slope_sem.at[slot]
        )

    @when
    def _():
        slot = lax.rem(i, 2)

        @pl.when(i == 0)
        def _():
            for copy in ffn_loads(0, 0):
                copy.start()
            kept[EY][...] = jnp.zeros_like(kept[EY])

        for copy in ffn_loads(i, slot):
            copy.wait()

        @pl.when(i < 7)
        def _():
            for copy in ffn_loads(i + 1, 1 - slot):
                copy.start()

        @pl.when(i >= 2)
        def _():
            slope_copy(i - 2, slot).wait()

        inner = dot_nn(kept[EH][...].astype(BF16), wi[slot])
        phi = 0.5 * (1.0 + lax.erf(inner * 0.7071067811865476))
        slope[slot] = (
            phi + inner * jnp.exp(inner * inner * -0.5) * 0.3989422804014327
        ).astype(BF16)
        slope_copy(i, slot).start()
        kept[EY][...] += dot_nn((inner * phi).astype(BF16), wo[slot])

    i, when = on(GATED)

    @when
    def _():
        for j in range(2):
            slope_copy(6 + j, j).wait()
        copy = load(full[0][ADAPTER], wad)
        copy.start()
        copy.wait()
        h = kept[EH][...]
        rows_in = h.astype(BF16)
        lanes = wad.shape[2] // 2
        extra = wad[0, attn_rows : attn_rows + 16, :].astype(F32)
        last = jnp.concatenate([extra[1 + r : 2 + r] for r in range(4)], axis=1)
        total = 4.0 * last
        for j in range(4):
            bias = wad[j, attn_rows : attn_rows + 16, :lanes].astype(F32)[0:1]
            pre = dot_nn(rows_in, wad[j, :attn_rows, :lanes]) + bias
            sig = 1.0 / (1.0 + jnp.exp(-pre))
            gated = (pre * sig).astype(BF16)
            kept[ES][j] = gated
            kept[EA][j] = (sig * (1.0 + pre * (1.0 - sig))).astype(BF16)
            total = total + 4.0 * dot_nt(gated, wad[j, :attn_rows, lanes:])
        normed, rstd = norm(h + (kept[EY][...] + total))
        kept[EY][...] = normed
        kept[EYR][...] = jnp.broadcast_to(rstd, kept[EYR].shape)
        keep(ES, EA, EY, EYR)

    projections(MEMORY, 2, 0, CROSS, lambda: kept[EY][...].astype(BF16), (MK, MV))
    _, when = on(CROSS_Q)

    @when
    def _():
        tiles4(1, CROSS, 0)
        rows_in = kept[DH][...].astype(BF16)
        for j in range(4):
            kept[CQ][j] = dot_nn(
                rows_in, wb[0, j * attn_rows : (j + 1) * attn_rows, :]
            ).astype(BF16)

    attend(CROSS_ATTN, 2, CQ, CO, CL, (3, 1, 2), False)
    out_norm(CROSS_OUT, 1, CROSS, attn_rows, lambda: kept[DH][...], CO, C2, C2R)

    @pl.when(step == steps - 1)
    def _():
        for g in (FFN_IN, FFN_OUT, ADAPTER):
            arrive(ORDER.index((1, g)))
        for n, k in items:
            pl.when(inner)(z_forward(n, k).wait_send)
            for j in range(2):
                near_copy(n, k, j).wait_send()
                forward_copy(n, k, j).wait_send()
            for j in range(4):
                sibling_copy(n, k, j).wait_send()
        for n in range(len(ORDER)):

            @pl.when(s == ORDER[n][0])
            def _():
                far(n).wait_send()
                for h in range(2):
                    z_copy(n, 1, h).wait_send()
                    pl.when(inner)(z_copy(n, 2, h).wait_send)

        for n in KEPT:
            pltpu.make_async_copy(kept[n], kept_out[n], out_sem.at[n]).wait()


def forward_call(shards, tokens, col, row, feats):
    rows, part, width = tokens.shape
    part //= 2
    length = 16 * part
    groups = len(ORDER)
    dma = pltpu.SemaphoreType.DMA
    anywhere = pl.BlockSpec(memory_space=pl.ANY)
    cols = shards[ATTN].shape[1]
    shapes = (
        ((4, length, cols), BF16),
        ((4, cols // HEAD // 2, 2, length), F32),
        ((length, width), F32),
        ((length, 128), F32),
        ((4, length, shards[ADAPTER].shape[1] // 2), BF16),
    )
    kept = [shapes[kind] for kind in KEPT.values()]
    hidden = shards[FFN_IN].shape[1]
    sizes = [
        (groups, 2, 2),
        (groups, 3),
        (groups, 3),
        (groups, 3, 2),
        (groups, 3, 2),
        (groups, 3, 2),
        (groups, 3, 2),
        (groups, 3, 4),
        (groups, 3, 4),
        (groups, 4),
        (2, 16, 2),
        (2, 16),
        (3, 4, 2),
        (3, 4, 2),
        (4,),
        (len(KEPT),),
        (2,),
    ]
    plan = plan_steps([v.size * 2 for v in shards])
    result = pl.pallas_call(
        functools.partial(forward_kernel, plan, rows),
        grid=(plan[2],),
        in_specs=[anywhere] * 6
        + [
            pl.BlockSpec(col.shape, lambda i: (0, 0)),
            pl.BlockSpec(row.shape, lambda i: (0, 0)),
            pl.BlockSpec(feats.shape, lambda i: (0, 0, 0)),
        ],
        out_specs=[anywhere] * (11 + len(KEPT)),
        out_shape=[jax.ShapeDtypeStruct((4,) + v.shape, v.dtype) for v in shards] * 2
        + [jax.ShapeDtypeStruct((4, length, hidden), BF16)]
        + [jax.ShapeDtypeStruct(*v) for v in kept],
        scratch_shapes=[pltpu.VMEM(*v) for v in kept]
        + [pltpu.VMEM((16, part, width), BF16)] * 2
        + [
            pltpu.VMEM((2,) + shards[ATTN].shape, BF16),
            pltpu.VMEM((2, width, hidden // 2), BF16),
            pltpu.VMEM((2, hidden // 2, width), BF16),
            pltpu.VMEM((4,) + shards[ADAPTER].shape, BF16),
            pltpu.VMEM((2, length, hidden // 2), BF16),
            pltpu.VMEM(shards[ATTN].shape, BF16),
            pltpu.VMEM(shards[FFN_IN].shape, BF16),
        ]
        + [dma(size) for size in sizes],
        compiler_params=pltpu.CompilerParams(
            collective_id=0, has_side_effects=True, vmem_limit_bytes=60 * 2**20
        ),
        name="forward",
    )(*shards, tokens, col, row, feats)
    return result[:5], result[5:10], result[10], result[11:]


def ids_kernel(ids, out, send, recv):
    s = lax.axis_index(SECTION)
    c = lax.axis_index(CTX)
    t = lax.axis_index(TP)
    barrier = pltpu.get_barrier_semaphore()
    for j in (1, 2, 3):
        pl.semaphore_signal(
            barrier,
            1,
            device_id=(s, lax.rem(c + j, 4), t),
            device_id_type=pl.DeviceIdType.MESH,
        )
    pl.semaphore_wait(barrier, 3)
    out[c] = ids[...]
    ways = [
        remote(ids, out.at[c], send.at[j - 1], recv.at[j - 1], (s, lax.rem(c + j, 4), t))
        for j in (1, 2, 3)
    ]
    for way in ways:
        way.start()
    for j, way in enumerate(ways):
        way.wait_send()
        region = out.at[lax.rem(c + 3 - j, 4)]
        remote(region, region, send.at[j], recv.at[j], (s, c, t)).wait_recv()


def ids_call(ids):
    spec = pl.BlockSpec(memory_space=pltpu.VMEM)
    return pl.pallas_call(
        ids_kernel,
        in_specs=[spec],
        out_specs=spec,
        out_shape=jax.ShapeDtypeStruct((4,) + ids.shape, ids.dtype),
        scratch_shapes=[pltpu.SemaphoreType.DMA((3,)), pltpu.SemaphoreType.DMA((3,))],
        compiler_params=pltpu.CompilerParams(collective_id=1, has_side_effects=True),
        name="ids",
    )(ids)


SPLIT = 1


def tail_kernel(rider, *refs):
    refs = list(refs)

    def take(count):
        got = refs[:count]
        del refs[:count]
        return got

    h_ref, w_in_ref, w_out_ref, adapter_ref = take(4)
    ride_ins = take(len(rider.inputs))
    slope_ref, s_ref, a_ref, y_ref, yr_ref, out_ref = take(6)
    ride = (ride_ins, take(len(rider.inputs)), take(len(rider.scratch)))
    rows_in, acc = refs
    step = pl.program_id(0)
    width = acc.shape[1]
    lanes = adapter_ref.shape[2] // 2

    @pl.when(step == 0)
    def _():
        rider.start(*ride)
        extra = adapter_ref[0, width : width + 16, :].astype(F32)
        cuts = width // adapter_ref.shape[2]
        last = jnp.concatenate([extra[1 + r : 2 + r] for r in range(cuts)], axis=1)
        acc[...] = h_ref[...] + 4.0 * last
        rows_in[...] = h_ref[...].astype(BF16)

    @pl.when(step < 4)
    def _():
        bias = adapter_ref[0, width : width + 16, :lanes].astype(F32)[0:1]
        pre = dot_nn(rows_in[...], adapter_ref[0, :width, :lanes]) + bias
        sig = 1.0 / (1.0 + jnp.exp(-pre))
        gated = (pre * sig).astype(BF16)
        s_ref[0] = gated
        a_ref[0] = (sig * (1.0 + pre * (1.0 - sig))).astype(BF16)
        acc[...] += 4.0 * dot_nt(gated, adapter_ref[0, :width, lanes:])

    @pl.when((step >= 4) & (step < 4 + 4 * SPLIT))
    def _():
        inner = dot_nn(rows_in[...], w_in_ref[0])
        phi = 0.5 * (1.0 + lax.erf(inner * 0.7071067811865476))
        slope_ref[0] = (
            phi + inner * jnp.exp(inner * inner * -0.5) * 0.3989422804014327
        ).astype(BF16)
        acc[...] += dot_nn((inner * phi).astype(BF16), w_out_ref[0])

    @pl.when(step == 4 + 4 * SPLIT)
    def _():
        normed, rstd = norm(acc[...])
        y_ref[...] = normed
        yr_ref[...] = jnp.broadcast_to(rstd, yr_ref.shape)
        out_ref[...] = normed.astype(BF16)
        rider.finish(*ride)


def tail_call(h, tail_w, rider):
    w_in, w_out, adapter = tail_w
    length, width = h.shape
    groups, _, hidden = w_in.shape
    lanes = adapter.shape[2] // 2
    anywhere = pl.BlockSpec(memory_space=pl.ANY)

    def tile(j):
        j = jnp.clip(j - groups, 0, groups * SPLIT - 1)
        return j // SPLIT, lax.rem(j, SPLIT)

    def group(j):
        return jnp.minimum(j, groups - 1)

    wide = pl.BlockSpec((length, width), lambda j: (0, 0))
    gated = pl.BlockSpec((1, length, lanes), lambda j: (group(j), 0, 0))
    cut = lambda rows: pl.BlockSpec(
        (1, rows, hidden // SPLIT), lambda j: (tile(j)[0], 0, tile(j)[1])
    )
    result = pl.pallas_call(
        functools.partial(tail_kernel, rider),
        grid=(groups * (1 + SPLIT) + 1,),
        in_specs=[
            wide,
            cut(width),
            pl.BlockSpec((1, hidden // SPLIT, width), lambda j: (tile(j)[0], tile(j)[1], 0)),
            pl.BlockSpec((1,) + adapter.shape[1:], lambda j: (group(j), 0, 0)),
        ]
        + [anywhere] * len(rider.inputs),
        out_specs=[
            cut(length),
            gated,
            gated,
            wide,
            pl.BlockSpec((length, 128), lambda j: (0, 0)),
            wide,
        ]
        + [anywhere] * len(rider.inputs),
        out_shape=[
            jax.ShapeDtypeStruct((groups, length, hidden), BF16),
            jax.ShapeDtypeStruct((groups, length, lanes), BF16),
            jax.ShapeDtypeStruct((groups, length, lanes), BF16),
            jax.ShapeDtypeStruct((length, width), F32),
            jax.ShapeDtypeStruct((length, 128), F32),
            jax.ShapeDtypeStruct((length, width), BF16),
        ]
        + rider.shapes,
        scratch_shapes=rider.scratch
        + [pltpu.VMEM((length, width), BF16), pltpu.VMEM((length, width), F32)],
        compiler_params=pltpu.CompilerParams(
            collective_id=rider.call_id, has_side_effects=True, vmem_limit_bytes=60 * 2**20
        ),
        name="tail",
    )(h, w_in, w_out, adapter, *rider.inputs)
    return result[:6], result[6:]


def norm_back_rows(normed, rstd, grad):
    return rstd * (
        grad
        - jnp.mean(grad, axis=-1, keepdims=True)
        - normed * jnp.mean(grad * normed, axis=-1, keepdims=True)
    )


def head_grads(da, w_ref, do_ref):
    for g in range(w_ref.shape[0]):
        do_ref[g] = dot_nn(da, w_ref[g]).astype(BF16)


def sibling_of():
    return (1 - lax.axis_index(SECTION), lax.axis_index(CTX), lax.axis_index(TP))


def tail_back_kernel(rider, *refs):
    refs = list(refs)

    def take(count):
        got = refs[:count]
        del refs[:count]
        return got

    grad_ref, y_ref, yr_ref, h_ref, hr_ref, slope_ref = take(6)
    w_out_ref, w_in_ref, adapter_ref, s_ref, a_ref, w_do_ref = take(6)
    ride_ins = take(len(rider.inputs))
    dpre_ref, do_ref, pieces_ref, tails_ref = take(4)
    ride = (ride_ins, take(len(rider.inputs)), take(len(rider.scratch)))
    db, acc, mine, away, got, send, recv = refs
    step = pl.program_id(0)
    groups = away.shape[0]
    width = acc.shape[1]
    lanes = adapter_ref.shape[2] // 2
    first = lax.axis_index(SECTION) == 0

    def to_sibling(g):
        return remote(
            away.at[g], got.at[g], send.at[g], recv.at[g], sibling_of()
        )

    @pl.when(step == 0)
    def _():
        rider.start(*ride)
        dpre = norm_back_rows(y_ref[...], yr_ref[:, 0:1], grad_ref[...].astype(F32))
        acc[...] = dpre
        db[...] = dpre.astype(BF16)

    @pl.when(step == 0)
    def _():
        branch = db[...]
        rows_in = h_ref[...].astype(BF16)
        beside = lambda r: jnp.concatenate([r[g] for g in range(groups)], axis=1)
        a_in = jnp.concatenate(
            [adapter_ref[g, :width, :lanes] for g in range(groups)], axis=1
        )
        a_out = jnp.concatenate(
            [adapter_ref[g, :width, lanes:] for g in range(groups)], axis=1
        )
        ds = 4.0 * dot_nn(branch, a_out)
        du = (ds * beside(a_ref).astype(F32)).astype(BF16)
        acc[...] += dot_nt(du, a_in)
        d_in = dot_tn(du, rows_in)
        d_out = 4.0 * dot_tn(beside(s_ref), branch)
        last = 4.0 * jnp.sum(branch.astype(F32), axis=0, keepdims=True)
        bias = jnp.sum(du.astype(F32), axis=0, keepdims=True)
        cut = width // 4
        blank = jnp.zeros((1, cut - lanes), F32)
        row = lax.broadcasted_iota(jnp.int32, (16, cut), 0)
        part = lanes // 4
        for g in range(groups):
            own = bias[:, g * lanes : (g + 1) * lanes]
            second = jnp.where(row == 1, jnp.concatenate([own, blank], axis=1), 0.0)
            for c in range(4):
                start = g * lanes + c * part
                one = d_in[start : start + part]
                two = d_out[start : start + part]
                mine[g, c] = jnp.where(first, one, two)
                away[g, c] = jnp.where(first, two, one).astype(BF16)
                tails_ref[c, g] = jnp.where(
                    row == 0, last[:, c * cut : (c + 1) * cut], second
                ).astype(BF16)
            to_sibling(g).start()

    @pl.when((step >= 1) & (step < 1 + groups * SPLIT))
    def _():
        dg = dot_nt(db[...], w_out_ref[0])
        df = (dg * slope_ref[0].astype(F32)).astype(BF16)
        acc[...] += dot_nt(df, w_in_ref[0])

    @pl.when(step == 1 + groups * SPLIT)
    def _():
        dpre = norm_back_rows(h_ref[...], hr_ref[:, 0:1], acc[...])
        dpre_ref[...] = dpre
        head_grads(dpre.astype(BF16), w_do_ref, do_ref)
        for g in range(groups):
            copy = to_sibling(g)
            copy.wait_send()
            copy.wait_recv()
            for c in range(4):
                pieces_ref[c, g] = (mine[g, c] + got[g, c].astype(F32)).astype(BF16)
        rider.finish(*ride)


def tail_back(grad, y, yr, h, hr, slope, tail_w, s_act, a_slope, w_do, do_block, rider):
    w_in, w_out, adapter = tail_w
    length, width = y.shape
    groups, _, hidden = slope.shape
    lanes = s_act.shape[2]
    cols = w_do.shape[2]
    part = lanes // 4
    anywhere = pl.BlockSpec(memory_space=pl.ANY)

    def whole(v):
        return pl.BlockSpec(v.shape, lambda j: (0, 0))

    def tile(j):
        j = jnp.clip(j - 1, 0, groups * SPLIT - 1)
        return j // SPLIT, lax.rem(j, SPLIT)

    result = pl.pallas_call(
        functools.partial(tail_back_kernel, rider),
        grid=(groups * SPLIT + 2,),
        in_specs=[whole(v) for v in (grad, y, yr, h, hr)]
        + [
            pl.BlockSpec((1, length, hidden // SPLIT), lambda j: (tile(j)[0], 0, tile(j)[1])),
            pl.BlockSpec((1, hidden // SPLIT, width), lambda j: (tile(j)[0], tile(j)[1], 0)),
            pl.BlockSpec((1, width, hidden // SPLIT), lambda j: (tile(j)[0], 0, tile(j)[1])),
            pl.BlockSpec(adapter.shape, lambda j: (0, 0, 0)),
            pl.BlockSpec((groups, length, lanes), lambda j: (0, 0, 0)),
            pl.BlockSpec((groups, length, lanes), lambda j: (0, 0, 0)),
            pl.BlockSpec((groups, width, cols), lambda j: (0, do_block, 0)),
        ]
        + [anywhere] * len(rider.inputs),
        out_specs=[
            pl.BlockSpec((length, width), lambda j: (0, 0)),
            pl.BlockSpec((groups, length, cols), lambda j: (0, 0, 0)),
            pl.BlockSpec((4, groups, part, width), lambda j: (0, 0, 0, 0)),
            pl.BlockSpec((4, groups, 16, width // 4), lambda j: (0, 0, 0, 0)),
        ]
        + [anywhere] * len(rider.inputs),
        out_shape=[
            jax.ShapeDtypeStruct((length, width), F32),
            jax.ShapeDtypeStruct((groups, length, cols), BF16),
            jax.ShapeDtypeStruct((4, groups, part, width), BF16),
            jax.ShapeDtypeStruct((4, groups, 16, width // 4), BF16),
        ]
        + rider.shapes,
        scratch_shapes=rider.scratch
        + [
            pltpu.VMEM((length, width), BF16),
            pltpu.VMEM((length, width), F32),
            pltpu.VMEM((groups, 4, part, width), F32),
            pltpu.VMEM((groups, 4, part, width), BF16),
            pltpu.VMEM((groups, 4, part, width), BF16),
            pltpu.SemaphoreType.DMA((groups,)),
            pltpu.SemaphoreType.DMA((groups,)),
        ],
        compiler_params=pltpu.CompilerParams(
            collective_id=rider.call_id, has_side_effects=True, vmem_limit_bytes=60 * 2**20
        ),
        name="tail_back",
    )(grad, y, yr, h, hr, slope, w_out, w_in, adapter, s_act, a_slope, w_do, *rider.inputs)
    return result[:2], result[2:4], result[4:]


def attn_back_kernel(causal, cross, rider, *refs):
    refs = list(refs)

    def take(count):
        got = refs[:count]
        del refs[:count]
        return got

    q_ref, k_ref, kx_ref, v_ref, vx_ref, o_ref, do_ref, lse_ref = take(8)
    if cross:
        wq_ref, wkv_ref, rest_ref, h_ref, hr_ref, w_do_ref = take(6)
    else:
        w_ref, rest_ref = take(2)
    feats, (qi_ref, ki_ref) = take(3), take(2)
    ride_ins = take(len(rider.inputs))
    if cross:
        dpre_ref, do_next_ref, memory_ref = take(3)
    else:
        (dx_ref,) = take(1)
    ride_outs = take(len(rider.inputs))
    ride_sems = take(len(rider.scratch))
    ride = (ride_ins, ride_outs, ride_sems)
    dq_s, own_k, own_v, away_k, away_v, got_k, got_v, acc, send, recv = take(10)
    if cross:
        (acc2,) = take(1)
    step = pl.program_id(0)
    groups = away_k.shape[0]
    width = acc.shape[1]

    def to_sibling(g):
        return [
            remote(a.at[g], b.at[g], send.at[g, j], recv.at[g, j], sibling_of())
            for j, (a, b) in enumerate(((away_k, got_k), (away_v, got_v)))
        ]

    @pl.when(step == 0)
    def _():
        rider.start(*ride)
        acc[...] = rest_ref[...]
        if cross:
            acc2[...] = jnp.zeros_like(acc2)

    @pl.when(step > 0)
    def _():
        g = step - 1
        slot = lax.rem(g, 2)
        for copy in to_sibling(g):
            copy.wait_send()
            copy.wait_recv()
        dk = (own_k[slot] + got_k[g].astype(F32)).astype(BF16)
        dv = (own_v[slot] + got_v[g].astype(F32)).astype(BF16)
        dq = dq_s[slot]
        if cross:
            acc[...] += dot_nt(dq, wq_ref[0])
            acc2[...] += dot_nt(dk, wkv_ref[0, :width]) + dot_nt(dv, wkv_ref[0, width:])
        else:
            acc[...] += (
                dot_nt(dq, w_ref[0, :width])
                + dot_nt(dk, w_ref[0, width : 2 * width])
                + dot_nt(dv, w_ref[0, 2 * width :])
            )

    @pl.when(step < groups)
    def _():
        slot = lax.rem(step, 2)
        attend_back_group(
            (q_ref, (k_ref, kx_ref), (v_ref, vx_ref), o_ref, do_ref, lse_ref),
            (dq_s, slot),
            ((own_k, slot), (away_k, step)),
            ((own_v, slot), (away_v, step)),
            feats,
            qi_ref,
            ki_ref,
            causal,
        )
        for copy in to_sibling(step):
            copy.start()

    @pl.when(step == groups)
    def _():
        if cross:
            dpre = norm_back_rows(h_ref[...], hr_ref[:, 0:1], acc[...])
            dpre_ref[...] = dpre
            head_grads(dpre.astype(BF16), w_do_ref, do_next_ref)
            memory_ref[...] = acc2[...]
        else:
            dx_ref[...] = acc[...].astype(dx_ref.dtype)
        rider.finish(*ride)


def attn_back(heads, ids, causal, rider, rest, weights, cross=None):
    groups, length, cols = heads[0].shape
    width = rest.shape[1]
    anywhere = pl.BlockSpec(memory_space=pl.ANY)

    def now(shape):
        return pl.BlockSpec((1,) + shape[1:], lambda t: (jnp.minimum(t, groups - 1), 0, 0))

    def past(rows):
        return pl.BlockSpec((1, rows, cols), lambda t: (jnp.maximum(t - 1, 0), 0, 0))

    def whole(v):
        return pl.BlockSpec(v.shape, lambda t: (0,) * len(v.shape))

    wide = jax.ShapeDtypeStruct((length, width), F32)
    if cross:
        h, hr, w_do = cross
        wq, wkv = weights
        extra = [wq, wkv, rest, h, hr, w_do]
        specs = [
            past(width),
            past(2 * width),
            whole(rest),
            whole(h),
            whole(hr),
            pl.BlockSpec((groups, width, cols), lambda t: (0, 3, 0)),
        ]
        outs = [wide, jax.ShapeDtypeStruct(heads[0].shape, BF16), wide]
    else:
        extra = [weights, rest]
        specs = [past(3 * width), whole(rest)]
        outs = [jax.ShapeDtypeStruct((length, width), BF16)]
    moving = pltpu.VMEM((groups, length, cols), BF16)
    result = pl.pallas_call(
        functools.partial(attn_back_kernel, causal, bool(cross), rider),
        grid=(groups + 1,),
        in_specs=[now(v.shape) for v in heads]
        + specs
        + [whole(v) for v in ids]
        + [anywhere] * len(rider.inputs),
        out_specs=[whole(v) for v in outs] + [anywhere] * len(rider.inputs),
        out_shape=outs + rider.shapes,
        scratch_shapes=rider.scratch
        + [
            pltpu.VMEM((2, length, cols), BF16),
            pltpu.VMEM((2, length, cols), F32),
            pltpu.VMEM((2, length, cols), F32),
            moving,
            moving,
            moving,
            moving,
            pltpu.VMEM((length, width), F32),
            pltpu.SemaphoreType.DMA((groups, 2)),
            pltpu.SemaphoreType.DMA((groups, 2)),
        ]
        + ([pltpu.VMEM((length, width), F32)] if cross else []),
        compiler_params=pltpu.CompilerParams(
            collective_id=rider.call_id,
            has_side_effects=True,
            vmem_limit_bytes=60 * 2**20,
        ),
        name="attn_back",
    )(*heads, *extra, *ids, *rider.inputs)
    return result[: len(outs)], result[len(outs) :]


def gather_plain(entry, shards):
    full = [lax.all_gather(lax.all_gather(v, TP), SECTION) for v in shards]
    return [v[entry] for v in full]


def spread(blocks):
    chips = lax.axis_size(CTX) * lax.axis_size(TP)
    kinds, rows, part, width = blocks.shape
    blocks = jnp.pad(blocks, ((0, 0), (0, chips - rows), (0, 0), (0, 0)))
    moved = lax.all_to_all(
        jnp.moveaxis(blocks, 1, 0), (CTX, TP), 0, 0, tiled=True
    )
    return jnp.moveaxis(moved, 0, 1).reshape(kinds, chips * part, width)


def collect(tokens, rows):
    chips = lax.axis_size(CTX) * lax.axis_size(TP)
    kinds, length, width = tokens.shape
    part = length // chips
    blocks = jnp.moveaxis(tokens.reshape(kinds, chips, part, width), 1, 0)
    moved = lax.all_to_all(blocks, (CTX, TP), 0, 0, tiled=True)
    return jnp.moveaxis(moved, 0, 1)[:, :rows]


def per_device(
    layer_inputs,
    out_grad,
    src_seg,
    tgt_seg,
    qkv_weights,
    out_weights,
    cross_weights,
    ffn_in,
    ffn_out,
    adapter_in,
    adapter_in_bias,
    adapter_out,
    adapter_out_bias,
):
    core = lax.axis_index(SECTION)
    is_first = core == 0
    tp = lax.axis_size(TP)
    chips = lax.axis_size(CTX) * tp
    chip = lax.axis_index(CTX) * tp + lax.axis_index(TP)
    _, micro, per_micro, part, width = layer_inputs.shape
    row_count = micro * per_micro
    half = part // 2
    length = half * chips

    def pick(first, second):
        return jnp.where(is_first, first, second)

    x = layer_inputs.reshape(row_count, part, width)
    grads = out_grad.reshape(row_count, part, width)
    grads = pick(grads[:, :half], grads[:, half:])
    near = lax.axis_size(CTX) == 4 and tp == 4
    lanes = adapter_in_bias.shape[1]
    cols = out_weights.shape[2]
    pad = lambda v, n: jnp.pad(v, [(0, n - v.shape[0])] + [(0, 0)] * (v.ndim - 1))
    biases = jnp.concatenate(
        [pad(adapter_in_bias[0], cols)[None], adapter_out_bias[0].reshape(-1, cols)]
    )
    shards = [
        jnp.concatenate([qkv_weights[0], out_weights], axis=0).reshape(-1, cols),
        ffn_in[0],
        ffn_out[0],
        jnp.concatenate(
            [
                jnp.concatenate([adapter_in[0], adapter_out[0].T], axis=1),
                pad(biases, 256),
            ],
            axis=0,
        ),
        cross_weights[0].reshape(-1, cols),
    ]
    if near:
        ids = ids_call(jnp.stack([src_seg, tgt_seg]).reshape(2 * row_count, -1))
        flat_ids = ids.swapaxes(0, 1).reshape(2, row_count, -1)
    else:
        flat_ids = [
            lax.all_gather(v.reshape(row_count, -1), CTX, axis=1, tiled=True)
            for v in (src_seg, tgt_seg)
        ]

    def unpack(full):
        attn, w_in, w_out, adapter, cross = full
        attn = attn.reshape(tp, 4, -1, cols)
        cross = cross.reshape(tp, 2, -1, cols)
        b_out = adapter[0, width + 1 : width + 1 + width // cols].reshape(width)
        tail = (
            w_in,
            w_out,
            adapter[:, :width, :lanes],
            adapter[:, width, :lanes],
            adapter[:, :width, lanes:],
            b_out,
        )
        return attn, cross, tail

    def ids_of(flat):
        row = lax.dynamic_index_in_dim(
            flat, jnp.minimum(chip, row_count - 1), 0, keepdims=False
        )
        return row.reshape(chips, 2, half)

    index = jnp.arange(length, dtype=jnp.int32)
    place = (index // half) * part + index % half

    def cut(seg, which):
        own = lax.dynamic_index_in_dim(seg, which, 1, keepdims=False).reshape(length)
        return own, place + which * half

    src_ids, tgt_ids = ids_of(flat_ids[0]), ids_of(flat_ids[1])

    def id_arrays(seg_q, seg_k):
        qi = jnp.stack(cut(seg_q, core))
        ki = jnp.stack(cut(seg_k, core) + cut(seg_k, 1 - core))
        return (qi.T, ki), (qi, ki.T)

    enc_ids = id_arrays(src_ids, src_ids)
    dec_ids = id_arrays(tgt_ids, tgt_ids)
    cross_ids = id_arrays(tgt_ids, src_ids)

    def scatter(arrays, call_id):
        return Scatter(arrays, row_count, call_id) if near else None

    def tokens(value):
        return value.astype(BF16).reshape(chips, half, width)

    def scatter(arrays, call_id):
        return Scatter(arrays, row_count, call_id) if near else None

    def tokens(value):
        return value.astype(BF16).reshape(chips, half, width)

    if near:
        src_own, place_own = cut(src_ids, core)
        src_oth, place_oth = cut(src_ids, 1 - core)
        tgt_own, tgt_oth = cut(tgt_ids, core)[0], cut(tgt_ids, 1 - core)[0]
        feats = jnp.stack(
            [
                id_columns(src_own, False),
                id_columns(src_own, True),
                id_columns(src_oth, True),
                id_columns(tgt_own, False),
                id_columns(tgt_own, True),
                id_columns(tgt_oth, True),
            ]
        )
        enc_w, dec_w, slope, kept = forward_call(
            shards,
            x,
            place_own[:, None],
            jnp.stack([place_own, place_oth] * 4),
            feats,
        )
        (dec_slope, dec_s, dec_a, dec_y, dec_yr, decoded), (placed,) = tail_call(
            kept[C2],
            (dec_w[1], dec_w[2], dec_w[3]),
            scatter([(grads, Scatter.BRING)], 8),
        )
        cotangent = placed.reshape(length, width)
        encoded_bf = kept[EY].astype(BF16)
    else:
        low, high = x[:, :half], x[:, half:]
        other = swap(pick(high, low))
        source, target, cotangent = spread(
            jnp.stack([pick(low, other), pick(other, high), grads])
        )
        enc_attn, enc_cross, enc_tail_w = unpack(gather_plain(0, shards))
        dec_attn, dec_cross, dec_tail_w = unpack(gather_plain(1, shards))
        enc_mid, enc_self = self_forward(
            source, source.astype(F32), enc_attn, enc_ids, False
        )
        encoded, enc_tail = tail_forward(enc_mid, enc_tail_w)
        encoded_bf = encoded.astype(BF16)
        memory = [project(encoded_bf, enc_cross[:, j]).astype(BF16) for j in range(2)]
        memory_other = swap(jnp.stack(memory))
        mem_keys = (memory[0], memory_other[0], memory[1], memory_other[1])
        dec_mid, dec_self = self_forward(
            target, target.astype(F32), dec_attn, dec_ids, True
        )
        queries = project(dec_mid.astype(BF16), dec_cross[:, 0]).astype(BF16)
        cross_o, cross_lse = attention_forward(
            queries, mem_keys, cross_ids[0], False
        )
        second, second_rstd = norm(dec_mid + unproject(cross_o, dec_cross[:, 1]))
        decoded, dec_tail = tail_forward(second, dec_tail_w)

    if near:

        def heads(q, k, kx, v, vx, o, lse, do):
            flat = kept[lse].reshape(kept[lse].shape[0], -1, length)
            return [kept[n] for n in (q, k, kx, v, vx, o)] + [do, flat]

        def pieces(parts):
            return [v.reshape((chips,) + v.shape[2:]) for v in parts]

        (grad_cross, do), dec_parts, (out_enc,) = tail_back(
            cotangent,
            dec_y,
            dec_yr,
            kept[C2],
            kept[C2R],
            dec_slope,
            (dec_w[1], dec_w[2], dec_w[3]),
            dec_s,
            dec_a,
            dec_w[4],
            1,
            scatter([(tokens(encoded_bf), 0)], 2),
        )
        (dpre, do, grad_encoded), (out_dec,) = attn_back(
            heads(CQ, MK, MKX, MV, MVX, CO, CL, do),
            [feats[3], feats[1], feats[2], *cross_ids[1]],
            False,
            scatter([(tokens(decoded), 1)], 3),
            grad_cross,
            (dec_w[4], enc_w[4]),
            (kept[DH], kept[DR], dec_w[0]),
        )
        (grad_target,), dec_sum = attn_back(
            heads(DQ, DK, DKX, DV, DVX, DO, DL, do),
            [feats[3], feats[4], feats[5], *dec_ids[1]],
            True,
            scatter([(v, 1) for v in pieces(dec_parts)], 4),
            dpre,
            dec_w[0],
        )
        (dpre, do), enc_parts, (moved,) = tail_back(
            grad_encoded,
            kept[EY],
            kept[EYR],
            kept[EH],
            kept[ER],
            slope,
            (enc_w[1], enc_w[2], enc_w[3]),
            kept[ES],
            kept[EA],
            enc_w[0],
            3,
            scatter([(tokens(grad_target), 1)], 5),
        )
        (grad_source,), enc_sum = attn_back(
            heads(EQ, EK, EKX, EV, EVX, EO, EL, do),
            [feats[0], feats[1], feats[2], *enc_ids[1]],
            False,
            scatter([(v, 0) for v in pieces(enc_parts)], 6),
            dpre,
            enc_w[0],
        )
        outs = pick(out_enc, out_dec)
        sums, ends = [
            jnp.sum(pick(a, b).astype(F32), axis=0) for a, b in zip(enc_sum, dec_sum)
        ]
        part_rows = lanes // 4
        ends = jnp.pad(jnp.sum(ends, axis=0), ((0, 0), (0, width - width // 4)))
        mine = jnp.concatenate([sums.reshape(2 * part_rows, width), ends]).astype(BF16)
        (last,), whole = send_call(scatter([(tokens(grad_source), 0)], 7), mine)
        grads = pick(last, moved).astype(F32)
        whole = whole.astype(F32)
        weights = whole[:, : 2 * part_rows].reshape(4, 2, part_rows, width)
        ends = whole[:, 2 * part_rows :, : width // 4]
        return (
            outs.reshape(layer_inputs.shape),
            grads.reshape(layer_inputs.shape),
            weights[:, 0].reshape(lanes, width).T[None],
            ends[0, 1, :lanes][None],
            weights[:, 1].reshape(1, lanes, width),
            ends[:, 0].reshape(1, width),
        )

    grad_second, dec_terms = tail_backward(cotangent.astype(F32), dec_tail, dec_tail_w)
    grad_cross = norm_back(second, second_rstd, grad_second)
    do = project(grad_cross.astype(BF16), dec_cross[:, 1]).astype(BF16)
    dqc, dmk, dmv = attend_back(
        queries, mem_keys, cross_o, do, cross_lse, cross_ids, False
    )
    grad_first = unproject(dqc, dec_cross[:, 0]) + grad_cross
    grad_target = self_backward(grad_first, dec_self, dec_attn, dec_ids, True)

    grad_encoded = unproject(dmk, enc_cross[:, 0]) + unproject(dmv, enc_cross[:, 1])
    grad_mid, enc_terms = tail_backward(grad_encoded, enc_tail, enc_tail_w)
    grad_source = self_backward(grad_mid, enc_self, enc_attn, enc_ids, False)

    has_row = chip < row_count

    def total(enc_term, dec_term):
        enc_term = jnp.where(has_row, enc_term, 0.0).astype(BF16)
        dec_term = jnp.where(has_row, dec_term, 0.0).astype(BF16)
        got = swap(pick(dec_term, enc_term))
        return (pick(enc_term, dec_term).astype(F32) + got.astype(F32)).astype(BF16)

    sums = [total(e, d) for e, d in zip(enc_terms, dec_terms)]
    scattered = [
        lax.psum_scatter(v, TP, scatter_dimension=0, tiled=False) for v in sums[:3]
    ]
    scattered = [lax.psum(v, CTX).astype(F32) for v in scattered]
    bias_sum = lax.psum(sums[3], (CTX, TP)).astype(F32)

    results = jnp.stack(
        [
            encoded_bf,
            decoded.astype(BF16),
            grad_source.astype(BF16),
            grad_target.astype(BF16),
        ]
    )
    placed = collect(results, row_count)

    def join(enc_part, dec_part):
        mine = pick(enc_part, dec_part)
        got = swap(pick(dec_part, enc_part))
        return jnp.concatenate([pick(mine, got), pick(got, mine)], axis=1)

    outs = join(placed[0], placed[1]).reshape(layer_inputs.shape)
    grads = join(placed[2], placed[3]).astype(F32).reshape(layer_inputs.shape)
    return (
        outs,
        grads,
        scattered[0][None],
        scattered[1][None],
        scattered[2].T[None],
        bias_sum[None],
    )


def solution(mesh):
    return jax.shard_map(
        per_device,
        mesh=mesh,
        in_specs=(
            P(SECTION, None, None, (CTX, TP), None),
            P(None, None, (CTX, TP), None),
            P(None, None, CTX),
            P(None, None, CTX),
            P(SECTION, None, None, TP),
            P(SECTION, None, TP),
            P(SECTION, None, None, TP),
            P(SECTION, None, TP),
            P(SECTION, TP, None),
            P(SECTION, None, TP),
            P(SECTION, TP),
            P(SECTION, TP, None),
            P(SECTION, None),
        ),
        out_specs=(
            P(SECTION, None, None, (CTX, TP), None),
            P(SECTION, None, None, (CTX, TP), None),
            P(SECTION, None, TP),
            P(SECTION, TP),
            P(SECTION, TP, None),
            P(SECTION, None),
        ),
        check_vma=False,
    )
```

```python
import functools

import jax
import jax.numpy as jnp
from jax import lax
from jax.experimental import pallas as pl
from jax.experimental.pallas import tpu as pltpu
from jax.sharding import PartitionSpec as P

HEAD = 64
SCALE = HEAD**-0.5
EPS = 1e-05
MASKED = -1e30
F32 = jnp.float32
BF16 = jnp.bfloat16
SECTION, CTX, TP = "section", "ctx", "tp"


def swap(value):
    return lax.ppermute(value, SECTION, [(0, 1), (1, 0)])


def remote(src, dst, send, recv, where):
    return pltpu.make_async_remote_copy(
        src_ref=src,
        dst_ref=dst,
        send_sem=send,
        recv_sem=recv,
        device_id=where,
        device_id_type=pl.DeviceIdType.MESH,
    )


def device_of(section, chip):
    return (section, chip // 4, lax.rem(chip, 4))


def greet_all():
    s = lax.axis_index(SECTION)
    chip = lax.axis_index(CTX) * 4 + lax.axis_index(TP)
    barrier = pltpu.get_barrier_semaphore()
    for core in (0, 1):
        for i in range(core, 16):
            pl.semaphore_signal(
                barrier,
                1,
                device_id=device_of(lax.rem(s + 1 - core, 2), lax.rem(chip + i, 16)),
                device_id_type=pl.DeviceIdType.MESH,
            )
    pl.semaphore_wait(barrier, 31)


class Scatter:
    BRING = 2

    def __init__(self, arrays, rows, call_id):
        self.inputs = [a for a, _ in arrays]
        self.kinds = [k for _, k in arrays]
        self.rows = rows
        self.call_id = call_id
        self.shapes = [
            jax.ShapeDtypeStruct(
                ((16,) if k == self.BRING else (rows, 2)) + a.shape[1:], a.dtype
            )
            for a, k in arrays
        ]
        count = len(arrays)
        self.scratch = [
            pltpu.SemaphoreType.DMA((count, 16)),
            pltpu.SemaphoreType.DMA((count, 16, 2)),
        ]

    def sends(self, ins, outs, sems):
        send, recv = sems
        s = lax.axis_index(SECTION)
        chip = lax.axis_index(CTX) * 4 + lax.axis_index(TP)
        for a, kind in enumerate(self.kinds):
            for i in range(16):
                p = lax.rem(chip + i, 16)
                if kind == self.BRING:
                    ready = p < self.rows
                    src = ins[a].at[jnp.minimum(p, self.rows - 1)]
                    dst = outs[a].at[chip]
                    core, mark = s, 0
                    stays = True
                else:
                    ready = chip < self.rows
                    src = ins[a].at[p]
                    dst = outs[a].at[jnp.minimum(chip, self.rows - 1), s]
                    core, mark = kind, s
                    stays = s == kind
                near = pltpu.make_async_copy(src, dst, send.at[a, i])
                far = remote(
                    src, dst, send.at[a, i], recv.at[a, i, mark], device_of(core, p)
                )
                yield i, ready, stays, near, far

    def start(self, ins, outs, sems):
        greet_all()
        for i, ready, stays, near, far in self.sends(ins, outs, sems):

            @pl.when(ready)
            def _():
                if i:
                    far.start()
                elif stays is True:
                    near.start()
                else:
                    pl.when(stays)(near.start)
                    pl.when(jnp.logical_not(stays))(far.start)

    def finish(self, ins, outs, sems):
        send, recv = sems
        s = lax.axis_index(SECTION)
        chip = lax.axis_index(CTX) * 4 + lax.axis_index(TP)
        for i, ready, stays, near, far in self.sends(ins, outs, sems):

            @pl.when(ready)
            def _():
                if i:
                    far.wait_send()
                elif stays is True:
                    near.wait()
                else:
                    pl.when(stays)(near.wait)
                    pl.when(jnp.logical_not(stays))(far.wait_send)

        def got(region, sem):
            remote(region, region, send.at[0, 0], sem, (1 - s, 0, 0)).wait_recv()

        for a, kind in enumerate(self.kinds):
            for i in range(16):
                sender = lax.rem(chip + 16 - i, 16)
                if kind == self.BRING:
                    if i:

                        @pl.when(chip < self.rows)
                        def _():
                            got(outs[a].at[sender], recv.at[a, i, 0])

                    continue

                @pl.when((s == kind) & (sender < self.rows))
                def _():
                    for core in (0, 1) if i else (1 - kind,):
                        region = outs[a].at[jnp.minimum(sender, self.rows - 1), core]
                        got(region, recv.at[a, i, core])


def send_kernel(rider, *refs):
    n = len(rider.inputs)
    block_in, (own, spread_out) = refs[n], (refs[n], refs[2 * n + 1])
    ins, outs = refs[:n], refs[n + 1 : 2 * n + 1]
    sems = refs[2 * n + 2 : 2 * n + 4]
    b_send, b_recv = refs[2 * n + 4 :]
    rider.start(ins, outs, sems)
    s = lax.axis_index(SECTION)
    c = lax.axis_index(CTX)
    t = lax.axis_index(TP)
    dst = spread_out.at[c]
    keep = pltpu.make_async_copy(own, dst, b_send.at[0])
    keep.start()
    ways = [
        remote(own, dst, b_send.at[j], b_recv.at[j], (s, lax.rem(c + j, 4), t))
        for j in (1, 2, 3)
    ]
    for way in ways:
        way.start()
    keep.wait()
    for j, way in enumerate(ways):
        way.wait_send()
        region = spread_out.at[lax.rem(c + 3 - j, 4)]
        remote(region, region, b_send.at[0], b_recv.at[j + 1], (s, c, t)).wait_recv()
    rider.finish(ins, outs, sems)


def send_call(rider, block):
    anywhere = pl.BlockSpec(memory_space=pl.ANY)
    count = len(rider.inputs)
    result = pl.pallas_call(
        functools.partial(send_kernel, rider),
        in_specs=[anywhere] * (count + 1),
        out_specs=[anywhere] * (count + 1),
        out_shape=rider.shapes + [jax.ShapeDtypeStruct((4,) + block.shape, block.dtype)],
        scratch_shapes=rider.scratch
        + [pltpu.SemaphoreType.DMA((4,)), pltpu.SemaphoreType.DMA((4,))],
        compiler_params=pltpu.CompilerParams(
            collective_id=rider.call_id, has_side_effects=True
        ),
        name="send_last",
    )(*rider.inputs, block)
    return result[:count], result[count]


def dot_nt(left, right, **kw):
    return lax.dot_general(
        left, right, (((1,), (1,)), ((), ())), preferred_element_type=F32, **kw
    )


def dot_nn(left, right):
    return lax.dot_general(
        left, right, (((1,), (0,)), ((), ())), preferred_element_type=F32
    )


def dot_tn(left, right):
    return lax.dot_general(
        left, right, (((0,), (0,)), ((), ())), preferred_element_type=F32
    )


def attn_fwd_kernel(
    causal, q_ref, ko_ref, kx_ref, vo_ref, vx_ref, fq, fo, fx, qi_ref, ki_ref, o_ref, lse_ref
):
    for pair in range(lse_ref.shape[1]):
        attend_pair(
            0,
            pair,
            q_ref,
            (ko_ref, kx_ref),
            (vo_ref, vx_ref),
            o_ref,
            lse_ref,
            (fq, fo, fx),
            (qi_ref[:, 1:2], (ki_ref[1:2, :], ki_ref[3:4, :])),
            causal,
        )


def attention_call(kernel, name, causal, blocks, small, outs):
    def group_spec(v):
        return pl.BlockSpec((1,) + v.shape[1:], lambda t: (t,) + (0,) * (len(v.shape) - 1))

    return pl.pallas_call(
        functools.partial(kernel, causal),
        grid=(blocks[0].shape[0],),
        in_specs=[group_spec(v) for v in blocks]
        + [pl.BlockSpec(v.shape, lambda t: (0, 0)) for v in small],
        out_specs=[group_spec(v) for v in outs],
        out_shape=outs,
        compiler_params=pltpu.CompilerParams(vmem_limit_bytes=48 * 2**20),
        name=name,
    )(*blocks, *small)


def id_columns(ids, keys):
    lane = jnp.arange(2 * HEAD, dtype=jnp.int32)[None] % HEAD
    same = ids[:, None] == lane
    value = jnp.where(same, 1.0, 0.0) if keys else jnp.where(same, 0.0, MASKED)
    return jnp.where(lane < 4, value, 0.0).astype(BF16)


def attention_forward(q, keys, ids, causal):
    groups, length, width = q.shape
    pairs = width // HEAD // 2
    outs = [
        jax.ShapeDtypeStruct(q.shape, BF16),
        jax.ShapeDtypeStruct((groups, pairs, 2, length), F32),
    ]
    feats = [
        id_columns(ids[0][:, 0], False),
        id_columns(ids[1][0], True),
        id_columns(ids[1][2], True),
    ]
    o, lse = attention_call(
        attn_fwd_kernel, "attn_fwd", causal, [q, *keys], [*feats, *ids], outs
    )
    return o, lse.reshape(groups, 2 * pairs, length)


def attend_back_group(ins, dq_out, dk_outs, dv_outs, feats, qi_ref, ki_ref, causal):
    q_ref, k_refs, v_refs, o_ref, do_ref, lse_ref = ins
    length = q_ref.shape[1]
    block = length // 2
    posq = qi_ref[1:2, :]
    ones = jnp.ones((16, 2 * HEAD), BF16)

    def put(out, rows, lanes, value):
        out[0][out[1], rows, lanes] = value.astype(out[0].dtype)

    for pair in range(q_ref.shape[2] // (2 * HEAD)):
        lanes = slice(pair * 2 * HEAD, (pair + 1) * 2 * HEAD)
        q2 = q_ref[0, :, lanes] * jnp.asarray(SCALE, BF16)
        do2 = do_ref[0, :, lanes]
        prod2 = do2.astype(F32) * o_ref[0, :, lanes].astype(F32)
        dq, dk, dv = [None, None], {}, {}
        for j in range(2):
            here = head_mask(length, j)
            q_all = jnp.where(here, q2, feats[0][...])
            q_only = jnp.where(here, q2, jnp.zeros_like(q2))
            do_all = jnp.where(here, do2, jnp.zeros_like(do2))
            prod = jnp.where(here, prod2, 0.0)
            high = prod.astype(BF16)
            rest = (prod - high.astype(F32)).astype(BF16)
            delta = (dot_nt(ones, high) + dot_nt(ones, rest))[0:1]
            lse = lse_ref[0, 2 * pair + j : 2 * pair + j + 1, :]
            for n in range(2):
                for b in range(2):
                    rows = slice(b * block, (b + 1) * block)
                    first = b * block if causal else 0
                    k2 = k_refs[n][0, rows, lanes]
                    there = head_mask(block, j)
                    k = jnp.where(there, k2, feats[1 + n][rows])
                    k_only = jnp.where(there, k2, jnp.zeros_like(k2))
                    s = dot_nt(k, q_all[first:])
                    p = jnp.exp(s - lse[:, first:])
                    if causal:
                        ok = posq[:, first:] >= ki_ref[rows, 2 * n + 1 : 2 * n + 2]
                        p = jnp.where(ok, p, 0.0)
                    dp = dot_nt(v_refs[n][0, rows, lanes], do_all[first:])
                    ds = (p * (dp - delta[:, first:])).astype(BF16)
                    add = lambda old, new: new if old is None else old + new
                    dv[n, b] = add(
                        dv.get((n, b)), dot_nn(p.astype(BF16), do_all[first:])
                    )
                    dk[n, b] = add(dk.get((n, b)), dot_nn(ds, q_only[first:]))
                    part = dot_tn(k_only, ds)
                    if not first:
                        dq[0] = add(dq[0], part[:, :block])
                    dq[1] = add(dq[1], part[:, block - first :])
        for n in range(2):
            for b in range(2):
                rows = slice(b * block, (b + 1) * block)
                put(dv_outs[n], rows, lanes, dv[n, b])
                put(dk_outs[n], rows, lanes, dk[n, b])
        for b in range(2):
            put(dq_out, slice(b * block, (b + 1) * block), lanes, (dq[b] * SCALE).T)


def attn_bwd_kernel(
    causal,
    q_ref,
    ko_ref,
    kx_ref,
    vo_ref,
    vx_ref,
    o_ref,
    do_ref,
    lse_ref,
    fq,
    fo,
    fx,
    qi_ref,
    ki_ref,
    dq_ref,
    dko_ref,
    dkx_ref,
    dvo_ref,
    dvx_ref,
):
    attend_back_group(
        (q_ref, (ko_ref, kx_ref), (vo_ref, vx_ref), o_ref, do_ref, lse_ref),
        (dq_ref, 0),
        ((dko_ref, 0), (dkx_ref, 0)),
        ((dvo_ref, 0), (dvx_ref, 0)),
        (fq, fo, fx),
        qi_ref,
        ki_ref,
        causal,
    )


def back_feats(ids):
    return [
        id_columns(ids[0][0], False),
        id_columns(ids[1][:, 0], True),
        id_columns(ids[1][:, 2], True),
    ]


def attention_backward(q, keys, o, do, lse, ids, causal):
    outs = [jax.ShapeDtypeStruct(q.shape, BF16)] * 5
    small = [*back_feats(ids), *ids]
    return attention_call(
        attn_bwd_kernel, "attn_bwd", causal, [q, *keys, o, do, lse], small, outs
    )


def norm(value):
    mean = jnp.mean(value, axis=-1, keepdims=True)
    centered = value - mean
    rstd = lax.rsqrt(jnp.mean(centered * centered, axis=-1, keepdims=True) + EPS)
    return centered * rstd, rstd


def norm_back(normed, rstd, grad):
    return rstd * (
        grad
        - jnp.mean(grad, axis=-1, keepdims=True)
        - normed * jnp.mean(grad * normed, axis=-1, keepdims=True)
    )


def project(rows, weight):
    return jnp.einsum("pk,tkm->tpm", rows, weight, preferred_element_type=F32)


def unproject(blocks, weight):
    return jnp.einsum("tpm,tkm->pk", blocks, weight, preferred_element_type=F32)


def self_forward(rows_bf, rows, w_attn, ids, causal):
    kv = [project(rows_bf, w_attn[:, j]).astype(BF16) for j in (1, 2)]
    other = swap(jnp.stack(kv))
    q = project(rows_bf, w_attn[:, 0]).astype(BF16)
    keys = (kv[0], other[0], kv[1], other[1])
    o, lse = attention_forward(q, keys, ids[0], causal)
    h, rstd = norm(rows + unproject(o, w_attn[:, 3]))
    return h, (q, keys, o, lse, h, rstd)


def attend_back(q, keys, o, do, lse, ids, causal):
    dq, dko, dkx, dvo, dvx = attention_backward(q, keys, o, do, lse, ids[1], causal)
    other = swap(jnp.stack([dkx, dvx])).astype(F32)
    dk = (dko.astype(F32) + other[0]).astype(BF16)
    dv = (dvo.astype(F32) + other[1]).astype(BF16)
    return dq, dk, dv


def self_backward(grad, kept, w_attn, ids, causal):
    q, keys, o, lse, h, rstd = kept
    dpre = norm_back(h, rstd, grad)
    do = project(dpre.astype(BF16), w_attn[:, 3]).astype(BF16)
    dq, dk, dv = attend_back(q, keys, o, do, lse, ids, causal)
    return (
        unproject(dq, w_attn[:, 0])
        + unproject(dk, w_attn[:, 1])
        + unproject(dv, w_attn[:, 2])
        + dpre
    )


def tail_forward(h, tail_w):
    w_in, w_out, a_in, b_in, a_out, b_out = tail_w
    rows = h.astype(BF16)
    inner = project(rows, w_in)
    phi = 0.5 * (1.0 + lax.erf(inner * 0.7071067811865476))
    g = (inner * phi).astype(BF16)
    slope = phi + inner * jnp.exp(inner * inner * -0.5) * 0.3989422804014327
    pre = project(rows, a_in) + b_in.astype(F32)[:, None, :]
    sig = jax.nn.sigmoid(pre)
    s = (pre * sig).astype(BF16)
    a_slope = sig * (1.0 + pre * (1.0 - sig))
    total = jnp.einsum("tpm,tmk->pk", g, w_out, preferred_element_type=F32)
    total += 4.0 * (
        jnp.einsum("tpm,tkm->pk", s, a_out, preferred_element_type=F32)
        + b_out.astype(F32)
    )
    y, rstd = norm(h + total)
    return y, (rows, slope.astype(BF16), s, a_slope.astype(BF16), y, rstd)


def tail_backward(grad, kept, tail_w):
    w_in, w_out, a_in, b_in, a_out, b_out = tail_w
    rows, slope, s, a_slope, y, rstd = kept
    dpre = norm_back(y, rstd, grad)
    db = dpre.astype(BF16)
    dg = jnp.einsum("pk,tmk->tpm", db, w_out, preferred_element_type=F32)
    df = (dg * slope.astype(F32)).astype(BF16)
    ds = 4.0 * jnp.einsum("pk,tkm->tpm", db, a_out, preferred_element_type=F32)
    du = (ds * a_slope.astype(F32)).astype(BF16)
    terms = (
        jnp.einsum("pk,tpm->tkm", rows, du, preferred_element_type=F32),
        jnp.sum(du.astype(F32), axis=1),
        4.0 * jnp.einsum("pk,tpm->tkm", db, s, preferred_element_type=F32),
        4.0 * jnp.sum(db.astype(F32), axis=0),
    )
    return unproject(df, w_in) + unproject(du, a_in) + dpre, terms


def head_mask(rows, j):
    lane = lax.broadcasted_iota(jnp.int32, (rows, 2 * HEAD), 1)
    return (lane < HEAD) if j == 0 else (lane >= HEAD)


def attend_pair(t, pair, q_ref, k_refs, v_refs, o_ref, lse_ref, feats, places, causal):
    length = q_ref.shape[1]
    block = length // 2
    lanes = pl.ds(pl.multiple_of(pair * 2 * HEAD, 2 * HEAD), 2 * HEAD)
    posq, posk = places
    for b in range(2):
        rows = slice(b * block, (b + 1) * block)
        q2 = q_ref[t, rows, lanes] * jnp.asarray(SCALE, BF16)
        cuts = [(n, a) for n in range(2) for a in range(b + 1 if causal else 2)]
        outs = []
        for j in range(2):
            q = jnp.where(head_mask(block, j), q2, feats[0][rows])
            parts = []
            for n, a in cuts:
                span = slice(a * block, (a + 1) * block)
                k = jnp.where(
                    head_mask(block, j), k_refs[n][t, span, lanes], feats[1 + n][span]
                )
                s = dot_nt(q, k)
                if causal and a == b:
                    s = jnp.where(posq[rows] >= posk[n][:, span], s, MASKED)
                parts.append(s)
            top = functools.reduce(
                jnp.maximum, [jnp.max(s, axis=1, keepdims=True) for s in parts]
            )
            ex = [jnp.exp(s - top) for s in parts]
            total = sum(jnp.sum(e, axis=1, keepdims=True) for e in ex)
            out = sum(
                dot_nn(
                    e.astype(BF16), v_refs[n][t, a * block : (a + 1) * block, lanes]
                )
                for e, (n, a) in zip(ex, cuts)
            )
            outs.append(out / total)
            lse = top + jnp.log(total)
            lse_ref[t, pair, j : j + 1, rows] = jnp.broadcast_to(lse, (block, 128)).T[
                0:1
            ]
        o_ref[t, rows, lanes] = jnp.where(head_mask(block, 0), *outs).astype(BF16)


ATTN, FFN_IN, FFN_OUT, ADAPTER, CROSS = range(5)
ORDER = (
    (0, ATTN),
    (1, ATTN),
    (0, FFN_IN),
    (0, FFN_OUT),
    (0, ADAPTER),
    (0, CROSS),
    (1, CROSS),
    (1, FFN_IN),
    (1, FFN_OUT),
    (1, ADAPTER),
)
(
    ENC_QKV,
    ENC_ATTN,
    ENC_OUT,
    DEC_QKV,
    DEC_ATTN,
    DEC_OUT,
    HIDDEN,
    GATED,
    MEMORY,
    CROSS_Q,
    CROSS_ATTN,
    CROSS_OUT,
    END,
) = range(13)
WORK = (
    (ENC_QKV, 4, (0, ATTN), 2.0),
    (ENC_ATTN, 8, None, 2.3),
    (ENC_OUT, 1, None, 4.0),
    (DEC_QKV, 4, (1, ATTN), 2.0),
    (DEC_ATTN, 8, None, 2.1),
    (DEC_OUT, 1, None, 4.0),
    (HIDDEN, 8, (0, FFN_OUT), 2.5),
    (GATED, 1, (0, ADAPTER), 4.0),
    (MEMORY, 4, (0, CROSS), 1.5),
    (CROSS_Q, 1, (1, CROSS), 4.0),
    (CROSS_ATTN, 8, None, 2.3),
    (CROSS_OUT, 1, None, 4.0),
    (END, 1, (1, ADAPTER), 0.0),
)


LAG = 2


def plan_steps(sizes):
    ready, clock = [], 20.0
    for e, g in ORDER:
        for _ in range(3):
            clock += sizes[g] / 3 * 11e-6
            ready.append(clock)
    ticks = len(ready) + 2 * LAG
    ready += [clock + 4 * n for n in range(1, 2 * LAG + 1)]
    starts, at, step, now, done = {}, {}, 0, 0.0, 0
    for name, count, need, cost in WORK:
        starts[name] = step
        for n in range(count):
            while done < ticks and (
                ready[done] <= now
                or (need and done <= 3 * ORDER.index(need) + 2 + 2 * LAG)
            ):
                at[done] = step
                now = max(now, ready[done])
                done += 1
            now += cost
            step += 1
    for n in range(done, ticks):
        at[n] = step - 1
    return starts, at, step


HEADS, LSE, WIDE, RSTD, LANES = range(5)
(
    EQ,
    EK,
    EKX,
    EV,
    EVX,
    EO,
    EL,
    EH,
    ER,
    ES,
    EA,
    EY,
    EYR,
    DQ,
    DK,
    DKX,
    DV,
    DVX,
    DO,
    DL,
    DH,
    DR,
    MK,
    MKX,
    MV,
    MVX,
    CQ,
    CO,
    CL,
    C2,
    C2R,
) = range(31)
KEPT = {
    EQ: HEADS,
    EK: HEADS,
    EKX: HEADS,
    EV: HEADS,
    EVX: HEADS,
    EO: HEADS,
    EL: LSE,
    EH: WIDE,
    ER: RSTD,
    ES: LANES,
    EA: LANES,
    EY: WIDE,
    EYR: RSTD,
    DQ: HEADS,
    DK: HEADS,
    DKX: HEADS,
    DV: HEADS,
    DVX: HEADS,
    DO: HEADS,
    DL: LSE,
    DH: WIDE,
    DR: RSTD,
    MK: HEADS,
    MKX: HEADS,
    MV: HEADS,
    MVX: HEADS,
    CQ: HEADS,
    CO: HEADS,
    CL: LSE,
    C2: WIDE,
    C2R: RSTD,
}


def forward_kernel(plan, rows, *refs):
    starts, tick_step, steps = plan
    refs = list(refs)

    def take(count):
        got = refs[:count]
        del refs[:count]
        return got

    shards = take(5)
    (tokens,) = take(1)
    col_ref, row_ref, feat_ref = take(3)
    full = (take(5), take(5))
    (slope_out,) = take(1)
    kept_out = take(len(KEPT))
    kept = take(len(KEPT))
    xs = take(2)
    wb, wi, wo, wad, slope = take(5)
    store_a, store_f = take(2)
    (
        z_send,
        z_recv,
        h_send,
        n_send,
        n_recv,
        f_send,
        f_recv,
        s_send,
        s_recv,
        own_sem,
        t_send,
        t_recv,
        kv_send,
        kv_recv,
        load_sem,
        out_sem,
        slope_sem,
    ) = refs
    step = pl.program_id(0)
    s = lax.axis_index(SECTION)
    c = lax.axis_index(CTX)
    t = lax.axis_index(TP)
    chips = 16
    chip = c * 4 + t
    cx = c + 1 - 2 * lax.rem(c, 2)
    cy = lax.rem(c + 2, 4)
    cd = 3 - c
    sib = (1 - s, c, t)

    inner = (t == 1) | (t == 2)

    def xor(k):
        return {1: t + 1 - 2 * lax.rem(t, 2), 2: 2 - t // 2, 3: 3 - 3 * (t // 2)}[k]

    part = xs[0].shape[1]

    def token_copy(kind, i, h):
        p = lax.rem(chip + i, chips)
        src = tokens.at[jnp.minimum(p, rows - 1), pl.ds(h * part, part)]
        dst = xs[kind].at[chip]
        if i == 0 and h == kind:
            return p, pltpu.make_async_copy(src, dst, t_send.at[kind, 0, h])
        return p, remote(
            src, dst, t_send.at[kind, i, h], t_recv.at[kind, i], device_of(h, p)
        )

    def send_tokens(kind):
        @pl.when(s == kind)
        def _():
            for i in range(chips):
                for h in range(2):
                    p, copy = token_copy(kind, i, h)
                    pl.when(p < rows)(copy.start)

    def got(region, sem):
        remote(region, region, load_sem.at[0], sem, sib).wait_recv()

    def wait_tokens(kind):
        @pl.when(s == kind)
        def _():
            for i in range(chips):
                for h in range(2):
                    p, copy = token_copy(kind, i, h)
                    stays = i == 0 and h == kind
                    pl.when(p < rows)(copy.wait if stays else copy.wait_send)

        @pl.when(chip < rows)
        def _():
            for i in range(chips):
                region = xs[kind].at[lax.rem(chip + chips - i, chips)]
                if i:
                    got(region, t_recv.at[kind, i])
                else:

                    @pl.when(s != kind)
                    def _():
                        got(region, t_recv.at[kind, 0])

    items = [(n, k) for n in range(len(ORDER)) for k in (1, 2, 3)]
    window = 4

    def block(n, who, h, q, u=None):
        e, g = ORDER[n]
        size = shards[g].shape[0]
        start = h * (size // 2) + q * (size // 8)
        length = size // 8
        if u is not None:
            length = size // 16
            start = start + u * length
        return full[e][g].at[who, pl.ds(pl.multiple_of(start, 16), length)]

    def z_copy(n, k, h):
        g = ORDER[n][1]
        size = shards[g].shape[0]
        start = h * (size // 2) + c * (size // 8)
        return remote(
            shards[g].at[pl.ds(pl.multiple_of(start, 16), size // 8)],
            block(n, t, h, c),
            z_send.at[n, k - 1, h],
            z_recv.at[n, k - 1],
            (h, c, xor(1) if k == 1 else jnp.clip(3 - t, 1, 2)),
        )

    def z_forward(n, k):
        src = block(n, xor(k), s, c)
        to = 3 - t if k == 1 else 3 * t - 3
        return remote(
            src,
            src,
            h_send.at[n, k - 1],
            z_recv.at[n, (2, 1, 2)[k - 1]],
            (s, c, jnp.clip(to, 0, 3)),
        )

    def store(g):
        if g in (FFN_IN, FFN_OUT):
            return store_f
        return store_a.at[pl.ds(0, shards[g].shape[0])]

    def fetch(n):
        g = ORDER[n][1]
        return pltpu.make_async_copy(shards[g], store(g), own_sem.at[n, 3])

    def put(n):
        e, g = ORDER[n]
        return pltpu.make_async_copy(store(g), full[e][g].at[t], own_sem.at[n, 0])

    def far(n):
        e, g = ORDER[n]
        return remote(
            shards[g], full[e][g].at[t], own_sem.at[n, 1], own_sem.at[n, 2], sib
        )

    def before(n):
        e, g = ORDER[n]
        pool = (FFN_IN, FFN_OUT) if g in (FFN_IN, FFN_OUT) else (ATTN, ADAPTER, CROSS)
        olds = [m for m in range(n) if ORDER[m][0] == e and ORDER[m][1] in pool]
        return olds[-1] if olds else None

    def start_z(i):
        n, k = items[i]

        @pl.when(s == ORDER[n][0])
        def _():
            if k == 1:
                far(n).start()
            if k < 3:

                @pl.when(inner | (k == 1))
                def _():
                    for h in range(2):
                        z_copy(n, k, h).start()

    def near_copy(n, k, j):
        src = block(n, xor(k), s, c)
        return remote(
            src,
            src,
            n_send.at[n, k - 1, j],
            n_recv.at[n, k - 1, j],
            (s, (cx, cy)[j], t),
        )

    def sibling_copy(n, k, j):
        src = block(n, xor(k), s, (c, cx, cy, cd)[j])
        return remote(src, src, s_send.at[n, k - 1, j], s_recv.at[n, k - 1, j], sib)

    def forward_copy(n, k, j):
        src = block(n, xor(k), s, (cx, cy)[j], j)
        return remote(
            src,
            src,
            f_send.at[n, k - 1, j],
            f_recv.at[n, k - 1, j],
            (s, (cy, cx)[j], t),
        )

    def stage2(i):
        n, k = items[i]
        got(block(n, xor(k), s, c), z_recv.at[n, k - 1])
        pl.when(inner)(z_forward(n, k).start)
        near_copy(n, k, 0).start()
        near_copy(n, k, 1).start()
        sibling_copy(n, k, 0).start()
        if k == 2:
            return

        @pl.when(s == ORDER[n][0])
        def _():
            if k == 1:
                old = before(n)
                if old is not None and not put_read_first(old, i):
                    put(old).wait()
                fetch(n).start()
            else:
                fetch(n).wait()
                put(n).start()

    def stage3(i):
        n, k = items[i]
        for j, q in ((0, cx), (1, cy)):
            got(block(n, xor(k), s, q), n_recv.at[n, k - 1, j])
            forward_copy(n, k, j).start()
            sibling_copy(n, k, j + 1).start()

    def stage4(i):
        n, k = items[i]
        for u in range(2):
            got(block(n, xor(k), s, cd, u), f_recv.at[n, k - 1, u])
        sibling_copy(n, k, 3).start()

    count = len(items)

    def tick(i):
        if i < count:
            stage2(i)
            if i + window < count:
                start_z(i + window)
        if 0 <= i - LAG < count:
            stage3(i - LAG)
        if 0 <= i - 2 * LAG < count:
            stage4(i - 2 * LAG)
        if i == 6:
            send_tokens(1)

    def arrive_step(n):
        for name, _, need, _ in WORK[:-1]:
            if need == ORDER[n]:
                return starts[name]
        return starts[HIDDEN] if ORDER[n] == (0, FFN_IN) else steps - 1

    def put_read_first(n, i):
        return arrive_step(n) < tick_step[i]

    def put_left(n):
        after = [m for m in range(len(ORDER)) if before(m) == n]
        return not after or put_read_first(n, 3 * after[0])

    def arrive(n):
        e, g = ORDER[n]
        for k in (1, 2, 3):
            for j, q in enumerate((c, cx, cy, cd)):
                got(block(n, xor(k), 1 - s, q), s_recv.at[n, k - 1, j])

        @pl.when(s == e)
        def _():
            if put_left(n):
                put(n).wait()

        @pl.when(s != e)
        def _():
            got(full[e][g].at[t], own_sem.at[n, 2])

    @pl.when(step == 0)
    def _():
        greet_all()
        send_tokens(0)
        for i in range(window):
            start_z(i)

    for i in range(count + 2 * LAG):
        pl.when(step == tick_step[i])(functools.partial(tick, i))

    def on(name):
        first = starts[name]
        last = first + [w[1] for w in WORK if w[0] == name][0]
        need = [w[2] for w in WORK if w[0] == name][0]
        if need and name != END:
            pl.when(step == first)(functools.partial(arrive, ORDER.index(need)))
        return step - first, pl.when((step >= first) & (step < last))

    def load(src, dst, slot=0):
        return pltpu.make_async_copy(src, dst, load_sem.at[slot])

    def keep(*names):
        for n in names:
            pltpu.make_async_copy(kept[n], kept_out[n], out_sem.at[n]).start()

    attn_rows = full[0][ATTN].shape[1] // 4

    def kv_copies(which, g, names):
        k, kx, v, vx = names
        return [
            remote(
                kept[a].at[g], kept[b].at[g], kv_send.at[which, g, j], kv_recv.at[which, g, j], sib
            )
            for j, (a, b) in enumerate(((k, kx), (v, vx)))
        ]

    def projections(name, which, e, g_id, x, names):
        i, when = on(name)
        tiles = len(names)
        height = tiles * attn_rows

        def source(j):
            return full[e][g_id].at[j, pl.ds(0, height)]

        @when
        def _():
            slot = lax.rem(i, 2)

            @pl.when(i == 0)
            def _():
                load(source(0), wb.at[0, pl.ds(0, height)]).start()

            load(source(0), wb.at[slot, pl.ds(0, height)]).wait()

            @pl.when(i < 3)
            def _():
                load(source(jnp.minimum(i + 1, 3)), wb.at[1 - slot, pl.ds(0, height)]).start()

            rows_in = x()
            for n, name_out in enumerate(names):
                w = wb[slot, n * attn_rows : (n + 1) * attn_rows, :]
                kept[name_out][i] = dot_nn(rows_in, w).astype(BF16)
            for copy in kv_copies(which, i, keys_of[which]):
                copy.start()

    keys_of = (
        (EK, EKX, EV, EVX),
        (DK, DKX, DV, DVX),
        (MK, MKX, MV, MVX),
    )

    def attend(name, which, q, o, lse, feats, causal):
        i, when = on(name)
        k, kx, v, vx = keys_of[which]

        @when
        def _():
            g, pair = i // 2, lax.rem(i, 2)

            @pl.when(pair == 0)
            def _():
                for copy in kv_copies(which, g, keys_of[which]):
                    copy.wait_send()
                    copy.wait_recv()

            attend_pair(
                g,
                pair,
                kept[q],
                (kept[k], kept[kx]),
                (kept[v], kept[vx]),
                kept[o],
                kept[lse],
                [feat_ref.at[f] for f in feats],
                (col_ref[...], (row_ref[0:1, :], row_ref[1:2, :])),
                causal,
            )

            @pl.when(i == 7)
            def _():
                keep(q, k, kx, v, vx, o, lse)

    def tiles4(e, g_id, first_row):
        copies = [
            load(
                full[e][g_id].at[j, pl.ds(first_row, attn_rows)],
                wb.at[0, pl.ds(j * attn_rows, attn_rows)],
                j,
            )
            for j in range(4)
        ]
        for copy in copies:
            copy.start()
        for copy in copies:
            copy.wait()

    def out_norm(name, e, g_id, first_row, residual, source, wide, rstd_name):
        _, when = on(name)

        @when
        def _():
            tiles4(e, g_id, first_row)
            total = residual()
            for j in range(4):
                total = total + dot_nt(
                    kept[source][j], wb[0, j * attn_rows : (j + 1) * attn_rows, :]
                )
            normed, rstd = norm(total)
            kept[wide][...] = normed
            kept[rstd_name][...] = jnp.broadcast_to(rstd, kept[rstd_name].shape)
            keep(wide, rstd_name)

    def flat_x(n):
        shape = xs[n].shape
        return xs[n][...].reshape(shape[0] * shape[1], shape[2])

    blocks = (
        (ENC_QKV, ENC_ATTN, ENC_OUT, EQ, EK, EV, EO, EL, EH, ER, (0, 1, 2)),
        (DEC_QKV, DEC_ATTN, DEC_OUT, DQ, DK, DV, DO, DL, DH, DR, (3, 4, 5)),
    )
    for e, (qkv, attn, out, q, k, v, o, lse, h, r, feats) in enumerate(blocks):
        pl.when(step == starts[qkv])(functools.partial(wait_tokens, e))
        projections(qkv, e, e, ATTN, functools.partial(flat_x, e), (q, k, v))
        attend(attn, e, q, o, lse, feats, e == 1)
        residual = lambda e=e: flat_x(e).astype(F32)
        out_norm(out, e, ATTN, 3 * attn_rows, residual, o, h, r)

    i, when = on(HIDDEN)
    hidden = wi.shape[2]

    @pl.when(step == starts[HIDDEN])
    def _():
        arrive(ORDER.index((0, FFN_IN)))

    def ffn_loads(j, slot):
        g, u = j // 2, lax.rem(j, 2)
        span = pl.ds(pl.multiple_of(u * hidden, 128), hidden)
        return (
            load(full[0][FFN_IN].at[g, :, span], wi.at[slot], 2 * slot),
            load(full[0][FFN_OUT].at[g, span], wo.at[slot], 2 * slot + 1),
        )

    def slope_copy(j, slot):
        g, u = j // 2, lax.rem(j, 2)
        span = pl.ds(pl.multiple_of(u * hidden, 128), hidden)
        return pltpu.make_async_copy(
            slope.at[slot], slope_out.at[g, :, span], slope_sem.at[slot]
        )

    @when
    def _():
        slot = lax.rem(i, 2)

        @pl.when(i == 0)
        def _():
            for copy in ffn_loads(0, 0):
                copy.start()
            kept[EY][...] = jnp.zeros_like(kept[EY])

        for copy in ffn_loads(i, slot):
            copy.wait()

        @pl.when(i < 7)
        def _():
            for copy in ffn_loads(i + 1, 1 - slot):
                copy.start()

        @pl.when(i >= 2)
        def _():
            slope_copy(i - 2, slot).wait()

        inner = dot_nn(kept[EH][...].astype(BF16), wi[slot])
        phi = 0.5 * (1.0 + lax.erf(inner * 0.7071067811865476))
        slope[slot] = (
            phi + inner * jnp.exp(inner * inner * -0.5) * 0.3989422804014327
        ).astype(BF16)
        slope_copy(i, slot).start()
        kept[EY][...] += dot_nn((inner * phi).astype(BF16), wo[slot])

    i, when = on(GATED)

    @when
    def _():
        for j in range(2):
            slope_copy(6 + j, j).wait()
        copy = load(full[0][ADAPTER], wad)
        copy.start()
        copy.wait()
        h = kept[EH][...]
        rows_in = h.astype(BF16)
        lanes = wad.shape[2] // 2
        extra = wad[0, attn_rows : attn_rows + 16, :].astype(F32)
        last = jnp.concatenate([extra[1 + r : 2 + r] for r in range(4)], axis=1)
        total = 4.0 * last
        for j in range(4):
            bias = wad[j, attn_rows : attn_rows + 16, :lanes].astype(F32)[0:1]
            pre = dot_nn(rows_in, wad[j, :attn_rows, :lanes]) + bias
            sig = 1.0 / (1.0 + jnp.exp(-pre))
            gated = (pre * sig).astype(BF16)
            kept[ES][j] = gated
            kept[EA][j] = (sig * (1.0 + pre * (1.0 - sig))).astype(BF16)
            total = total + 4.0 * dot_nt(gated, wad[j, :attn_rows, lanes:])
        normed, rstd = norm(h + (kept[EY][...] + total))
        kept[EY][...] = normed
        kept[EYR][...] = jnp.broadcast_to(rstd, kept[EYR].shape)
        keep(ES, EA, EY, EYR)

    projections(MEMORY, 2, 0, CROSS, lambda: kept[EY][...].astype(BF16), (MK, MV))
    _, when = on(CROSS_Q)

    @when
    def _():
        tiles4(1, CROSS, 0)
        rows_in = kept[DH][...].astype(BF16)
        for j in range(4):
            kept[CQ][j] = dot_nn(
                rows_in, wb[0, j * attn_rows : (j + 1) * attn_rows, :]
            ).astype(BF16)

    attend(CROSS_ATTN, 2, CQ, CO, CL, (3, 1, 2), False)
    out_norm(CROSS_OUT, 1, CROSS, attn_rows, lambda: kept[DH][...], CO, C2, C2R)

    @pl.when(step == steps - 1)
    def _():
        for g in (FFN_IN, FFN_OUT, ADAPTER):
            arrive(ORDER.index((1, g)))
        for n, k in items:
            pl.when(inner)(z_forward(n, k).wait_send)
            for j in range(2):
                near_copy(n, k, j).wait_send()
                forward_copy(n, k, j).wait_send()
            for j in range(4):
                sibling_copy(n, k, j).wait_send()
        for n in range(len(ORDER)):

            @pl.when(s == ORDER[n][0])
            def _():
                far(n).wait_send()
                for h in range(2):
                    z_copy(n, 1, h).wait_send()
                    pl.when(inner)(z_copy(n, 2, h).wait_send)

        for n in KEPT:
            pltpu.make_async_copy(kept[n], kept_out[n], out_sem.at[n]).wait()


def forward_call(shards, tokens, col, row, feats):
    rows, part, width = tokens.shape
    part //= 2
    length = 16 * part
    groups = len(ORDER)
    dma = pltpu.SemaphoreType.DMA
    anywhere = pl.BlockSpec(memory_space=pl.ANY)
    cols = shards[ATTN].shape[1]
    shapes = (
        ((4, length, cols), BF16),
        ((4, cols // HEAD // 2, 2, length), F32),
        ((length, width), F32),
        ((length, 128), F32),
        ((4, length, shards[ADAPTER].shape[1] // 2), BF16),
    )
    kept = [shapes[kind] for kind in KEPT.values()]
    hidden = shards[FFN_IN].shape[1]
    sizes = [
        (groups, 2, 2),
        (groups, 3),
        (groups, 3),
        (groups, 3, 2),
        (groups, 3, 2),
        (groups, 3, 2),
        (groups, 3, 2),
        (groups, 3, 4),
        (groups, 3, 4),
        (groups, 4),
        (2, 16, 2),
        (2, 16),
        (3, 4, 2),
        (3, 4, 2),
        (4,),
        (len(KEPT),),
        (2,),
    ]
    plan = plan_steps([v.size * 2 for v in shards])
    result = pl.pallas_call(
        functools.partial(forward_kernel, plan, rows),
        grid=(plan[2],),
        in_specs=[anywhere] * 6
        + [
            pl.BlockSpec(col.shape, lambda i: (0, 0)),
            pl.BlockSpec(row.shape, lambda i: (0, 0)),
            pl.BlockSpec(feats.shape, lambda i: (0, 0, 0)),
        ],
        out_specs=[anywhere] * (11 + len(KEPT)),
        out_shape=[jax.ShapeDtypeStruct((4,) + v.shape, v.dtype) for v in shards] * 2
        + [jax.ShapeDtypeStruct((4, length, hidden), BF16)]
        + [jax.ShapeDtypeStruct(*v) for v in kept],
        scratch_shapes=[pltpu.VMEM(*v) for v in kept]
        + [pltpu.VMEM((16, part, width), BF16)] * 2
        + [
            pltpu.VMEM((2,) + shards[ATTN].shape, BF16),
            pltpu.VMEM((2, width, hidden // 2), BF16),
            pltpu.VMEM((2, hidden // 2, width), BF16),
            pltpu.VMEM((4,) + shards[ADAPTER].shape, BF16),
            pltpu.VMEM((2, length, hidden // 2), BF16),
            pltpu.VMEM(shards[ATTN].shape, BF16),
            pltpu.VMEM(shards[FFN_IN].shape, BF16),
        ]
        + [dma(size) for size in sizes],
        compiler_params=pltpu.CompilerParams(
            collective_id=0, has_side_effects=True, vmem_limit_bytes=60 * 2**20
        ),
        name="forward",
    )(*shards, tokens, col, row, feats)
    return result[:5], result[5:10], result[10], result[11:]


def ids_kernel(ids, out, send, recv):
    s = lax.axis_index(SECTION)
    c = lax.axis_index(CTX)
    t = lax.axis_index(TP)
    barrier = pltpu.get_barrier_semaphore()
    for j in (1, 2, 3):
        pl.semaphore_signal(
            barrier,
            1,
            device_id=(s, lax.rem(c + j, 4), t),
            device_id_type=pl.DeviceIdType.MESH,
        )
    pl.semaphore_wait(barrier, 3)
    out[c] = ids[...]
    ways = [
        remote(ids, out.at[c], send.at[j - 1], recv.at[j - 1], (s, lax.rem(c + j, 4), t))
        for j in (1, 2, 3)
    ]
    for way in ways:
        way.start()
    for j, way in enumerate(ways):
        way.wait_send()
        region = out.at[lax.rem(c + 3 - j, 4)]
        remote(region, region, send.at[j], recv.at[j], (s, c, t)).wait_recv()


def ids_call(ids):
    spec = pl.BlockSpec(memory_space=pltpu.VMEM)
    return pl.pallas_call(
        ids_kernel,
        in_specs=[spec],
        out_specs=spec,
        out_shape=jax.ShapeDtypeStruct((4,) + ids.shape, ids.dtype),
        scratch_shapes=[pltpu.SemaphoreType.DMA((3,)), pltpu.SemaphoreType.DMA((3,))],
        compiler_params=pltpu.CompilerParams(collective_id=1, has_side_effects=True),
        name="ids",
    )(ids)


SPLIT = 1


def tail_kernel(rider, *refs):
    refs = list(refs)

    def take(count):
        got = refs[:count]
        del refs[:count]
        return got

    h_ref, w_in_ref, w_out_ref, adapter_ref = take(4)
    ride_ins = take(len(rider.inputs))
    slope_ref, s_ref, a_ref, y_ref, yr_ref, out_ref = take(6)
    ride = (ride_ins, take(len(rider.inputs)), take(len(rider.scratch)))
    rows_in, acc = refs
    step = pl.program_id(0)
    width = acc.shape[1]
    lanes = adapter_ref.shape[2] // 2

    @pl.when(step == 0)
    def _():
        rider.start(*ride)
        extra = adapter_ref[0, width : width + 16, :].astype(F32)
        cuts = width // adapter_ref.shape[2]
        last = jnp.concatenate([extra[1 + r : 2 + r] for r in range(cuts)], axis=1)
        acc[...] = h_ref[...] + 4.0 * last
        rows_in[...] = h_ref[...].astype(BF16)

    @pl.when(step < 4)
    def _():
        bias = adapter_ref[0, width : width + 16, :lanes].astype(F32)[0:1]
        pre = dot_nn(rows_in[...], adapter_ref[0, :width, :lanes]) + bias
        sig = 1.0 / (1.0 + jnp.exp(-pre))
        gated = (pre * sig).astype(BF16)
        s_ref[0] = gated
        a_ref[0] = (sig * (1.0 + pre * (1.0 - sig))).astype(BF16)
        acc[...] += 4.0 * dot_nt(gated, adapter_ref[0, :width, lanes:])

    @pl.when((step >= 4) & (step < 4 + 4 * SPLIT))
    def _():
        inner = dot_nn(rows_in[...], w_in_ref[0])
        phi = 0.5 * (1.0 + lax.erf(inner * 0.7071067811865476))
        slope_ref[0] = (
            phi + inner * jnp.exp(inner * inner * -0.5) * 0.3989422804014327
        ).astype(BF16)
        acc[...] += dot_nn((inner * phi).astype(BF16), w_out_ref[0])

    @pl.when(step == 4 + 4 * SPLIT)
    def _():
        normed, rstd = norm(acc[...])
        y_ref[...] = normed
        yr_ref[...] = jnp.broadcast_to(rstd, yr_ref.shape)
        out_ref[...] = normed.astype(BF16)
        rider.finish(*ride)


def tail_call(h, tail_w, rider):
    w_in, w_out, adapter = tail_w
    length, width = h.shape
    groups, _, hidden = w_in.shape
    lanes = adapter.shape[2] // 2
    anywhere = pl.BlockSpec(memory_space=pl.ANY)

    def tile(j):
        j = jnp.clip(j - groups, 0, groups * SPLIT - 1)
        return j // SPLIT, lax.rem(j, SPLIT)

    def group(j):
        return jnp.minimum(j, groups - 1)

    wide = pl.BlockSpec((length, width), lambda j: (0, 0))
    gated = pl.BlockSpec((1, length, lanes), lambda j: (group(j), 0, 0))
    cut = lambda rows: pl.BlockSpec(
        (1, rows, hidden // SPLIT), lambda j: (tile(j)[0], 0, tile(j)[1])
    )
    result = pl.pallas_call(
        functools.partial(tail_kernel, rider),
        grid=(groups * (1 + SPLIT) + 1,),
        in_specs=[
            wide,
            cut(width),
            pl.BlockSpec((1, hidden // SPLIT, width), lambda j: (tile(j)[0], tile(j)[1], 0)),
            pl.BlockSpec((1,) + adapter.shape[1:], lambda j: (group(j), 0, 0)),
        ]
        + [anywhere] * len(rider.inputs),
        out_specs=[
            cut(length),
            gated,
            gated,
            wide,
            pl.BlockSpec((length, 128), lambda j: (0, 0)),
            wide,
        ]
        + [anywhere] * len(rider.inputs),
        out_shape=[
            jax.ShapeDtypeStruct((groups, length, hidden), BF16),
            jax.ShapeDtypeStruct((groups, length, lanes), BF16),
            jax.ShapeDtypeStruct((groups, length, lanes), BF16),
            jax.ShapeDtypeStruct((length, width), F32),
            jax.ShapeDtypeStruct((length, 128), F32),
            jax.ShapeDtypeStruct((length, width), BF16),
        ]
        + rider.shapes,
        scratch_shapes=rider.scratch
        + [pltpu.VMEM((length, width), BF16), pltpu.VMEM((length, width), F32)],
        compiler_params=pltpu.CompilerParams(
            collective_id=rider.call_id, has_side_effects=True, vmem_limit_bytes=60 * 2**20
        ),
        name="tail",
    )(h, w_in, w_out, adapter, *rider.inputs)
    return result[:6], result[6:]


def norm_back_rows(normed, rstd, grad):
    return rstd * (
        grad
        - jnp.mean(grad, axis=-1, keepdims=True)
        - normed * jnp.mean(grad * normed, axis=-1, keepdims=True)
    )


def head_grads(da, w_ref, do_ref):
    for g in range(w_ref.shape[0]):
        do_ref[g] = dot_nn(da, w_ref[g]).astype(BF16)


def sibling_of():
    return (1 - lax.axis_index(SECTION), lax.axis_index(CTX), lax.axis_index(TP))


def tail_back_kernel(rider, *refs):
    refs = list(refs)

    def take(count):
        got = refs[:count]
        del refs[:count]
        return got

    grad_ref, y_ref, yr_ref, h_ref, hr_ref, slope_ref = take(6)
    w_out_ref, w_in_ref, adapter_ref, s_ref, a_ref, w_do_ref = take(6)
    ride_ins = take(len(rider.inputs))
    dpre_ref, do_ref, pieces_ref, tails_ref = take(4)
    ride = (ride_ins, take(len(rider.inputs)), take(len(rider.scratch)))
    db, acc, mine, away, got, send, recv = refs
    step = pl.program_id(0)
    groups = away.shape[0]
    width = acc.shape[1]
    lanes = adapter_ref.shape[2] // 2
    first = lax.axis_index(SECTION) == 0

    def to_sibling(g):
        return remote(
            away.at[g], got.at[g], send.at[g], recv.at[g], sibling_of()
        )

    @pl.when(step == 0)
    def _():
        rider.start(*ride)
        dpre = norm_back_rows(y_ref[...], yr_ref[:, 0:1], grad_ref[...].astype(F32))
        acc[...] = dpre
        db[...] = dpre.astype(BF16)

    @pl.when(step == 0)
    def _():
        branch = db[...]
        rows_in = h_ref[...].astype(BF16)
        beside = lambda r: jnp.concatenate([r[g] for g in range(groups)], axis=1)
        a_in = jnp.concatenate(
            [adapter_ref[g, :width, :lanes] for g in range(groups)], axis=1
        )
        a_out = jnp.concatenate(
            [adapter_ref[g, :width, lanes:] for g in range(groups)], axis=1
        )
        ds = 4.0 * dot_nn(branch, a_out)
        du = (ds * beside(a_ref).astype(F32)).astype(BF16)
        acc[...] += dot_nt(du, a_in)
        d_in = dot_tn(du, rows_in)
        d_out = 4.0 * dot_tn(beside(s_ref), branch)
        last = 4.0 * jnp.sum(branch.astype(F32), axis=0, keepdims=True)
        bias = jnp.sum(du.astype(F32), axis=0, keepdims=True)
        cut = width // 4
        blank = jnp.zeros((1, cut - lanes), F32)
        row = lax.broadcasted_iota(jnp.int32, (16, cut), 0)
        part = lanes // 4
        for g in range(groups):
            own = bias[:, g * lanes : (g + 1) * lanes]
            second = jnp.where(row == 1, jnp.concatenate([own, blank], axis=1), 0.0)
            for c in range(4):
                start = g * lanes + c * part
                one = d_in[start : start + part]
                two = d_out[start : start + part]
                mine[g, c] = jnp.where(first, one, two)
                away[g, c] = jnp.where(first, two, one).astype(BF16)
                tails_ref[c, g] = jnp.where(
                    row == 0, last[:, c * cut : (c + 1) * cut], second
                ).astype(BF16)
            to_sibling(g).start()

    @pl.when((step >= 1) & (step < 1 + groups * SPLIT))
    def _():
        dg = dot_nt(db[...], w_out_ref[0])
        df = (dg * slope_ref[0].astype(F32)).astype(BF16)
        acc[...] += dot_nt(df, w_in_ref[0])

    @pl.when(step == 1 + groups * SPLIT)
    def _():
        dpre = norm_back_rows(h_ref[...], hr_ref[:, 0:1], acc[...])
        dpre_ref[...] = dpre
        head_grads(dpre.astype(BF16), w_do_ref, do_ref)
        for g in range(groups):
            copy = to_sibling(g)
            copy.wait_send()
            copy.wait_recv()
            for c in range(4):
                pieces_ref[c, g] = (mine[g, c] + got[g, c].astype(F32)).astype(BF16)
        rider.finish(*ride)


def tail_back(grad, y, yr, h, hr, slope, tail_w, s_act, a_slope, w_do, do_block, rider):
    w_in, w_out, adapter = tail_w
    length, width = y.shape
    groups, _, hidden = slope.shape
    lanes = s_act.shape[2]
    cols = w_do.shape[2]
    part = lanes // 4
    anywhere = pl.BlockSpec(memory_space=pl.ANY)

    def whole(v):
        return pl.BlockSpec(v.shape, lambda j: (0, 0))

    def tile(j):
        j = jnp.clip(j - 1, 0, groups * SPLIT - 1)
        return j // SPLIT, lax.rem(j, SPLIT)

    result = pl.pallas_call(
        functools.partial(tail_back_kernel, rider),
        grid=(groups * SPLIT + 2,),
        in_specs=[whole(v) for v in (grad, y, yr, h, hr)]
        + [
            pl.BlockSpec((1, length, hidden // SPLIT), lambda j: (tile(j)[0], 0, tile(j)[1])),
            pl.BlockSpec((1, hidden // SPLIT, width), lambda j: (tile(j)[0], tile(j)[1], 0)),
            pl.BlockSpec((1, width, hidden // SPLIT), lambda j: (tile(j)[0], 0, tile(j)[1])),
            pl.BlockSpec(adapter.shape, lambda j: (0, 0, 0)),
            pl.BlockSpec((groups, length, lanes), lambda j: (0, 0, 0)),
            pl.BlockSpec((groups, length, lanes), lambda j: (0, 0, 0)),
            pl.BlockSpec((groups, width, cols), lambda j: (0, do_block, 0)),
        ]
        + [anywhere] * len(rider.inputs),
        out_specs=[
            pl.BlockSpec((length, width), lambda j: (0, 0)),
            pl.BlockSpec((groups, length, cols), lambda j: (0, 0, 0)),
            pl.BlockSpec((4, groups, part, width), lambda j: (0, 0, 0, 0)),
            pl.BlockSpec((4, groups, 16, width // 4), lambda j: (0, 0, 0, 0)),
        ]
        + [anywhere] * len(rider.inputs),
        out_shape=[
            jax.ShapeDtypeStruct((length, width), F32),
            jax.ShapeDtypeStruct((groups, length, cols), BF16),
            jax.ShapeDtypeStruct((4, groups, part, width), BF16),
            jax.ShapeDtypeStruct((4, groups, 16, width // 4), BF16),
        ]
        + rider.shapes,
        scratch_shapes=rider.scratch
        + [
            pltpu.VMEM((length, width), BF16),
            pltpu.VMEM((length, width), F32),
            pltpu.VMEM((groups, 4, part, width), F32),
            pltpu.VMEM((groups, 4, part, width), BF16),
            pltpu.VMEM((groups, 4, part, width), BF16),
            pltpu.SemaphoreType.DMA((groups,)),
            pltpu.SemaphoreType.DMA((groups,)),
        ],
        compiler_params=pltpu.CompilerParams(
            collective_id=rider.call_id, has_side_effects=True, vmem_limit_bytes=60 * 2**20
        ),
        name="tail_back",
    )(grad, y, yr, h, hr, slope, w_out, w_in, adapter, s_act, a_slope, w_do, *rider.inputs)
    return result[:2], result[2:4], result[4:]


def attn_back_kernel(causal, cross, rider, *refs):
    refs = list(refs)

    def take(count):
        got = refs[:count]
        del refs[:count]
        return got

    q_ref, k_ref, kx_ref, v_ref, vx_ref, o_ref, do_ref, lse_ref = take(8)
    if cross:
        wq_ref, wkv_ref, rest_ref, h_ref, hr_ref, w_do_ref = take(6)
    else:
        w_ref, rest_ref = take(2)
    feats, (qi_ref, ki_ref) = take(3), take(2)
    ride_ins = take(len(rider.inputs))
    if cross:
        dpre_ref, do_next_ref, memory_ref = take(3)
    else:
        (dx_ref,) = take(1)
    ride_outs = take(len(rider.inputs))
    ride_sems = take(len(rider.scratch))
    ride = (ride_ins, ride_outs, ride_sems)
    dq_s, own_k, own_v, away_k, away_v, got_k, got_v, acc, send, recv = take(10)
    if cross:
        (acc2,) = take(1)
    step = pl.program_id(0)
    groups = away_k.shape[0]
    width = acc.shape[1]

    def to_sibling(g):
        return [
            remote(a.at[g], b.at[g], send.at[g, j], recv.at[g, j], sibling_of())
            for j, (a, b) in enumerate(((away_k, got_k), (away_v, got_v)))
        ]

    @pl.when(step == 0)
    def _():
        rider.start(*ride)
        acc[...] = rest_ref[...]
        if cross:
            acc2[...] = jnp.zeros_like(acc2)

    @pl.when(step > 0)
    def _():
        g = step - 1
        slot = lax.rem(g, 2)
        for copy in to_sibling(g):
            copy.wait_send()
            copy.wait_recv()
        dk = (own_k[slot] + got_k[g].astype(F32)).astype(BF16)
        dv = (own_v[slot] + got_v[g].astype(F32)).astype(BF16)
        dq = dq_s[slot]
        if cross:
            acc[...] += dot_nt(dq, wq_ref[0])
            acc2[...] += dot_nt(dk, wkv_ref[0, :width]) + dot_nt(dv, wkv_ref[0, width:])
        else:
            acc[...] += (
                dot_nt(dq, w_ref[0, :width])
                + dot_nt(dk, w_ref[0, width : 2 * width])
                + dot_nt(dv, w_ref[0, 2 * width :])
            )

    @pl.when(step < groups)
    def _():
        slot = lax.rem(step, 2)
        attend_back_group(
            (q_ref, (k_ref, kx_ref), (v_ref, vx_ref), o_ref, do_ref, lse_ref),
            (dq_s, slot),
            ((own_k, slot), (away_k, step)),
            ((own_v, slot), (away_v, step)),
            feats,
            qi_ref,
            ki_ref,
            causal,
        )
        for copy in to_sibling(step):
            copy.start()

    @pl.when(step == groups)
    def _():
        if cross:
            dpre = norm_back_rows(h_ref[...], hr_ref[:, 0:1], acc[...])
            dpre_ref[...] = dpre
            head_grads(dpre.astype(BF16), w_do_ref, do_next_ref)
            memory_ref[...] = acc2[...]
        else:
            dx_ref[...] = acc[...].astype(dx_ref.dtype)
        rider.finish(*ride)


def attn_back(heads, ids, causal, rider, rest, weights, cross=None):
    groups, length, cols = heads[0].shape
    width = rest.shape[1]
    anywhere = pl.BlockSpec(memory_space=pl.ANY)

    def now(shape):
        return pl.BlockSpec((1,) + shape[1:], lambda t: (jnp.minimum(t, groups - 1), 0, 0))

    def past(rows):
        return pl.BlockSpec((1, rows, cols), lambda t: (jnp.maximum(t - 1, 0), 0, 0))

    def whole(v):
        return pl.BlockSpec(v.shape, lambda t: (0,) * len(v.shape))

    wide = jax.ShapeDtypeStruct((length, width), F32)
    if cross:
        h, hr, w_do = cross
        wq, wkv = weights
        extra = [wq, wkv, rest, h, hr, w_do]
        specs = [
            past(width),
            past(2 * width),
            whole(rest),
            whole(h),
            whole(hr),
            pl.BlockSpec((groups, width, cols), lambda t: (0, 3, 0)),
        ]
        outs = [wide, jax.ShapeDtypeStruct(heads[0].shape, BF16), wide]
    else:
        extra = [weights, rest]
        specs = [past(3 * width), whole(rest)]
        outs = [jax.ShapeDtypeStruct((length, width), BF16)]
    moving = pltpu.VMEM((groups, length, cols), BF16)
    result = pl.pallas_call(
        functools.partial(attn_back_kernel, causal, bool(cross), rider),
        grid=(groups + 1,),
        in_specs=[now(v.shape) for v in heads]
        + specs
        + [whole(v) for v in ids]
        + [anywhere] * len(rider.inputs),
        out_specs=[whole(v) for v in outs] + [anywhere] * len(rider.inputs),
        out_shape=outs + rider.shapes,
        scratch_shapes=rider.scratch
        + [
            pltpu.VMEM((2, length, cols), BF16),
            pltpu.VMEM((2, length, cols), F32),
            pltpu.VMEM((2, length, cols), F32),
            moving,
            moving,
            moving,
            moving,
            pltpu.VMEM((length, width), F32),
            pltpu.SemaphoreType.DMA((groups, 2)),
            pltpu.SemaphoreType.DMA((groups, 2)),
        ]
        + ([pltpu.VMEM((length, width), F32)] if cross else []),
        compiler_params=pltpu.CompilerParams(
            collective_id=rider.call_id,
            has_side_effects=True,
            vmem_limit_bytes=60 * 2**20,
        ),
        name="attn_back",
    )(*heads, *extra, *ids, *rider.inputs)
    return result[: len(outs)], result[len(outs) :]


def gather_plain(entry, shards):
    full = [lax.all_gather(lax.all_gather(v, TP), SECTION) for v in shards]
    return [v[entry] for v in full]


def spread(blocks):
    chips = lax.axis_size(CTX) * lax.axis_size(TP)
    kinds, rows, part, width = blocks.shape
    blocks = jnp.pad(blocks, ((0, 0), (0, chips - rows), (0, 0), (0, 0)))
    moved = lax.all_to_all(
        jnp.moveaxis(blocks, 1, 0), (CTX, TP), 0, 0, tiled=True
    )
    return jnp.moveaxis(moved, 0, 1).reshape(kinds, chips * part, width)


def collect(tokens, rows):
    chips = lax.axis_size(CTX) * lax.axis_size(TP)
    kinds, length, width = tokens.shape
    part = length // chips
    blocks = jnp.moveaxis(tokens.reshape(kinds, chips, part, width), 1, 0)
    moved = lax.all_to_all(blocks, (CTX, TP), 0, 0, tiled=True)
    return jnp.moveaxis(moved, 0, 1)[:, :rows]


def per_device(
    layer_inputs,
    out_grad,
    src_seg,
    tgt_seg,
    qkv_weights,
    out_weights,
    cross_weights,
    ffn_in,
    ffn_out,
    adapter_in,
    adapter_in_bias,
    adapter_out,
    adapter_out_bias,
):
    core = lax.axis_index(SECTION)
    is_first = core == 0
    tp = lax.axis_size(TP)
    chips = lax.axis_size(CTX) * tp
    chip = lax.axis_index(CTX) * tp + lax.axis_index(TP)
    _, micro, per_micro, part, width = layer_inputs.shape
    row_count = micro * per_micro
    half = part // 2
    length = half * chips

    def pick(first, second):
        return jnp.where(is_first, first, second)

    x = layer_inputs.reshape(row_count, part, width)
    grads = out_grad.reshape(row_count, part, width)
    grads = pick(grads[:, :half], grads[:, half:])
    near = lax.axis_size(CTX) == 4 and tp == 4
    lanes = adapter_in_bias.shape[1]
    cols = out_weights.shape[2]
    pad = lambda v, n: jnp.pad(v, [(0, n - v.shape[0])] + [(0, 0)] * (v.ndim - 1))
    biases = jnp.concatenate(
        [pad(adapter_in_bias[0], cols)[None], adapter_out_bias[0].reshape(-1, cols)]
    )
    shards = [
        jnp.concatenate([qkv_weights[0], out_weights], axis=0).reshape(-1, cols),
        ffn_in[0],
        ffn_out[0],
        jnp.concatenate(
            [
                jnp.concatenate([adapter_in[0], adapter_out[0].T], axis=1),
                pad(biases, 256),
            ],
            axis=0,
        ),
        cross_weights[0].reshape(-1, cols),
    ]
    if near:
        ids = ids_call(jnp.stack([src_seg, tgt_seg]).reshape(2 * row_count, -1))
        flat_ids = ids.swapaxes(0, 1).reshape(2, row_count, -1)
    else:
        flat_ids = [
            lax.all_gather(v.reshape(row_count, -1), CTX, axis=1, tiled=True)
            for v in (src_seg, tgt_seg)
        ]

    def unpack(full):
        attn, w_in, w_out, adapter, cross = full
        attn = attn.reshape(tp, 4, -1, cols)
        cross = cross.reshape(tp, 2, -1, cols)
        b_out = adapter[0, width + 1 : width + 1 + width // cols].reshape(width)
        tail = (
            w_in,
            w_out,
            adapter[:, :width, :lanes],
            adapter[:, width, :lanes],
            adapter[:, :width, lanes:],
            b_out,
        )
        return attn, cross, tail

    def ids_of(flat):
        row = lax.dynamic_index_in_dim(
            flat, jnp.minimum(chip, row_count - 1), 0, keepdims=False
        )
        return row.reshape(chips, 2, half)

    index = jnp.arange(length, dtype=jnp.int32)
    place = (index // half) * part + index % half

    def cut(seg, which):
        own = lax.dynamic_index_in_dim(seg, which, 1, keepdims=False).reshape(length)
        return own, place + which * half

    src_ids, tgt_ids = ids_of(flat_ids[0]), ids_of(flat_ids[1])

    def id_arrays(seg_q, seg_k):
        qi = jnp.stack(cut(seg_q, core))
        ki = jnp.stack(cut(seg_k, core) + cut(seg_k, 1 - core))
        return (qi.T, ki), (qi, ki.T)

    enc_ids = id_arrays(src_ids, src_ids)
    dec_ids = id_arrays(tgt_ids, tgt_ids)
    cross_ids = id_arrays(tgt_ids, src_ids)

    def scatter(arrays, call_id):
        return Scatter(arrays, row_count, call_id) if near else None

    def tokens(value):
        return value.astype(BF16).reshape(chips, half, width)

    def scatter(arrays, call_id):
        return Scatter(arrays, row_count, call_id) if near else None

    def tokens(value):
        return value.astype(BF16).reshape(chips, half, width)

    if near:
        src_own, place_own = cut(src_ids, core)
        src_oth, place_oth = cut(src_ids, 1 - core)
        tgt_own, tgt_oth = cut(tgt_ids, core)[0], cut(tgt_ids, 1 - core)[0]
        feats = jnp.stack(
            [
                id_columns(src_own, False),
                id_columns(src_own, True),
                id_columns(src_oth, True),
                id_columns(tgt_own, False),
                id_columns(tgt_own, True),
                id_columns(tgt_oth, True),
            ]
        )
        enc_w, dec_w, slope, kept = forward_call(
            shards,
            x,
            place_own[:, None],
            jnp.stack([place_own, place_oth] * 4),
            feats,
        )
        (dec_slope, dec_s, dec_a, dec_y, dec_yr, decoded), (placed,) = tail_call(
            kept[C2],
            (dec_w[1], dec_w[2], dec_w[3]),
            scatter([(grads, Scatter.BRING)], 8),
        )
        cotangent = placed.reshape(length, width)
        encoded_bf = kept[EY].astype(BF16)
    else:
        low, high = x[:, :half], x[:, half:]
        other = swap(pick(high, low))
        source, target, cotangent = spread(
            jnp.stack([pick(low, other), pick(other, high), grads])
        )
        enc_attn, enc_cross, enc_tail_w = unpack(gather_plain(0, shards))
        dec_attn, dec_cross, dec_tail_w = unpack(gather_plain(1, shards))
        enc_mid, enc_self = self_forward(
            source, source.astype(F32), enc_attn, enc_ids, False
        )
        encoded, enc_tail = tail_forward(enc_mid, enc_tail_w)
        encoded_bf = encoded.astype(BF16)
        memory = [project(encoded_bf, enc_cross[:, j]).astype(BF16) for j in range(2)]
        memory_other = swap(jnp.stack(memory))
        mem_keys = (memory[0], memory_other[0], memory[1], memory_other[1])
        dec_mid, dec_self = self_forward(
            target, target.astype(F32), dec_attn, dec_ids, True
        )
        queries = project(dec_mid.astype(BF16), dec_cross[:, 0]).astype(BF16)
        cross_o, cross_lse = attention_forward(
            queries, mem_keys, cross_ids[0], False
        )
        second, second_rstd = norm(dec_mid + unproject(cross_o, dec_cross[:, 1]))
        decoded, dec_tail = tail_forward(second, dec_tail_w)

    if near:

        def heads(q, k, kx, v, vx, o, lse, do):
            flat = kept[lse].reshape(kept[lse].shape[0], -1, length)
            return [kept[n] for n in (q, k, kx, v, vx, o)] + [do, flat]

        def pieces(parts):
            return [v.reshape((chips,) + v.shape[2:]) for v in parts]

        (grad_cross, do), dec_parts, (out_enc,) = tail_back(
            cotangent,
            dec_y,
            dec_yr,
            kept[C2],
            kept[C2R],
            dec_slope,
            (dec_w[1], dec_w[2], dec_w[3]),
            dec_s,
            dec_a,
            dec_w[4],
            1,
            scatter([(tokens(encoded_bf), 0)], 2),
        )
        (dpre, do, grad_encoded), (out_dec,) = attn_back(
            heads(CQ, MK, MKX, MV, MVX, CO, CL, do),
            [feats[3], feats[1], feats[2], *cross_ids[1]],
            False,
            scatter([(tokens(decoded), 1)], 3),
            grad_cross,
            (dec_w[4], enc_w[4]),
            (kept[DH], kept[DR], dec_w[0]),
        )
        (grad_target,), dec_sum = attn_back(
            heads(DQ, DK, DKX, DV, DVX, DO, DL, do),
            [feats[3], feats[4], feats[5], *dec_ids[1]],
            True,
            scatter([(v, 1) for v in pieces(dec_parts)], 4),
            dpre,
            dec_w[0],
        )
        (dpre, do), enc_parts, (moved,) = tail_back(
            grad_encoded,
            kept[EY],
            kept[EYR],
            kept[EH],
            kept[ER],
            slope,
            (enc_w[1], enc_w[2], enc_w[3]),
            kept[ES],
            kept[EA],
            enc_w[0],
            3,
            scatter([(tokens(grad_target), 1)], 5),
        )
        (grad_source,), enc_sum = attn_back(
            heads(EQ, EK, EKX, EV, EVX, EO, EL, do),
            [feats[0], feats[1], feats[2], *enc_ids[1]],
            False,
            scatter([(v, 0) for v in pieces(enc_parts)], 6),
            dpre,
            enc_w[0],
        )
        outs = pick(out_enc, out_dec)
        sums, ends = [
            jnp.sum(pick(a, b).astype(F32), axis=0) for a, b in zip(enc_sum, dec_sum)
        ]
        part_rows = lanes // 4
        ends = jnp.pad(jnp.sum(ends, axis=0), ((0, 0), (0, width - width // 4)))
        mine = jnp.concatenate([sums.reshape(2 * part_rows, width), ends]).astype(BF16)
        (last,), whole = send_call(scatter([(tokens(grad_source), 0)], 7), mine)
        grads = pick(last, moved).astype(F32)
        whole = whole.astype(F32)
        weights = whole[:, : 2 * part_rows].reshape(4, 2, part_rows, width)
        ends = whole[:, 2 * part_rows :, : width // 4]
        return (
            outs.reshape(layer_inputs.shape),
            grads.reshape(layer_inputs.shape),
            weights[:, 0].reshape(lanes, width).T[None],
            ends[0, 1, :lanes][None],
            weights[:, 1].reshape(1, lanes, width),
            ends[:, 0].reshape(1, width),
        )

    grad_second, dec_terms = tail_backward(cotangent.astype(F32), dec_tail, dec_tail_w)
    grad_cross = norm_back(second, second_rstd, grad_second)
    do = project(grad_cross.astype(BF16), dec_cross[:, 1]).astype(BF16)
    dqc, dmk, dmv = attend_back(
        queries, mem_keys, cross_o, do, cross_lse, cross_ids, False
    )
    grad_first = unproject(dqc, dec_cross[:, 0]) + grad_cross
    grad_target = self_backward(grad_first, dec_self, dec_attn, dec_ids, True)

    grad_encoded = unproject(dmk, enc_cross[:, 0]) + unproject(dmv, enc_cross[:, 1])
    grad_mid, enc_terms = tail_backward(grad_encoded, enc_tail, enc_tail_w)
    grad_source = self_backward(grad_mid, enc_self, enc_attn, enc_ids, False)

    has_row = chip < row_count

    def total(enc_term, dec_term):
        enc_term = jnp.where(has_row, enc_term, 0.0).astype(BF16)
        dec_term = jnp.where(has_row, dec_term, 0.0).astype(BF16)
        got = swap(pick(dec_term, enc_term))
        return (pick(enc_term, dec_term).astype(F32) + got.astype(F32)).astype(BF16)

    sums = [total(e, d) for e, d in zip(enc_terms, dec_terms)]
    scattered = [
        lax.psum_scatter(v, TP, scatter_dimension=0, tiled=False) for v in sums[:3]
    ]
    scattered = [lax.psum(v, CTX).astype(F32) for v in scattered]
    bias_sum = lax.psum(sums[3], (CTX, TP)).astype(F32)

    results = jnp.stack(
        [
            encoded_bf,
            decoded.astype(BF16),
            grad_source.astype(BF16),
            grad_target.astype(BF16),
        ]
    )
    placed = collect(results, row_count)

    def join(enc_part, dec_part):
        mine = pick(enc_part, dec_part)
        got = swap(pick(dec_part, enc_part))
        return jnp.concatenate([pick(mine, got), pick(got, mine)], axis=1)

    outs = join(placed[0], placed[1]).reshape(layer_inputs.shape)
    grads = join(placed[2], placed[3]).astype(F32).reshape(layer_inputs.shape)
    return (
        outs,
        grads,
        scattered[0][None],
        scattered[1][None],
        scattered[2].T[None],
        bias_sum[None],
    )


def solution(mesh):
    return jax.shard_map(
        per_device,
        mesh=mesh,
        in_specs=(
            P(SECTION, None, None, (CTX, TP), None),
            P(None, None, (CTX, TP), None),
            P(None, None, CTX),
            P(None, None, CTX),
            P(SECTION, None, None, TP),
            P(SECTION, None, TP),
            P(SECTION, None, None, TP),
            P(SECTION, None, TP),
            P(SECTION, TP, None),
            P(SECTION, None, TP),
            P(SECTION, TP),
            P(SECTION, TP, None),
            P(SECTION, None),
        ),
        out_specs=(
            P(SECTION, None, None, (CTX, TP), None),
            P(SECTION, None, None, (CTX, TP), None),
            P(SECTION, None, TP),
            P(SECTION, TP),
            P(SECTION, TP, None),
            P(SECTION, None),
        ),
        check_vma=False,
    )
```

```python
import functools

import jax
import jax.numpy as jnp
from jax import lax
from jax.experimental import pallas as pl
from jax.experimental.pallas import tpu as pltpu
from jax.sharding import PartitionSpec as P

HEAD = 64
SCALE = HEAD**-0.5
EPS = 1e-05
MASKED = -1e30
F32 = jnp.float32
BF16 = jnp.bfloat16
SECTION, CTX, TP = "section", "ctx", "tp"


def swap(value):
    return lax.ppermute(value, SECTION, [(0, 1), (1, 0)])


def remote(src, dst, send, recv, where):
    return pltpu.make_async_remote_copy(
        src_ref=src,
        dst_ref=dst,
        send_sem=send,
        recv_sem=recv,
        device_id=where,
        device_id_type=pl.DeviceIdType.MESH,
    )


def device_of(section, chip):
    return (section, chip // 4, lax.rem(chip, 4))


def greet_all():
    s = lax.axis_index(SECTION)
    chip = lax.axis_index(CTX) * 4 + lax.axis_index(TP)
    barrier = pltpu.get_barrier_semaphore()
    for core in (0, 1):
        for i in range(core, 16):
            pl.semaphore_signal(
                barrier,
                1,
                device_id=device_of(lax.rem(s + 1 - core, 2), lax.rem(chip + i, 16)),
                device_id_type=pl.DeviceIdType.MESH,
            )
    pl.semaphore_wait(barrier, 31)


class Scatter:
    BRING = 2

    def __init__(self, arrays, rows, call_id):
        self.inputs = [a for a, _ in arrays]
        self.kinds = [k for _, k in arrays]
        self.rows = rows
        self.call_id = call_id
        self.shapes = [
            jax.ShapeDtypeStruct(
                ((16,) if k == self.BRING else (rows, 2)) + a.shape[1:], a.dtype
            )
            for a, k in arrays
        ]
        count = max(len(arrays), 1)
        self.scratch = [
            pltpu.SemaphoreType.DMA((count, 16)),
            pltpu.SemaphoreType.DMA((count, 16, 2)),
        ]

    def sends(self, ins, outs, sems):
        send, recv = sems
        s = lax.axis_index(SECTION)
        chip = lax.axis_index(CTX) * 4 + lax.axis_index(TP)
        for a, kind in enumerate(self.kinds):
            for i in range(16):
                p = lax.rem(chip + i, 16)
                if kind == self.BRING:
                    ready = p < self.rows
                    src = ins[a].at[jnp.minimum(p, self.rows - 1)]
                    dst = outs[a].at[chip]
                    core, mark = s, 0
                    stays = True
                else:
                    ready = chip < self.rows
                    src = ins[a].at[p]
                    dst = outs[a].at[jnp.minimum(chip, self.rows - 1), s]
                    core, mark = kind, s
                    stays = s == kind
                near = pltpu.make_async_copy(src, dst, send.at[a, i])
                far = remote(
                    src, dst, send.at[a, i], recv.at[a, i, mark], device_of(core, p)
                )
                yield i, ready, stays, near, far

    def start(self, ins, outs, sems):
        greet_all()
        for i, ready, stays, near, far in self.sends(ins, outs, sems):

            @pl.when(ready)
            def _():
                if i:
                    far.start()
                elif stays is True:
                    near.start()
                else:
                    pl.when(stays)(near.start)
                    pl.when(jnp.logical_not(stays))(far.start)

    def finish(self, ins, outs, sems):
        send, recv = sems
        s = lax.axis_index(SECTION)
        chip = lax.axis_index(CTX) * 4 + lax.axis_index(TP)
        for i, ready, stays, near, far in self.sends(ins, outs, sems):

            @pl.when(ready)
            def _():
                if i:
                    far.wait_send()
                elif stays is True:
                    near.wait()
                else:
                    pl.when(stays)(near.wait)
                    pl.when(jnp.logical_not(stays))(far.wait_send)

        def got(region, sem):
            remote(region, region, send.at[0, 0], sem, (1 - s, 0, 0)).wait_recv()

        for a, kind in enumerate(self.kinds):
            for i in range(16):
                sender = lax.rem(chip + 16 - i, 16)
                if kind == self.BRING:
                    if i:

                        @pl.when(chip < self.rows)
                        def _():
                            got(outs[a].at[sender], recv.at[a, i, 0])

                    continue

                @pl.when((s == kind) & (sender < self.rows))
                def _():
                    for core in (0, 1) if i else (1 - kind,):
                        region = outs[a].at[jnp.minimum(sender, self.rows - 1), core]
                        got(region, recv.at[a, i, core])


def send_kernel(rider, *refs):
    n = len(rider.inputs)
    block_in, (own, spread_out) = refs[n], (refs[n], refs[2 * n + 1])
    ins, outs = refs[:n], refs[n + 1 : 2 * n + 1]
    sems = refs[2 * n + 2 : 2 * n + 4]
    b_send, b_recv = refs[2 * n + 4 :]
    rider.start(ins, outs, sems)
    s = lax.axis_index(SECTION)
    c = lax.axis_index(CTX)
    t = lax.axis_index(TP)
    dst = spread_out.at[c]
    keep = pltpu.make_async_copy(own, dst, b_send.at[0])
    keep.start()
    ways = [
        remote(own, dst, b_send.at[j], b_recv.at[j], (s, lax.rem(c + j, 4), t))
        for j in (1, 2, 3)
    ]
    for way in ways:
        way.start()
    keep.wait()
    for j, way in enumerate(ways):
        way.wait_send()
        region = spread_out.at[lax.rem(c + 3 - j, 4)]
        remote(region, region, b_send.at[0], b_recv.at[j + 1], (s, c, t)).wait_recv()
    rider.finish(ins, outs, sems)


def send_call(rider, block):
    anywhere = pl.BlockSpec(memory_space=pl.ANY)
    count = len(rider.inputs)
    result = pl.pallas_call(
        functools.partial(send_kernel, rider),
        in_specs=[anywhere] * (count + 1),
        out_specs=[anywhere] * (count + 1),
        out_shape=rider.shapes + [jax.ShapeDtypeStruct((4,) + block.shape, block.dtype)],
        scratch_shapes=rider.scratch
        + [pltpu.SemaphoreType.DMA((4,)), pltpu.SemaphoreType.DMA((4,))],
        compiler_params=pltpu.CompilerParams(
            collective_id=rider.call_id, has_side_effects=True
        ),
        name="send_last",
    )(*rider.inputs, block)
    return result[:count], result[count]


def dot_nt(left, right, **kw):
    return lax.dot_general(
        left, right, (((1,), (1,)), ((), ())), preferred_element_type=F32, **kw
    )


def dot_nn(left, right):
    return lax.dot_general(
        left, right, (((1,), (0,)), ((), ())), preferred_element_type=F32
    )


def dot_tn(left, right):
    return lax.dot_general(
        left, right, (((0,), (0,)), ((), ())), preferred_element_type=F32
    )


def attn_fwd_kernel(
    causal, q_ref, ko_ref, kx_ref, vo_ref, vx_ref, fq, fo, fx, qi_ref, ki_ref, o_ref, lse_ref
):
    for pair in range(lse_ref.shape[1]):
        attend_pair(
            0,
            pair,
            q_ref,
            (ko_ref, kx_ref),
            (vo_ref, vx_ref),
            o_ref,
            lse_ref,
            (fq, fo, fx),
            (qi_ref[:, 1:2], (ki_ref[1:2, :], ki_ref[3:4, :])),
            causal,
        )


def attention_call(kernel, name, causal, blocks, small, outs):
    def group_spec(v):
        return pl.BlockSpec((1,) + v.shape[1:], lambda t: (t,) + (0,) * (len(v.shape) - 1))

    return pl.pallas_call(
        functools.partial(kernel, causal),
        grid=(blocks[0].shape[0],),
        in_specs=[group_spec(v) for v in blocks]
        + [pl.BlockSpec(v.shape, lambda t: (0, 0)) for v in small],
        out_specs=[group_spec(v) for v in outs],
        out_shape=outs,
        compiler_params=pltpu.CompilerParams(vmem_limit_bytes=48 * 2**20),
        name=name,
    )(*blocks, *small)


def id_columns(ids, keys):
    lane = jnp.arange(2 * HEAD, dtype=jnp.int32)[None] % HEAD
    same = ids[:, None] == lane
    value = jnp.where(same, 1.0, 0.0) if keys else jnp.where(same, 0.0, MASKED)
    return jnp.where(lane < 4, value, 0.0).astype(BF16)


def attention_forward(q, keys, ids, causal):
    groups, length, width = q.shape
    pairs = width // HEAD // 2
    outs = [
        jax.ShapeDtypeStruct(q.shape, BF16),
        jax.ShapeDtypeStruct((groups, pairs, 2, length), F32),
    ]
    feats = [
        id_columns(ids[0][:, 0], False),
        id_columns(ids[1][0], True),
        id_columns(ids[1][2], True),
    ]
    o, lse = attention_call(
        attn_fwd_kernel, "attn_fwd", causal, [q, *keys], [*feats, *ids], outs
    )
    return o, lse.reshape(groups, 2 * pairs, length)


def attend_back_group(ins, dq_out, dk_outs, dv_outs, feats, qi_ref, ki_ref, causal):
    q_ref, k_refs, v_refs, o_ref, do_ref, lse_ref = ins
    length = q_ref.shape[1]
    block = length // 2
    posq = qi_ref[1:2, :]
    ones = jnp.ones((16, 2 * HEAD), BF16)

    def put(out, rows, lanes, value):
        out[0][out[1], rows, lanes] = value.astype(out[0].dtype)

    for pair in range(q_ref.shape[2] // (2 * HEAD)):
        lanes = slice(pair * 2 * HEAD, (pair + 1) * 2 * HEAD)
        q2 = q_ref[0, :, lanes] * jnp.asarray(SCALE, BF16)
        do2 = do_ref[0, :, lanes]
        prod2 = do2.astype(F32) * o_ref[0, :, lanes].astype(F32)
        dq, dk, dv = [None, None], {}, {}
        for j in range(2):
            here = head_mask(length, j)
            q_all = jnp.where(here, q2, feats[0][...])
            q_only = jnp.where(here, q2, jnp.zeros_like(q2))
            do_all = jnp.where(here, do2, jnp.zeros_like(do2))
            prod = jnp.where(here, prod2, 0.0)
            high = prod.astype(BF16)
            rest = (prod - high.astype(F32)).astype(BF16)
            delta = (dot_nt(ones, high) + dot_nt(ones, rest))[0:1]
            lse = lse_ref[0, 2 * pair + j : 2 * pair + j + 1, :]
            for n in range(2):
                for b in range(2):
                    rows = slice(b * block, (b + 1) * block)
                    first = b * block if causal else 0
                    k2 = k_refs[n][0, rows, lanes]
                    there = head_mask(block, j)
                    k = jnp.where(there, k2, feats[1 + n][rows])
                    k_only = jnp.where(there, k2, jnp.zeros_like(k2))
                    s = dot_nt(k, q_all[first:])
                    p = jnp.exp(s - lse[:, first:])
                    if causal:
                        ok = posq[:, first:] >= ki_ref[rows, 2 * n + 1 : 2 * n + 2]
                        p = jnp.where(ok, p, 0.0)
                    dp = dot_nt(v_refs[n][0, rows, lanes], do_all[first:])
                    ds = (p * (dp - delta[:, first:])).astype(BF16)
                    add = lambda old, new: new if old is None else old + new
                    dv[n, b] = add(
                        dv.get((n, b)), dot_nn(p.astype(BF16), do_all[first:])
                    )
                    dk[n, b] = add(dk.get((n, b)), dot_nn(ds, q_only[first:]))
                    part = dot_tn(k_only, ds)
                    if not first:
                        dq[0] = add(dq[0], part[:, :block])
                    dq[1] = add(dq[1], part[:, block - first :])
        for n in range(2):
            for b in range(2):
                rows = slice(b * block, (b + 1) * block)
                put(dv_outs[n], rows, lanes, dv[n, b])
                put(dk_outs[n], rows, lanes, dk[n, b])
        for b in range(2):
            put(dq_out, slice(b * block, (b + 1) * block), lanes, (dq[b] * SCALE).T)


def attn_bwd_kernel(
    causal,
    q_ref,
    ko_ref,
    kx_ref,
    vo_ref,
    vx_ref,
    o_ref,
    do_ref,
    lse_ref,
    fq,
    fo,
    fx,
    qi_ref,
    ki_ref,
    dq_ref,
    dko_ref,
    dkx_ref,
    dvo_ref,
    dvx_ref,
):
    attend_back_group(
        (q_ref, (ko_ref, kx_ref), (vo_ref, vx_ref), o_ref, do_ref, lse_ref),
        (dq_ref, 0),
        ((dko_ref, 0), (dkx_ref, 0)),
        ((dvo_ref, 0), (dvx_ref, 0)),
        (fq, fo, fx),
        qi_ref,
        ki_ref,
        causal,
    )


def back_feats(ids):
    return [
        id_columns(ids[0][0], False),
        id_columns(ids[1][:, 0], True),
        id_columns(ids[1][:, 2], True),
    ]


def attention_backward(q, keys, o, do, lse, ids, causal):
    outs = [jax.ShapeDtypeStruct(q.shape, BF16)] * 5
    small = [*back_feats(ids), *ids]
    return attention_call(
        attn_bwd_kernel, "attn_bwd", causal, [q, *keys, o, do, lse], small, outs
    )


def norm(value):
    mean = jnp.mean(value, axis=-1, keepdims=True)
    centered = value - mean
    rstd = lax.rsqrt(jnp.mean(centered * centered, axis=-1, keepdims=True) + EPS)
    return centered * rstd, rstd


def norm_back(normed, rstd, grad):
    return rstd * (
        grad
        - jnp.mean(grad, axis=-1, keepdims=True)
        - normed * jnp.mean(grad * normed, axis=-1, keepdims=True)
    )


def project(rows, weight):
    return jnp.einsum("pk,tkm->tpm", rows, weight, preferred_element_type=F32)


def unproject(blocks, weight):
    return jnp.einsum("tpm,tkm->pk", blocks, weight, preferred_element_type=F32)


def self_forward(rows_bf, rows, w_attn, ids, causal):
    kv = [project(rows_bf, w_attn[:, j]).astype(BF16) for j in (1, 2)]
    other = swap(jnp.stack(kv))
    q = project(rows_bf, w_attn[:, 0]).astype(BF16)
    keys = (kv[0], other[0], kv[1], other[1])
    o, lse = attention_forward(q, keys, ids[0], causal)
    h, rstd = norm(rows + unproject(o, w_attn[:, 3]))
    return h, (q, keys, o, lse, h, rstd)


def attend_back(q, keys, o, do, lse, ids, causal):
    dq, dko, dkx, dvo, dvx = attention_backward(q, keys, o, do, lse, ids[1], causal)
    other = swap(jnp.stack([dkx, dvx])).astype(F32)
    dk = (dko.astype(F32) + other[0]).astype(BF16)
    dv = (dvo.astype(F32) + other[1]).astype(BF16)
    return dq, dk, dv


def self_backward(grad, kept, w_attn, ids, causal):
    q, keys, o, lse, h, rstd = kept
    dpre = norm_back(h, rstd, grad)
    do = project(dpre.astype(BF16), w_attn[:, 3]).astype(BF16)
    dq, dk, dv = attend_back(q, keys, o, do, lse, ids, causal)
    return (
        unproject(dq, w_attn[:, 0])
        + unproject(dk, w_attn[:, 1])
        + unproject(dv, w_attn[:, 2])
        + dpre
    )


def tail_forward(h, tail_w):
    w_in, w_out, a_in, b_in, a_out, b_out = tail_w
    rows = h.astype(BF16)
    inner = project(rows, w_in)
    phi = 0.5 * (1.0 + lax.erf(inner * 0.7071067811865476))
    g = (inner * phi).astype(BF16)
    slope = phi + inner * jnp.exp(inner * inner * -0.5) * 0.3989422804014327
    pre = project(rows, a_in) + b_in.astype(F32)[:, None, :]
    sig = jax.nn.sigmoid(pre)
    s = (pre * sig).astype(BF16)
    a_slope = sig * (1.0 + pre * (1.0 - sig))
    total = jnp.einsum("tpm,tmk->pk", g, w_out, preferred_element_type=F32)
    total += 4.0 * (
        jnp.einsum("tpm,tkm->pk", s, a_out, preferred_element_type=F32)
        + b_out.astype(F32)
    )
    y, rstd = norm(h + total)
    return y, (rows, slope.astype(BF16), s, a_slope.astype(BF16), y, rstd)


def tail_backward(grad, kept, tail_w):
    w_in, w_out, a_in, b_in, a_out, b_out = tail_w
    rows, slope, s, a_slope, y, rstd = kept
    dpre = norm_back(y, rstd, grad)
    db = dpre.astype(BF16)
    dg = jnp.einsum("pk,tmk->tpm", db, w_out, preferred_element_type=F32)
    df = (dg * slope.astype(F32)).astype(BF16)
    ds = 4.0 * jnp.einsum("pk,tkm->tpm", db, a_out, preferred_element_type=F32)
    du = (ds * a_slope.astype(F32)).astype(BF16)
    terms = (
        jnp.einsum("pk,tpm->tkm", rows, du, preferred_element_type=F32),
        jnp.sum(du.astype(F32), axis=1),
        4.0 * jnp.einsum("pk,tpm->tkm", db, s, preferred_element_type=F32),
        4.0 * jnp.sum(db.astype(F32), axis=0),
    )
    return unproject(df, w_in) + unproject(du, a_in) + dpre, terms


def head_mask(rows, j):
    lane = lax.broadcasted_iota(jnp.int32, (rows, 2 * HEAD), 1)
    return (lane < HEAD) if j == 0 else (lane >= HEAD)


def attend_pair(t, pair, q_ref, k_refs, v_refs, o_ref, lse_ref, feats, places, causal):
    length = q_ref.shape[1]
    block = length // 2
    lanes = pl.ds(pl.multiple_of(pair * 2 * HEAD, 2 * HEAD), 2 * HEAD)
    posq, posk = places
    for b in range(2):
        rows = slice(b * block, (b + 1) * block)
        q2 = q_ref[t, rows, lanes] * jnp.asarray(SCALE, BF16)
        cuts = [(n, a) for n in range(2) for a in range(b + 1 if causal else 2)]
        outs = []
        for j in range(2):
            q = jnp.where(head_mask(block, j), q2, feats[0][rows])
            parts = []
            for n, a in cuts:
                span = slice(a * block, (a + 1) * block)
                k = jnp.where(
                    head_mask(block, j), k_refs[n][t, span, lanes], feats[1 + n][span]
                )
                s = dot_nt(q, k)
                if causal and a == b:
                    s = jnp.where(posq[rows] >= posk[n][:, span], s, MASKED)
                parts.append(s)
            top = functools.reduce(
                jnp.maximum, [jnp.max(s, axis=1, keepdims=True) for s in parts]
            )
            ex = [jnp.exp(s - top) for s in parts]
            total = sum(jnp.sum(e, axis=1, keepdims=True) for e in ex)
            out = sum(
                dot_nn(
                    e.astype(BF16), v_refs[n][t, a * block : (a + 1) * block, lanes]
                )
                for e, (n, a) in zip(ex, cuts)
            )
            outs.append(out / total)
            lse = top + jnp.log(total)
            lse_ref[t, pair, j : j + 1, rows] = jnp.broadcast_to(lse, (block, 128)).T[
                0:1
            ]
        o_ref[t, rows, lanes] = jnp.where(head_mask(block, 0), *outs).astype(BF16)


ATTN, FFN_IN, FFN_OUT, ADAPTER, CROSS = range(5)
ORDER = (
    (0, ATTN),
    (1, ATTN),
    (0, FFN_IN),
    (0, FFN_OUT),
    (0, ADAPTER),
    (0, CROSS),
    (1, CROSS),
    (1, FFN_IN),
    (1, FFN_OUT),
    (1, ADAPTER),
)
(
    ENC_QKV,
    ENC_ATTN,
    ENC_OUT,
    DEC_QKV,
    DEC_ATTN,
    DEC_OUT,
    HIDDEN,
    GATED,
    MEMORY,
    CROSS_Q,
    CROSS_ATTN,
    CROSS_OUT,
    END,
) = range(13)
WORK = (
    (ENC_QKV, 4, (0, ATTN), 2.0),
    (ENC_ATTN, 8, None, 2.3),
    (ENC_OUT, 1, None, 4.0),
    (DEC_QKV, 4, (1, ATTN), 2.0),
    (DEC_ATTN, 8, None, 2.1),
    (DEC_OUT, 1, None, 4.0),
    (HIDDEN, 8, (0, FFN_OUT), 2.5),
    (GATED, 1, (0, ADAPTER), 4.0),
    (MEMORY, 4, (0, CROSS), 1.5),
    (CROSS_Q, 1, (1, CROSS), 4.0),
    (CROSS_ATTN, 8, None, 2.3),
    (CROSS_OUT, 1, None, 4.0),
    (END, 1, (1, ADAPTER), 0.0),
)


LAG = 2


def plan_steps(sizes):
    ready, clock = [], 20.0
    for e, g in ORDER:
        for _ in range(3):
            clock += sizes[g] / 3 * 11e-6
            ready.append(clock)
    ticks = len(ready) + 2 * LAG
    ready += [clock + 4 * n for n in range(1, 2 * LAG + 1)]
    starts, at, step, now, done = {}, {}, 0, 0.0, 0
    for name, count, need, cost in WORK:
        starts[name] = step
        for n in range(count):
            while done < ticks and (
                ready[done] <= now
                or (need and done <= 3 * ORDER.index(need) + 2 + 2 * LAG)
            ):
                at[done] = step
                now = max(now, ready[done])
                done += 1
            now += cost
            step += 1
    for n in range(done, ticks):
        at[n] = step - 1
    return starts, at, step


HEADS, LSE, WIDE, RSTD, LANES = range(5)
(
    EQ,
    EK,
    EKX,
    EV,
    EVX,
    EO,
    EL,
    EH,
    ER,
    ES,
    EA,
    EY,
    EYR,
    DQ,
    DK,
    DKX,
    DV,
    DVX,
    DO,
    DL,
    DH,
    DR,
    MK,
    MKX,
    MV,
    MVX,
    CQ,
    CO,
    CL,
    C2,
    C2R,
) = range(31)
KEPT = {
    EQ: HEADS,
    EK: HEADS,
    EKX: HEADS,
    EV: HEADS,
    EVX: HEADS,
    EO: HEADS,
    EL: LSE,
    EH: WIDE,
    ER: RSTD,
    ES: LANES,
    EA: LANES,
    EY: WIDE,
    EYR: RSTD,
    DQ: HEADS,
    DK: HEADS,
    DKX: HEADS,
    DV: HEADS,
    DVX: HEADS,
    DO: HEADS,
    DL: LSE,
    DH: WIDE,
    DR: RSTD,
    MK: HEADS,
    MKX: HEADS,
    MV: HEADS,
    MVX: HEADS,
    CQ: HEADS,
    CO: HEADS,
    CL: LSE,
    C2: WIDE,
    C2R: RSTD,
}


def forward_kernel(plan, rows, *refs):
    starts, tick_step, steps = plan
    refs = list(refs)

    def take(count):
        got = refs[:count]
        del refs[:count]
        return got

    shards = take(5)
    (tokens,) = take(1)
    col_ref, row_ref, feat_ref = take(3)
    full = (take(5), take(5))
    (slope_out,) = take(1)
    kept_out = take(len(KEPT))
    kept = take(len(KEPT))
    xs = take(2)
    wb, wi, wo, wad, slope = take(5)
    store_a, store_f = take(2)
    (
        z_send,
        z_recv,
        h_send,
        n_send,
        n_recv,
        f_send,
        f_recv,
        s_send,
        s_recv,
        own_sem,
        t_send,
        t_recv,
        kv_send,
        kv_recv,
        load_sem,
        out_sem,
        slope_sem,
    ) = refs
    step = pl.program_id(0)
    s = lax.axis_index(SECTION)
    c = lax.axis_index(CTX)
    t = lax.axis_index(TP)
    chips = 16
    chip = c * 4 + t
    cx = c + 1 - 2 * lax.rem(c, 2)
    cy = lax.rem(c + 2, 4)
    cd = 3 - c
    sib = (1 - s, c, t)

    inner = (t == 1) | (t == 2)

    def xor(k):
        return {1: t + 1 - 2 * lax.rem(t, 2), 2: 2 - t // 2, 3: 3 - 3 * (t // 2)}[k]

    part = xs[0].shape[1]

    def token_copy(kind, i, h):
        p = lax.rem(chip + i, chips)
        src = tokens.at[jnp.minimum(p, rows - 1), pl.ds(h * part, part)]
        dst = xs[kind].at[chip]
        if i == 0 and h == kind:
            return p, pltpu.make_async_copy(src, dst, t_send.at[kind, 0, h])
        return p, remote(
            src, dst, t_send.at[kind, i, h], t_recv.at[kind, i], device_of(h, p)
        )

    def send_tokens(kind):
        @pl.when(s == kind)
        def _():
            for i in range(chips):
                for h in range(2):
                    p, copy = token_copy(kind, i, h)
                    pl.when(p < rows)(copy.start)

    def got(region, sem):
        remote(region, region, load_sem.at[0], sem, sib).wait_recv()

    def wait_tokens(kind):
        @pl.when(s == kind)
        def _():
            for i in range(chips):
                for h in range(2):
                    p, copy = token_copy(kind, i, h)
                    stays = i == 0 and h == kind
                    pl.when(p < rows)(copy.wait if stays else copy.wait_send)

        @pl.when(chip < rows)
        def _():
            for i in range(chips):
                region = xs[kind].at[lax.rem(chip + chips - i, chips)]
                if i:
                    got(region, t_recv.at[kind, i])
                else:

                    @pl.when(s != kind)
                    def _():
                        got(region, t_recv.at[kind, 0])

    items = [(n, k) for n in range(len(ORDER)) for k in (1, 2, 3)]
    window = 4

    def block(n, who, h, q, u=None):
        e, g = ORDER[n]
        size = shards[g].shape[0]
        start = h * (size // 2) + q * (size // 8)
        length = size // 8
        if u is not None:
            length = size // 16
            start = start + u * length
        return full[e][g].at[who, pl.ds(pl.multiple_of(start, 16), length)]

    def z_copy(n, k, h):
        g = ORDER[n][1]
        size = shards[g].shape[0]
        start = h * (size // 2) + c * (size // 8)
        return remote(
            shards[g].at[pl.ds(pl.multiple_of(start, 16), size // 8)],
            block(n, t, h, c),
            z_send.at[n, k - 1, h],
            z_recv.at[n, k - 1],
            (h, c, xor(1) if k == 1 else jnp.clip(3 - t, 1, 2)),
        )

    def z_forward(n, k):
        src = block(n, xor(k), s, c)
        to = 3 - t if k == 1 else 3 * t - 3
        return remote(
            src,
            src,
            h_send.at[n, k - 1],
            z_recv.at[n, (2, 1, 2)[k - 1]],
            (s, c, jnp.clip(to, 0, 3)),
        )

    def store(g):
        if g in (FFN_IN, FFN_OUT):
            return store_f
        return store_a.at[pl.ds(0, shards[g].shape[0])]

    def fetch(n):
        g = ORDER[n][1]
        return pltpu.make_async_copy(shards[g], store(g), own_sem.at[n, 3])

    def put(n):
        e, g = ORDER[n]
        return pltpu.make_async_copy(store(g), full[e][g].at[t], own_sem.at[n, 0])

    def far(n):
        e, g = ORDER[n]
        return remote(
            shards[g], full[e][g].at[t], own_sem.at[n, 1], own_sem.at[n, 2], sib
        )

    def before(n):
        e, g = ORDER[n]
        pool = (FFN_IN, FFN_OUT) if g in (FFN_IN, FFN_OUT) else (ATTN, ADAPTER, CROSS)
        olds = [m for m in range(n) if ORDER[m][0] == e and ORDER[m][1] in pool]
        return olds[-1] if olds else None

    def start_z(i):
        n, k = items[i]

        @pl.when(s == ORDER[n][0])
        def _():
            if k == 1:
                far(n).start()
            if k < 3:

                @pl.when(inner | (k == 1))
                def _():
                    for h in range(2):
                        z_copy(n, k, h).start()

    def near_copy(n, k, j):
        src = block(n, xor(k), s, c)
        return remote(
            src,
            src,
            n_send.at[n, k - 1, j],
            n_recv.at[n, k - 1, j],
            (s, (cx, cy)[j], t),
        )

    def sibling_copy(n, k, j):
        src = block(n, xor(k), s, (c, cx, cy, cd)[j])
        return remote(src, src, s_send.at[n, k - 1, j], s_recv.at[n, k - 1, j], sib)

    def forward_copy(n, k, j):
        src = block(n, xor(k), s, (cx, cy)[j], j)
        return remote(
            src,
            src,
            f_send.at[n, k - 1, j],
            f_recv.at[n, k - 1, j],
            (s, (cy, cx)[j], t),
        )

    def stage2(i):
        n, k = items[i]
        got(block(n, xor(k), s, c), z_recv.at[n, k - 1])
        pl.when(inner)(z_forward(n, k).start)
        near_copy(n, k, 0).start()
        near_copy(n, k, 1).start()
        sibling_copy(n, k, 0).start()
        if k == 2:
            return

        @pl.when(s == ORDER[n][0])
        def _():
            if k == 1:
                old = before(n)
                if old is not None and not put_read_first(old, i):
                    put(old).wait()
                fetch(n).start()
            else:
                fetch(n).wait()
                put(n).start()

    def stage3(i):
        n, k = items[i]
        for j, q in ((0, cx), (1, cy)):
            got(block(n, xor(k), s, q), n_recv.at[n, k - 1, j])
            forward_copy(n, k, j).start()
            sibling_copy(n, k, j + 1).start()

    def stage4(i):
        n, k = items[i]
        for u in range(2):
            got(block(n, xor(k), s, cd, u), f_recv.at[n, k - 1, u])
        sibling_copy(n, k, 3).start()

    count = len(items)

    def tick(i):
        if i < count:
            stage2(i)
            if i + window < count:
                start_z(i + window)
        if 0 <= i - LAG < count:
            stage3(i - LAG)
        if 0 <= i - 2 * LAG < count:
            stage4(i - 2 * LAG)
        if i == 6:
            send_tokens(1)

    def arrive_step(n):
        for name, _, need, _ in WORK[:-1]:
            if need == ORDER[n]:
                return starts[name]
        return starts[HIDDEN] if ORDER[n] == (0, FFN_IN) else steps - 1

    def put_read_first(n, i):
        return arrive_step(n) < tick_step[i]

    def put_left(n):
        after = [m for m in range(len(ORDER)) if before(m) == n]
        return not after or put_read_first(n, 3 * after[0])

    def arrive(n):
        e, g = ORDER[n]
        for k in (1, 2, 3):
            for j, q in enumerate((c, cx, cy, cd)):
                got(block(n, xor(k), 1 - s, q), s_recv.at[n, k - 1, j])

        @pl.when(s == e)
        def _():
            if put_left(n):
                put(n).wait()

        @pl.when(s != e)
        def _():
            got(full[e][g].at[t], own_sem.at[n, 2])

    @pl.when(step == 0)
    def _():
        greet_all()
        send_tokens(0)
        for i in range(window):
            start_z(i)

    for i in range(count + 2 * LAG):
        pl.when(step == tick_step[i])(functools.partial(tick, i))

    def on(name):
        first = starts[name]
        last = first + [w[1] for w in WORK if w[0] == name][0]
        need = [w[2] for w in WORK if w[0] == name][0]
        if need and name != END:
            pl.when(step == first)(functools.partial(arrive, ORDER.index(need)))
        return step - first, pl.when((step >= first) & (step < last))

    def load(src, dst, slot=0):
        return pltpu.make_async_copy(src, dst, load_sem.at[slot])

    def keep(*names):
        for n in names:
            pltpu.make_async_copy(kept[n], kept_out[n], out_sem.at[n]).start()

    attn_rows = full[0][ATTN].shape[1] // 4

    def kv_copies(which, g, names):
        k, kx, v, vx = names
        return [
            remote(
                kept[a].at[g], kept[b].at[g], kv_send.at[which, g, j], kv_recv.at[which, g, j], sib
            )
            for j, (a, b) in enumerate(((k, kx), (v, vx)))
        ]

    def projections(name, which, e, g_id, x, names):
        i, when = on(name)
        tiles = len(names)
        height = tiles * attn_rows

        def source(j):
            return full[e][g_id].at[j, pl.ds(0, height)]

        @when
        def _():
            slot = lax.rem(i, 2)

            @pl.when(i == 0)
            def _():
                load(source(0), wb.at[0, pl.ds(0, height)]).start()

            load(source(0), wb.at[slot, pl.ds(0, height)]).wait()

            @pl.when(i < 3)
            def _():
                load(source(jnp.minimum(i + 1, 3)), wb.at[1 - slot, pl.ds(0, height)]).start()

            rows_in = x()
            for n, name_out in enumerate(names):
                w = wb[slot, n * attn_rows : (n + 1) * attn_rows, :]
                kept[name_out][i] = dot_nn(rows_in, w).astype(BF16)
            for copy in kv_copies(which, i, keys_of[which]):
                copy.start()

    keys_of = (
        (EK, EKX, EV, EVX),
        (DK, DKX, DV, DVX),
        (MK, MKX, MV, MVX),
    )

    def attend(name, which, q, o, lse, feats, causal):
        i, when = on(name)
        k, kx, v, vx = keys_of[which]

        @when
        def _():
            g, pair = i // 2, lax.rem(i, 2)

            @pl.when(pair == 0)
            def _():
                for copy in kv_copies(which, g, keys_of[which]):
                    copy.wait_send()
                    copy.wait_recv()

            attend_pair(
                g,
                pair,
                kept[q],
                (kept[k], kept[kx]),
                (kept[v], kept[vx]),
                kept[o],
                kept[lse],
                [feat_ref.at[f] for f in feats],
                (col_ref[...], (row_ref[0:1, :], row_ref[1:2, :])),
                causal,
            )

            @pl.when(i == 7)
            def _():
                keep(q, k, kx, v, vx, o, lse)

    def tiles4(e, g_id, first_row):
        copies = [
            load(
                full[e][g_id].at[j, pl.ds(first_row, attn_rows)],
                wb.at[0, pl.ds(j * attn_rows, attn_rows)],
                j,
            )
            for j in range(4)
        ]
        for copy in copies:
            copy.start()
        for copy in copies:
            copy.wait()

    def out_norm(name, e, g_id, first_row, residual, source, wide, rstd_name):
        _, when = on(name)

        @when
        def _():
            tiles4(e, g_id, first_row)
            total = residual()
            for j in range(4):
                total = total + dot_nt(
                    kept[source][j], wb[0, j * attn_rows : (j + 1) * attn_rows, :]
                )
            normed, rstd = norm(total)
            kept[wide][...] = normed
            kept[rstd_name][...] = jnp.broadcast_to(rstd, kept[rstd_name].shape)
            keep(wide, rstd_name)

    def flat_x(n):
        shape = xs[n].shape
        return xs[n][...].reshape(shape[0] * shape[1], shape[2])

    blocks = (
        (ENC_QKV, ENC_ATTN, ENC_OUT, EQ, EK, EV, EO, EL, EH, ER, (0, 1, 2)),
        (DEC_QKV, DEC_ATTN, DEC_OUT, DQ, DK, DV, DO, DL, DH, DR, (3, 4, 5)),
    )
    for e, (qkv, attn, out, q, k, v, o, lse, h, r, feats) in enumerate(blocks):
        pl.when(step == starts[qkv])(functools.partial(wait_tokens, e))
        projections(qkv, e, e, ATTN, functools.partial(flat_x, e), (q, k, v))
        attend(attn, e, q, o, lse, feats, e == 1)
        residual = lambda e=e: flat_x(e).astype(F32)
        out_norm(out, e, ATTN, 3 * attn_rows, residual, o, h, r)

    i, when = on(HIDDEN)
    hidden = wi.shape[2]

    @pl.when(step == starts[HIDDEN])
    def _():
        arrive(ORDER.index((0, FFN_IN)))

    def ffn_loads(j, slot):
        g, u = j // 2, lax.rem(j, 2)
        span = pl.ds(pl.multiple_of(u * hidden, 128), hidden)
        return (
            load(full[0][FFN_IN].at[g, :, span], wi.at[slot], 2 * slot),
            load(full[0][FFN_OUT].at[g, span], wo.at[slot], 2 * slot + 1),
        )

    def slope_copy(j, slot):
        g, u = j // 2, lax.rem(j, 2)
        span = pl.ds(pl.multiple_of(u * hidden, 128), hidden)
        return pltpu.make_async_copy(
            slope.at[slot], slope_out.at[g, :, span], slope_sem.at[slot]
        )

    @when
    def _():
        slot = lax.rem(i, 2)

        @pl.when(i == 0)
        def _():
            for copy in ffn_loads(0, 0):
                copy.start()
            kept[EY][...] = jnp.zeros_like(kept[EY])

        for copy in ffn_loads(i, slot):
            copy.wait()

        @pl.when(i < 7)
        def _():
            for copy in ffn_loads(i + 1, 1 - slot):
                copy.start()

        @pl.when(i >= 2)
        def _():
            slope_copy(i - 2, slot).wait()

        inner = dot_nn(kept[EH][...].astype(BF16), wi[slot])
        phi = 0.5 * (1.0 + lax.erf(inner * 0.7071067811865476))
        slope[slot] = (
            phi + inner * jnp.exp(inner * inner * -0.5) * 0.3989422804014327
        ).astype(BF16)
        slope_copy(i, slot).start()
        kept[EY][...] += dot_nn((inner * phi).astype(BF16), wo[slot])

    i, when = on(GATED)

    @when
    def _():
        for j in range(2):
            slope_copy(6 + j, j).wait()
        copy = load(full[0][ADAPTER], wad)
        copy.start()
        copy.wait()
        h = kept[EH][...]
        rows_in = h.astype(BF16)
        lanes = wad.shape[2] // 2
        extra = wad[0, attn_rows : attn_rows + 16, :].astype(F32)
        last = jnp.concatenate([extra[1 + r : 2 + r] for r in range(4)], axis=1)
        total = 4.0 * last
        for j in range(4):
            bias = wad[j, attn_rows : attn_rows + 16, :lanes].astype(F32)[0:1]
            pre = dot_nn(rows_in, wad[j, :attn_rows, :lanes]) + bias
            sig = 1.0 / (1.0 + jnp.exp(-pre))
            gated = (pre * sig).astype(BF16)
            kept[ES][j] = gated
            kept[EA][j] = (sig * (1.0 + pre * (1.0 - sig))).astype(BF16)
            total = total + 4.0 * dot_nt(gated, wad[j, :attn_rows, lanes:])
        normed, rstd = norm(h + (kept[EY][...] + total))
        kept[EY][...] = normed
        kept[EYR][...] = jnp.broadcast_to(rstd, kept[EYR].shape)
        keep(ES, EA, EY, EYR)

    projections(MEMORY, 2, 0, CROSS, lambda: kept[EY][...].astype(BF16), (MK, MV))
    _, when = on(CROSS_Q)

    @when
    def _():
        tiles4(1, CROSS, 0)
        rows_in = kept[DH][...].astype(BF16)
        for j in range(4):
            kept[CQ][j] = dot_nn(
                rows_in, wb[0, j * attn_rows : (j + 1) * attn_rows, :]
            ).astype(BF16)

    attend(CROSS_ATTN, 2, CQ, CO, CL, (3, 1, 2), False)
    out_norm(CROSS_OUT, 1, CROSS, attn_rows, lambda: kept[DH][...], CO, C2, C2R)

    @pl.when(step == steps - 1)
    def _():
        for g in (FFN_IN, FFN_OUT, ADAPTER):
            arrive(ORDER.index((1, g)))
        for n, k in items:
            pl.when(inner)(z_forward(n, k).wait_send)
            for j in range(2):
                near_copy(n, k, j).wait_send()
                forward_copy(n, k, j).wait_send()
            for j in range(4):
                sibling_copy(n, k, j).wait_send()
        for n in range(len(ORDER)):

            @pl.when(s == ORDER[n][0])
            def _():
                far(n).wait_send()
                for h in range(2):
                    z_copy(n, 1, h).wait_send()
                    pl.when(inner)(z_copy(n, 2, h).wait_send)

        for n in KEPT:
            pltpu.make_async_copy(kept[n], kept_out[n], out_sem.at[n]).wait()


def forward_call(shards, tokens, col, row, feats):
    rows, part, width = tokens.shape
    part //= 2
    length = 16 * part
    groups = len(ORDER)
    dma = pltpu.SemaphoreType.DMA
    anywhere = pl.BlockSpec(memory_space=pl.ANY)
    cols = shards[ATTN].shape[1]
    shapes = (
        ((4, length, cols), BF16),
        ((4, cols // HEAD // 2, 2, length), F32),
        ((length, width), F32),
        ((length, 128), F32),
        ((4, length, shards[ADAPTER].shape[1] // 2), BF16),
    )
    kept = [shapes[kind] for kind in KEPT.values()]
    hidden = shards[FFN_IN].shape[1]
    sizes = [
        (groups, 2, 2),
        (groups, 3),
        (groups, 3),
        (groups, 3, 2),
        (groups, 3, 2),
        (groups, 3, 2),
        (groups, 3, 2),
        (groups, 3, 4),
        (groups, 3, 4),
        (groups, 4),
        (2, 16, 2),
        (2, 16),
        (3, 4, 2),
        (3, 4, 2),
        (4,),
        (len(KEPT),),
        (2,),
    ]
    plan = plan_steps([v.size * 2 for v in shards])
    result = pl.pallas_call(
        functools.partial(forward_kernel, plan, rows),
        grid=(plan[2],),
        in_specs=[anywhere] * 6
        + [
            pl.BlockSpec(col.shape, lambda i: (0, 0)),
            pl.BlockSpec(row.shape, lambda i: (0, 0)),
            pl.BlockSpec(feats.shape, lambda i: (0, 0, 0)),
        ],
        out_specs=[anywhere] * (11 + len(KEPT)),
        out_shape=[jax.ShapeDtypeStruct((4,) + v.shape, v.dtype) for v in shards] * 2
        + [jax.ShapeDtypeStruct((4, length, hidden), BF16)]
        + [jax.ShapeDtypeStruct(*v) for v in kept],
        scratch_shapes=[pltpu.VMEM(*v) for v in kept]
        + [pltpu.VMEM((16, part, width), BF16)] * 2
        + [
            pltpu.VMEM((2,) + shards[ATTN].shape, BF16),
            pltpu.VMEM((2, width, hidden // 2), BF16),
            pltpu.VMEM((2, hidden // 2, width), BF16),
            pltpu.VMEM((4,) + shards[ADAPTER].shape, BF16),
            pltpu.VMEM((2, length, hidden // 2), BF16),
            pltpu.VMEM(shards[ATTN].shape, BF16),
            pltpu.VMEM(shards[FFN_IN].shape, BF16),
        ]
        + [dma(size) for size in sizes],
        compiler_params=pltpu.CompilerParams(
            collective_id=0, has_side_effects=True, vmem_limit_bytes=60 * 2**20
        ),
        name="forward",
    )(*shards, tokens, col, row, feats)
    return result[:5], result[5:10], result[10], result[11:]


def ids_kernel(ids, out, send, recv):
    s = lax.axis_index(SECTION)
    c = lax.axis_index(CTX)
    t = lax.axis_index(TP)
    barrier = pltpu.get_barrier_semaphore()
    for j in (1, 2, 3):
        pl.semaphore_signal(
            barrier,
            1,
            device_id=(s, lax.rem(c + j, 4), t),
            device_id_type=pl.DeviceIdType.MESH,
        )
    pl.semaphore_wait(barrier, 3)
    out[c] = ids[...]
    ways = [
        remote(ids, out.at[c], send.at[j - 1], recv.at[j - 1], (s, lax.rem(c + j, 4), t))
        for j in (1, 2, 3)
    ]
    for way in ways:
        way.start()
    for j, way in enumerate(ways):
        way.wait_send()
        region = out.at[lax.rem(c + 3 - j, 4)]
        remote(region, region, send.at[j], recv.at[j], (s, c, t)).wait_recv()


def ids_call(ids):
    spec = pl.BlockSpec(memory_space=pltpu.VMEM)
    return pl.pallas_call(
        ids_kernel,
        in_specs=[spec],
        out_specs=spec,
        out_shape=jax.ShapeDtypeStruct((4,) + ids.shape, ids.dtype),
        scratch_shapes=[pltpu.SemaphoreType.DMA((3,)), pltpu.SemaphoreType.DMA((3,))],
        compiler_params=pltpu.CompilerParams(collective_id=1, has_side_effects=True),
        name="ids",
    )(ids)


SPLIT = 1


def tail_kernel(rider, *refs):
    refs = list(refs)

    def take(count):
        got = refs[:count]
        del refs[:count]
        return got

    h_ref, w_in_ref, w_out_ref, adapter_ref = take(4)
    ride_ins = take(len(rider.inputs))
    slope_ref, s_ref, a_ref, y_ref, yr_ref, out_ref = take(6)
    ride = (ride_ins, take(len(rider.inputs)), take(len(rider.scratch)))
    rows_in, acc = refs
    step = pl.program_id(0)
    width = acc.shape[1]
    lanes = adapter_ref.shape[2] // 2

    @pl.when(step == 0)
    def _():
        rider.start(*ride)
        extra = adapter_ref[0, width : width + 16, :].astype(F32)
        cuts = width // adapter_ref.shape[2]
        last = jnp.concatenate([extra[1 + r : 2 + r] for r in range(cuts)], axis=1)
        acc[...] = h_ref[...] + 4.0 * last
        rows_in[...] = h_ref[...].astype(BF16)

    @pl.when(step < 4)
    def _():
        bias = adapter_ref[0, width : width + 16, :lanes].astype(F32)[0:1]
        pre = dot_nn(rows_in[...], adapter_ref[0, :width, :lanes]) + bias
        sig = 1.0 / (1.0 + jnp.exp(-pre))
        gated = (pre * sig).astype(BF16)
        s_ref[0] = gated
        a_ref[0] = (sig * (1.0 + pre * (1.0 - sig))).astype(BF16)
        acc[...] += 4.0 * dot_nt(gated, adapter_ref[0, :width, lanes:])

    @pl.when((step >= 4) & (step < 4 + 4 * SPLIT))
    def _():
        inner = dot_nn(rows_in[...], w_in_ref[0])
        phi = 0.5 * (1.0 + lax.erf(inner * 0.7071067811865476))
        slope_ref[0] = (
            phi + inner * jnp.exp(inner * inner * -0.5) * 0.3989422804014327
        ).astype(BF16)
        acc[...] += dot_nn((inner * phi).astype(BF16), w_out_ref[0])

    @pl.when(step == 4 + 4 * SPLIT)
    def _():
        normed, rstd = norm(acc[...])
        y_ref[...] = normed
        yr_ref[...] = jnp.broadcast_to(rstd, yr_ref.shape)
        out_ref[...] = normed.astype(BF16)
        rider.finish(*ride)


def tail_call(h, tail_w, rider):
    w_in, w_out, adapter = tail_w
    length, width = h.shape
    groups, _, hidden = w_in.shape
    lanes = adapter.shape[2] // 2
    anywhere = pl.BlockSpec(memory_space=pl.ANY)

    def tile(j):
        j = jnp.clip(j - groups, 0, groups * SPLIT - 1)
        return j // SPLIT, lax.rem(j, SPLIT)

    def group(j):
        return jnp.minimum(j, groups - 1)

    wide = pl.BlockSpec((length, width), lambda j: (0, 0))
    gated = pl.BlockSpec((1, length, lanes), lambda j: (group(j), 0, 0))
    cut = lambda rows: pl.BlockSpec(
        (1, rows, hidden // SPLIT), lambda j: (tile(j)[0], 0, tile(j)[1])
    )
    result = pl.pallas_call(
        functools.partial(tail_kernel, rider),
        grid=(groups * (1 + SPLIT) + 1,),
        in_specs=[
            wide,
            cut(width),
            pl.BlockSpec((1, hidden // SPLIT, width), lambda j: (tile(j)[0], tile(j)[1], 0)),
            pl.BlockSpec((1,) + adapter.shape[1:], lambda j: (group(j), 0, 0)),
        ]
        + [anywhere] * len(rider.inputs),
        out_specs=[
            cut(length),
            gated,
            gated,
            wide,
            pl.BlockSpec((length, 128), lambda j: (0, 0)),
            wide,
        ]
        + [anywhere] * len(rider.inputs),
        out_shape=[
            jax.ShapeDtypeStruct((groups, length, hidden), BF16),
            jax.ShapeDtypeStruct((groups, length, lanes), BF16),
            jax.ShapeDtypeStruct((groups, length, lanes), BF16),
            jax.ShapeDtypeStruct((length, width), F32),
            jax.ShapeDtypeStruct((length, 128), F32),
            jax.ShapeDtypeStruct((length, width), BF16),
        ]
        + rider.shapes,
        scratch_shapes=rider.scratch
        + [pltpu.VMEM((length, width), BF16), pltpu.VMEM((length, width), F32)],
        compiler_params=pltpu.CompilerParams(
            collective_id=rider.call_id, has_side_effects=True, vmem_limit_bytes=60 * 2**20
        ),
        name="tail",
    )(h, w_in, w_out, adapter, *rider.inputs)
    return result[:6], result[6:]


def norm_back_rows(normed, rstd, grad):
    return rstd * (
        grad
        - jnp.mean(grad, axis=-1, keepdims=True)
        - normed * jnp.mean(grad * normed, axis=-1, keepdims=True)
    )


def head_grads(da, w_ref, do_ref):
    for g in range(w_ref.shape[0]):
        do_ref[g] = dot_nn(da, w_ref[g]).astype(BF16)


def sibling_of():
    return (1 - lax.axis_index(SECTION), lax.axis_index(CTX), lax.axis_index(TP))


def tail_back_kernel(rider, *refs):
    refs = list(refs)

    def take(count):
        got = refs[:count]
        del refs[:count]
        return got

    grad_ref, y_ref, yr_ref, h_ref, hr_ref, slope_ref = take(6)
    w_out_ref, w_in_ref, adapter_ref, s_ref, a_ref, w_do_ref = take(6)
    ride_ins = take(len(rider.inputs))
    dpre_ref, do_ref, pieces_ref, tails_ref = take(4)
    ride = (ride_ins, take(len(rider.inputs)), take(len(rider.scratch)))
    db, acc, mine, away, got, send, recv = refs
    step = pl.program_id(0)
    groups = away.shape[0]
    width = acc.shape[1]
    lanes = adapter_ref.shape[2] // 2
    first = lax.axis_index(SECTION) == 0

    def to_sibling(g):
        return remote(
            away.at[g], got.at[g], send.at[g], recv.at[g], sibling_of()
        )

    @pl.when(step == 0)
    def _():
        rider.start(*ride)
        dpre = norm_back_rows(y_ref[...], yr_ref[:, 0:1], grad_ref[...].astype(F32))
        acc[...] = dpre
        db[...] = dpre.astype(BF16)

    @pl.when(step == 0)
    def _():
        branch = db[...]
        rows_in = h_ref[...].astype(BF16)
        beside = lambda r: jnp.concatenate([r[g] for g in range(groups)], axis=1)
        a_in = jnp.concatenate(
            [adapter_ref[g, :width, :lanes] for g in range(groups)], axis=1
        )
        a_out = jnp.concatenate(
            [adapter_ref[g, :width, lanes:] for g in range(groups)], axis=1
        )
        ds = 4.0 * dot_nn(branch, a_out)
        du = (ds * beside(a_ref).astype(F32)).astype(BF16)
        acc[...] += dot_nt(du, a_in)
        d_in = dot_tn(du, rows_in)
        d_out = 4.0 * dot_tn(beside(s_ref), branch)
        last = 4.0 * jnp.sum(branch.astype(F32), axis=0, keepdims=True)
        bias = jnp.sum(du.astype(F32), axis=0, keepdims=True)
        cut = width // 4
        blank = jnp.zeros((1, cut - lanes), F32)
        row = lax.broadcasted_iota(jnp.int32, (16, cut), 0)
        part = lanes // 4
        for g in range(groups):
            own = bias[:, g * lanes : (g + 1) * lanes]
            second = jnp.where(row == 1, jnp.concatenate([own, blank], axis=1), 0.0)
            for c in range(4):
                start = g * lanes + c * part
                one = d_in[start : start + part]
                two = d_out[start : start + part]
                mine[g, c] = jnp.where(first, one, two)
                away[g, c] = jnp.where(first, two, one).astype(BF16)
                tails_ref[c, g] = jnp.where(
                    row == 0, last[:, c * cut : (c + 1) * cut], second
                ).astype(BF16)
            to_sibling(g).start()

    @pl.when((step >= 1) & (step < 1 + groups * SPLIT))
    def _():
        dg = dot_nt(db[...], w_out_ref[0])
        df = (dg * slope_ref[0].astype(F32)).astype(BF16)
        acc[...] += dot_nt(df, w_in_ref[0])

    @pl.when(step == 1 + groups * SPLIT)
    def _():
        dpre = norm_back_rows(h_ref[...], hr_ref[:, 0:1], acc[...])
        dpre_ref[...] = dpre
        head_grads(dpre.astype(BF16), w_do_ref, do_ref)
        for g in range(groups):
            copy = to_sibling(g)
            copy.wait_send()
            copy.wait_recv()
            for c in range(4):
                pieces_ref[c, g] = (mine[g, c] + got[g, c].astype(F32)).astype(BF16)
        rider.finish(*ride)


def tail_back(grad, y, yr, h, hr, slope, tail_w, s_act, a_slope, w_do, do_block, rider):
    w_in, w_out, adapter = tail_w
    length, width = y.shape
    groups, _, hidden = slope.shape
    lanes = s_act.shape[2]
    cols = w_do.shape[2]
    part = lanes // 4
    anywhere = pl.BlockSpec(memory_space=pl.ANY)

    def whole(v):
        return pl.BlockSpec(v.shape, lambda j: (0, 0))

    def tile(j):
        j = jnp.clip(j - 1, 0, groups * SPLIT - 1)
        return j // SPLIT, lax.rem(j, SPLIT)

    result = pl.pallas_call(
        functools.partial(tail_back_kernel, rider),
        grid=(groups * SPLIT + 2,),
        in_specs=[whole(v) for v in (grad, y, yr, h, hr)]
        + [
            pl.BlockSpec((1, length, hidden // SPLIT), lambda j: (tile(j)[0], 0, tile(j)[1])),
            pl.BlockSpec((1, hidden // SPLIT, width), lambda j: (tile(j)[0], tile(j)[1], 0)),
            pl.BlockSpec((1, width, hidden // SPLIT), lambda j: (tile(j)[0], 0, tile(j)[1])),
            pl.BlockSpec(adapter.shape, lambda j: (0, 0, 0)),
            pl.BlockSpec((groups, length, lanes), lambda j: (0, 0, 0)),
            pl.BlockSpec((groups, length, lanes), lambda j: (0, 0, 0)),
            pl.BlockSpec((groups, width, cols), lambda j: (0, do_block, 0)),
        ]
        + [anywhere] * len(rider.inputs),
        out_specs=[
            pl.BlockSpec((length, width), lambda j: (0, 0)),
            pl.BlockSpec((groups, length, cols), lambda j: (0, 0, 0)),
            pl.BlockSpec((4, groups, part, width), lambda j: (0, 0, 0, 0)),
            pl.BlockSpec((4, groups, 16, width // 4), lambda j: (0, 0, 0, 0)),
        ]
        + [anywhere] * len(rider.inputs),
        out_shape=[
            jax.ShapeDtypeStruct((length, width), F32),
            jax.ShapeDtypeStruct((groups, length, cols), BF16),
            jax.ShapeDtypeStruct((4, groups, part, width), BF16),
            jax.ShapeDtypeStruct((4, groups, 16, width // 4), BF16),
        ]
        + rider.shapes,
        scratch_shapes=rider.scratch
        + [
            pltpu.VMEM((length, width), BF16),
            pltpu.VMEM((length, width), F32),
            pltpu.VMEM((groups, 4, part, width), F32),
            pltpu.VMEM((groups, 4, part, width), BF16),
            pltpu.VMEM((groups, 4, part, width), BF16),
            pltpu.SemaphoreType.DMA((groups,)),
            pltpu.SemaphoreType.DMA((groups,)),
        ],
        compiler_params=pltpu.CompilerParams(
            collective_id=rider.call_id, has_side_effects=True, vmem_limit_bytes=60 * 2**20
        ),
        name="tail_back",
    )(grad, y, yr, h, hr, slope, w_out, w_in, adapter, s_act, a_slope, w_do, *rider.inputs)
    return result[:2], result[2:4], result[4:]


def attn_back_kernel(causal, cross, rider, *refs):
    refs = list(refs)

    def take(count):
        got = refs[:count]
        del refs[:count]
        return got

    q_ref, k_ref, kx_ref, v_ref, vx_ref, o_ref, do_ref, lse_ref = take(8)
    if cross:
        wq_ref, wkv_ref, rest_ref, h_ref, hr_ref, w_do_ref = take(6)
    else:
        w_ref, rest_ref = take(2)
    feats, (qi_ref, ki_ref) = take(3), take(2)
    ride_ins = take(len(rider.inputs))
    if cross:
        dpre_ref, do_next_ref, memory_ref = take(3)
    else:
        (dx_ref,) = take(1)
    ride_outs = take(len(rider.inputs))
    ride_sems = take(len(rider.scratch))
    ride = (ride_ins, ride_outs, ride_sems)
    dq_s, own_k, own_v, away_k, away_v, got_k, got_v, acc, send, recv = take(10)
    if cross:
        (acc2,) = take(1)
    step = pl.program_id(0)
    groups = away_k.shape[0]
    width = acc.shape[1]

    def to_sibling(g):
        return [
            remote(a.at[g], b.at[g], send.at[g, j], recv.at[g, j], sibling_of())
            for j, (a, b) in enumerate(((away_k, got_k), (away_v, got_v)))
        ]

    @pl.when(step == 0)
    def _():
        rider.start(*ride)
        acc[...] = rest_ref[...]
        if cross:
            acc2[...] = jnp.zeros_like(acc2)

    @pl.when(step > 0)
    def _():
        g = step - 1
        slot = lax.rem(g, 2)
        for copy in to_sibling(g):
            copy.wait_send()
            copy.wait_recv()
        dk = (own_k[slot] + got_k[g].astype(F32)).astype(BF16)
        dv = (own_v[slot] + got_v[g].astype(F32)).astype(BF16)
        dq = dq_s[slot]
        if cross:
            acc[...] += dot_nt(dq, wq_ref[0])
            acc2[...] += dot_nt(dk, wkv_ref[0, :width]) + dot_nt(dv, wkv_ref[0, width:])
        else:
            acc[...] += (
                dot_nt(dq, w_ref[0, :width])
                + dot_nt(dk, w_ref[0, width : 2 * width])
                + dot_nt(dv, w_ref[0, 2 * width :])
            )

    @pl.when(step < groups)
    def _():
        slot = lax.rem(step, 2)
        attend_back_group(
            (q_ref, (k_ref, kx_ref), (v_ref, vx_ref), o_ref, do_ref, lse_ref),
            (dq_s, slot),
            ((own_k, slot), (away_k, step)),
            ((own_v, slot), (away_v, step)),
            feats,
            qi_ref,
            ki_ref,
            causal,
        )
        for copy in to_sibling(step):
            copy.start()

    @pl.when(step == groups)
    def _():
        if cross:
            dpre = norm_back_rows(h_ref[...], hr_ref[:, 0:1], acc[...])
            dpre_ref[...] = dpre
            head_grads(dpre.astype(BF16), w_do_ref, do_next_ref)
            memory_ref[...] = acc2[...]
        else:
            dx_ref[...] = acc[...].astype(dx_ref.dtype)
        rider.finish(*ride)


def attn_back(heads, ids, causal, rider, rest, weights, cross=None):
    groups, length, cols = heads[0].shape
    width = rest.shape[1]
    anywhere = pl.BlockSpec(memory_space=pl.ANY)

    def now(shape):
        return pl.BlockSpec((1,) + shape[1:], lambda t: (jnp.minimum(t, groups - 1), 0, 0))

    def past(rows):
        return pl.BlockSpec((1, rows, cols), lambda t: (jnp.maximum(t - 1, 0), 0, 0))

    def whole(v):
        return pl.BlockSpec(v.shape, lambda t: (0,) * len(v.shape))

    wide = jax.ShapeDtypeStruct((length, width), F32)
    if cross:
        h, hr, w_do = cross
        wq, wkv = weights
        extra = [wq, wkv, rest, h, hr, w_do]
        specs = [
            past(width),
            past(2 * width),
            whole(rest),
            whole(h),
            whole(hr),
            pl.BlockSpec((groups, width, cols), lambda t: (0, 3, 0)),
        ]
        outs = [wide, jax.ShapeDtypeStruct(heads[0].shape, BF16), wide]
    else:
        extra = [weights, rest]
        specs = [past(3 * width), whole(rest)]
        outs = [jax.ShapeDtypeStruct((length, width), BF16)]
    moving = pltpu.VMEM((groups, length, cols), BF16)
    result = pl.pallas_call(
        functools.partial(attn_back_kernel, causal, bool(cross), rider),
        grid=(groups + 1,),
        in_specs=[now(v.shape) for v in heads]
        + specs
        + [whole(v) for v in ids]
        + [anywhere] * len(rider.inputs),
        out_specs=[whole(v) for v in outs] + [anywhere] * len(rider.inputs),
        out_shape=outs + rider.shapes,
        scratch_shapes=rider.scratch
        + [
            pltpu.VMEM((2, length, cols), BF16),
            pltpu.VMEM((2, length, cols), F32),
            pltpu.VMEM((2, length, cols), F32),
            moving,
            moving,
            moving,
            moving,
            pltpu.VMEM((length, width), F32),
            pltpu.SemaphoreType.DMA((groups, 2)),
            pltpu.SemaphoreType.DMA((groups, 2)),
        ]
        + ([pltpu.VMEM((length, width), F32)] if cross else []),
        compiler_params=pltpu.CompilerParams(
            collective_id=rider.call_id,
            has_side_effects=True,
            vmem_limit_bytes=60 * 2**20,
        ),
        name="attn_back",
    )(*heads, *extra, *ids, *rider.inputs)
    return result[: len(outs)], result[len(outs) :]


def gather_plain(entry, shards):
    full = [lax.all_gather(lax.all_gather(v, TP), SECTION) for v in shards]
    return [v[entry] for v in full]


def spread(blocks):
    chips = lax.axis_size(CTX) * lax.axis_size(TP)
    kinds, rows, part, width = blocks.shape
    blocks = jnp.pad(blocks, ((0, 0), (0, chips - rows), (0, 0), (0, 0)))
    moved = lax.all_to_all(
        jnp.moveaxis(blocks, 1, 0), (CTX, TP), 0, 0, tiled=True
    )
    return jnp.moveaxis(moved, 0, 1).reshape(kinds, chips * part, width)


def collect(tokens, rows):
    chips = lax.axis_size(CTX) * lax.axis_size(TP)
    kinds, length, width = tokens.shape
    part = length // chips
    blocks = jnp.moveaxis(tokens.reshape(kinds, chips, part, width), 1, 0)
    moved = lax.all_to_all(blocks, (CTX, TP), 0, 0, tiled=True)
    return jnp.moveaxis(moved, 0, 1)[:, :rows]


def per_device(
    layer_inputs,
    out_grad,
    src_seg,
    tgt_seg,
    qkv_weights,
    out_weights,
    cross_weights,
    ffn_in,
    ffn_out,
    adapter_in,
    adapter_in_bias,
    adapter_out,
    adapter_out_bias,
):
    core = lax.axis_index(SECTION)
    is_first = core == 0
    tp = lax.axis_size(TP)
    chips = lax.axis_size(CTX) * tp
    chip = lax.axis_index(CTX) * tp + lax.axis_index(TP)
    _, micro, per_micro, part, width = layer_inputs.shape
    row_count = micro * per_micro
    half = part // 2
    length = half * chips

    def pick(first, second):
        return jnp.where(is_first, first, second)

    x = layer_inputs.reshape(row_count, part, width)
    grads = out_grad.reshape(row_count, part, width)
    grads = pick(grads[:, :half], grads[:, half:])
    near = lax.axis_size(CTX) == 4 and tp == 4
    lanes = adapter_in_bias.shape[1]
    cols = out_weights.shape[2]
    pad = lambda v, n: jnp.pad(v, [(0, n - v.shape[0])] + [(0, 0)] * (v.ndim - 1))
    biases = jnp.concatenate(
        [pad(adapter_in_bias[0], cols)[None], adapter_out_bias[0].reshape(-1, cols)]
    )
    shards = [
        jnp.concatenate([qkv_weights[0], out_weights], axis=0).reshape(-1, cols),
        ffn_in[0],
        ffn_out[0],
        jnp.concatenate(
            [
                jnp.concatenate([adapter_in[0], adapter_out[0].T], axis=1),
                pad(biases, 256),
            ],
            axis=0,
        ),
        cross_weights[0].reshape(-1, cols),
    ]
    if near:
        ids = ids_call(jnp.stack([src_seg, tgt_seg]).reshape(2 * row_count, -1))
        flat_ids = ids.swapaxes(0, 1).reshape(2, row_count, -1)
    else:
        flat_ids = [
            lax.all_gather(v.reshape(row_count, -1), CTX, axis=1, tiled=True)
            for v in (src_seg, tgt_seg)
        ]

    def unpack(full):
        attn, w_in, w_out, adapter, cross = full
        attn = attn.reshape(tp, 4, -1, cols)
        cross = cross.reshape(tp, 2, -1, cols)
        b_out = adapter[0, width + 1 : width + 1 + width // cols].reshape(width)
        tail = (
            w_in,
            w_out,
            adapter[:, :width, :lanes],
            adapter[:, width, :lanes],
            adapter[:, :width, lanes:],
            b_out,
        )
        return attn, cross, tail

    def ids_of(flat):
        row = lax.dynamic_index_in_dim(
            flat, jnp.minimum(chip, row_count - 1), 0, keepdims=False
        )
        return row.reshape(chips, 2, half)

    index = jnp.arange(length, dtype=jnp.int32)
    place = (index // half) * part + index % half

    def cut(seg, which):
        own = lax.dynamic_index_in_dim(seg, which, 1, keepdims=False).reshape(length)
        return own, place + which * half

    src_ids, tgt_ids = ids_of(flat_ids[0]), ids_of(flat_ids[1])

    def id_arrays(seg_q, seg_k):
        qi = jnp.stack(cut(seg_q, core))
        ki = jnp.stack(cut(seg_k, core) + cut(seg_k, 1 - core))
        return (qi.T, ki), (qi, ki.T)

    enc_ids = id_arrays(src_ids, src_ids)
    dec_ids = id_arrays(tgt_ids, tgt_ids)
    cross_ids = id_arrays(tgt_ids, src_ids)

    def scatter(arrays, call_id):
        return Scatter(arrays, row_count, call_id) if near else None

    def tokens(value):
        return value.astype(BF16).reshape(chips, half, width)

    def scatter(arrays, call_id):
        return Scatter(arrays, row_count, call_id) if near else None

    def tokens(value):
        return value.astype(BF16).reshape(chips, half, width)

    if near:
        src_own, place_own = cut(src_ids, core)
        src_oth, place_oth = cut(src_ids, 1 - core)
        tgt_own, tgt_oth = cut(tgt_ids, core)[0], cut(tgt_ids, 1 - core)[0]
        feats = jnp.stack(
            [
                id_columns(src_own, False),
                id_columns(src_own, True),
                id_columns(src_oth, True),
                id_columns(tgt_own, False),
                id_columns(tgt_own, True),
                id_columns(tgt_oth, True),
            ]
        )
        enc_w, dec_w, slope, kept = forward_call(
            shards,
            x,
            place_own[:, None],
            jnp.stack([place_own, place_oth] * 4),
            feats,
        )
        (dec_slope, dec_s, dec_a, dec_y, dec_yr, decoded), (placed,) = tail_call(
            kept[C2],
            (dec_w[1], dec_w[2], dec_w[3]),
            scatter([(grads, Scatter.BRING)], 8),
        )
        cotangent = placed.reshape(length, width)
        encoded_bf = kept[EY].astype(BF16)
    else:
        low, high = x[:, :half], x[:, half:]
        other = swap(pick(high, low))
        source, target, cotangent = spread(
            jnp.stack([pick(low, other), pick(other, high), grads])
        )
        enc_attn, enc_cross, enc_tail_w = unpack(gather_plain(0, shards))
        dec_attn, dec_cross, dec_tail_w = unpack(gather_plain(1, shards))
        enc_mid, enc_self = self_forward(
            source, source.astype(F32), enc_attn, enc_ids, False
        )
        encoded, enc_tail = tail_forward(enc_mid, enc_tail_w)
        encoded_bf = encoded.astype(BF16)
        memory = [project(encoded_bf, enc_cross[:, j]).astype(BF16) for j in range(2)]
        memory_other = swap(jnp.stack(memory))
        mem_keys = (memory[0], memory_other[0], memory[1], memory_other[1])
        dec_mid, dec_self = self_forward(
            target, target.astype(F32), dec_attn, dec_ids, True
        )
        queries = project(dec_mid.astype(BF16), dec_cross[:, 0]).astype(BF16)
        cross_o, cross_lse = attention_forward(
            queries, mem_keys, cross_ids[0], False
        )
        second, second_rstd = norm(dec_mid + unproject(cross_o, dec_cross[:, 1]))
        decoded, dec_tail = tail_forward(second, dec_tail_w)

    if near:

        def heads(q, k, kx, v, vx, o, lse, do):
            flat = kept[lse].reshape(kept[lse].shape[0], -1, length)
            return [kept[n] for n in (q, k, kx, v, vx, o)] + [do, flat]

        def pieces(parts):
            return [v.reshape((chips,) + v.shape[2:]) for v in parts]

        (grad_cross, do), dec_parts, _ = tail_back(
            cotangent,
            dec_y,
            dec_yr,
            kept[C2],
            kept[C2R],
            dec_slope,
            (dec_w[1], dec_w[2], dec_w[3]),
            dec_s,
            dec_a,
            dec_w[4],
            1,
            scatter([], 2),
        )
        (dpre, do, grad_encoded), (out_enc, out_dec) = attn_back(
            heads(CQ, MK, MKX, MV, MVX, CO, CL, do),
            [feats[3], feats[1], feats[2], *cross_ids[1]],
            False,
            scatter([(tokens(encoded_bf), 0), (tokens(decoded), 1)], 3),
            grad_cross,
            (dec_w[4], enc_w[4]),
            (kept[DH], kept[DR], dec_w[0]),
        )
        (grad_target,), dec_sum = attn_back(
            heads(DQ, DK, DKX, DV, DVX, DO, DL, do),
            [feats[3], feats[4], feats[5], *dec_ids[1]],
            True,
            scatter([(v, 1) for v in pieces(dec_parts)], 4),
            dpre,
            dec_w[0],
        )
        (dpre, do), enc_parts, (moved,) = tail_back(
            grad_encoded,
            kept[EY],
            kept[EYR],
            kept[EH],
            kept[ER],
            slope,
            (enc_w[1], enc_w[2], enc_w[3]),
            kept[ES],
            kept[EA],
            enc_w[0],
            3,
            scatter([(tokens(grad_target), 1)], 5),
        )
        (grad_source,), enc_sum = attn_back(
            heads(EQ, EK, EKX, EV, EVX, EO, EL, do),
            [feats[0], feats[1], feats[2], *enc_ids[1]],
            False,
            scatter([(v, 0) for v in pieces(enc_parts)], 6),
            dpre,
            enc_w[0],
        )
        outs = pick(out_enc, out_dec)
        sums, ends = [
            jnp.sum(pick(a, b).astype(F32), axis=0) for a, b in zip(enc_sum, dec_sum)
        ]
        part_rows = lanes // 4
        ends = jnp.pad(jnp.sum(ends, axis=0), ((0, 0), (0, width - width // 4)))
        mine = jnp.concatenate([sums.reshape(2 * part_rows, width), ends]).astype(BF16)
        (last,), whole = send_call(scatter([(tokens(grad_source), 0)], 7), mine)
        grads = pick(last, moved).astype(F32)
        whole = whole.astype(F32)
        weights = whole[:, : 2 * part_rows].reshape(4, 2, part_rows, width)
        ends = whole[:, 2 * part_rows :, : width // 4]
        return (
            outs.reshape(layer_inputs.shape),
            grads.reshape(layer_inputs.shape),
            weights[:, 0].reshape(lanes, width).T[None],
            ends[0, 1, :lanes][None],
            weights[:, 1].reshape(1, lanes, width),
            ends[:, 0].reshape(1, width),
        )

    grad_second, dec_terms = tail_backward(cotangent.astype(F32), dec_tail, dec_tail_w)
    grad_cross = norm_back(second, second_rstd, grad_second)
    do = project(grad_cross.astype(BF16), dec_cross[:, 1]).astype(BF16)
    dqc, dmk, dmv = attend_back(
        queries, mem_keys, cross_o, do, cross_lse, cross_ids, False
    )
    grad_first = unproject(dqc, dec_cross[:, 0]) + grad_cross
    grad_target = self_backward(grad_first, dec_self, dec_attn, dec_ids, True)

    grad_encoded = unproject(dmk, enc_cross[:, 0]) + unproject(dmv, enc_cross[:, 1])
    grad_mid, enc_terms = tail_backward(grad_encoded, enc_tail, enc_tail_w)
    grad_source = self_backward(grad_mid, enc_self, enc_attn, enc_ids, False)

    has_row = chip < row_count

    def total(enc_term, dec_term):
        enc_term = jnp.where(has_row, enc_term, 0.0).astype(BF16)
        dec_term = jnp.where(has_row, dec_term, 0.0).astype(BF16)
        got = swap(pick(dec_term, enc_term))
        return (pick(enc_term, dec_term).astype(F32) + got.astype(F32)).astype(BF16)

    sums = [total(e, d) for e, d in zip(enc_terms, dec_terms)]
    scattered = [
        lax.psum_scatter(v, TP, scatter_dimension=0, tiled=False) for v in sums[:3]
    ]
    scattered = [lax.psum(v, CTX).astype(F32) for v in scattered]
    bias_sum = lax.psum(sums[3], (CTX, TP)).astype(F32)

    results = jnp.stack(
        [
            encoded_bf,
            decoded.astype(BF16),
            grad_source.astype(BF16),
            grad_target.astype(BF16),
        ]
    )
    placed = collect(results, row_count)

    def join(enc_part, dec_part):
        mine = pick(enc_part, dec_part)
        got = swap(pick(dec_part, enc_part))
        return jnp.concatenate([pick(mine, got), pick(got, mine)], axis=1)

    outs = join(placed[0], placed[1]).reshape(layer_inputs.shape)
    grads = join(placed[2], placed[3]).astype(F32).reshape(layer_inputs.shape)
    return (
        outs,
        grads,
        scattered[0][None],
        scattered[1][None],
        scattered[2].T[None],
        bias_sum[None],
    )


def solution(mesh):
    return jax.shard_map(
        per_device,
        mesh=mesh,
        in_specs=(
            P(SECTION, None, None, (CTX, TP), None),
            P(None, None, (CTX, TP), None),
            P(None, None, CTX),
            P(None, None, CTX),
            P(SECTION, None, None, TP),
            P(SECTION, None, TP),
            P(SECTION, None, None, TP),
            P(SECTION, None, TP),
            P(SECTION, TP, None),
            P(SECTION, None, TP),
            P(SECTION, TP),
            P(SECTION, TP, None),
            P(SECTION, None),
        ),
        out_specs=(
            P(SECTION, None, None, (CTX, TP), None),
            P(SECTION, None, None, (CTX, TP), None),
            P(SECTION, None, TP),
            P(SECTION, TP),
            P(SECTION, TP, None),
            P(SECTION, None),
        ),
        check_vma=False,
    )
```
